32 devices in a mesh: grid: 4 (over x, core), mark: 8 (over z, y).
Axes of the slice: x: 2, y: 2, z: 4, core: 2. Of those that a mesh axis runs over, the one named last changes fastest.
Arguments:
- velocity: float32 [3, 128, 128, 256], P(None, 'grid', 'mark'), may hold values from -6 to 6
- pressure: float32 [128, 128, 256], P('grid', 'mark'), may hold values from -6 to 6
- cell_visc: float32 [128, 128, 256], P('grid', 'mark'), may hold values from 0.2 to 5
- cell_dens: float32 [128, 128, 256], P('grid', 'mark'), may hold values from 0.5 to 1.5
- block_brick: int32 [256, 48], P(('grid', 'mark')), may hold values from 0 to 1023
- block_counts: int32 [32, 8], P(('grid', 'mark')), may hold values from 0 to 48, as said below
- positions: float32 [256, 3, 48, 256], P(('grid', 'mark')), may hold values from 0 to 1
- start_visc: float32 [256, 48, 256], P(('grid', 'mark')), may hold values from 0.2 to 5
- marker_dens: float32 [256, 48, 256], P(('grid', 'mark')), may hold values from 0.5 to 1.5
Outputs:
- velocity_next: float32 [3, 128, 128, 256], P(None, 'grid', 'mark')
- pressure_next: float32 [128, 128, 256], P('grid', 'mark')
- visc_next: float32 [128, 128, 256], P('grid', 'mark')
- dens_next: float32 [128, 128, 256], P('grid', 'mark')
- marker_visc: float32 [256, 48, 256], P(('grid', 'mark'))
The draws below stay inside these ranges and needn't reach their ends.
Inputs may be any that keep to these rules, and one draw needn't show every extreme that they name: `block_counts`: entry q of a marker device's row counts its live slots toward the grid device of mark index q in its group; in every group some grid device gets exactly 48 live slots from every marker device. `block_brick`: dead slots name bricks too.
All inputs are finite; a program needn't handle non-finite values.
Results may differ from the reference program's by a relative error of at most 0.0003.
Values sent between devices are 32-bit elements; how exact they have to be, the bound alone decides.
No kernel may reach another device: no remote copies, remote signals or barrier semaphores. Data moves between devices by JAX's collectives and lax.ppermute only.
A program may use at most 128 MiB of HBM per device.

```python
import math
import jax
import jax.numpy as jnp
from jax import lax

CX = 32
CY = 16
CZ = 256
CAP = 48
BLOCK = 256
ITERS = 4
NX = 128
NY = 128
BRICKS_DEV = 1024
SLOT_ROWS = 256
N_GRID = 4
N_MARK = 8


def draw_block_counts(key, part):
    key = jax.random.fold_in(key, 11)
    level_key, count_key, owner_key = jax.random.split(key, 3)
    levels = jax.random.randint(level_key, (N_GRID * N_MARK, 1), 0, 4)
    ceiling = jnp.array([CAP // 8, CAP // 4, CAP // 2, CAP], dtype=jnp.int32)[levels]
    lowest = ceiling // 2
    counts = jax.random.randint(count_key, (N_GRID * N_MARK, N_MARK), lowest, ceiling + 1)
    full_owner = jax.random.randint(owner_key, (N_GRID, 1), 0, N_MARK)
    chosen = jnp.repeat(full_owner, N_MARK, axis=0) == jnp.arange(N_MARK, dtype=jnp.int32)[None, :]
    return jnp.where(chosen, CAP, counts).astype(jnp.int32)


def set_ends(entries, stream_key, smallest, top_value):
    shape = entries.shape
    spot = [jax.random.randint(jax.random.fold_in(stream_key, axis), (), 0, shape[axis]) for axis in range(len(shape))]
    entries = entries.at[tuple(spot)].set(smallest)
    longest = shape.index(max(shape))
    spot[longest] = (spot[longest] + 1) % shape[longest]
    return entries.at[tuple(spot)].set(top_value)


def block_levels(own_key, dims, cuts, smallest, largest):
    loudness, own = 1.0, jax.random.fold_in(own_key, 6)
    for dim, shards_of in cuts:
        steps = jnp.exp(jax.random.uniform(jax.random.fold_in(own, dim), (shards_of,), jnp.float32, smallest / len(cuts), largest / len(cuts)))
        loudness = loudness * jnp.repeat(steps, dims[dim] // shards_of).reshape([-1 if axis == dim else 1 for axis in range(len(dims))])
    return loudness


def scatter_about(key, dims, deviation, most, cuts=(), kind=jnp.bfloat16):
    result = jax.random.normal(key, dims, jnp.float32) * deviation
    if len(cuts) > 0:
        result = block_levels(key, dims, cuts, -0.22, 0.18) * result
    return jnp.clip(result, min=-most, max=most).astype(kind)


def setup_inputs(seed: int = 0) -> dict:
    keys = jax.random.split(jax.random.key(seed), 10)
    velocity = scatter_about(keys[0], (3, NX, NY, CZ), 1.0, 6.0, ((1, 4), (2, 8)), jnp.float32)
    pressure = scatter_about(keys[1], (NX, NY, CZ), 1.0, 6.0, ((0, 4), (1, 8)), jnp.float32)
    cell_visc = jnp.clip(jnp.exp(math.log(5.0) - 3.218876 * jax.random.uniform(keys[2], (NX, NY, CZ), jnp.float32) ** block_levels(keys[2], (NX, NY, CZ), ((0, 4), (1, 8)), -0.2, 0.2)), 0.2, 5.0)
    cell_dens = jnp.clip(0.5 + 1.0 * jax.random.uniform(keys[3], (NX, NY, CZ), jnp.float32) ** block_levels(keys[3], (NX, NY, CZ), ((0, 4), (1, 8)), -0.2, 0.2), 0.5, 1.5)
    block_brick = set_ends(jax.random.randint(keys[4], (SLOT_ROWS, CAP), 0, BRICKS_DEV), jax.random.fold_in(keys[4], 1), 0, BRICKS_DEV - 1).astype(jnp.int32)
    block_counts = draw_block_counts(jax.random.fold_in(keys[9], 71), 0)
    positions = jnp.clip(1.0 * jax.random.uniform(keys[6], (SLOT_ROWS, 3, CAP, BLOCK), jnp.float32) ** block_levels(keys[6], (SLOT_ROWS, 3, CAP, BLOCK), ((0, 32),), -0.2, 0.2), 0.0, 1.0)
    start_visc = jnp.clip(jnp.exp(math.log(5.0) - 3.218876 * jax.random.uniform(keys[7], (SLOT_ROWS, CAP, BLOCK), jnp.float32) ** block_levels(keys[7], (SLOT_ROWS, CAP, BLOCK), ((0, 32),), -0.2, 0.2)), 0.2, 5.0)
    marker_dens = jnp.clip(0.5 + 1.0 * jax.random.uniform(keys[8], (SLOT_ROWS, CAP, BLOCK), jnp.float32) ** block_levels(keys[8], (SLOT_ROWS, CAP, BLOCK), ((0, 32),), -0.2, 0.2), 0.5, 1.5)
    return {"velocity": velocity, "pressure": pressure, "cell_visc": cell_visc, "cell_dens": cell_dens, "block_brick": block_brick, "block_counts": block_counts, "positions": positions, "start_visc": start_visc, "marker_dens": marker_dens}


relax_weight = 0.6
pressure_rate = 0.25
gravity = 1.0
strain_scale = 0.5


def neighbours(padded):
    centre = padded[1:-1, 1:-1, 1:-1]
    return centre, [padded[2:, 1:-1, 1:-1], padded[:-2, 1:-1, 1:-1], padded[1:-1, 2:, 1:-1], padded[1:-1, :-2, 1:-1], padded[1:-1, 1:-1, 2:], padded[1:-1, 1:-1, :-2]]


def relax_sweep(padded_velocity, padded_pressure, padded_visc, density):
    viscosity, visc_near = neighbours(padded_visc)
    couplings = [0.5 * (viscosity + nearby) for nearby in visc_near]
    diagonal = sum(couplings)
    pressure, pressure_near = neighbours(padded_pressure)
    divergence = jnp.zeros_like(pressure)
    updated = []
    for component in range(3):
        current, current_near = neighbours(padded_velocity[component])
        laplace = sum(weight * (nearby - current) for weight, nearby in zip(couplings, current_near))
        forcing = laplace - (pressure - pressure_near[2 * component + 1])
        if component == 2:
            forcing = forcing - gravity * density
        updated.append(current + relax_weight * forcing / diagonal)
        divergence = divergence + current_near[2 * component] - current
    return jnp.stack(updated), pressure - pressure_rate * viscosity * divergence


def kernel(fraction, number_cells):
    position = fraction * number_cells
    centres = jnp.arange(number_cells, dtype=jnp.float32) + 0.5
    offset = position[:, None, :] - centres[None, :, None]
    gaussian = jnp.exp(-offset * offset)
    weights = gaussian / jnp.sum(gaussian, axis=1, keepdims=True)
    slopes = weights * (2.0 * jnp.sum(weights * offset, axis=1, keepdims=True) - 2.0 * offset)
    return weights, slopes


def marker_blocks(bricks, positions, start_visc, density, live_slots):
    highest = lax.Precision.HIGHEST
    blocks = bricks.shape[0]
    markers = positions.shape[-1]
    across_x, slope_x = kernel(positions[0], 4)
    across_y, slope_y = kernel(positions[1], 4)
    across_z, slope_z = kernel(positions[2], 8)
    values = bricks.reshape(blocks, 48, 8)
    interpolated = jnp.einsum("kcz,kzm->kcm", values, across_z, precision=highest).reshape(blocks, 3, 4, 4, markers)
    rising = jnp.einsum("kcz,kzm->kcm", values, slope_z, precision=highest).reshape(blocks, 3, 4, 4, markers)
    plane_xy = across_x[:, :, None, :] * across_y[:, None, :, :]
    plane_dx = slope_x[:, :, None, :] * across_y[:, None, :, :]
    plane_dy = across_x[:, :, None, :] * slope_y[:, None, :, :]
    grad_x = jnp.sum(interpolated * plane_dx[:, None], axis=(2, 3))
    grad_y = jnp.sum(interpolated * plane_dy[:, None], axis=(2, 3))
    grad_z = jnp.sum(rising * plane_xy[:, None], axis=(2, 3))
    normal = grad_x[:, 0] ** 2 + grad_y[:, 1] ** 2 + grad_z[:, 2] ** 2
    shear_xy = 0.5 * (grad_y[:, 0] + grad_x[:, 1])
    shear_xz = 0.5 * (grad_z[:, 0] + grad_x[:, 2])
    shear_yz = 0.5 * (grad_z[:, 1] + grad_y[:, 2])
    invariant = 0.5 * normal + shear_xy ** 2 + shear_xz ** 2 + shear_yz ** 2
    weakened = start_visc * jnp.exp(-jnp.log(1.0 + invariant / (strain_scale * strain_scale)) / 3.0)
    marker_visc = jnp.where(live_slots[:, None], weakened, 0.0)
    filled = jnp.broadcast_to(live_slots[:, None], weakened.shape).astype(jnp.float32)
    carried = jnp.stack([filled, filled * jnp.log(weakened), filled * density], axis=1)
    spread = (carried[:, :, None, None, :] * plane_xy[:, None]).reshape(blocks, 48, markers)
    moments = jnp.einsum("kcm,kzm->kcz", spread, across_z, precision=highest).reshape(blocks, 384)
    return marker_visc, moments


def reference(velocity, pressure, cell_visc, cell_dens, block_brick, block_counts, positions, start_visc, marker_dens):
    padded_visc = jnp.pad(cell_visc, 1)
    velocity_now, pressure_now = velocity, pressure
    for iteration in range(ITERS):
        velocity_now, pressure_now = relax_sweep(jnp.pad(velocity_now, ((0, 0), (1, 1), (1, 1), (1, 1))), jnp.pad(pressure_now, 1), padded_visc, cell_dens)
    shaped = velocity.reshape(3, N_GRID, CX // 4, 4, N_MARK, CY // 4, 4, CZ // 8, 8)
    bricks = shaped.transpose(1, 4, 2, 5, 7, 0, 3, 6, 8).reshape(N_GRID, N_MARK, BRICKS_DEV, 384)
    owners = jnp.arange(N_MARK, dtype=jnp.int32)
    devices = N_GRID * N_MARK

    def visit_device(totals, inputs):
        device, brick_ids, counts, places, visc_start, dens_start = inputs
        group_index = device // N_MARK
        group_bricks = bricks[group_index]
        fetched = group_bricks[owners[:, None], brick_ids]
        live_slots = (jnp.arange(CAP, dtype=jnp.int32)[None, :] < counts[:, None]).reshape(-1)
        flat_places = jnp.moveaxis(places, 1, 0).reshape(3, N_MARK * CAP, BLOCK)
        marker_visc, moments = marker_blocks(fetched.reshape(-1, 384), flat_places, visc_start.reshape(-1, BLOCK), dens_start.reshape(-1, BLOCK), live_slots)
        totals = totals.at[group_index, owners[:, None], brick_ids].add(moments.reshape(N_MARK, CAP, 384))
        return totals, marker_visc.reshape(N_MARK, CAP, BLOCK)

    inputs = (jnp.arange(devices, dtype=jnp.int32), block_brick.reshape(devices, N_MARK, CAP), block_counts, positions.reshape(devices, N_MARK, 3, CAP, BLOCK), start_visc.reshape(devices, N_MARK, CAP, BLOCK), marker_dens.reshape(devices, N_MARK, CAP, BLOCK))
    totals, marker_out = lax.scan(visit_device, jnp.zeros((N_GRID, N_MARK, BRICKS_DEV, 384), jnp.float32), inputs)
    moment_sums = totals.reshape(N_GRID, N_MARK, CX // 4, CY // 4, CZ // 8, 3, 4, 4, 8).transpose(5, 0, 2, 6, 1, 3, 7, 4, 8).reshape(3, NX, NY, CZ)
    visc_next = jnp.exp((moment_sums[1] + jnp.log(cell_visc)) / (moment_sums[0] + 1.0))
    dens_next = (moment_sums[2] + cell_dens) / (moment_sums[0] + 1.0)
    return velocity_now, pressure_now, visc_next, dens_next, marker_out.reshape(SLOT_ROWS, CAP, BLOCK)
```

```python
import functools

import jax
import jax.numpy as jnp
import numpy as np
from jax import lax
from jax.experimental import pallas as pl
from jax.experimental.pallas import tpu as pltpu
from jax.sharding import PartitionSpec as P

SWEEPS = 4
RELAX = 0.6
PRESSURE_RATE = 0.25
GRAVITY = 1.0
STRAIN_SCALE = 0.5

BX, BY, BZ = 4, 4, 8
PLANE = BX * BY
ROWS = 3 * PLANE
LANES = 128
GROUP = LANES // BZ
HALF = 8

f32, bf16 = jnp.float32, jnp.bfloat16


def vmem_limit(mib):
    return pltpu.CompilerParams(vmem_limit_bytes=mib * 1024 * 1024)


def pick_body(asked, vel, out, table):
    size_x, size_y, size_z = vel.shape[1:]
    bricks_y, halves = size_y // BY, size_z // LANES

    def repack(block_x, carry):
        for block_y in range(bricks_y):
            for half in range(halves):
                place = (block_x * bricks_y + block_y) * halves + half
                for c in range(3):
                    for i in range(BX):
                        row = (c * BX + i) * BY
                        table[place, row : row + BY, :] = vel[
                            c,
                            block_x * BX + i,
                            block_y * BY : (block_y + 1) * BY,
                            half * LANES : (half + 1) * LANES,
                        ]
        return carry

    lax.fori_loop(0, size_x // BX, repack, 0)
    groups = out.shape[1]
    lane_slot = lax.broadcasted_iota(jnp.int32, (ROWS, LANES), 1) // BZ

    def one_group(step, carry):
        device, group = step // groups, step % groups
        packed = jnp.zeros((ROWS, LANES), f32)
        for slot in range(GROUP):
            brick = asked[device, group * GROUP + slot]
            shift = (BZ * slot - BZ * (brick % GROUP) + LANES) % LANES
            rolled = pltpu.roll(table[brick // GROUP], shift, 1)
            packed = jnp.where(lane_slot == slot, rolled, packed)
        out[device, group] = packed
        return carry

    lax.fori_loop(0, out.shape[0] * groups, one_group, 0)


def pick_bricks(asked, velocity):
    devices, slots = asked.shape
    size_x, size_y, size_z = velocity.shape[1:]
    places = (size_x // BX) * (size_y // BY) * (size_z // LANES)
    return pl.pallas_call(
        pick_body,
        out_shape=jax.ShapeDtypeStruct((devices, slots // GROUP, ROWS, LANES), f32),
        in_specs=[
            pl.BlockSpec(memory_space=pltpu.SMEM),
            pl.BlockSpec(memory_space=pltpu.VMEM),
        ],
        out_specs=pl.BlockSpec(memory_space=pltpu.VMEM),
        scratch_shapes=[pltpu.VMEM((places, ROWS, LANES), f32)],
        compiler_params=vmem_limit(32),
        name="pick_bricks",
    )(asked, velocity)


def permutations():
    spread = np.zeros((2, 2, LANES, 4 * BZ * HALF), np.float32)
    gather = np.zeros((2, 2 * BZ * HALF, LANES), np.float32)
    for half in range(2):
        for slot in range(HALF):
            for z in range(BZ):
                outer, inner = (half * HALF + slot) * BZ + z, z * HALF + slot
                for part in range(4):
                    spread[half, part // 2, outer, part * BZ * HALF + inner] = 1
                for part in range(2):
                    gather[half, part * BZ * HALF + inner, outer] = 1
    return jnp.asarray(spread, bf16), jnp.asarray(gather, bf16)


def split(value):
    high = value.astype(bf16)
    return high, (value - high.astype(f32)).astype(bf16)


def axis_weights(position, cells):
    offsets = [position - (i + 0.5) for i in range(cells)]
    bells = [jnp.exp(-offset * offset) for offset in offsets]
    scale = 1.0 / functools.reduce(jnp.add, bells)
    weights = [bell * scale for bell in bells]
    mean = functools.reduce(jnp.add, [w * offset for w, offset in zip(weights, offsets)])
    slopes = [w * (2.0 * (mean - offset)) for w, offset in zip(weights, offsets)]
    return weights, slopes


def dot(a, b):
    return jnp.dot(a, b, preferred_element_type=f32)


def marker_half(half, live_count, spread, gather, places, start, dens, brick, visc_out, work):
    permuted, left, right, products, heights, lows = work
    lo, hi = half * HALF, (half + 1) * HALF
    markers = places.shape[-1]
    brick_high, brick_low = split(brick)
    permuted[...] = dot(brick_high, spread[half, 0]) + dot(brick_low, spread[half, 1])
    lane = lax.broadcasted_iota(jnp.int32, (HALF, 4 * BZ * HALF), 1)
    sub = lax.broadcasted_iota(jnp.int32, (HALF, 4 * BZ * HALF), 0)
    own = (lane % HALF == sub).astype(f32)
    for row in range(0, ROWS, 2):
        pair = [
            jnp.broadcast_to(permuted[r : r + 1, :], own.shape) * own for r in (row, row + 1)
        ]
        left[row * HALF : (row + 2) * HALF, :] = jnp.concatenate(pair, axis=0).astype(bf16)

    weight_x, slope_x = axis_weights(places[0, 0, lo:hi, :] * BX, BX)
    weight_y, slope_y = axis_weights(places[0, 1, lo:hi, :] * BY, BY)
    weight_z, slope_z = axis_weights(places[0, 2, lo:hi, :] * BZ, BZ)
    part_rows = BZ * HALF
    for z in range(0, BZ, 2):
        rows = slice(z * HALF, (z + 2) * HALF)
        for column, values in ((0, weight_z), (1, slope_z)):
            high, low = split(jnp.concatenate(values[z : z + 2], axis=0))
            columns = slice(column * markers, (column + 1) * markers)
            for part in range(4):
                begin = part * part_rows + z * HALF
                right[begin : begin + 2 * HALF, columns] = low if part % 2 else high
    products[...] = dot(left[...], right[...])

    grads = []
    for c in range(3):
        along_x = along_y = along_z = None
        for i in range(BX):
            sum_w = sum_d = sum_r = None
            for j in range(BY):
                row = ((c * BX + i) * BY + j) * HALF
                still = products[row : row + HALF, :markers]
                rising = products[row : row + HALF, markers:]
                terms = (weight_y[j] * still, slope_y[j] * still, weight_y[j] * rising)
                if j == 0:
                    sum_w, sum_d, sum_r = terms
                else:
                    sum_w, sum_d, sum_r = sum_w + terms[0], sum_d + terms[1], sum_r + terms[2]
            terms = (slope_x[i] * sum_w, weight_x[i] * sum_d, weight_x[i] * sum_r)
            if i == 0:
                along_x, along_y, along_z = terms
            else:
                along_x, along_y, along_z = (
                    along_x + terms[0],
                    along_y + terms[1],
                    along_z + terms[2],
                )
        grads.append((along_x, along_y, along_z))
    normal = grads[0][0] ** 2 + grads[1][1] ** 2 + grads[2][2] ** 2
    shear_xy = 0.5 * (grads[0][1] + grads[1][0])
    shear_xz = 0.5 * (grads[0][2] + grads[2][0])
    shear_yz = 0.5 * (grads[1][2] + grads[2][1])
    invariant = 0.5 * normal + shear_xy**2 + shear_xz**2 + shear_yz**2
    third = jnp.log(1.0 + invariant * (1.0 / (STRAIN_SCALE * STRAIN_SCALE))) * (1.0 / 3.0)
    first = start[0, lo:hi, :]
    weakened = first * jnp.exp(-third)
    slot = lax.broadcasted_iota(jnp.int32, first.shape, 0) + lo
    live = slot < live_count
    visc_out[0, lo:hi, :] = jnp.where(live, weakened, 0.0)
    filled = live.astype(f32)
    carried = (filled, filled * (jnp.log(first) - third), filled * dens[0, lo:hi, :])

    for c in range(3):
        for i in range(BX):
            line = carried[c] * weight_x[i]
            for j in range(0, BY, 2):
                row = ((c * BX + i) * BY + j) * HALF
                pair = jnp.concatenate([line * weight_y[j], line * weight_y[j + 1]], axis=0)
                high, low = split(pair)
                heights[row : row + 2 * HALF, :] = high
                lows[row : row + 2 * HALF, :] = low
    vertical = right[: 2 * part_rows, :markers]
    contract = (((1,), (1,)), ((), ()))
    sums = lax.dot_general(
        heights[...], vertical, contract, preferred_element_type=f32
    ) + lax.dot_general(lows[...], vertical, contract, preferred_element_type=f32)
    chosen = sums.reshape(ROWS, HALF, 2 * part_rows) * own[None, :, : 2 * part_rows]
    moments = jnp.sum(chosen, axis=1)
    high, low = split(moments)
    return dot(high, gather[half]) + dot(low, gather[half])


def marker_body(counts, spread, gather, places, start, dens, brick, visc_out, moments_out, *work):
    owner, group = pl.program_id(0), pl.program_id(1)
    live_count = counts[0, owner] - group * GROUP

    @pl.when(live_count <= 0)
    def _():
        visc_out[...] = jnp.zeros_like(visc_out)
        moments_out[...] = jnp.zeros_like(moments_out)

    @pl.when(live_count > 0)
    def _():
        total = None
        for half in range(2):
            part = marker_half(
                half, live_count, spread, gather, places, start, dens, brick[0, 0], visc_out, work
            )
            total = part if total is None else total + part
        moments_out[0, 0] = total


def marker_work(counts, positions, start_visc, marker_dens, bricks):
    owners, _, slots, markers = positions.shape
    groups = slots // GROUP
    spread, gather = permutations()
    width = 4 * BZ * HALF
    return pl.pallas_call(
        marker_body,
        grid=(owners, groups),
        out_shape=(
            jax.ShapeDtypeStruct((owners, slots, markers), f32),
            jax.ShapeDtypeStruct((owners, groups, ROWS, LANES), f32),
        ),
        in_specs=[
            pl.BlockSpec(memory_space=pltpu.SMEM),
            pl.BlockSpec(spread.shape, lambda q, g: (0, 0, 0, 0)),
            pl.BlockSpec(gather.shape, lambda q, g: (0, 0, 0)),
            pl.BlockSpec((1, 3, GROUP, markers), lambda q, g: (q, 0, g, 0)),
            pl.BlockSpec((1, GROUP, markers), lambda q, g: (q, g, 0)),
            pl.BlockSpec((1, GROUP, markers), lambda q, g: (q, g, 0)),
            pl.BlockSpec((1, 1, ROWS, LANES), lambda q, g: (q, g, 0, 0)),
        ],
        out_specs=(
            pl.BlockSpec((1, GROUP, markers), lambda q, g: (q, g, 0)),
            pl.BlockSpec((1, 1, ROWS, LANES), lambda q, g: (q, g, 0, 0)),
        ),
        scratch_shapes=[
            pltpu.VMEM((ROWS, width), f32),
            pltpu.VMEM((ROWS * HALF, width), bf16),
            pltpu.VMEM((width, 2 * markers), bf16),
            pltpu.VMEM((ROWS * HALF, 2 * markers), f32),
            pltpu.VMEM((ROWS * HALF, markers), bf16),
            pltpu.VMEM((ROWS * HALF, markers), bf16),
        ],
        compiler_params=vmem_limit(32),
        name="marker_work",
    )(counts, spread, gather, positions, start_visc, marker_dens, bricks)


def settle_body(asked, moments, visc, dens, visc_out, dens_out, table):
    size_x, size_y, size_z = visc.shape
    bricks_y, halves = size_y // BY, size_z // LANES
    table[...] = jnp.zeros_like(table)
    groups = moments.shape[1]
    lane_slot = lax.broadcasted_iota(jnp.int32, (ROWS, LANES), 1) // BZ

    def one_group(step, carry):
        device, group = step // groups, step % groups
        packed = moments[device, group]
        for slot in range(GROUP):
            brick = asked[device, group * GROUP + slot]
            shift = (BZ * (brick % GROUP) - BZ * slot + LANES) % LANES
            piece = pltpu.roll(jnp.where(lane_slot == slot, packed, 0.0), shift, 1)
            place = brick // GROUP
            table[place] = table[place] + piece
        return carry

    lax.fori_loop(0, moments.shape[0] * groups, one_group, 0)

    def finish(block_x, carry):
        for block_y in range(bricks_y):
            for half in range(halves):
                place = (block_x * bricks_y + block_y) * halves + half
                for i in range(BX):
                    here = (
                        block_x * BX + i,
                        slice(block_y * BY, (block_y + 1) * BY),
                        slice(half * LANES, (half + 1) * LANES),
                    )
                    sums = [
                        table[place, (c * BX + i) * BY : (c * BX + i + 1) * BY, :]
                        for c in range(3)
                    ]
                    scale = 1.0 / (sums[0] + 1.0)
                    visc_out[here] = jnp.exp((sums[1] + jnp.log(visc[here])) * scale)
                    dens_out[here] = (sums[2] + dens[here]) * scale
        return carry

    lax.fori_loop(0, size_x // BX, finish, 0)


def settle(asked, moments, cell_visc, cell_dens):
    size_x, size_y, size_z = cell_visc.shape
    places = (size_x // BX) * (size_y // BY) * (size_z // LANES)
    whole = pl.BlockSpec(memory_space=pltpu.VMEM)
    shape = jax.ShapeDtypeStruct(cell_visc.shape, f32)
    return pl.pallas_call(
        settle_body,
        out_shape=(shape, shape),
        in_specs=[pl.BlockSpec(memory_space=pltpu.SMEM), whole, whole, whole],
        out_specs=(whole, whole),
        scratch_shapes=[pltpu.VMEM((places, ROWS, LANES), f32)],
        compiler_params=vmem_limit(32),
        name="settle",
    )(asked, moments, cell_visc, cell_dens)


def sweep_body(vel, pres, visc, dens, low_x, high_x, side_y, vel_out, pres_out, *work):
    fields, coefs, rate, relax, forcing = work
    size_x, size_y, size_z = visc.shape
    width = low_x.shape[1]
    long_x = size_x + 2 * width
    ring = fields.shape[3]
    inner = slice(width, width + size_x)
    own = slice(0, size_y)
    for c in range(3):
        fields[0, c, inner, own, :] = vel[c]
    fields[0, 3, inner, own, :] = pres[...]
    fields[1, 0, inner, own, :] = visc[...]
    fields[1, 1, inner, own, :] = dens[...]
    for f in range(6):
        slot = (0, f) if f < 4 else (1, f - 4)
        fields[slot[0], slot[1], :width, own, :] = low_x[f]
        fields[slot[0], slot[1], width + size_x :, own, :] = high_x[f]
        fields[slot[0], slot[1], :, size_y:, :] = side_y[f]

    lane = lax.broadcasted_iota(jnp.int32, (ring, size_z), 1)
    not_last = (lane < size_z - 1).astype(f32)
    not_first = (lane > 0).astype(f32)

    def up_y(a):
        return pltpu.roll(a, ring - 1, 0)

    def down_y(a):
        return pltpu.roll(a, 1, 0)

    def up_z(a):
        return pltpu.roll(a, size_z - 1, 1)

    def down_z(a):
        return pltpu.roll(a, 1, 1)

    def prepare(i, carry):
        here = fields[1, 0, i]
        near = [
            fields[1, 0, i + 1],
            fields[1, 0, i - 1],
            up_y(here),
            down_y(here),
            up_z(here) * not_last,
            down_z(here) * not_first,
        ]
        links = [0.5 * (here + other) for other in near]
        diagonal = functools.reduce(jnp.add, links)
        scale = jnp.where(here > 0.0, RELAX / diagonal, 0.0)
        links[4] = links[4] * not_last
        links[5] = links[5] * not_first
        for n in range(6):
            coefs[n, i] = links[n] * scale
        relax[i] = scale
        forcing[i] = fields[1, 1, i] * (-GRAVITY * scale)
        rate[i] = PRESSURE_RATE * here
        return carry

    lax.fori_loop(1, long_x - 1, prepare, 0)

    for sweep in range(SWEEPS):
        old, new = sweep % 2, (sweep + 1) % 2
        last = sweep == SWEEPS - 1

        def one_plane(i, carry, old=old, new=new, last=last):
            pressure = fields[old, 3, i]
            links = [coefs[n, i] for n in range(6)]
            scale = relax[i]
            before = (
                fields[old, 3, i - 1],
                down_y(pressure),
                down_z(pressure) * not_first,
            )
            divergence = None
            for c in range(3):
                here = fields[old, c, i]
                near = [
                    fields[old, c, i + 1],
                    fields[old, c, i - 1],
                    up_y(here),
                    down_y(here),
                    up_z(here),
                    down_z(here),
                ]
                total = (1.0 - RELAX) * here - scale * (pressure - before[c])
                for link, other in zip(links, near):
                    total = total + link * other
                ahead = near[2 * c]
                if c == 2:
                    total = total + forcing[i]
                    ahead = ahead * not_last
                change = ahead - here
                divergence = change if divergence is None else divergence + change
                if last:
                    vel_out[c, i - width] = total[:size_y]
                else:
                    fields[new, c, i] = total
            pressed = pressure - rate[i] * divergence
            if last:
                pres_out[i - width] = pressed[:size_y]
            else:
                fields[new, 3, i] = pressed
            return carry

        lax.fori_loop(1 + sweep, long_x - 1 - sweep, one_plane, 0)


def all_sweeps(velocity, pressure, cell_visc, cell_dens, low_x, high_x, side_y):
    size_x, size_y, size_z = cell_visc.shape
    width = low_x.shape[1]
    long_x, ring = size_x + 2 * width, size_y + side_y.shape[2]
    whole = pl.BlockSpec(memory_space=pltpu.VMEM)
    block = (long_x, ring, size_z)
    return pl.pallas_call(
        sweep_body,
        out_shape=(
            jax.ShapeDtypeStruct(velocity.shape, f32),
            jax.ShapeDtypeStruct(pressure.shape, f32),
        ),
        in_specs=[whole] * 7,
        out_specs=(whole, whole),
        scratch_shapes=[
            pltpu.VMEM((2, 4) + block, f32),
            pltpu.VMEM((6,) + block, f32),
            pltpu.VMEM(block, f32),
            pltpu.VMEM(block, f32),
            pltpu.VMEM(block, f32),
        ],
        compiler_params=vmem_limit(48),
        name="all_sweeps",
    )(velocity, pressure, cell_visc, cell_dens, low_x, high_x, side_y)


def shift(value, axis, step):
    size = lax.axis_size(axis)
    pairs = [(i, i + step) for i in range(size) if 0 <= i + step < size]
    return lax.ppermute(value, axis, pairs)


def per_device(
    velocity,
    pressure,
    cell_visc,
    cell_dens,
    block_brick,
    block_counts,
    positions,
    start_visc,
    marker_dens,
):
    width = SWEEPS
    size_x, size_y, _ = cell_visc.shape
    asked = lax.all_to_all(block_brick, "mark", 0, 0, tiled=True)

    fields = (velocity, pressure[None], cell_visc[None], cell_dens[None])
    low_x = shift(jnp.concatenate([f[:, size_x - width :] for f in fields]), "grid", 1)
    high_x = shift(jnp.concatenate([f[:, :width] for f in fields]), "grid", -1)

    def face_y(rows):
        own = jnp.concatenate([f[:, :, rows] for f in fields])
        return jnp.concatenate([low_x[:, :, rows], own, high_x[:, :, rows]], axis=1)

    low_y = shift(face_y(slice(size_y - width, size_y)), "mark", 1)
    high_y = shift(face_y(slice(0, width)), "mark", -1)
    side_y = jnp.concatenate([high_y, low_y], axis=2)

    picked = pick_bricks(asked, velocity)
    bricks = lax.all_to_all(picked, "mark", 0, 0, tiled=True)
    marker_visc, moments = marker_work(
        block_counts, positions, start_visc, marker_dens, bricks
    )
    gathered = lax.all_to_all(moments, "mark", 0, 0, tiled=True)
    velocity_next, pressure_next = all_sweeps(
        velocity, pressure, cell_visc, cell_dens, low_x, high_x, side_y
    )
    visc_next, dens_next = settle(asked, gathered, cell_visc, cell_dens)
    return velocity_next, pressure_next, visc_next, dens_next, marker_visc


def solution(mesh):
    in_specs = (
        P(None, "grid", "mark", None),
        P("grid", "mark", None),
        P("grid", "mark", None),
        P("grid", "mark", None),
        P(("grid", "mark"), None),
        P(("grid", "mark"), None),
        P(("grid", "mark"), None, None, None),
        P(("grid", "mark"), None, None),
        P(("grid", "mark"), None, None),
    )
    out_specs = (
        P(None, "grid", "mark", None),
        P("grid", "mark", None),
        P("grid", "mark", None),
        P("grid", "mark", None),
        P(("grid", "mark"), None, None),
    )
    return jax.shard_map(
        per_device, mesh=mesh, in_specs=in_specs, out_specs=out_specs, check_vma=False
    )
```

```python
import functools

import jax
import jax.numpy as jnp
import numpy as np
from jax import lax
from jax.experimental import pallas as pl
from jax.experimental.pallas import tpu as pltpu
from jax.sharding import PartitionSpec as P

SWEEPS = 4
RELAX = 0.6
PRESSURE_RATE = 0.25
GRAVITY = 1.0
STRAIN_SCALE = 0.5

BX, BY, BZ = 4, 4, 8
PLANE = BX * BY
ROWS = 3 * PLANE
LANES = 128
GROUP = LANES // BZ
HALF = 8

f32, bf16 = jnp.float32, jnp.bfloat16


def vmem_limit(mib):
    return pltpu.CompilerParams(vmem_limit_bytes=mib * 1024 * 1024)


def pick_body(asked, vel, out, table):
    size_x, size_y, size_z = vel.shape[1:]
    bricks_y, halves = size_y // BY, size_z // LANES

    def repack(block_x, carry):
        for block_y in range(bricks_y):
            for half in range(halves):
                place = (block_x * bricks_y + block_y) * halves + half
                for c in range(3):
                    for i in range(BX):
                        row = (c * BX + i) * BY
                        table[place, row : row + BY, :] = vel[
                            c,
                            block_x * BX + i,
                            block_y * BY : (block_y + 1) * BY,
                            half * LANES : (half + 1) * LANES,
                        ]
        return carry

    lax.fori_loop(0, size_x // BX, repack, 0)
    groups = out.shape[1]
    lane_slot = lax.broadcasted_iota(jnp.int32, (ROWS, LANES), 1) // BZ

    def one_group(step, carry):
        device, group = step // groups, step % groups
        packed = jnp.zeros((ROWS, LANES), f32)
        for slot in range(GROUP):
            brick = asked[device, group * GROUP + slot]
            shift = (BZ * slot - BZ * (brick % GROUP) + LANES) % LANES
            rolled = pltpu.roll(table[brick // GROUP], shift, 1)
            packed = jnp.where(lane_slot == slot, rolled, packed)
        out[device, group] = packed
        return carry

    lax.fori_loop(0, out.shape[0] * groups, one_group, 0)


def pick_bricks(asked, velocity):
    devices, slots = asked.shape
    size_x, size_y, size_z = velocity.shape[1:]
    places = (size_x // BX) * (size_y // BY) * (size_z // LANES)
    return pl.pallas_call(
        pick_body,
        out_shape=jax.ShapeDtypeStruct((devices, slots // GROUP, ROWS, LANES), f32),
        in_specs=[
            pl.BlockSpec(memory_space=pltpu.SMEM),
            pl.BlockSpec(memory_space=pltpu.VMEM),
        ],
        out_specs=pl.BlockSpec(memory_space=pltpu.VMEM),
        scratch_shapes=[pltpu.VMEM((places, ROWS, LANES), f32)],
        compiler_params=vmem_limit(32),
        name="pick_bricks",
    )(asked, velocity)


def permutations():
    inside = BZ * HALF
    spread = np.zeros((2, 2, LANES, 4 * inside), np.float32)
    gather = np.zeros((2 * BY * inside, BY * LANES), np.float32)
    for half in range(2):
        for slot in range(HALF):
            for z in range(BZ):
                outer, inner = (half * HALF + slot) * BZ + z, z * HALF + slot
                for part in range(4):
                    spread[half, part // 2, outer, part * inside + inner] = 1
                for j in range(BY):
                    gather[(half * BY + j) * inside + inner, j * LANES + outer] = 1
    return jnp.asarray(spread, bf16), jnp.asarray(gather, bf16)


def split(value):
    high = value.astype(bf16)
    return high, (value - high.astype(f32)).astype(bf16)


def add_all(values):
    return functools.reduce(jnp.add, values)


def axis_weights(fraction, cells):
    middle = (cells - 1) / 2
    base = jnp.exp(fraction * (2.0 * cells) - float(cells))
    powers = [None, base]
    for i in range(2, cells):
        powers.append(powers[i // 2] * powers[i - i // 2])
    factors = [float(np.exp(middle**2 - (i - middle) ** 2)) for i in range(cells)]
    bells = [None] + [powers[i] * factors[i] for i in range(1, cells)]
    scale = 1.0 / (add_all(bells[1:]) + factors[0])
    weights = [scale * factors[0]] + [bell * scale for bell in bells[1:]]
    mean = add_all(
        [
            (weights[cells - 1 - i] - weights[i]) * (2.0 * (middle - i))
            for i in range(cells // 2)
        ]
    )
    slopes = [w * (2.0 * (i - middle) - mean) for i, w in enumerate(weights)]
    return weights, slopes


def dot(a, b):
    return jnp.dot(a, b, preferred_element_type=f32)


def gradients(products, weights_x, weights_y, markers):
    (weight_x, slope_x), (weight_y, slope_y) = weights_x, weights_y
    grads = []
    for c in range(3):
        lines = [[], [], []]
        for i in range(BX):
            rows = [((c * BX + i) * BY + j) * HALF for j in range(BY)]
            still = [products[row : row + HALF, :markers] for row in rows]
            rising = [products[row : row + HALF, markers:] for row in rows]
            lines[0].append(slope_x[i] * add_all([w * t for w, t in zip(weight_y, still)]))
            lines[1].append(weight_x[i] * add_all([w * t for w, t in zip(slope_y, still)]))
            lines[2].append(weight_x[i] * add_all([w * t for w, t in zip(weight_y, rising)]))
        grads.append([add_all(line) for line in lines])
    return grads


def marker_halves(halves, live_count, spread, gather, places, start, dens, brick, visc_out, work):
    permuted, left, right, products, factors, planes_high, planes_low, sums = work
    markers = places.shape[-1]
    inside = BZ * HALF
    lane = lax.broadcasted_iota(jnp.int32, (HALF, 4 * inside), 1)
    sub = lax.broadcasted_iota(jnp.int32, (HALF, 4 * inside), 0)
    own = (lane % HALF == sub).astype(f32)
    parts = split(brick)
    weights = {}
    for half in halves:
        permuted[half] = dot(parts[0], spread[half, 0]) + dot(parts[1], spread[half, 1])
        lo, hi = half * HALF, (half + 1) * HALF
        weight_z, slope_z = axis_weights(places[0, 2, lo:hi, :], BZ)
        for z in range(0, BZ, 2):
            for column, values in ((0, weight_z), (1, slope_z)):
                high, low = split(jnp.concatenate(values[z : z + 2], axis=0))
                columns = slice(column * markers, (column + 1) * markers)
                for part in range(4):
                    begin = part * inside + z * HALF
                    right[half, begin : begin + 2 * HALF, columns] = low if part % 2 else high
        for row in range(0, ROWS, 2):
            pair = [
                jnp.broadcast_to(permuted[half, r : r + 1, :], own.shape) * own
                for r in (row, row + 1)
            ]
            left[half, row * HALF : (row + 2) * HALF, :] = jnp.concatenate(pair, axis=0).astype(
                bf16
            )
        products[half] = dot(left[half], right[half])

        weights_x = axis_weights(places[0, 0, lo:hi, :], BX)
        weights_y = axis_weights(places[0, 1, lo:hi, :], BY)
        weights[half] = (weights_x, weights_y)
        for j in range(BY):
            for z in range(0, BZ, 2):
                pair = [weights_y[0][j] * weight_z[z + k] for k in range(2)]
                rows = slice((j * BZ + z) * HALF, (j * BZ + z + 2) * HALF)
                high, low = split(jnp.concatenate(pair, axis=0))
                planes_high[half, rows, :] = high
                planes_low[half, rows, :] = low

    contract = (((1,), (1,)), ((), ()))
    for half in halves:
        lo, hi = half * HALF, (half + 1) * HALF
        weights_x, weights_y = weights[half]
        grads = gradients(products.at[half], weights_x, weights_y, markers)
        normal = grads[0][0] ** 2 + grads[1][1] ** 2 + grads[2][2] ** 2
        shear_xy = 0.5 * (grads[0][1] + grads[1][0])
        shear_xz = 0.5 * (grads[0][2] + grads[2][0])
        shear_yz = 0.5 * (grads[1][2] + grads[2][1])
        invariant = 0.5 * normal + shear_xy**2 + shear_xz**2 + shear_yz**2
        third = jnp.log(1.0 + invariant * (1.0 / (STRAIN_SCALE * STRAIN_SCALE))) * (1.0 / 3.0)
        first = start[0, lo:hi, :]
        slot = lax.broadcasted_iota(jnp.int32, first.shape, 0) + lo
        live = slot < live_count
        visc_out[0, lo:hi, :] = jnp.where(live, first * jnp.exp(-third), 0.0)
        carried = (
            live.astype(f32),
            jnp.where(live, jnp.log(first) - third, 0.0),
            jnp.where(live, dens[0, lo:hi, :], 0.0),
        )
        count = 3 * BX * HALF
        for c in range(3):
            for i in range(0, BX, 2):
                pair = [carried[c] * weights_x[0][i + k] for k in range(2)]
                row = (c * BX + i) * HALF
                high, low = split(jnp.concatenate(pair, axis=0))
                factors[half, row : row + 2 * HALF, :] = high
                factors[half, count + row : count + row + 2 * HALF, :] = low
        both = lax.dot_general(
            factors[half], planes_high[half], contract, preferred_element_type=f32
        )
        rest = lax.dot_general(
            factors[half, :count], planes_low[half], contract, preferred_element_type=f32
        )
        total = both[:count] + both[count:] + rest
        chosen = total.reshape(3 * BX, HALF, BY * inside) * own[None]
        packed = jnp.sum(chosen, axis=1)
        high, low = split(packed)
        columns = slice(half * BY * inside, (half + 1) * BY * inside)
        sums[: 3 * BX, columns] = high.astype(f32)
        sums[16 : 16 + 3 * BX, columns] = low.astype(f32)


def marker_body(counts, spread, gather, places, start, dens, brick, visc_out, moments_out, *work):
    owner, group = pl.program_id(0), pl.program_id(1)
    live_count = counts[0, owner] - group * GROUP
    sums = work[-1]

    def run(halves):
        marker_halves(
            halves, live_count, spread, gather, places, start, dens, brick[0, 0], visc_out, work
        )
        moved = dot(sums[...].astype(bf16), gather[...])
        moved = moved[: 3 * BX] + moved[16 : 16 + 3 * BX]
        for j in range(BY):
            rows = pl.ds(j, 3 * BX, stride=BY)
            moments_out[0, 0, rows, :] = moved[:, j * LANES : (j + 1) * LANES]

    @pl.when(live_count <= 0)
    def _():
        visc_out[...] = jnp.zeros_like(visc_out)
        moments_out[...] = jnp.zeros_like(moments_out)

    @pl.when(jnp.logical_and(live_count > 0, live_count <= HALF))
    def _():
        sums[...] = jnp.zeros_like(sums)
        visc_out[:, HALF:, :] = jnp.zeros((1, HALF, visc_out.shape[-1]), f32)
        run((0,))

    @pl.when(live_count > HALF)
    def _():
        sums[...] = jnp.zeros_like(sums)
        run((0, 1))


def marker_work(counts, positions, start_visc, marker_dens, bricks):
    owners, _, slots, markers = positions.shape
    groups = slots // GROUP
    spread, gather = permutations()
    width = 4 * BZ * HALF
    return pl.pallas_call(
        marker_body,
        grid=(owners, groups),
        out_shape=(
            jax.ShapeDtypeStruct((owners, slots, markers), f32),
            jax.ShapeDtypeStruct((owners, groups, ROWS, LANES), f32),
        ),
        in_specs=[
            pl.BlockSpec(memory_space=pltpu.SMEM),
            pl.BlockSpec(spread.shape, lambda q, g: (0, 0, 0, 0)),
            pl.BlockSpec(gather.shape, lambda q, g: (0, 0)),
            pl.BlockSpec((1, 3, GROUP, markers), lambda q, g: (q, 0, g, 0)),
            pl.BlockSpec((1, GROUP, markers), lambda q, g: (q, g, 0)),
            pl.BlockSpec((1, GROUP, markers), lambda q, g: (q, g, 0)),
            pl.BlockSpec((1, 1, ROWS, LANES), lambda q, g: (q, g, 0, 0)),
        ],
        out_specs=(
            pl.BlockSpec((1, GROUP, markers), lambda q, g: (q, g, 0)),
            pl.BlockSpec((1, 1, ROWS, LANES), lambda q, g: (q, g, 0, 0)),
        ),
        scratch_shapes=[
            pltpu.VMEM((2, ROWS, width), f32),
            pltpu.VMEM((2, ROWS * HALF, width), bf16),
            pltpu.VMEM((2, width, 2 * markers), bf16),
            pltpu.VMEM((2, ROWS * HALF, 2 * markers), f32),
            pltpu.VMEM((2, 2 * 3 * BX * HALF, markers), bf16),
            pltpu.VMEM((2, BY * BZ * HALF, markers), bf16),
            pltpu.VMEM((2, BY * BZ * HALF, markers), bf16),
            pltpu.VMEM((32, 2 * BY * BZ * HALF), f32),
        ],
        compiler_params=vmem_limit(60),
        name="marker_work",
    )(counts, spread, gather, positions, start_visc, marker_dens, bricks)


def settle_body(asked, moments, visc, dens, visc_out, dens_out, table):
    size_x, size_y, size_z = visc.shape
    bricks_y, halves = size_y // BY, size_z // LANES
    table[...] = jnp.zeros_like(table)
    groups = moments.shape[1]
    lane_slot = lax.broadcasted_iota(jnp.int32, (ROWS, LANES), 1) // BZ

    def one_group(step, carry):
        device, group = step // groups, step % groups
        packed = moments[device, group]
        for slot in range(GROUP):
            brick = asked[device, group * GROUP + slot]
            shift = (BZ * (brick % GROUP) - BZ * slot + LANES) % LANES
            piece = pltpu.roll(jnp.where(lane_slot == slot, packed, 0.0), shift, 1)
            place = brick // GROUP
            table[place] = table[place] + piece
        return carry

    lax.fori_loop(0, moments.shape[0] * groups, one_group, 0)

    def finish(block_x, carry):
        for block_y in range(bricks_y):
            for half in range(halves):
                place = (block_x * bricks_y + block_y) * halves + half
                for i in range(BX):
                    here = (
                        block_x * BX + i,
                        slice(block_y * BY, (block_y + 1) * BY),
                        slice(half * LANES, (half + 1) * LANES),
                    )
                    sums = [
                        table[place, (c * BX + i) * BY : (c * BX + i + 1) * BY, :]
                        for c in range(3)
                    ]
                    scale = 1.0 / (sums[0] + 1.0)
                    visc_out[here] = jnp.exp((sums[1] + jnp.log(visc[here])) * scale)
                    dens_out[here] = (sums[2] + dens[here]) * scale
        return carry

    lax.fori_loop(0, size_x // BX, finish, 0)


def settle(asked, moments, cell_visc, cell_dens):
    size_x, size_y, size_z = cell_visc.shape
    places = (size_x // BX) * (size_y // BY) * (size_z // LANES)
    whole = pl.BlockSpec(memory_space=pltpu.VMEM)
    shape = jax.ShapeDtypeStruct(cell_visc.shape, f32)
    return pl.pallas_call(
        settle_body,
        out_shape=(shape, shape),
        in_specs=[pl.BlockSpec(memory_space=pltpu.SMEM), whole, whole, whole],
        out_specs=(whole, whole),
        scratch_shapes=[pltpu.VMEM((places, ROWS, LANES), f32)],
        compiler_params=vmem_limit(32),
        name="settle",
    )(asked, moments, cell_visc, cell_dens)


def sweep_body(vel, pres, visc, dens, low_x, high_x, side_y, vel_out, pres_out, *work):
    fields, coefs, rate, relax, forcing = work
    size_x, size_y, size_z = visc.shape
    width = low_x.shape[1]
    long_x = size_x + 2 * width
    ring = fields.shape[3]
    inner = slice(width, width + size_x)
    own = slice(0, size_y)
    for c in range(3):
        fields[0, c, inner, own, :] = vel[c]
    fields[0, 3, inner, own, :] = pres[...]
    fields[1, 0, inner, own, :] = visc[...]
    fields[1, 1, inner, own, :] = dens[...]
    for f in range(6):
        slot = (0, f) if f < 4 else (1, f - 4)
        fields[slot[0], slot[1], :width, own, :] = low_x[f]
        fields[slot[0], slot[1], width + size_x :, own, :] = high_x[f]
        fields[slot[0], slot[1], :, size_y:, :] = side_y[f]

    lane = lax.broadcasted_iota(jnp.int32, (ring, size_z), 1)
    not_last = (lane < size_z - 1).astype(f32)
    not_first = (lane > 0).astype(f32)

    def up_y(a):
        return pltpu.roll(a, ring - 1, 0)

    def down_y(a):
        return pltpu.roll(a, 1, 0)

    def up_z(a):
        return pltpu.roll(a, size_z - 1, 1)

    def down_z(a):
        return pltpu.roll(a, 1, 1)

    def prepare(i, carry):
        here = fields[1, 0, i]
        near = [
            fields[1, 0, i + 1],
            fields[1, 0, i - 1],
            up_y(here),
            down_y(here),
            up_z(here) * not_last,
            down_z(here) * not_first,
        ]
        links = [0.5 * (here + other) for other in near]
        diagonal = functools.reduce(jnp.add, links)
        scale = jnp.where(here > 0.0, RELAX / diagonal, 0.0)
        links[4] = links[4] * not_last
        links[5] = links[5] * not_first
        for n in range(6):
            coefs[n, i] = links[n] * scale
        relax[i] = scale
        forcing[i] = fields[1, 1, i] * (-GRAVITY * scale)
        rate[i] = PRESSURE_RATE * here
        return carry

    lax.fori_loop(1, long_x - 1, prepare, 0)

    for sweep in range(SWEEPS):
        old, new = sweep % 2, (sweep + 1) % 2
        last = sweep == SWEEPS - 1

        def one_plane(i, carry, old=old, new=new, last=last):
            pressure = fields[old, 3, i]
            links = [coefs[n, i] for n in range(6)]
            scale = relax[i]
            before = (
                fields[old, 3, i - 1],
                down_y(pressure),
                down_z(pressure) * not_first,
            )
            divergence = None
            for c in range(3):
                here = fields[old, c, i]
                near = [
                    fields[old, c, i + 1],
                    fields[old, c, i - 1],
                    up_y(here),
                    down_y(here),
                    up_z(here),
                    down_z(here),
                ]
                total = (1.0 - RELAX) * here - scale * (pressure - before[c])
                for link, other in zip(links, near):
                    total = total + link * other
                ahead = near[2 * c]
                if c == 2:
                    total = total + forcing[i]
                    ahead = ahead * not_last
                change = ahead - here
                divergence = change if divergence is None else divergence + change
                if last:
                    vel_out[c, i - width] = total[:size_y]
                else:
                    fields[new, c, i] = total
            pressed = pressure - rate[i] * divergence
            if last:
                pres_out[i - width] = pressed[:size_y]
            else:
                fields[new, 3, i] = pressed
            return carry

        lax.fori_loop(1 + sweep, long_x - 1 - sweep, one_plane, 0)


def all_sweeps(velocity, pressure, cell_visc, cell_dens, low_x, high_x, side_y):
    size_x, size_y, size_z = cell_visc.shape
    width = low_x.shape[1]
    long_x, ring = size_x + 2 * width, size_y + side_y.shape[2]
    whole = pl.BlockSpec(memory_space=pltpu.VMEM)
    block = (long_x, ring, size_z)
    return pl.pallas_call(
        sweep_body,
        out_shape=(
            jax.ShapeDtypeStruct(velocity.shape, f32),
            jax.ShapeDtypeStruct(pressure.shape, f32),
        ),
        in_specs=[whole] * 7,
        out_specs=(whole, whole),
        scratch_shapes=[
            pltpu.VMEM((2, 4) + block, f32),
            pltpu.VMEM((6,) + block, f32),
            pltpu.VMEM(block, f32),
            pltpu.VMEM(block, f32),
            pltpu.VMEM(block, f32),
        ],
        compiler_params=vmem_limit(48),
        name="all_sweeps",
    )(velocity, pressure, cell_visc, cell_dens, low_x, high_x, side_y)


def shift(value, axis, step):
    size = lax.axis_size(axis)
    pairs = [(i, i + step) for i in range(size) if 0 <= i + step < size]
    return lax.ppermute(value, axis, pairs)


def per_device(
    velocity,
    pressure,
    cell_visc,
    cell_dens,
    block_brick,
    block_counts,
    positions,
    start_visc,
    marker_dens,
):
    width = SWEEPS
    size_x, size_y, _ = cell_visc.shape
    asked = lax.all_to_all(block_brick, "mark", 0, 0, tiled=True)

    fields = (velocity, pressure[None], cell_visc[None], cell_dens[None])
    low_x = shift(jnp.concatenate([f[:, size_x - width :] for f in fields]), "grid", 1)
    high_x = shift(jnp.concatenate([f[:, :width] for f in fields]), "grid", -1)

    def face_y(rows):
        own = jnp.concatenate([f[:, :, rows] for f in fields])
        return jnp.concatenate([low_x[:, :, rows], own, high_x[:, :, rows]], axis=1)

    low_y = shift(face_y(slice(size_y - width, size_y)), "mark", 1)
    high_y = shift(face_y(slice(0, width)), "mark", -1)
    side_y = jnp.concatenate([high_y, low_y], axis=2)

    picked = pick_bricks(asked, velocity)
    bricks = lax.all_to_all(picked, "mark", 0, 0, tiled=True)
    marker_visc, moments = marker_work(
        block_counts, positions, start_visc, marker_dens, bricks
    )
    gathered = lax.all_to_all(moments, "mark", 0, 0, tiled=True)
    velocity_next, pressure_next = all_sweeps(
        velocity, pressure, cell_visc, cell_dens, low_x, high_x, side_y
    )
    visc_next, dens_next = settle(asked, gathered, cell_visc, cell_dens)
    return velocity_next, pressure_next, visc_next, dens_next, marker_visc


def solution(mesh):
    in_specs = (
        P(None, "grid", "mark", None),
        P("grid", "mark", None),
        P("grid", "mark", None),
        P("grid", "mark", None),
        P(("grid", "mark"), None),
        P(("grid", "mark"), None),
        P(("grid", "mark"), None, None, None),
        P(("grid", "mark"), None, None),
        P(("grid", "mark"), None, None),
    )
    out_specs = (
        P(None, "grid", "mark", None),
        P("grid", "mark", None),
        P("grid", "mark", None),
        P("grid", "mark", None),
        P(("grid", "mark"), None, None),
    )
    return jax.shard_map(
        per_device, mesh=mesh, in_specs=in_specs, out_specs=out_specs, check_vma=False
    )
```

```python
import functools

import jax
import jax.numpy as jnp
import numpy as np
from jax import lax
from jax.experimental import pallas as pl
from jax.experimental.pallas import tpu as pltpu
from jax.sharding import PartitionSpec as P

SWEEPS = 4
RELAX = 0.6
PRESSURE_RATE = 0.25
GRAVITY = 1.0
STRAIN_SCALE = 0.5

BX, BY, BZ = 4, 4, 8
PLANE = BX * BY
ROWS = 3 * PLANE
LANES = 128
GROUP = LANES // BZ
HALF = 8

f32, bf16 = jnp.float32, jnp.bfloat16


def vmem_limit(mib):
    return pltpu.CompilerParams(vmem_limit_bytes=mib * 1024 * 1024)


def pick_body(asked, vel, out, table):
    size_x, size_y, size_z = vel.shape[1:]
    bricks_y, halves = size_y // BY, size_z // LANES

    def repack(block_x, carry):
        for block_y in range(bricks_y):
            for half in range(halves):
                place = (block_x * bricks_y + block_y) * halves + half
                for c in range(3):
                    for i in range(BX):
                        row = (c * BX + i) * BY
                        table[place, row : row + BY, :] = vel[
                            c,
                            block_x * BX + i,
                            block_y * BY : (block_y + 1) * BY,
                            half * LANES : (half + 1) * LANES,
                        ]
        return carry

    lax.fori_loop(0, size_x // BX, repack, 0)
    groups = out.shape[1]
    lane_slot = lax.broadcasted_iota(jnp.int32, (ROWS, LANES), 1) // BZ

    def one_group(step, carry):
        device, group = step // groups, step % groups
        packed = jnp.zeros((ROWS, LANES), f32)
        for slot in range(GROUP):
            brick = asked[device, group * GROUP + slot]
            shift = (BZ * slot - BZ * (brick % GROUP) + LANES) % LANES
            rolled = pltpu.roll(table[brick // GROUP], shift, 1)
            packed = jnp.where(lane_slot == slot, rolled, packed)
        out[device, group] = packed
        return carry

    lax.fori_loop(0, out.shape[0] * groups, one_group, 0)


def pick_bricks(asked, velocity):
    devices, slots = asked.shape
    size_x, size_y, size_z = velocity.shape[1:]
    places = (size_x // BX) * (size_y // BY) * (size_z // LANES)
    return pl.pallas_call(
        pick_body,
        out_shape=jax.ShapeDtypeStruct((devices, slots // GROUP, ROWS, LANES), f32),
        in_specs=[
            pl.BlockSpec(memory_space=pltpu.SMEM),
            pl.BlockSpec(memory_space=pltpu.VMEM),
        ],
        out_specs=pl.BlockSpec(memory_space=pltpu.VMEM),
        scratch_shapes=[pltpu.VMEM((places, ROWS, LANES), f32)],
        compiler_params=vmem_limit(32),
        name="pick_bricks",
    )(asked, velocity)


def permutations():
    inside = BZ * HALF
    spread = np.zeros((2, 2, LANES, 4 * inside), np.float32)
    gather = np.zeros((2 * BY * inside, BY * LANES), np.float32)
    for half in range(2):
        for slot in range(HALF):
            for z in range(BZ):
                outer, inner = (half * HALF + slot) * BZ + z, z * HALF + slot
                for part in range(4):
                    spread[half, part // 2, outer, part * inside + inner] = 1
                for j in range(BY):
                    gather[(half * BY + j) * inside + inner, j * LANES + outer] = 1
    return jnp.asarray(spread, bf16), jnp.asarray(gather, bf16)


def split(value):
    high = value.astype(bf16)
    return high, (value - high.astype(f32)).astype(bf16)


def add_all(values):
    return functools.reduce(jnp.add, values)


def axis_weights(fraction, cells):
    middle = (cells - 1) / 2
    base = jnp.exp(fraction * (2.0 * cells) - float(cells))
    powers = [None, base]
    for i in range(2, cells):
        powers.append(powers[i // 2] * powers[i - i // 2])
    factors = [float(np.exp(middle**2 - (i - middle) ** 2)) for i in range(cells)]
    bells = [None] + [powers[i] * factors[i] for i in range(1, cells)]
    scale = 1.0 / (add_all(bells[1:]) + factors[0])
    weights = [scale * factors[0]] + [bell * scale for bell in bells[1:]]
    mean = add_all(
        [
            (weights[cells - 1 - i] - weights[i]) * (2.0 * (middle - i))
            for i in range(cells // 2)
        ]
    )
    slopes = [w * (2.0 * (i - middle) - mean) for i, w in enumerate(weights)]
    return weights, slopes


def dot(a, b):
    return jnp.dot(a, b, preferred_element_type=f32)


def gradients(products, weights_x, weights_y, markers):
    (weight_x, slope_x), (weight_y, slope_y) = weights_x, weights_y
    grads = []
    for c in range(3):
        lines = [[], [], []]
        for i in range(BX):
            rows = [((c * BX + i) * BY + j) * HALF for j in range(BY)]
            still = [products[row : row + HALF, :markers] for row in rows]
            rising = [products[row : row + HALF, markers:] for row in rows]
            lines[0].append(slope_x[i] * add_all([w * t for w, t in zip(weight_y, still)]))
            lines[1].append(weight_x[i] * add_all([w * t for w, t in zip(slope_y, still)]))
            lines[2].append(weight_x[i] * add_all([w * t for w, t in zip(weight_y, rising)]))
        grads.append([add_all(line) for line in lines])
    return grads


def marker_halves(halves, live_count, spread, gather, places, start, dens, brick, visc_out, work):
    permuted, left, right, products, factors, planes_high, planes_low, sums = work
    markers = places.shape[-1]
    inside = BZ * HALF
    lane = lax.broadcasted_iota(jnp.int32, (HALF, 4 * inside), 1)
    sub = lax.broadcasted_iota(jnp.int32, (HALF, 4 * inside), 0)
    own = (lane % HALF == sub).astype(f32)
    parts = split(brick)
    weights = {}
    for half in halves:
        permuted[half] = dot(parts[0], spread[half, 0]) + dot(parts[1], spread[half, 1])
        lo, hi = half * HALF, (half + 1) * HALF
        weight_z, slope_z = axis_weights(places[0, 2, lo:hi, :], BZ)
        for z in range(0, BZ, 2):
            for column, values in ((0, weight_z), (1, slope_z)):
                high, low = split(jnp.concatenate(values[z : z + 2], axis=0))
                columns = slice(column * markers, (column + 1) * markers)
                for part in range(4):
                    begin = part * inside + z * HALF
                    right[half, begin : begin + 2 * HALF, columns] = low if part % 2 else high
        for row in range(0, ROWS, 2):
            pair = [
                jnp.broadcast_to(permuted[half, r : r + 1, :], own.shape) * own
                for r in (row, row + 1)
            ]
            left[half, row * HALF : (row + 2) * HALF, :] = jnp.concatenate(pair, axis=0).astype(
                bf16
            )
        products[half] = dot(left[half], right[half])

        weights_x = axis_weights(places[0, 0, lo:hi, :], BX)
        weights_y = axis_weights(places[0, 1, lo:hi, :], BY)
        weights[half] = (weights_x, weights_y)
        for j in range(BY):
            for z in range(0, BZ, 2):
                pair = [weights_y[0][j] * weight_z[z + k] for k in range(2)]
                rows = slice((j * BZ + z) * HALF, (j * BZ + z + 2) * HALF)
                high, low = split(jnp.concatenate(pair, axis=0))
                planes_high[half, rows, :] = high
                planes_low[half, rows, :] = low

    contract = (((1,), (1,)), ((), ()))
    for half in halves:
        lo, hi = half * HALF, (half + 1) * HALF
        weights_x, weights_y = weights[half]
        grads = gradients(products.at[half], weights_x, weights_y, markers)
        normal = grads[0][0] ** 2 + grads[1][1] ** 2 + grads[2][2] ** 2
        shear_xy = 0.5 * (grads[0][1] + grads[1][0])
        shear_xz = 0.5 * (grads[0][2] + grads[2][0])
        shear_yz = 0.5 * (grads[1][2] + grads[2][1])
        invariant = 0.5 * normal + shear_xy**2 + shear_xz**2 + shear_yz**2
        third = jnp.log(1.0 + invariant * (1.0 / (STRAIN_SCALE * STRAIN_SCALE))) * (1.0 / 3.0)
        first = start[0, lo:hi, :]
        slot = lax.broadcasted_iota(jnp.int32, first.shape, 0) + lo
        live = slot < live_count
        visc_out[0, lo:hi, :] = jnp.where(live, first * jnp.exp(-third), 0.0)
        carried = (
            live.astype(f32),
            jnp.where(live, jnp.log(first) - third, 0.0),
            jnp.where(live, dens[0, lo:hi, :], 0.0),
        )
        count = 3 * BX * HALF
        for c in range(3):
            for i in range(0, BX, 2):
                pair = [carried[c] * weights_x[0][i + k] for k in range(2)]
                row = (c * BX + i) * HALF
                high, low = split(jnp.concatenate(pair, axis=0))
                factors[half, row : row + 2 * HALF, :] = high
                factors[half, count + row : count + row + 2 * HALF, :] = low
        both = lax.dot_general(
            factors[half], planes_high[half], contract, preferred_element_type=f32
        )
        rest = lax.dot_general(
            factors[half, :count], planes_low[half], contract, preferred_element_type=f32
        )
        total = both[:count] + both[count:] + rest
        chosen = total.reshape(3 * BX, HALF, BY * inside) * own[None]
        packed = jnp.sum(chosen, axis=1)
        high, low = split(packed)
        columns = slice(half * BY * inside, (half + 1) * BY * inside)
        sums[: 3 * BX, columns] = high.astype(f32)
        sums[16 : 16 + 3 * BX, columns] = low.astype(f32)


def marker_body(first_owner, aliased, counts, spread, gather, places, start, dens, brick, *rest):
    visc_out, moments_out, *work = rest[aliased:]
    owner, group = first_owner + pl.program_id(0), pl.program_id(1)
    live_count = counts[0, owner] - group * GROUP
    sums = work[-1]

    def run(halves):
        marker_halves(
            halves, live_count, spread, gather, places, start, dens, brick[0, 0], visc_out, work
        )
        moved = dot(sums[...].astype(bf16), gather[...])
        moved = moved[: 3 * BX] + moved[16 : 16 + 3 * BX]
        for j in range(BY):
            rows = pl.ds(j, 3 * BX, stride=BY)
            moments_out[0, 0, rows, :] = moved[:, j * LANES : (j + 1) * LANES]

    @pl.when(live_count <= 0)
    def _():
        visc_out[...] = jnp.zeros_like(visc_out)
        moments_out[...] = jnp.zeros_like(moments_out)

    @pl.when(jnp.logical_and(live_count > 0, live_count <= HALF))
    def _():
        sums[...] = jnp.zeros_like(sums)
        visc_out[:, HALF:, :] = jnp.zeros((1, HALF, visc_out.shape[-1]), f32)
        run((0,))

    @pl.when(live_count > HALF)
    def _():
        sums[...] = jnp.zeros_like(sums)
        run((0, 1))


def marker_work(counts, positions, start_visc, marker_dens, bricks, begin, end, earlier=()):
    owners, _, slots, markers = positions.shape
    groups = slots // GROUP
    spread, gather = permutations()
    width = 4 * BZ * HALF
    operands = (counts, spread, gather, positions, start_visc, marker_dens, bricks)
    visits = (end - begin) * slots * markers
    return pl.pallas_call(
        functools.partial(marker_body, begin, len(earlier)),
        grid=(end - begin, groups),
        out_shape=(
            jax.ShapeDtypeStruct((owners, slots, markers), f32),
            jax.ShapeDtypeStruct((owners, groups, ROWS, LANES), f32),
        ),
        in_specs=[
            pl.BlockSpec(memory_space=pltpu.SMEM),
            pl.BlockSpec(spread.shape, lambda q, g: (0, 0, 0, 0)),
            pl.BlockSpec(gather.shape, lambda q, g: (0, 0)),
            pl.BlockSpec((1, 3, GROUP, markers), lambda q, g: (q + begin, 0, g, 0)),
            pl.BlockSpec((1, GROUP, markers), lambda q, g: (q + begin, g, 0)),
            pl.BlockSpec((1, GROUP, markers), lambda q, g: (q + begin, g, 0)),
            pl.BlockSpec((1, 1, ROWS, LANES), lambda q, g: (q + begin, g, 0, 0)),
        ]
        + [pl.BlockSpec(memory_space=pl.ANY)] * len(earlier),
        out_specs=(
            pl.BlockSpec((1, GROUP, markers), lambda q, g: (q + begin, g, 0)),
            pl.BlockSpec((1, 1, ROWS, LANES), lambda q, g: (q + begin, g, 0, 0)),
        ),
        input_output_aliases={len(operands) + n: n for n in range(len(earlier))},
        scratch_shapes=[
            pltpu.VMEM((2, ROWS, width), f32),
            pltpu.VMEM((2, ROWS * HALF, width), bf16),
            pltpu.VMEM((2, width, 2 * markers), bf16),
            pltpu.VMEM((2, ROWS * HALF, 2 * markers), f32),
            pltpu.VMEM((2, 2 * 3 * BX * HALF, markers), bf16),
            pltpu.VMEM((2, BY * BZ * HALF, markers), bf16),
            pltpu.VMEM((2, BY * BZ * HALF, markers), bf16),
            pltpu.VMEM((32, 2 * BY * BZ * HALF), f32),
        ],
        compiler_params=vmem_limit(60),
        cost_estimate=pl.CostEstimate(
            flops=visits * 100000, bytes_accessed=visits * 32, transcendentals=visits * 8
        ),
        name="marker_work",
    )(*operands, *earlier)


def settle_body(asked, moments, visc, dens, visc_out, dens_out, table):
    size_x, size_y, size_z = visc.shape
    bricks_y, halves = size_y // BY, size_z // LANES
    table[...] = jnp.zeros_like(table)
    groups = moments.shape[1]
    lane_slot = lax.broadcasted_iota(jnp.int32, (ROWS, LANES), 1) // BZ

    def one_group(step, carry):
        device, group = step // groups, step % groups
        packed = moments[device, group]
        for slot in range(GROUP):
            brick = asked[device, group * GROUP + slot]
            shift = (BZ * (brick % GROUP) - BZ * slot + LANES) % LANES
            piece = pltpu.roll(jnp.where(lane_slot == slot, packed, 0.0), shift, 1)
            place = brick // GROUP
            table[place] = table[place] + piece
        return carry

    lax.fori_loop(0, moments.shape[0] * groups, one_group, 0)

    def finish(block_x, carry):
        for block_y in range(bricks_y):
            for half in range(halves):
                place = (block_x * bricks_y + block_y) * halves + half
                for i in range(BX):
                    here = (
                        block_x * BX + i,
                        slice(block_y * BY, (block_y + 1) * BY),
                        slice(half * LANES, (half + 1) * LANES),
                    )
                    sums = [
                        table[place, (c * BX + i) * BY : (c * BX + i + 1) * BY, :]
                        for c in range(3)
                    ]
                    scale = 1.0 / (sums[0] + 1.0)
                    visc_out[here] = jnp.exp((sums[1] + jnp.log(visc[here])) * scale)
                    dens_out[here] = (sums[2] + dens[here]) * scale
        return carry

    lax.fori_loop(0, size_x // BX, finish, 0)


def settle(asked, moments, cell_visc, cell_dens):
    size_x, size_y, size_z = cell_visc.shape
    places = (size_x // BX) * (size_y // BY) * (size_z // LANES)
    whole = pl.BlockSpec(memory_space=pltpu.VMEM)
    shape = jax.ShapeDtypeStruct(cell_visc.shape, f32)
    return pl.pallas_call(
        settle_body,
        out_shape=(shape, shape),
        in_specs=[pl.BlockSpec(memory_space=pltpu.SMEM), whole, whole, whole],
        out_specs=(whole, whole),
        scratch_shapes=[pltpu.VMEM((places, ROWS, LANES), f32)],
        compiler_params=vmem_limit(32),
        name="settle",
    )(asked, moments, cell_visc, cell_dens)


def pack_y_body(vel, pres, visc, dens, upward, downward):
    size_y = pres.shape[1]
    width = SWEEPS
    for f in range(6):
        field = vel.at[f] if f < 3 else (pres, visc, dens)[f - 3]
        rows = slice(f * width, (f + 1) * width)
        upward[:, rows, :] = field[:, size_y - width :, :]
        downward[:, rows, :] = field[:, :width, :]


def pack_y(velocity, pressure, cell_visc, cell_dens):
    size_x, size_y, size_z = cell_visc.shape
    step = 8
    block = pl.BlockSpec((step, size_y, size_z), lambda i: (i, 0, 0))
    face = pl.BlockSpec((step, 6 * SWEEPS, size_z), lambda i: (i, 0, 0))
    shape = jax.ShapeDtypeStruct((size_x, 6 * SWEEPS, size_z), f32)
    return pl.pallas_call(
        pack_y_body,
        grid=(size_x // step,),
        out_shape=(shape, shape),
        in_specs=[
            pl.BlockSpec((3, step, size_y, size_z), lambda i: (0, i, 0, 0)),
            block,
            block,
            block,
        ],
        out_specs=(face, face),
        compiler_params=vmem_limit(60),
        name="pack_y",
    )(velocity, pressure, cell_visc, cell_dens)


def pack_x_body(vels, press, viscs, denss, low_ys, high_ys, *outs):
    width = SWEEPS
    for side in range(2):
        vel, pres, visc, dens = vels[side], press[side], viscs[side], denss[side]
        size_y = pres.shape[1]
        for f in range(6):
            field = vel.at[f] if f < 3 else (pres, visc, dens)[f - 3]
            rows = slice(f * width, (f + 1) * width)
            outs[side][f, :, :size_y, :] = field[...]
            outs[side][f, :, size_y : size_y + width, :] = high_ys[side][:, rows, :]
            outs[side][f, :, size_y + width :, :] = low_ys[side][:, rows, :]


def pack_x(velocity, pressure, cell_visc, cell_dens, low_y, high_y, after):
    size_x, size_y, size_z = cell_visc.shape
    width = SWEEPS
    ends = (0, size_x // width - 1)
    ring = size_y + 2 * width

    def body(*refs):
        pairs = [refs[2 * n : 2 * n + 2] for n in range(6)]
        pack_x_body(*pairs, *refs[12 + len(after) :])

    def block(rows):
        return [pl.BlockSpec((width, rows, size_z), lambda i, e=e: (e, 0, 0)) for e in ends]

    whole = pl.BlockSpec((6, width, ring, size_z), lambda i: (0, 0, 0, 0))
    shape = jax.ShapeDtypeStruct((6, width, ring, size_z), f32)
    return pl.pallas_call(
        body,
        grid=(1,),
        out_shape=(shape, shape),
        in_specs=[
            pl.BlockSpec((3, width, size_y, size_z), lambda i, e=e: (0, e, 0, 0)) for e in ends
        ]
        + block(size_y) * 3
        + block(6 * width) * 2
        + [pl.BlockSpec(memory_space=pl.ANY)] * len(after),
        out_specs=(whole, whole),
        compiler_params=vmem_limit(60),
        name="pack_x",
    )(
        velocity,
        velocity,
        pressure,
        pressure,
        cell_visc,
        cell_visc,
        cell_dens,
        cell_dens,
        low_y,
        low_y,
        high_y,
        high_y,
        *after,
    )


def sweep_body(vel, pres, visc, dens, low_x, high_x, low_y, high_y, vel_out, pres_out, *work):
    fields, coefs, rate, relax, forcing = work
    size_x, size_y, size_z = visc.shape
    width = low_x.shape[1]
    long_x = size_x + 2 * width
    ring = fields.shape[3]
    inner = slice(width, width + size_x)
    own = slice(0, size_y)
    for c in range(3):
        fields[0, c, inner, own, :] = vel[c]
    fields[0, 3, inner, own, :] = pres[...]
    fields[1, 0, inner, own, :] = visc[...]
    fields[1, 1, inner, own, :] = dens[...]
    for f in range(6):
        slot = (0, f) if f < 4 else (1, f - 4)
        rows = slice(f * width, (f + 1) * width)
        fields[slot[0], slot[1], :width] = low_x[f]
        fields[slot[0], slot[1], width + size_x :] = high_x[f]
        fields[slot[0], slot[1], inner, size_y : size_y + width, :] = high_y[:, rows, :]
        fields[slot[0], slot[1], inner, size_y + width :, :] = low_y[:, rows, :]

    lane = lax.broadcasted_iota(jnp.int32, (ring, size_z), 1)
    not_last = (lane < size_z - 1).astype(f32)
    not_first = (lane > 0).astype(f32)

    def up_y(a):
        return pltpu.roll(a, ring - 1, 0)

    def down_y(a):
        return pltpu.roll(a, 1, 0)

    def up_z(a):
        return pltpu.roll(a, size_z - 1, 1)

    def down_z(a):
        return pltpu.roll(a, 1, 1)

    def prepare(i, carry):
        here = fields[1, 0, i]
        near = [
            fields[1, 0, i + 1],
            fields[1, 0, i - 1],
            up_y(here),
            down_y(here),
            up_z(here) * not_last,
            down_z(here) * not_first,
        ]
        links = [0.5 * (here + other) for other in near]
        diagonal = functools.reduce(jnp.add, links)
        scale = jnp.where(here > 0.0, RELAX / diagonal, 0.0)
        links[4] = links[4] * not_last
        links[5] = links[5] * not_first
        for n in range(6):
            coefs[n, i] = links[n] * scale
        relax[i] = scale
        forcing[i] = fields[1, 1, i] * (-GRAVITY * scale)
        rate[i] = PRESSURE_RATE * here
        return carry

    lax.fori_loop(1, long_x - 1, prepare, 0)

    for sweep in range(SWEEPS):
        old, new = sweep % 2, (sweep + 1) % 2
        last = sweep == SWEEPS - 1

        def one_plane(i, carry, old=old, new=new, last=last):
            pressure = fields[old, 3, i]
            links = [coefs[n, i] for n in range(6)]
            scale = relax[i]
            before = (
                fields[old, 3, i - 1],
                down_y(pressure),
                down_z(pressure) * not_first,
            )
            divergence = None
            for c in range(3):
                here = fields[old, c, i]
                near = [
                    fields[old, c, i + 1],
                    fields[old, c, i - 1],
                    up_y(here),
                    down_y(here),
                    up_z(here),
                    down_z(here),
                ]
                total = (1.0 - RELAX) * here - scale * (pressure - before[c])
                for link, other in zip(links, near):
                    total = total + link * other
                ahead = near[2 * c]
                if c == 2:
                    total = total + forcing[i]
                    ahead = ahead * not_last
                change = ahead - here
                divergence = change if divergence is None else divergence + change
                if last:
                    vel_out[c, i - width] = total[:size_y]
                else:
                    fields[new, c, i] = total
            pressed = pressure - rate[i] * divergence
            if last:
                pres_out[i - width] = pressed[:size_y]
            else:
                fields[new, 3, i] = pressed
            return carry

        lax.fori_loop(1 + sweep, long_x - 1 - sweep, one_plane, 0)


def all_sweeps(velocity, pressure, cell_visc, cell_dens, low_x, high_x, low_y, high_y):
    size_x, size_y, size_z = cell_visc.shape
    _, width, ring, _ = low_x.shape
    long_x = size_x + 2 * width
    whole = pl.BlockSpec(memory_space=pltpu.VMEM)
    block = (long_x, ring, size_z)
    return pl.pallas_call(
        sweep_body,
        out_shape=(
            jax.ShapeDtypeStruct(velocity.shape, f32),
            jax.ShapeDtypeStruct(pressure.shape, f32),
        ),
        in_specs=[whole] * 8,
        out_specs=(whole, whole),
        scratch_shapes=[
            pltpu.VMEM((2, 4) + block, f32),
            pltpu.VMEM((6,) + block, f32),
            pltpu.VMEM(block, f32),
            pltpu.VMEM(block, f32),
            pltpu.VMEM(block, f32),
        ],
        compiler_params=vmem_limit(48),
        name="all_sweeps",
    )(velocity, pressure, cell_visc, cell_dens, low_x, high_x, low_y, high_y)


def shift(value, axis, step):
    size = lax.axis_size(axis)
    pairs = [(i, i + step) for i in range(size) if 0 <= i + step < size]
    return lax.ppermute(value, axis, pairs)


def per_device(
    velocity,
    pressure,
    cell_visc,
    cell_dens,
    block_brick,
    block_counts,
    positions,
    start_visc,
    marker_dens,
):
    asked = lax.all_to_all(block_brick, "mark", 0, 0, tiled=True)
    fields = (velocity, pressure, cell_visc, cell_dens)
    upward, downward = pack_y(*fields)
    low_y, high_y = shift(upward, "mark", 1), shift(downward, "mark", -1)

    picked = pick_bricks(asked, velocity)
    bricks = lax.all_to_all(picked, "mark", 0, 0, tiled=True)
    owners = positions.shape[0]
    middle = owners // 2
    marker_data = (block_counts, positions, start_visc, marker_dens, bricks)
    earlier = marker_work(*marker_data, 0, middle)
    to_low, to_high = pack_x(*fields, low_y, high_y, earlier[1:])
    low_x, high_x = shift(to_high, "grid", 1), shift(to_low, "grid", -1)
    earlier, to_low, to_high = lax.optimization_barrier((earlier, to_low, to_high))
    marker_visc, moments = marker_work(*marker_data, middle, owners, earlier)
    gathered = lax.all_to_all(moments, "mark", 0, 0, tiled=True)
    velocity_next, pressure_next = all_sweeps(*fields, low_x, high_x, low_y, high_y)
    visc_next, dens_next = settle(asked, gathered, cell_visc, cell_dens)
    return velocity_next, pressure_next, visc_next, dens_next, marker_visc


def solution(mesh):
    in_specs = (
        P(None, "grid", "mark", None),
        P("grid", "mark", None),
        P("grid", "mark", None),
        P("grid", "mark", None),
        P(("grid", "mark"), None),
        P(("grid", "mark"), None),
        P(("grid", "mark"), None, None, None),
        P(("grid", "mark"), None, None),
        P(("grid", "mark"), None, None),
    )
    out_specs = (
        P(None, "grid", "mark", None),
        P("grid", "mark", None),
        P("grid", "mark", None),
        P("grid", "mark", None),
        P(("grid", "mark"), None, None),
    )
    return jax.shard_map(
        per_device, mesh=mesh, in_specs=in_specs, out_specs=out_specs, check_vma=False
    )
```

```python
import functools

import jax
import jax.numpy as jnp
import numpy as np
from jax import lax
from jax.experimental import pallas as pl
from jax.experimental.pallas import tpu as pltpu
from jax.sharding import PartitionSpec as P

SWEEPS = 4
RELAX = 0.6
PRESSURE_RATE = 0.25
GRAVITY = 1.0
STRAIN_SCALE = 0.5

BX, BY, BZ = 4, 4, 8
PLANE = BX * BY
ROWS = 3 * PLANE
LANES = 128
GROUP = LANES // BZ
HALF = 8

f32, bf16 = jnp.float32, jnp.bfloat16


def vmem_limit(mib):
    return pltpu.CompilerParams(vmem_limit_bytes=mib * 1024 * 1024)


def cost(microseconds):
    return pl.CostEstimate(
        flops=int(microseconds * 1.15e9), bytes_accessed=0, transcendentals=0
    )


def pick_body(asked, vel, out, table):
    size_x, size_y, size_z = vel.shape[1:]
    bricks_y, halves = size_y // BY, size_z // LANES

    def repack(block_x, carry):
        for block_y in range(bricks_y):
            for half in range(halves):
                place = (block_x * bricks_y + block_y) * halves + half
                for c in range(3):
                    for i in range(BX):
                        row = (c * BX + i) * BY
                        table[place, row : row + BY, :] = vel[
                            c,
                            block_x * BX + i,
                            block_y * BY : (block_y + 1) * BY,
                            half * LANES : (half + 1) * LANES,
                        ]
        return carry

    lax.fori_loop(0, size_x // BX, repack, 0)
    groups = out.shape[1]
    lane_slot = lax.broadcasted_iota(jnp.int32, (ROWS, LANES), 1) // BZ

    def one_group(step, carry):
        device, group = step // groups, step % groups
        packed = jnp.zeros((ROWS, LANES), f32)
        for slot in range(GROUP):
            brick = asked[device, group * GROUP + slot]
            shift = (BZ * slot - BZ * (brick % GROUP) + LANES) % LANES
            rolled = pltpu.roll(table[brick // GROUP], shift, 1)
            packed = jnp.where(lane_slot == slot, rolled, packed)
        out[device, group] = packed
        return carry

    lax.fori_loop(0, out.shape[0] * groups, one_group, 0)


def pick_bricks(asked, velocity):
    devices, slots = asked.shape
    size_x, size_y, size_z = velocity.shape[1:]
    places = (size_x // BX) * (size_y // BY) * (size_z // LANES)
    return pl.pallas_call(
        pick_body,
        out_shape=jax.ShapeDtypeStruct((devices, slots // GROUP, ROWS, LANES), f32),
        in_specs=[
            pl.BlockSpec(memory_space=pltpu.SMEM),
            pl.BlockSpec(memory_space=pltpu.VMEM),
        ],
        out_specs=pl.BlockSpec(memory_space=pltpu.VMEM),
        scratch_shapes=[pltpu.VMEM((places, ROWS, LANES), f32)],
        compiler_params=vmem_limit(60),
        cost_estimate=cost(7),
        name="pick_bricks",
    )(asked, velocity)


def permutations():
    inside = BZ * HALF
    spread = np.zeros((2, 2, LANES, 4 * inside), np.float32)
    gather = np.zeros((2 * BY * inside, BY * LANES), np.float32)
    for half in range(2):
        for slot in range(HALF):
            for z in range(BZ):
                outer, inner = (half * HALF + slot) * BZ + z, z * HALF + slot
                for part in range(4):
                    spread[half, part // 2, outer, part * inside + inner] = 1
                for j in range(BY):
                    gather[(half * BY + j) * inside + inner, j * LANES + outer] = 1
    return jnp.asarray(spread, bf16), jnp.asarray(gather, bf16)


def split(value):
    high = value.astype(bf16)
    return high, (value - high.astype(f32)).astype(bf16)


def add_all(values):
    return functools.reduce(jnp.add, values)


def axis_weights(fraction, cells):
    middle = (cells - 1) / 2
    base = jnp.exp(fraction * (2.0 * cells) - float(cells))
    powers = [None, base]
    for i in range(2, cells):
        powers.append(powers[i // 2] * powers[i - i // 2])
    factors = [float(np.exp(middle**2 - (i - middle) ** 2)) for i in range(cells)]
    bells = [None] + [powers[i] * factors[i] for i in range(1, cells)]
    scale = 1.0 / (add_all(bells[1:]) + factors[0])
    weights = [scale * factors[0]] + [bell * scale for bell in bells[1:]]
    mean = add_all(
        [
            (weights[cells - 1 - i] - weights[i]) * (2.0 * (middle - i))
            for i in range(cells // 2)
        ]
    )
    slopes = [w * (2.0 * (i - middle) - mean) for i, w in enumerate(weights)]
    return weights, slopes


def dot(a, b):
    return jnp.dot(a, b, preferred_element_type=f32)


def gradients(products, weights_x, weights_y, markers):
    (weight_x, slope_x), (weight_y, slope_y) = weights_x, weights_y
    grads = []
    for c in range(3):
        lines = [[], [], []]
        for i in range(BX):
            rows = [((c * BX + i) * BY + j) * HALF for j in range(BY)]
            still = [products[row : row + HALF, :markers] for row in rows]
            rising = [products[row : row + HALF, markers:] for row in rows]
            lines[0].append(slope_x[i] * add_all([w * t for w, t in zip(weight_y, still)]))
            lines[1].append(weight_x[i] * add_all([w * t for w, t in zip(slope_y, still)]))
            lines[2].append(weight_x[i] * add_all([w * t for w, t in zip(weight_y, rising)]))
        grads.append([add_all(line) for line in lines])
    return grads


def marker_halves(halves, live_count, spread, gather, places, start, dens, brick, visc_out, work):
    permuted, left, right, products, factors, planes_high, planes_low, sums = work
    markers = places.shape[-1]
    inside = BZ * HALF
    lane = lax.broadcasted_iota(jnp.int32, (HALF, 4 * inside), 1)
    sub = lax.broadcasted_iota(jnp.int32, (HALF, 4 * inside), 0)
    own = (lane % HALF == sub).astype(f32)
    parts = split(brick)
    weights = {}
    for half in halves:
        permuted[half] = dot(parts[0], spread[half, 0]) + dot(parts[1], spread[half, 1])
        lo, hi = half * HALF, (half + 1) * HALF
        weight_z, slope_z = axis_weights(places[0, 2, lo:hi, :], BZ)
        for z in range(0, BZ, 2):
            for column, values in ((0, weight_z), (1, slope_z)):
                high, low = split(jnp.concatenate(values[z : z + 2], axis=0))
                columns = slice(column * markers, (column + 1) * markers)
                for part in range(4):
                    begin = part * inside + z * HALF
                    right[half, begin : begin + 2 * HALF, columns] = low if part % 2 else high
        for row in range(0, ROWS, 2):
            pair = [
                jnp.broadcast_to(permuted[half, r : r + 1, :], own.shape) * own
                for r in (row, row + 1)
            ]
            left[half, row * HALF : (row + 2) * HALF, :] = jnp.concatenate(pair, axis=0).astype(
                bf16
            )
        products[half] = dot(left[half], right[half])

        weights_x = axis_weights(places[0, 0, lo:hi, :], BX)
        weights_y = axis_weights(places[0, 1, lo:hi, :], BY)
        weights[half] = (weights_x, weights_y)
        for j in range(BY):
            for z in range(0, BZ, 2):
                pair = [weights_y[0][j] * weight_z[z + k] for k in range(2)]
                rows = slice((j * BZ + z) * HALF, (j * BZ + z + 2) * HALF)
                high, low = split(jnp.concatenate(pair, axis=0))
                planes_high[half, rows, :] = high
                planes_low[half, rows, :] = low

    contract = (((1,), (1,)), ((), ()))
    for half in halves:
        lo, hi = half * HALF, (half + 1) * HALF
        weights_x, weights_y = weights[half]
        grads = gradients(products.at[half], weights_x, weights_y, markers)
        normal = grads[0][0] ** 2 + grads[1][1] ** 2 + grads[2][2] ** 2
        shear_xy = 0.5 * (grads[0][1] + grads[1][0])
        shear_xz = 0.5 * (grads[0][2] + grads[2][0])
        shear_yz = 0.5 * (grads[1][2] + grads[2][1])
        invariant = 0.5 * normal + shear_xy**2 + shear_xz**2 + shear_yz**2
        third = jnp.log(1.0 + invariant * (1.0 / (STRAIN_SCALE * STRAIN_SCALE))) * (1.0 / 3.0)
        first = start[0, lo:hi, :]
        slot = lax.broadcasted_iota(jnp.int32, first.shape, 0) + lo
        live = slot < live_count
        visc_out[0, lo:hi, :] = jnp.where(live, first * jnp.exp(-third), 0.0)
        carried = (
            live.astype(f32),
            jnp.where(live, jnp.log(first) - third, 0.0),
            jnp.where(live, dens[0, lo:hi, :], 0.0),
        )
        count = 3 * BX * HALF
        for c in range(3):
            for i in range(0, BX, 2):
                pair = [carried[c] * weights_x[0][i + k] for k in range(2)]
                row = (c * BX + i) * HALF
                high, low = split(jnp.concatenate(pair, axis=0))
                factors[half, row : row + 2 * HALF, :] = high
                factors[half, count + row : count + row + 2 * HALF, :] = low
        both = lax.dot_general(
            factors[half], planes_high[half], contract, preferred_element_type=f32
        )
        rest = lax.dot_general(
            factors[half, :count], planes_low[half], contract, preferred_element_type=f32
        )
        total = both[:count] + both[count:] + rest
        chosen = total.reshape(3 * BX, HALF, BY * inside) * own[None]
        packed = jnp.sum(chosen, axis=1)
        high, low = split(packed)
        columns = slice(half * BY * inside, (half + 1) * BY * inside)
        sums[: 3 * BX, columns] = high.astype(f32)
        sums[16 : 16 + 3 * BX, columns] = low.astype(f32)


def marker_body(
    counts, spread, gather, places, start, dens, brick, _, visc_out, moments_out, *work
):
    owner, group = pl.program_id(0), pl.program_id(1)
    live_count = counts[0, owner] - group * GROUP
    sums = work[-1]

    def run(halves):
        marker_halves(
            halves, live_count, spread, gather, places, start, dens, brick[0, 0], visc_out, work
        )
        moved = dot(sums[...].astype(bf16), gather[...])
        moved = moved[: 3 * BX] + moved[16 : 16 + 3 * BX]
        for j in range(BY):
            rows = pl.ds(j, 3 * BX, stride=BY)
            moments_out[0, 0, rows, :] = moved[:, j * LANES : (j + 1) * LANES]

    @pl.when(live_count <= 0)
    def _():
        visc_out[...] = jnp.zeros_like(visc_out)
        moments_out[...] = jnp.zeros_like(moments_out)

    @pl.when(jnp.logical_and(live_count > 0, live_count <= HALF))
    def _():
        sums[...] = jnp.zeros_like(sums)
        visc_out[:, HALF:, :] = jnp.zeros((1, HALF, visc_out.shape[-1]), f32)
        run((0,))

    @pl.when(live_count > HALF)
    def _():
        sums[...] = jnp.zeros_like(sums)
        run((0, 1))


def marker_work(counts, positions, start_visc, marker_dens, bricks, after):
    owners, _, slots, markers = positions.shape
    groups = slots // GROUP
    spread, gather = permutations()
    width = 4 * BZ * HALF
    return pl.pallas_call(
        marker_body,
        grid=(owners, groups),
        out_shape=(
            jax.ShapeDtypeStruct((owners, slots, markers), f32),
            jax.ShapeDtypeStruct((owners, groups, ROWS, LANES), f32),
        ),
        in_specs=[
            pl.BlockSpec(memory_space=pltpu.SMEM),
            pl.BlockSpec(spread.shape, lambda q, g: (0, 0, 0, 0)),
            pl.BlockSpec(gather.shape, lambda q, g: (0, 0)),
            pl.BlockSpec((1, 3, GROUP, markers), lambda q, g: (q, 0, g, 0)),
            pl.BlockSpec((1, GROUP, markers), lambda q, g: (q, g, 0)),
            pl.BlockSpec((1, GROUP, markers), lambda q, g: (q, g, 0)),
            pl.BlockSpec((1, 1, ROWS, LANES), lambda q, g: (q, g, 0, 0)),
            pl.BlockSpec(memory_space=pl.ANY),
        ],
        out_specs=(
            pl.BlockSpec((1, GROUP, markers), lambda q, g: (q, g, 0)),
            pl.BlockSpec((1, 1, ROWS, LANES), lambda q, g: (q, g, 0, 0)),
        ),
        scratch_shapes=[
            pltpu.VMEM((2, ROWS, width), f32),
            pltpu.VMEM((2, ROWS * HALF, width), bf16),
            pltpu.VMEM((2, width, 2 * markers), bf16),
            pltpu.VMEM((2, ROWS * HALF, 2 * markers), f32),
            pltpu.VMEM((2, 2 * 3 * BX * HALF, markers), bf16),
            pltpu.VMEM((2, BY * BZ * HALF, markers), bf16),
            pltpu.VMEM((2, BY * BZ * HALF, markers), bf16),
            pltpu.VMEM((32, 2 * BY * BZ * HALF), f32),
        ],
        compiler_params=vmem_limit(60),
        cost_estimate=cost(25),
        name="marker_work",
    )(counts, spread, gather, positions, start_visc, marker_dens, bricks, after)


def settle_body(asked, moments, visc, dens, visc_out, dens_out, *tables):
    size_x, size_y, size_z = visc.shape
    bricks_y, halves = size_y // BY, size_z // LANES
    for table in tables:
        table[...] = jnp.zeros_like(table)
    groups = moments.shape[1]
    lane_slot = lax.broadcasted_iota(jnp.int32, (ROWS, LANES), 1) // BZ

    def one_group(step, carry):
        device, group = step // groups, step % groups
        packed = moments[device, group]
        for slot in range(GROUP):
            table = tables[slot % len(tables)]
            brick = asked[device, group * GROUP + slot]
            shift = (BZ * (brick % GROUP) - BZ * slot + LANES) % LANES
            piece = pltpu.roll(jnp.where(lane_slot == slot, packed, 0.0), shift, 1)
            place = brick // GROUP
            table[place] = table[place] + piece
        return carry

    lax.fori_loop(0, moments.shape[0] * groups, one_group, 0)

    def finish(block_x, carry):
        for block_y in range(0, bricks_y, 2):
            for half in range(halves):
                for i in range(BX):
                    here = (
                        block_x * BX + i,
                        slice(block_y * BY, (block_y + 2) * BY),
                        slice(half * LANES, (half + 1) * LANES),
                    )
                    sums = []
                    for c in range(3):
                        rows = slice((c * BX + i) * BY, (c * BX + i + 1) * BY)
                        places = [
                            (block_x * bricks_y + block_y + k) * halves + half for k in range(2)
                        ]
                        sums.append(
                            jnp.concatenate(
                                [add_all([t[place, rows, :] for t in tables]) for place in places]
                            )
                        )
                    scale = 1.0 / (sums[0] + 1.0)
                    visc_out[here] = jnp.exp((sums[1] + jnp.log(visc[here])) * scale)
                    dens_out[here] = (sums[2] + dens[here]) * scale
        return carry

    lax.fori_loop(0, size_x // BX, finish, 0)


def settle(asked, moments, cell_visc, cell_dens):
    size_x, size_y, size_z = cell_visc.shape
    places = (size_x // BX) * (size_y // BY) * (size_z // LANES)
    whole = pl.BlockSpec(memory_space=pltpu.VMEM)
    shape = jax.ShapeDtypeStruct(cell_visc.shape, f32)
    return pl.pallas_call(
        settle_body,
        out_shape=(shape, shape),
        in_specs=[pl.BlockSpec(memory_space=pltpu.SMEM), whole, whole, whole],
        out_specs=(whole, whole),
        scratch_shapes=[pltpu.VMEM((places, ROWS, LANES), f32)] * 2,
        compiler_params=vmem_limit(60),
        cost_estimate=cost(7),
        name="settle",
    )(asked, moments, cell_visc, cell_dens)


def field_of(fields, index):
    return fields[0].at[index] if index < 3 else fields[index - 2]


def pack_x_body(*refs):
    ends, outs = refs[:8], refs[8:]
    for side in range(2):
        for f in range(6):
            outs[side][f] = field_of(ends[side::2], f)[...]


def pack_x(velocity, pressure, cell_visc, cell_dens):
    size_x, size_y, size_z = cell_visc.shape
    width = SWEEPS
    ends = (0, size_x // width - 1)
    vel = [
        pl.BlockSpec((3, width, size_y, size_z), lambda i, e=e: (0, e, 0, 0)) for e in ends
    ]
    block = [pl.BlockSpec((width, size_y, size_z), lambda i, e=e: (e, 0, 0)) for e in ends]
    whole = pl.BlockSpec((6, width, size_y, size_z), lambda i: (0, 0, 0, 0))
    shape = jax.ShapeDtypeStruct((6, width, size_y, size_z), f32)
    return pl.pallas_call(
        pack_x_body,
        grid=(1,),
        out_shape=(shape, shape),
        in_specs=vel + block * 3,
        out_specs=(whole, whole),
        compiler_params=vmem_limit(60),
        cost_estimate=cost(2),
        name="pack_x",
    )(velocity, velocity, pressure, pressure, cell_visc, cell_visc, cell_dens, cell_dens)


def corner_rows(field):
    found, width = [], SWEEPS
    per_field = width * (width - 1)
    for side in range(2):
        for far_x in range(1, width):
            for far_y in range(1, width - far_x + 1):
                flat = field * per_field + len(found)
                found.append((side, far_x, far_y, *divmod(flat, 6 * width)))
    return found


def pack_y_body(vel, pres, visc, dens, low_x, high_x, upward, downward):
    step_x, size_y, _ = pres.shape
    width = SWEEPS
    step = pl.program_id(0)
    planes = pl.ds(pl.multiple_of(step * step_x, step_x), step_x)
    for f in range(6):
        field = field_of((vel, pres, visc, dens), f)
        rows = slice(f * width, (f + 1) * width)
        upward[planes, rows, :] = field[:, size_y - width :, :]
        downward[planes, rows, :] = field[:, :width, :]

    @pl.when(step == 0)
    def _():
        size_x = pl.num_programs(0) * step_x
        for f in range(6):
            for side, far_x, far_y, plane, row in corner_rows(f):
                halo, at = (high_x, far_x - 1) if side else (low_x, width - far_x)
                upward[size_x + plane, row] = halo[f, at, size_y - far_y]
                downward[size_x + plane, row] = halo[f, at, far_y - 1]


def pack_y(velocity, pressure, cell_visc, cell_dens, low_x, high_x):
    size_x, size_y, size_z = cell_visc.shape
    step, width = 8, SWEEPS
    long_x = size_x + width - 1
    block = pl.BlockSpec((step, size_y, size_z), lambda i: (i, 0, 0))
    halo = pl.BlockSpec(low_x.shape, lambda i: (0, 0, 0, 0))
    face = pl.BlockSpec((long_x, 6 * width, size_z), lambda i: (0, 0, 0))
    shape = jax.ShapeDtypeStruct((long_x, 6 * width, size_z), f32)
    return pl.pallas_call(
        pack_y_body,
        grid=(size_x // step,),
        out_shape=(shape, shape),
        in_specs=[
            pl.BlockSpec((3, step, size_y, size_z), lambda i: (0, i, 0, 0)),
            block,
            block,
            block,
            halo,
            halo,
        ],
        out_specs=(face, face),
        compiler_params=vmem_limit(60),
        cost_estimate=cost(3),
        name="pack_y",
    )(velocity, pressure, cell_visc, cell_dens, low_x, high_x)


def sweep_body(vel, pres, visc, dens, low_x, high_x, low_y, high_y, vel_out, pres_out, *work):
    fields, coefs, rate, relax, forcing = work
    size_x, size_y, size_z = visc.shape
    width = low_x.shape[1]
    long_x = size_x + 2 * width
    ring = fields.shape[3]
    inner = slice(width, width + size_x)
    own = slice(0, size_y)
    for c in range(3):
        fields[0, c, inner, own, :] = vel[c]
    fields[0, 3, inner, own, :] = pres[...]
    fields[1, 0, inner, own, :] = visc[...]
    fields[1, 1, inner, own, :] = dens[...]
    for f in range(6):
        field = fields.at[0, f] if f < 4 else fields.at[1, f - 4]
        rows = slice(f * width, (f + 1) * width)
        for at, halo in ((0, low_x), (width + size_x, high_x)):
            field[at : at + width, own, :] = halo[f]
            field[at : at + width, size_y:, :] = jnp.zeros((width, 2 * width, size_z), f32)
        field[inner, size_y : size_y + width, :] = high_y[:size_x, rows, :]
        field[inner, size_y + width :, :] = low_y[:size_x, rows, :]
        for side, far_x, far_y, plane, row in corner_rows(f):
            at = width + size_x - 1 + far_x if side else width - far_x
            field[at, size_y + far_y - 1] = high_y[size_x + plane, row]
            field[at, ring - far_y] = low_y[size_x + plane, row]

    lane = lax.broadcasted_iota(jnp.int32, (ring, size_z), 1)
    not_last = (lane < size_z - 1).astype(f32)
    not_first = (lane > 0).astype(f32)

    def up_y(a):
        return pltpu.roll(a, ring - 1, 0)

    def down_y(a):
        return pltpu.roll(a, 1, 0)

    def up_z(a):
        return pltpu.roll(a, size_z - 1, 1)

    def down_z(a):
        return pltpu.roll(a, 1, 1)

    def prepare(i, carry):
        here = fields[1, 0, i]
        near = [
            fields[1, 0, i + 1],
            fields[1, 0, i - 1],
            up_y(here),
            down_y(here),
            up_z(here) * not_last,
            down_z(here) * not_first,
        ]
        links = [0.5 * (here + other) for other in near]
        diagonal = functools.reduce(jnp.add, links)
        scale = jnp.where(here > 0.0, RELAX / diagonal, 0.0)
        links[4] = links[4] * not_last
        links[5] = links[5] * not_first
        for n in range(6):
            coefs[n, i] = links[n] * scale
        relax[i] = scale
        forcing[i] = fields[1, 1, i] * (-GRAVITY * scale)
        rate[i] = PRESSURE_RATE * here
        return carry

    lax.fori_loop(1, long_x - 1, prepare, 0, unroll=2)

    for sweep in range(SWEEPS):
        old, new = sweep % 2, (sweep + 1) % 2
        last = sweep == SWEEPS - 1

        def one_plane(i, carry, old=old, new=new, last=last):
            pressure = fields[old, 3, i]
            scale = relax[i]
            before = (
                fields[old, 3, i - 1],
                down_y(pressure),
                down_z(pressure) * not_first,
            )
            divergence = None
            for c in range(3):
                here = fields[old, c, i]
                near = [
                    fields[old, c, i + 1],
                    fields[old, c, i - 1],
                    up_y(here),
                    down_y(here),
                    up_z(here),
                    down_z(here),
                ]
                total = (1.0 - RELAX) * here - scale * (pressure - before[c])
                for n, other in enumerate(near):
                    total = total + coefs[n, i] * other
                ahead = near[2 * c]
                if c == 2:
                    total = total + forcing[i]
                    ahead = ahead * not_last
                change = ahead - here
                divergence = change if divergence is None else divergence + change
                if last:
                    vel_out[c, i - width] = total[:size_y]
                else:
                    fields[new, c, i] = total
            pressed = pressure - rate[i] * divergence
            if last:
                pres_out[i - width] = pressed[:size_y]
            else:
                fields[new, 3, i] = pressed
            return carry

        lax.fori_loop(1 + sweep, long_x - 1 - sweep, one_plane, 0, unroll=2)


def all_sweeps(velocity, pressure, cell_visc, cell_dens, low_x, high_x, low_y, high_y):
    size_x, size_y, size_z = cell_visc.shape
    width = low_x.shape[1]
    long_x, ring = size_x + 2 * width, size_y + 2 * width
    whole = pl.BlockSpec(memory_space=pltpu.VMEM)
    block = (long_x, ring, size_z)
    return pl.pallas_call(
        sweep_body,
        out_shape=(
            jax.ShapeDtypeStruct(velocity.shape, f32),
            jax.ShapeDtypeStruct(pressure.shape, f32),
        ),
        in_specs=[whole] * 8,
        out_specs=(whole, whole),
        scratch_shapes=[
            pltpu.VMEM((2, 4) + block, f32),
            pltpu.VMEM((6,) + block, f32),
            pltpu.VMEM(block, f32),
            pltpu.VMEM(block, f32),
            pltpu.VMEM(block, f32),
        ],
        compiler_params=vmem_limit(60),
        cost_estimate=cost(20),
        name="all_sweeps",
    )(velocity, pressure, cell_visc, cell_dens, low_x, high_x, low_y, high_y)


def shift(value, axis, step):
    size = lax.axis_size(axis)
    pairs = [(i, i + step) for i in range(size) if 0 <= i + step < size]
    return lax.ppermute(value, axis, pairs)


def per_device(
    velocity,
    pressure,
    cell_visc,
    cell_dens,
    block_brick,
    block_counts,
    positions,
    start_visc,
    marker_dens,
):
    every = lax.all_gather(block_brick, "mark", axis=0)
    asked = lax.dynamic_index_in_dim(every, lax.axis_index("mark"), axis=1, keepdims=False)
    fields = (velocity, pressure, cell_visc, cell_dens)
    to_low, to_high = pack_x(*fields)
    low_x, high_x = shift(to_high, "grid", 1), shift(to_low, "grid", -1)
    upward, downward = pack_y(*fields, low_x, high_x)
    low_y, high_y = shift(upward, "mark", 1), shift(downward, "mark", -1)

    picked = pick_bricks(asked, velocity)
    bricks = lax.all_to_all(picked, "mark", 0, 0, tiled=True)
    marker_visc, moments = marker_work(
        block_counts, positions, start_visc, marker_dens, bricks, upward
    )
    gathered = lax.all_to_all(moments, "mark", 0, 0, tiled=True)
    velocity_next, pressure_next = all_sweeps(*fields, low_x, high_x, low_y, high_y)
    visc_next, dens_next = settle(asked, gathered, cell_visc, cell_dens)
    return velocity_next, pressure_next, visc_next, dens_next, marker_visc


def solution(mesh):
    in_specs = (
        P(None, "grid", "mark", None),
        P("grid", "mark", None),
        P("grid", "mark", None),
        P("grid", "mark", None),
        P(("grid", "mark"), None),
        P(("grid", "mark"), None),
        P(("grid", "mark"), None, None, None),
        P(("grid", "mark"), None, None),
        P(("grid", "mark"), None, None),
    )
    out_specs = (
        P(None, "grid", "mark", None),
        P("grid", "mark", None),
        P("grid", "mark", None),
        P("grid", "mark", None),
        P(("grid", "mark"), None, None),
    )
    return jax.shard_map(
        per_device, mesh=mesh, in_specs=in_specs, out_specs=out_specs, check_vma=False
    )
```

```python
import functools

import jax
import jax.numpy as jnp
import numpy as np
from jax import lax
from jax.experimental import pallas as pl
from jax.experimental.pallas import tpu as pltpu
from jax.sharding import PartitionSpec as P

SWEEPS = 4
RELAX = 0.6
PRESSURE_RATE = 0.25
GRAVITY = 1.0
STRAIN_SCALE = 0.5

BX, BY, BZ = 4, 4, 8
PLANE = BX * BY
ROWS = 3 * PLANE
LANES = 128
GROUP = LANES // BZ
HALF = 8

f32, bf16 = jnp.float32, jnp.bfloat16


def vmem_limit(mib):
    return pltpu.CompilerParams(vmem_limit_bytes=mib * 1024 * 1024)


def cost(microseconds):
    return pl.CostEstimate(
        flops=int(microseconds * 1.15e9), bytes_accessed=0, transcendentals=0
    )


def place_of(brick):
    return lax.shift_right_logical(brick, GROUP.bit_length() - 1), (brick & (GROUP - 1)) * BZ


def pick_body(asked, vel, out, table):
    size_x, size_y, size_z = vel.shape[1:]
    bricks_y, halves = size_y // BY, size_z // LANES

    def repack(block_x, carry):
        for block_y in range(bricks_y):
            for half in range(halves):
                place = (block_x * bricks_y + block_y) * halves + half
                for c in range(3):
                    for i in range(BX):
                        row = (c * BX + i) * BY
                        table[place, row : row + BY, :] = vel[
                            c,
                            block_x * BX + i,
                            block_y * BY : (block_y + 1) * BY,
                            half * LANES : (half + 1) * LANES,
                        ]
        return carry

    lax.fori_loop(0, size_x // BX, repack, 0)
    groups = out.shape[1]
    lane_slot = lax.broadcasted_iota(jnp.int32, (ROWS, LANES), 1) // BZ

    def one_group(step, carry):
        device, group = step // groups, step % groups
        packed = jnp.zeros((ROWS, LANES), f32)
        for slot in range(GROUP):
            place, lane = place_of(asked[device, group * GROUP + slot])
            rolled = pltpu.roll(table[place], (BZ * slot - lane) & (LANES - 1), 1)
            packed = jnp.where(lane_slot == slot, rolled, packed)
        out[device, group] = packed
        return carry

    lax.fori_loop(0, out.shape[0] * groups, one_group, 0)


def pick_bricks(asked, velocity):
    devices, slots = asked.shape
    size_x, size_y, size_z = velocity.shape[1:]
    places = (size_x // BX) * (size_y // BY) * (size_z // LANES)
    return pl.pallas_call(
        pick_body,
        out_shape=jax.ShapeDtypeStruct((devices, slots // GROUP, ROWS, LANES), f32),
        in_specs=[
            pl.BlockSpec(memory_space=pltpu.SMEM),
            pl.BlockSpec(memory_space=pltpu.VMEM),
        ],
        out_specs=pl.BlockSpec(memory_space=pltpu.VMEM),
        scratch_shapes=[pltpu.VMEM((places, ROWS, LANES), f32)],
        compiler_params=vmem_limit(24),
        cost_estimate=cost(3),
        name="pick_bricks",
    )(asked, velocity)


def permutations():
    inside = BZ * HALF
    spread = np.zeros((2, 2, LANES, 4 * inside), np.float32)
    gather = np.zeros((2 * BY * inside, BY * LANES), np.float32)
    for half in range(2):
        for slot in range(HALF):
            for z in range(BZ):
                outer, inner = (half * HALF + slot) * BZ + z, z * HALF + slot
                for part in range(4):
                    spread[half, part // 2, outer, part * inside + inner] = 1
                for j in range(BY):
                    gather[(half * BY + j) * inside + inner, j * LANES + outer] = 1
    return jnp.asarray(spread, bf16), jnp.asarray(gather, bf16)


def split(value):
    high = value.astype(bf16)
    return high, (value - high.astype(f32)).astype(bf16)


def add_all(values):
    return functools.reduce(jnp.add, values)


def axis_weights(fraction, cells):
    middle = (cells - 1) / 2
    base = jnp.exp(fraction * (2.0 * cells) - float(cells))
    powers = [None, base]
    for i in range(2, cells):
        powers.append(powers[i // 2] * powers[i - i // 2])
    factors = [float(np.exp(middle**2 - (i - middle) ** 2)) for i in range(cells)]
    bells = [None] + [powers[i] * factors[i] for i in range(1, cells)]
    scale = 1.0 / (add_all(bells[1:]) + factors[0])
    weights = [scale * factors[0]] + [bell * scale for bell in bells[1:]]
    mean = add_all(
        [
            (weights[cells - 1 - i] - weights[i]) * (2.0 * (middle - i))
            for i in range(cells // 2)
        ]
    )
    slopes = [w * (2.0 * (i - middle) - mean) for i, w in enumerate(weights)]
    return weights, slopes


def dot(a, b):
    return jnp.dot(a, b, preferred_element_type=f32)


def gradients(products, weights_x, weights_y, markers):
    (weight_x, slope_x), (weight_y, slope_y) = weights_x, weights_y
    grads = []
    for c in range(3):
        lines = [[], [], []]
        for i in range(BX):
            rows = [((c * BX + i) * BY + j) * HALF for j in range(BY)]
            still = [products[row : row + HALF, :markers] for row in rows]
            rising = [products[row : row + HALF, markers:] for row in rows]
            lines[0].append(slope_x[i] * add_all([w * t for w, t in zip(weight_y, still)]))
            lines[1].append(weight_x[i] * add_all([w * t for w, t in zip(slope_y, still)]))
            lines[2].append(weight_x[i] * add_all([w * t for w, t in zip(weight_y, rising)]))
        grads.append([add_all(line) for line in lines])
    return grads


def marker_halves(halves, live_count, spread, gather, places, start, dens, brick, visc_out, work):
    permuted, left, right, products, factors, planes_high, planes_low, sums = work
    markers = places.shape[-1]
    inside = BZ * HALF
    lane = lax.broadcasted_iota(jnp.int32, (HALF, 4 * inside), 1)
    sub = lax.broadcasted_iota(jnp.int32, (HALF, 4 * inside), 0)
    own = (lane % HALF == sub).astype(f32)
    parts = split(brick)
    weights = {}
    for half in halves:
        permuted[half] = dot(parts[0], spread[half, 0]) + dot(parts[1], spread[half, 1])
        lo, hi = half * HALF, (half + 1) * HALF
        weight_z, slope_z = axis_weights(places[0, 2, lo:hi, :], BZ)
        for z in range(0, BZ, 2):
            for column, values in ((0, weight_z), (1, slope_z)):
                high, low = split(jnp.concatenate(values[z : z + 2], axis=0))
                columns = slice(column * markers, (column + 1) * markers)
                for part in range(4):
                    begin = part * inside + z * HALF
                    right[half, begin : begin + 2 * HALF, columns] = low if part % 2 else high
        for row in range(0, ROWS, 2):
            pair = [
                jnp.broadcast_to(permuted[half, r : r + 1, :], own.shape) * own
                for r in (row, row + 1)
            ]
            left[half, row * HALF : (row + 2) * HALF, :] = jnp.concatenate(pair, axis=0).astype(
                bf16
            )
        products[half] = dot(left[half], right[half])

        weights_x = axis_weights(places[0, 0, lo:hi, :], BX)
        weights_y = axis_weights(places[0, 1, lo:hi, :], BY)
        weights[half] = (weights_x, weights_y)
        for j in range(BY):
            for z in range(0, BZ, 2):
                pair = [weights_y[0][j] * weight_z[z + k] for k in range(2)]
                rows = slice((j * BZ + z) * HALF, (j * BZ + z + 2) * HALF)
                high, low = split(jnp.concatenate(pair, axis=0))
                planes_high[half, rows, :] = high
                planes_low[half, rows, :] = low

    contract = (((1,), (1,)), ((), ()))
    for half in halves:
        lo, hi = half * HALF, (half + 1) * HALF
        weights_x, weights_y = weights[half]
        grads = gradients(products.at[half], weights_x, weights_y, markers)
        normal = grads[0][0] ** 2 + grads[1][1] ** 2 + grads[2][2] ** 2
        shear_xy = 0.5 * (grads[0][1] + grads[1][0])
        shear_xz = 0.5 * (grads[0][2] + grads[2][0])
        shear_yz = 0.5 * (grads[1][2] + grads[2][1])
        invariant = 0.5 * normal + shear_xy**2 + shear_xz**2 + shear_yz**2
        third = jnp.log(1.0 + invariant * (1.0 / (STRAIN_SCALE * STRAIN_SCALE))) * (1.0 / 3.0)
        first = start[0, lo:hi, :]
        slot = lax.broadcasted_iota(jnp.int32, first.shape, 0) + lo
        live = slot < live_count
        visc_out[0, lo:hi, :] = jnp.where(live, first * jnp.exp(-third), 0.0)
        carried = (
            live.astype(f32),
            jnp.where(live, jnp.log(first) - third, 0.0),
            jnp.where(live, dens[0, lo:hi, :], 0.0),
        )
        count = 3 * BX * HALF
        for c in range(3):
            for i in range(0, BX, 2):
                pair = [carried[c] * weights_x[0][i + k] for k in range(2)]
                row = (c * BX + i) * HALF
                high, low = split(jnp.concatenate(pair, axis=0))
                factors[half, row : row + 2 * HALF, :] = high
                factors[half, count + row : count + row + 2 * HALF, :] = low
        both = lax.dot_general(
            factors[half], planes_high[half], contract, preferred_element_type=f32
        )
        rest = lax.dot_general(
            factors[half, :count], planes_low[half], contract, preferred_element_type=f32
        )
        total = both[:count] + both[count:] + rest
        chosen = total.reshape(3 * BX, HALF, BY * inside) * own[None]
        packed = jnp.sum(chosen, axis=1)
        high, low = split(packed)
        columns = slice(half * BY * inside, (half + 1) * BY * inside)
        sums[: 3 * BX, columns] = high.astype(f32)
        sums[16 : 16 + 3 * BX, columns] = low.astype(f32)


def marker_body(
    counts, spread, gather, places, start, dens, brick, _, visc_out, moments_out, *work
):
    owner, group = pl.program_id(0), pl.program_id(1)
    live_count = counts[0, owner] - group * GROUP
    sums = work[-1]

    def run(halves):
        marker_halves(
            halves, live_count, spread, gather, places, start, dens, brick[0, 0], visc_out, work
        )
        moved = dot(sums[...].astype(bf16), gather[...])
        moved = moved[: 3 * BX] + moved[16 : 16 + 3 * BX]
        for j in range(BY):
            rows = pl.ds(j, 3 * BX, stride=BY)
            moments_out[0, 0, rows, :] = moved[:, j * LANES : (j + 1) * LANES]

    @pl.when(live_count <= 0)
    def _():
        visc_out[...] = jnp.zeros_like(visc_out)
        moments_out[...] = jnp.zeros_like(moments_out)

    @pl.when(jnp.logical_and(live_count > 0, live_count <= HALF))
    def _():
        sums[...] = jnp.zeros_like(sums)
        visc_out[:, HALF:, :] = jnp.zeros((1, HALF, visc_out.shape[-1]), f32)
        run((0,))

    @pl.when(live_count > HALF)
    def _():
        sums[...] = jnp.zeros_like(sums)
        run((0, 1))


def marker_work(counts, positions, start_visc, marker_dens, bricks, after):
    owners, _, slots, markers = positions.shape
    groups = slots // GROUP
    spread, gather = permutations()
    width = 4 * BZ * HALF
    return pl.pallas_call(
        marker_body,
        grid=(owners, groups),
        out_shape=(
            jax.ShapeDtypeStruct((owners, slots, markers), f32),
            jax.ShapeDtypeStruct((owners, groups, ROWS, LANES), f32),
        ),
        in_specs=[
            pl.BlockSpec(memory_space=pltpu.SMEM),
            pl.BlockSpec(spread.shape, lambda q, g: (0, 0, 0, 0)),
            pl.BlockSpec(gather.shape, lambda q, g: (0, 0)),
            pl.BlockSpec((1, 3, GROUP, markers), lambda q, g: (q, 0, g, 0)),
            pl.BlockSpec((1, GROUP, markers), lambda q, g: (q, g, 0)),
            pl.BlockSpec((1, GROUP, markers), lambda q, g: (q, g, 0)),
            pl.BlockSpec((1, 1, ROWS, LANES), lambda q, g: (q, g, 0, 0)),
            pl.BlockSpec(memory_space=pl.ANY),
        ],
        out_specs=(
            pl.BlockSpec((1, GROUP, markers), lambda q, g: (q, g, 0)),
            pl.BlockSpec((1, 1, ROWS, LANES), lambda q, g: (q, g, 0, 0)),
        ),
        scratch_shapes=[
            pltpu.VMEM((2, ROWS, width), f32),
            pltpu.VMEM((2, ROWS * HALF, width), bf16),
            pltpu.VMEM((2, width, 2 * markers), bf16),
            pltpu.VMEM((2, ROWS * HALF, 2 * markers), f32),
            pltpu.VMEM((2, 2 * 3 * BX * HALF, markers), bf16),
            pltpu.VMEM((2, BY * BZ * HALF, markers), bf16),
            pltpu.VMEM((2, BY * BZ * HALF, markers), bf16),
            pltpu.VMEM((32, 2 * BY * BZ * HALF), f32),
        ],
        compiler_params=vmem_limit(60),
        cost_estimate=cost(25),
        name="marker_work",
    )(counts, spread, gather, positions, start_visc, marker_dens, bricks, after)


def settle_body(asked, moments, visc, dens, visc_out, dens_out, *tables):
    size_x, size_y, size_z = visc.shape
    bricks_y, halves = size_y // BY, size_z // LANES
    for table in tables:
        table[...] = jnp.zeros_like(table)
    groups = moments.shape[1]
    lane_slot = lax.broadcasted_iota(jnp.int32, (ROWS, LANES), 1) // BZ

    def one_group(step, carry):
        device, group = step // groups, step % groups
        packed = moments[device, group]
        for slot in range(GROUP):
            table = tables[slot % len(tables)]
            place, lane = place_of(asked[device, group * GROUP + slot])
            piece = jnp.where(lane_slot == slot, packed, 0.0)
            piece = pltpu.roll(piece, (lane - BZ * slot) & (LANES - 1), 1)
            table[place] = table[place] + piece
        return carry

    lax.fori_loop(0, moments.shape[0] * groups, one_group, 0)

    def finish(block_x, carry):
        for block_y in range(0, bricks_y, 2):
            for half in range(halves):
                for i in range(BX):
                    here = (
                        block_x * BX + i,
                        slice(block_y * BY, (block_y + 2) * BY),
                        slice(half * LANES, (half + 1) * LANES),
                    )
                    sums = []
                    for c in range(3):
                        rows = slice((c * BX + i) * BY, (c * BX + i + 1) * BY)
                        places = [
                            (block_x * bricks_y + block_y + k) * halves + half for k in range(2)
                        ]
                        sums.append(
                            jnp.concatenate(
                                [add_all([t[place, rows, :] for t in tables]) for place in places]
                            )
                        )
                    scale = 1.0 / (sums[0] + 1.0)
                    visc_out[here] = jnp.exp((sums[1] + jnp.log(visc[here])) * scale)
                    dens_out[here] = (sums[2] + dens[here]) * scale
        return carry

    lax.fori_loop(0, size_x // BX, finish, 0)


def settle(asked, moments, cell_visc, cell_dens):
    size_x, size_y, size_z = cell_visc.shape
    places = (size_x // BX) * (size_y // BY) * (size_z // LANES)
    whole = pl.BlockSpec(memory_space=pltpu.VMEM)
    shape = jax.ShapeDtypeStruct(cell_visc.shape, f32)
    return pl.pallas_call(
        settle_body,
        out_shape=(shape, shape),
        in_specs=[pl.BlockSpec(memory_space=pltpu.SMEM), whole, whole, whole],
        out_specs=(whole, whole),
        scratch_shapes=[pltpu.VMEM((places, ROWS, LANES), f32)] * 2,
        compiler_params=vmem_limit(24),
        cost_estimate=cost(7),
        name="settle",
    )(asked, moments, cell_visc, cell_dens)


def field_of(fields, index):
    return fields[0].at[index] if index < 3 else fields[index - 2]


def pack_x_body(*refs):
    ends, outs = refs[:8], refs[8:]
    for side in range(2):
        for f in range(6):
            outs[side][f] = field_of(ends[side::2], f)[...]


def pack_x(velocity, pressure, cell_visc, cell_dens):
    size_x, size_y, size_z = cell_visc.shape
    width = SWEEPS
    ends = (0, size_x // width - 1)
    vel = [
        pl.BlockSpec((3, width, size_y, size_z), lambda i, e=e: (0, e, 0, 0)) for e in ends
    ]
    block = [pl.BlockSpec((width, size_y, size_z), lambda i, e=e: (e, 0, 0)) for e in ends]
    whole = pl.BlockSpec((6, width, size_y, size_z), lambda i: (0, 0, 0, 0))
    shape = jax.ShapeDtypeStruct((6, width, size_y, size_z), f32)
    return pl.pallas_call(
        pack_x_body,
        grid=(1,),
        out_shape=(shape, shape),
        in_specs=vel + block * 3,
        out_specs=(whole, whole),
        compiler_params=vmem_limit(24),
        cost_estimate=cost(2),
        name="pack_x",
    )(velocity, velocity, pressure, pressure, cell_visc, cell_visc, cell_dens, cell_dens)


def corner_rows(field):
    found, width = [], SWEEPS
    per_field = width * (width - 1)
    for side in range(2):
        for far_x in range(1, width):
            for far_y in range(1, width - far_x + 1):
                flat = field * per_field + len(found)
                found.append((side, far_x, far_y, *divmod(flat, 6 * width)))
    return found


def pack_y_body(vel, pres, visc, dens, low_x, high_x, upward, downward):
    step_x, size_y, _ = pres.shape
    width = SWEEPS
    step = pl.program_id(0)
    planes = pl.ds(pl.multiple_of(step * step_x, step_x), step_x)
    for f in range(6):
        field = field_of((vel, pres, visc, dens), f)
        rows = slice(f * width, (f + 1) * width)
        upward[planes, rows, :] = field[:, size_y - width :, :]
        downward[planes, rows, :] = field[:, :width, :]

    @pl.when(step == 0)
    def _():
        size_x = pl.num_programs(0) * step_x
        for f in range(6):
            for side, far_x, far_y, plane, row in corner_rows(f):
                halo, at = (high_x, far_x - 1) if side else (low_x, width - far_x)
                upward[size_x + plane, row] = halo[f, at, size_y - far_y]
                downward[size_x + plane, row] = halo[f, at, far_y - 1]


def pack_y(velocity, pressure, cell_visc, cell_dens, low_x, high_x):
    size_x, size_y, size_z = cell_visc.shape
    step, width = 8, SWEEPS
    long_x = size_x + width - 1
    block = pl.BlockSpec((step, size_y, size_z), lambda i: (i, 0, 0))
    halo = pl.BlockSpec(low_x.shape, lambda i: (0, 0, 0, 0))
    face = pl.BlockSpec((long_x, 6 * width, size_z), lambda i: (0, 0, 0))
    shape = jax.ShapeDtypeStruct((long_x, 6 * width, size_z), f32)
    return pl.pallas_call(
        pack_y_body,
        grid=(size_x // step,),
        out_shape=(shape, shape),
        in_specs=[
            pl.BlockSpec((3, step, size_y, size_z), lambda i: (0, i, 0, 0)),
            block,
            block,
            block,
            halo,
            halo,
        ],
        out_specs=(face, face),
        compiler_params=vmem_limit(24),
        cost_estimate=cost(15),
        name="pack_y",
    )(velocity, pressure, cell_visc, cell_dens, low_x, high_x)


def sweep_body(vel, pres, visc, dens, low_x, high_x, low_y, high_y, vel_out, pres_out, *work):
    fields, coefs, rate, relax, forcing = work
    size_x, size_y, size_z = visc.shape
    width = low_x.shape[1]
    long_x = size_x + 2 * width
    ring = fields.shape[3]
    inner = slice(width, width + size_x)
    own = slice(0, size_y)
    for c in range(3):
        fields[0, c, inner, own, :] = vel[c]
    fields[0, 3, inner, own, :] = pres[...]
    fields[1, 0, inner, own, :] = visc[...]
    fields[1, 1, inner, own, :] = dens[...]
    for f in range(6):
        field = fields.at[0, f] if f < 4 else fields.at[1, f - 4]
        rows = slice(f * width, (f + 1) * width)
        for at, halo in ((0, low_x), (width + size_x, high_x)):
            field[at : at + width, own, :] = halo[f]
            field[at : at + width, size_y:, :] = jnp.zeros((width, 2 * width, size_z), f32)
        field[inner, size_y : size_y + width, :] = high_y[:size_x, rows, :]
        field[inner, size_y + width :, :] = low_y[:size_x, rows, :]
        for side, far_x, far_y, plane, row in corner_rows(f):
            at = width + size_x - 1 + far_x if side else width - far_x
            field[at, size_y + far_y - 1] = high_y[size_x + plane, row]
            field[at, ring - far_y] = low_y[size_x + plane, row]

    lane = lax.broadcasted_iota(jnp.int32, (ring, size_z), 1)
    not_last = (lane < size_z - 1).astype(f32)
    not_first = (lane > 0).astype(f32)

    def up_y(a):
        return pltpu.roll(a, ring - 1, 0)

    def down_y(a):
        return pltpu.roll(a, 1, 0)

    def up_z(a):
        return pltpu.roll(a, size_z - 1, 1)

    def down_z(a):
        return pltpu.roll(a, 1, 1)

    def prepare(i, carry):
        here = fields[1, 0, i]
        near = [
            fields[1, 0, i + 1],
            fields[1, 0, i - 1],
            up_y(here),
            down_y(here),
            up_z(here) * not_last,
            down_z(here) * not_first,
        ]
        links = [0.5 * (here + other) for other in near]
        diagonal = functools.reduce(jnp.add, links)
        scale = jnp.where(here > 0.0, RELAX / diagonal, 0.0)
        links[4] = links[4] * not_last
        links[5] = links[5] * not_first
        for n in range(6):
            coefs[n, i] = links[n] * scale
        relax[i] = scale
        forcing[i] = fields[1, 1, i] * (-GRAVITY * scale)
        rate[i] = PRESSURE_RATE * here
        return carry

    lax.fori_loop(1, long_x - 1, prepare, 0, unroll=2)

    for sweep in range(SWEEPS):
        old, new = sweep % 2, (sweep + 1) % 2
        last = sweep == SWEEPS - 1

        def one_plane(i, carry, old=old, new=new, last=last):
            pressure = fields[old, 3, i]
            scale = relax[i]
            before = (
                fields[old, 3, i - 1],
                down_y(pressure),
                down_z(pressure) * not_first,
            )
            divergence = None
            for c in range(3):
                here = fields[old, c, i]
                near = [
                    fields[old, c, i + 1],
                    fields[old, c, i - 1],
                    up_y(here),
                    down_y(here),
                    up_z(here),
                    down_z(here),
                ]
                total = (1.0 - RELAX) * here - scale * (pressure - before[c])
                for n, other in enumerate(near):
                    total = total + coefs[n, i] * other
                ahead = near[2 * c]
                if c == 2:
                    total = total + forcing[i]
                    ahead = ahead * not_last
                change = ahead - here
                divergence = change if divergence is None else divergence + change
                if last:
                    vel_out[c, i - width] = total[:size_y]
                else:
                    fields[new, c, i] = total
            pressed = pressure - rate[i] * divergence
            if last:
                pres_out[i - width] = pressed[:size_y]
            else:
                fields[new, 3, i] = pressed
            return carry

        lax.fori_loop(1 + sweep, long_x - 1 - sweep, one_plane, 0, unroll=2)


def all_sweeps(velocity, pressure, cell_visc, cell_dens, low_x, high_x, low_y, high_y):
    size_x, size_y, size_z = cell_visc.shape
    width = low_x.shape[1]
    long_x, ring = size_x + 2 * width, size_y + 2 * width
    whole = pl.BlockSpec(memory_space=pltpu.VMEM)
    block = (long_x, ring, size_z)
    return pl.pallas_call(
        sweep_body,
        out_shape=(
            jax.ShapeDtypeStruct(velocity.shape, f32),
            jax.ShapeDtypeStruct(pressure.shape, f32),
        ),
        in_specs=[whole] * 8,
        out_specs=(whole, whole),
        scratch_shapes=[
            pltpu.VMEM((2, 4) + block, f32),
            pltpu.VMEM((6,) + block, f32),
            pltpu.VMEM(block, f32),
            pltpu.VMEM(block, f32),
            pltpu.VMEM(block, f32),
        ],
        compiler_params=vmem_limit(40),
        cost_estimate=cost(20),
        name="all_sweeps",
    )(velocity, pressure, cell_visc, cell_dens, low_x, high_x, low_y, high_y)


def shift(value, axis, step):
    size = lax.axis_size(axis)
    pairs = [(i, i + step) for i in range(size) if 0 <= i + step < size]
    return lax.ppermute(value, axis, pairs)


def per_device(
    velocity,
    pressure,
    cell_visc,
    cell_dens,
    block_brick,
    block_counts,
    positions,
    start_visc,
    marker_dens,
):
    asked = lax.all_to_all(block_brick, "mark", 0, 0, tiled=True)
    fields = (velocity, pressure, cell_visc, cell_dens)
    to_low, to_high = pack_x(*fields)
    low_x, high_x = shift(to_high, "grid", 1), shift(to_low, "grid", -1)
    upward, downward = pack_y(*fields, low_x, high_x)
    low_y, high_y = shift(upward, "mark", 1), shift(downward, "mark", -1)

    picked = pick_bricks(asked, velocity)
    bricks = lax.all_to_all(picked, "mark", 0, 0, tiled=True)
    marker_visc, moments = marker_work(
        block_counts, positions, start_visc, marker_dens, bricks, upward
    )
    gathered = lax.all_to_all(moments, "mark", 0, 0, tiled=True)
    velocity_next, pressure_next = all_sweeps(*fields, low_x, high_x, low_y, high_y)
    visc_next, dens_next = settle(asked, gathered, cell_visc, cell_dens)
    return velocity_next, pressure_next, visc_next, dens_next, marker_visc


def solution(mesh):
    in_specs = (
        P(None, "grid", "mark", None),
        P("grid", "mark", None),
        P("grid", "mark", None),
        P("grid", "mark", None),
        P(("grid", "mark"), None),
        P(("grid", "mark"), None),
        P(("grid", "mark"), None, None, None),
        P(("grid", "mark"), None, None),
        P(("grid", "mark"), None, None),
    )
    out_specs = (
        P(None, "grid", "mark", None),
        P("grid", "mark", None),
        P("grid", "mark", None),
        P("grid", "mark", None),
        P(("grid", "mark"), None, None),
    )
    return jax.shard_map(
        per_device, mesh=mesh, in_specs=in_specs, out_specs=out_specs, check_vma=False
    )
```

```python
import functools

import jax
import jax.numpy as jnp
import numpy as np
from jax import lax
from jax.experimental import pallas as pl
from jax.experimental.pallas import tpu as pltpu
from jax.sharding import PartitionSpec as P

SWEEPS = 4
RELAX = 0.6
PRESSURE_RATE = 0.25
GRAVITY = 1.0
STRAIN_SCALE = 0.5

BX, BY, BZ = 4, 4, 8
PLANE = BX * BY
ROWS = 3 * PLANE
LANES = 128
GROUP = LANES // BZ
HALF = 8

f32, bf16 = jnp.float32, jnp.bfloat16


def vmem_limit(mib):
    return pltpu.CompilerParams(vmem_limit_bytes=mib * 1024 * 1024)


def cost(microseconds):
    return pl.CostEstimate(
        flops=int(microseconds * 1.15e9), bytes_accessed=0, transcendentals=0
    )


def place_of(brick):
    return lax.shift_right_logical(brick, GROUP.bit_length() - 1), (brick & (GROUP - 1)) * BZ


def pick_body(asked, vel, out, table):
    size_x, size_y, size_z = vel.shape[1:]
    bricks_y, halves = size_y // BY, size_z // LANES

    def repack(block_x, carry):
        for block_y in range(bricks_y):
            for half in range(halves):
                place = (block_x * bricks_y + block_y) * halves + half
                for c in range(3):
                    for i in range(BX):
                        row = (c * BX + i) * BY
                        table[place, row : row + BY, :] = vel[
                            c,
                            block_x * BX + i,
                            block_y * BY : (block_y + 1) * BY,
                            half * LANES : (half + 1) * LANES,
                        ]
        return carry

    lax.fori_loop(0, size_x // BX, repack, 0)
    groups = out.shape[1]
    lane_slot = lax.broadcasted_iota(jnp.int32, (ROWS, LANES), 1) // BZ

    def one_group(step, carry):
        device, group = step // groups, step % groups
        packed = jnp.zeros((ROWS, LANES), f32)
        for slot in range(GROUP):
            place, lane = place_of(asked[device, group * GROUP + slot])
            rolled = pltpu.roll(table[place], (BZ * slot - lane) & (LANES - 1), 1)
            packed = jnp.where(lane_slot == slot, rolled, packed)
        out[device, group] = packed
        return carry

    lax.fori_loop(0, out.shape[0] * groups, one_group, 0)


def pick_bricks(asked, velocity):
    devices, slots = asked.shape
    size_x, size_y, size_z = velocity.shape[1:]
    places = (size_x // BX) * (size_y // BY) * (size_z // LANES)
    return pl.pallas_call(
        pick_body,
        out_shape=jax.ShapeDtypeStruct((devices, slots // GROUP, ROWS, LANES), f32),
        in_specs=[
            pl.BlockSpec(memory_space=pltpu.SMEM),
            pl.BlockSpec(memory_space=pltpu.VMEM),
        ],
        out_specs=pl.BlockSpec(memory_space=pltpu.VMEM),
        scratch_shapes=[pltpu.VMEM((places, ROWS, LANES), f32)],
        compiler_params=vmem_limit(24),
        cost_estimate=cost(25),
        name="pick_bricks",
    )(asked, velocity)


def permutations():
    inside = BZ * HALF
    spread = np.zeros((2, 2, LANES, 4 * inside), np.float32)
    gather = np.zeros((2, BY * inside, BY * LANES), np.float32)
    for half in range(2):
        for slot in range(HALF):
            for z in range(BZ):
                outer, inner = (half * HALF + slot) * BZ + z, z * HALF + slot
                for part in range(4):
                    spread[half, part // 2, outer, part * inside + inner] = 1
                for j in range(BY):
                    gather[half, j * inside + inner, j * LANES + outer] = 1
    return jnp.asarray(spread, bf16), jnp.asarray(gather, bf16)


def split(value):
    high = value.astype(bf16)
    return high, (value - high.astype(f32)).astype(bf16)


def add_all(values):
    return functools.reduce(jnp.add, values)


def axis_weights(fraction, cells):
    middle = (cells - 1) / 2
    base = jnp.exp(fraction * (2.0 * cells) - float(cells))
    powers = [None, base]
    for i in range(2, cells):
        powers.append(powers[i // 2] * powers[i - i // 2])
    factors = [float(np.exp(middle**2 - (i - middle) ** 2)) for i in range(cells)]
    bells = [None] + [powers[i] * factors[i] for i in range(1, cells)]
    scale = 1.0 / (add_all(bells[1:]) + factors[0])
    weights = [scale * factors[0]] + [bell * scale for bell in bells[1:]]
    mean = add_all(
        [
            (weights[cells - 1 - i] - weights[i]) * (2.0 * (middle - i))
            for i in range(cells // 2)
        ]
    )
    slopes = [w * (2.0 * (i - middle) - mean) for i, w in enumerate(weights)]
    return weights, slopes


def dot(a, b):
    return jnp.dot(a, b, preferred_element_type=f32)


def gradients(products, weights, markers):
    weight_x, slope_x, weight_y, slope_y = ([weights[4 * n + i] for i in range(4)] for n in range(4))
    grads = []
    for c in range(3):
        lines = [[], [], []]
        for i in range(BX):
            rows = [((c * BX + i) * BY + j) * HALF for j in range(BY)]
            still = [products[row : row + HALF, :markers] for row in rows]
            rising = [products[row : row + HALF, markers:] for row in rows]
            lines[0].append(slope_x[i] * add_all([w * t for w, t in zip(weight_y, still)]))
            lines[1].append(weight_x[i] * add_all([w * t for w, t in zip(slope_y, still)]))
            lines[2].append(weight_x[i] * add_all([w * t for w, t in zip(weight_y, rising)]))
        grads.append([add_all(line) for line in lines])
    return grads


def own_lanes():
    shape = (HALF, 4 * BZ * HALF)
    lane = lax.broadcasted_iota(jnp.int32, shape, 1)
    return (lane % HALF == lax.broadcasted_iota(jnp.int32, shape, 0)).astype(f32)


def first_stage(unit, ins, buffers):
    spread, _, places, _, _, brick = ins
    permuted, left, right, products, weights, _, planes_high, planes_low = buffers
    owner, part = unit
    markers = places.shape[-1]
    inside = BZ * HALF
    own = own_lanes()
    half = part & 1
    parts = split(brick[owner, lax.shift_right_logical(part, 1)])
    permuted[...] = dot(parts[0], spread[half, 0]) + dot(parts[1], spread[half, 1])
    weight_z, slope_z = axis_weights(places[owner, 2, part], BZ)
    for z in range(0, BZ, 2):
        for column, values in ((0, weight_z), (1, slope_z)):
            high, low = split(jnp.concatenate(values[z : z + 2], axis=0))
            columns = slice(column * markers, (column + 1) * markers)
            for n in range(4):
                begin = n * inside + z * HALF
                right[begin : begin + 2 * HALF, columns] = low if n % 2 else high
    for row in range(0, ROWS, 2):
        pair = [jnp.broadcast_to(permuted[r : r + 1, :], own.shape) * own for r in (row, row + 1)]
        left[row * HALF : (row + 2) * HALF, :] = jnp.concatenate(pair, axis=0).astype(bf16)
    products[...] = dot(left[...], right[...])
    weights_x = axis_weights(places[owner, 0, part], BX)
    weights_y = axis_weights(places[owner, 1, part], BY)
    for n, values in enumerate((*weights_x, *weights_y)):
        for i, value in enumerate(values):
            weights[4 * n + i] = value
    for j in range(BY):
        for z in range(0, BZ, 2):
            pair = [weights_y[0][j] * weight_z[z + k] for k in range(2)]
            rows = slice((j * BZ + z) * HALF, (j * BZ + z + 2) * HALF)
            high, low = split(jnp.concatenate(pair, axis=0))
            planes_high[rows, :] = high
            planes_low[rows, :] = low


def second_stage(unit, counts, ins, buffers, outs, sums):
    _, gather, places, start, dens, _ = ins
    visc_out, moments_out = outs
    _, _, _, products, weights, factors, planes_high, planes_low = buffers
    owner, part = unit
    markers = places.shape[-1]
    inside = BZ * HALF
    grads = gradients(products, weights, markers)
    normal = grads[0][0] ** 2 + grads[1][1] ** 2 + grads[2][2] ** 2
    shear_xy = 0.5 * (grads[0][1] + grads[1][0])
    shear_xz = 0.5 * (grads[0][2] + grads[2][0])
    shear_yz = 0.5 * (grads[1][2] + grads[2][1])
    invariant = 0.5 * normal + shear_xy**2 + shear_xz**2 + shear_yz**2
    third = jnp.log(1.0 + invariant * (1.0 / (STRAIN_SCALE * STRAIN_SCALE))) * (1.0 / 3.0)
    first = start[owner, part]
    slot = lax.broadcasted_iota(jnp.int32, first.shape, 0) + part * HALF
    live = slot < counts[0, owner]
    visc_out[owner, part] = jnp.where(live, first * jnp.exp(-third), 0.0)
    carried = (
        live.astype(f32),
        jnp.where(live, jnp.log(first) - third, 0.0),
        jnp.where(live, dens[owner, part], 0.0),
    )
    count = 3 * BX * HALF
    for c in range(3):
        for i in range(0, BX, 2):
            pair = [carried[c] * weights[i + k] for k in range(2)]
            row = (c * BX + i) * HALF
            high, low = split(jnp.concatenate(pair, axis=0))
            factors[row : row + 2 * HALF, :] = high
            factors[count + row : count + row + 2 * HALF, :] = low
    contract = (((1,), (1,)), ((), ()))
    both = lax.dot_general(factors[...], planes_high[...], contract, preferred_element_type=f32)
    rest = lax.dot_general(factors[:count], planes_low[...], contract, preferred_element_type=f32)
    total = both[:count] + both[count:] + rest
    chosen = total.reshape(3 * BX, HALF, BY * inside) * own_lanes()[None]
    high, low = split(jnp.sum(chosen, axis=1))
    sums[: 3 * BX, :] = high.astype(f32)
    sums[16 : 16 + 3 * BX, :] = low.astype(f32)
    moved = dot(sums[...].astype(bf16), gather[part & 1])
    moved = moved[: 3 * BX] + moved[16 : 16 + 3 * BX]
    group = lax.shift_right_logical(part, 1)
    for j in range(BY):
        rows = pl.ds(j, 3 * BX, stride=BY)
        before = moments_out[owner, group, rows, :]
        moments_out[owner, group, rows, :] = before + moved[:, j * LANES : (j + 1) * LANES]


def marker_body(counts, *refs):
    ins, outs, scratch = refs[:6], refs[7:9], refs[9:]
    units, sums, *buffers = scratch
    buffers = (buffers[0::2], buffers[1::2])
    visc_out, moments_out = outs
    owners, parts = visc_out.shape[:2]
    visc_out[...] = jnp.zeros_like(visc_out)
    moments_out[...] = jnp.zeros_like(moments_out)
    sums[...] = jnp.zeros_like(sums)

    def list_units(index, found):
        number, dead = found
        owner, part = index // parts, index % parts
        live = part * HALF < counts[0, owner]

        @pl.when(live)
        def _():
            units[2 * number] = owner
            units[2 * number + 1] = part

        return jnp.where(live, number + 1, number), jnp.where(live, dead, index)

    number, dead = lax.fori_loop(0, owners * parts, list_units, (0, 0))

    @pl.when(number % 2 == 1)
    def _():
        units[2 * number] = dead // parts
        units[2 * number + 1] = dead % parts

    pairs = (number + 1) // 2

    def unit(index):
        return units[2 * index], units[2 * index + 1]

    def first(index, buffer):
        first_stage(unit(index), ins, buffers[buffer])

    def second(index, buffer):
        second_stage(unit(index), counts, ins, buffers[buffer], outs, sums)

    @pl.when(pairs > 0)
    def _():
        first(0, 0)

        def both(pair, carry):
            first(2 * pair + 1, 1)
            second(2 * pair, 0)
            first(2 * pair + 2, 0)
            second(2 * pair + 1, 1)
            return carry

        lax.fori_loop(0, pairs - 1, both, 0)
        first(2 * pairs - 1, 1)
        second(2 * pairs - 2, 0)
        second(2 * pairs - 1, 1)


def marker_work(counts, positions, start_visc, marker_dens, bricks, after):
    owners, _, slots, markers = positions.shape
    groups, parts = slots // GROUP, slots // HALF
    spread, gather = permutations()
    width = 4 * BZ * HALF
    whole = pl.BlockSpec(memory_space=pltpu.VMEM)
    buffers = (
        pltpu.VMEM((ROWS, width), f32),
        pltpu.VMEM((ROWS * HALF, width), bf16),
        pltpu.VMEM((width, 2 * markers), bf16),
        pltpu.VMEM((ROWS * HALF, 2 * markers), f32),
        pltpu.VMEM((4 * 4, HALF, markers), f32),
        pltpu.VMEM((2 * 3 * BX * HALF, markers), bf16),
        pltpu.VMEM((BY * BZ * HALF, markers), bf16),
        pltpu.VMEM((BY * BZ * HALF, markers), bf16),
    )
    visc, moments = pl.pallas_call(
        marker_body,
        out_shape=(
            jax.ShapeDtypeStruct((owners, parts, HALF, markers), f32),
            jax.ShapeDtypeStruct((owners, groups, ROWS, LANES), f32),
        ),
        in_specs=[pl.BlockSpec(memory_space=pltpu.SMEM)]
        + [whole] * 6
        + [pl.BlockSpec(memory_space=pl.ANY)],
        out_specs=(whole, whole),
        scratch_shapes=[
            pltpu.SMEM((2 * (owners * parts + 1),), jnp.int32),
            pltpu.VMEM((32, BY * BZ * HALF), f32),
        ]
        + [buffer for buffer in buffers for _ in range(2)],
        compiler_params=vmem_limit(60),
        cost_estimate=cost(25),
        name="marker_work",
    )(
        counts,
        spread,
        gather,
        positions.reshape(owners, 3, parts, HALF, markers),
        start_visc.reshape(owners, parts, HALF, markers),
        marker_dens.reshape(owners, parts, HALF, markers),
        bricks,
        after,
    )
    return visc.reshape(owners, slots, markers), moments


def settle_body(asked, moments, visc, dens, visc_out, dens_out, *tables):
    size_x, size_y, size_z = visc.shape
    bricks_y, halves = size_y // BY, size_z // LANES
    for table in tables:
        table[...] = jnp.zeros_like(table)
    groups = moments.shape[1]
    lane_slot = lax.broadcasted_iota(jnp.int32, (ROWS, LANES), 1) // BZ

    def one_group(step, carry):
        device, group = step // groups, step % groups
        packed = moments[device, group]
        for slot in range(GROUP):
            table = tables[slot % len(tables)]
            place, lane = place_of(asked[device, group * GROUP + slot])
            piece = jnp.where(lane_slot == slot, packed, 0.0)
            piece = pltpu.roll(piece, (lane - BZ * slot) & (LANES - 1), 1)
            table[place] = table[place] + piece
        return carry

    lax.fori_loop(0, moments.shape[0] * groups, one_group, 0)

    def finish(block_x, carry):
        for block_y in range(0, bricks_y, 2):
            for half in range(halves):
                for i in range(BX):
                    here = (
                        block_x * BX + i,
                        slice(block_y * BY, (block_y + 2) * BY),
                        slice(half * LANES, (half + 1) * LANES),
                    )
                    sums = []
                    for c in range(3):
                        rows = slice((c * BX + i) * BY, (c * BX + i + 1) * BY)
                        places = [
                            (block_x * bricks_y + block_y + k) * halves + half for k in range(2)
                        ]
                        sums.append(
                            jnp.concatenate(
                                [add_all([t[place, rows, :] for t in tables]) for place in places]
                            )
                        )
                    scale = 1.0 / (sums[0] + 1.0)
                    visc_out[here] = jnp.exp((sums[1] + jnp.log(visc[here])) * scale)
                    dens_out[here] = (sums[2] + dens[here]) * scale
        return carry

    lax.fori_loop(0, size_x // BX, finish, 0)


def settle(asked, moments, cell_visc, cell_dens):
    size_x, size_y, size_z = cell_visc.shape
    places = (size_x // BX) * (size_y // BY) * (size_z // LANES)
    whole = pl.BlockSpec(memory_space=pltpu.VMEM)
    shape = jax.ShapeDtypeStruct(cell_visc.shape, f32)
    return pl.pallas_call(
        settle_body,
        out_shape=(shape, shape),
        in_specs=[pl.BlockSpec(memory_space=pltpu.SMEM), whole, whole, whole],
        out_specs=(whole, whole),
        scratch_shapes=[pltpu.VMEM((places, ROWS, LANES), f32)] * 2,
        compiler_params=vmem_limit(24),
        cost_estimate=cost(7),
        name="settle",
    )(asked, moments, cell_visc, cell_dens)


def field_of(fields, index):
    return fields[0].at[index] if index < 3 else fields[index - 2]


def pack_x_body(*refs):
    ends, outs = refs[:8], refs[8:]
    for side in range(2):
        for f in range(6):
            outs[side][f] = field_of(ends[side::2], f)[...]


def pack_x(velocity, pressure, cell_visc, cell_dens):
    size_x, size_y, size_z = cell_visc.shape
    width = SWEEPS
    ends = (0, size_x // width - 1)
    vel = [
        pl.BlockSpec((3, width, size_y, size_z), lambda i, e=e: (0, e, 0, 0)) for e in ends
    ]
    block = [pl.BlockSpec((width, size_y, size_z), lambda i, e=e: (e, 0, 0)) for e in ends]
    whole = pl.BlockSpec((6, width, size_y, size_z), lambda i: (0, 0, 0, 0))
    shape = jax.ShapeDtypeStruct((6, width, size_y, size_z), f32)
    return pl.pallas_call(
        pack_x_body,
        grid=(1,),
        out_shape=(shape, shape),
        in_specs=vel + block * 3,
        out_specs=(whole, whole),
        compiler_params=vmem_limit(60),
        cost_estimate=cost(2),
        name="pack_x",
    )(velocity, velocity, pressure, pressure, cell_visc, cell_visc, cell_dens, cell_dens)


def corner_rows(field):
    found, width = [], SWEEPS
    per_field = width * (width - 1)
    for side in range(2):
        for far_x in range(1, width):
            for far_y in range(1, width - far_x + 1):
                flat = field * per_field + len(found)
                found.append((side, far_x, far_y, *divmod(flat, 6 * width)))
    return found


def pack_y_body(vel, pres, visc, dens, low_x, high_x, upward, downward):
    step_x, size_y, _ = pres.shape
    width = SWEEPS
    step = pl.program_id(0)
    planes = pl.ds(pl.multiple_of(step * step_x, step_x), step_x)
    for f in range(6):
        field = field_of((vel, pres, visc, dens), f)
        rows = slice(f * width, (f + 1) * width)
        upward[planes, rows, :] = field[:, size_y - width :, :]
        downward[planes, rows, :] = field[:, :width, :]

    @pl.when(step == 0)
    def _():
        size_x = pl.num_programs(0) * step_x
        for f in range(6):
            for side, far_x, far_y, plane, row in corner_rows(f):
                halo, at = (high_x, far_x - 1) if side else (low_x, width - far_x)
                upward[size_x + plane, row] = halo[f, at, size_y - far_y]
                downward[size_x + plane, row] = halo[f, at, far_y - 1]


def pack_y(velocity, pressure, cell_visc, cell_dens, low_x, high_x):
    size_x, size_y, size_z = cell_visc.shape
    step, width = 8, SWEEPS
    long_x = size_x + width - 1
    block = pl.BlockSpec((step, size_y, size_z), lambda i: (i, 0, 0))
    halo = pl.BlockSpec(low_x.shape, lambda i: (0, 0, 0, 0))
    face = pl.BlockSpec((long_x, 6 * width, size_z), lambda i: (0, 0, 0))
    shape = jax.ShapeDtypeStruct((long_x, 6 * width, size_z), f32)
    return pl.pallas_call(
        pack_y_body,
        grid=(size_x // step,),
        out_shape=(shape, shape),
        in_specs=[
            pl.BlockSpec((3, step, size_y, size_z), lambda i: (0, i, 0, 0)),
            block,
            block,
            block,
            halo,
            halo,
        ],
        out_specs=(face, face),
        compiler_params=vmem_limit(24),
        cost_estimate=cost(15),
        name="pack_y",
    )(velocity, pressure, cell_visc, cell_dens, low_x, high_x)


def sweep_body(vel, pres, visc, dens, low_x, high_x, low_y, high_y, vel_out, pres_out, *work):
    fields, coefs, rate, relax, forcing = work
    size_x, size_y, size_z = visc.shape
    width = low_x.shape[1]
    long_x = size_x + 2 * width
    ring = fields.shape[3]
    inner = slice(width, width + size_x)
    own = slice(0, size_y)
    for c in range(3):
        fields[0, c, inner, own, :] = vel[c]
    fields[0, 3, inner, own, :] = pres[...]
    fields[1, 0, inner, own, :] = visc[...]
    fields[1, 1, inner, own, :] = dens[...]
    for f in range(6):
        field = fields.at[0, f] if f < 4 else fields.at[1, f - 4]
        rows = slice(f * width, (f + 1) * width)
        for at, halo in ((0, low_x), (width + size_x, high_x)):
            field[at : at + width, own, :] = halo[f]
            field[at : at + width, size_y:, :] = jnp.zeros((width, 2 * width, size_z), f32)
        field[inner, size_y : size_y + width, :] = high_y[:size_x, rows, :]
        field[inner, size_y + width :, :] = low_y[:size_x, rows, :]
        for side, far_x, far_y, plane, row in corner_rows(f):
            at = width + size_x - 1 + far_x if side else width - far_x
            field[at, size_y + far_y - 1] = high_y[size_x + plane, row]
            field[at, ring - far_y] = low_y[size_x + plane, row]

    lane = lax.broadcasted_iota(jnp.int32, (ring, size_z), 1)
    not_last = (lane < size_z - 1).astype(f32)
    not_first = (lane > 0).astype(f32)

    def up_y(a):
        return pltpu.roll(a, ring - 1, 0)

    def down_y(a):
        return pltpu.roll(a, 1, 0)

    def up_z(a):
        return pltpu.roll(a, size_z - 1, 1)

    def down_z(a):
        return pltpu.roll(a, 1, 1)

    def prepare(i, carry):
        here = fields[1, 0, i]
        near = [
            fields[1, 0, i + 1],
            fields[1, 0, i - 1],
            up_y(here),
            down_y(here),
            up_z(here) * not_last,
            down_z(here) * not_first,
        ]
        links = [0.5 * (here + other) for other in near]
        diagonal = functools.reduce(jnp.add, links)
        scale = jnp.where(here > 0.0, RELAX / diagonal, 0.0)
        links[4] = links[4] * not_last
        links[5] = links[5] * not_first
        for n in range(6):
            coefs[n, i] = links[n] * scale
        relax[i] = scale
        forcing[i] = fields[1, 1, i] * (-GRAVITY * scale)
        rate[i] = PRESSURE_RATE * here
        return carry

    lax.fori_loop(1, long_x - 1, prepare, 0, unroll=2)

    for sweep in range(SWEEPS):
        old, new = sweep % 2, (sweep + 1) % 2
        last = sweep == SWEEPS - 1

        def one_plane(i, carry, old=old, new=new, last=last):
            pressure = fields[old, 3, i]
            scale = relax[i]
            before = (
                fields[old, 3, i - 1],
                down_y(pressure),
                down_z(pressure) * not_first,
            )
            divergence = None
            for c in range(3):
                here = fields[old, c, i]
                near = [
                    fields[old, c, i + 1],
                    fields[old, c, i - 1],
                    up_y(here),
                    down_y(here),
                    up_z(here),
                    down_z(here),
                ]
                total = (1.0 - RELAX) * here - scale * (pressure - before[c])
                for n, other in enumerate(near):
                    total = total + coefs[n, i] * other
                ahead = near[2 * c]
                if c == 2:
                    total = total + forcing[i]
                    ahead = ahead * not_last
                change = ahead - here
                divergence = change if divergence is None else divergence + change
                if last:
                    vel_out[c, i - width] = total[:size_y]
                else:
                    fields[new, c, i] = total
            pressed = pressure - rate[i] * divergence
            if last:
                pres_out[i - width] = pressed[:size_y]
            else:
                fields[new, 3, i] = pressed
            return carry

        lax.fori_loop(1 + sweep, long_x - 1 - sweep, one_plane, 0, unroll=2)


def all_sweeps(velocity, pressure, cell_visc, cell_dens, low_x, high_x, low_y, high_y):
    size_x, size_y, size_z = cell_visc.shape
    width = low_x.shape[1]
    long_x, ring = size_x + 2 * width, size_y + 2 * width
    whole = pl.BlockSpec(memory_space=pltpu.VMEM)
    block = (long_x, ring, size_z)
    return pl.pallas_call(
        sweep_body,
        out_shape=(
            jax.ShapeDtypeStruct(velocity.shape, f32),
            jax.ShapeDtypeStruct(pressure.shape, f32),
        ),
        in_specs=[whole] * 8,
        out_specs=(whole, whole),
        scratch_shapes=[
            pltpu.VMEM((2, 4) + block, f32),
            pltpu.VMEM((6,) + block, f32),
            pltpu.VMEM(block, f32),
            pltpu.VMEM(block, f32),
            pltpu.VMEM(block, f32),
        ],
        compiler_params=vmem_limit(40),
        cost_estimate=cost(20),
        name="all_sweeps",
    )(velocity, pressure, cell_visc, cell_dens, low_x, high_x, low_y, high_y)


def shift(value, axis, step):
    size = lax.axis_size(axis)
    pairs = [(i, i + step) for i in range(size) if 0 <= i + step < size]
    return lax.ppermute(value, axis, pairs)


def per_device(
    velocity,
    pressure,
    cell_visc,
    cell_dens,
    block_brick,
    block_counts,
    positions,
    start_visc,
    marker_dens,
):
    asked = lax.all_to_all(block_brick, "mark", 0, 0, tiled=True)
    fields = (velocity, pressure, cell_visc, cell_dens)
    to_low, to_high = pack_x(*fields)
    low_x, high_x = shift(to_high, "grid", 1), shift(to_low, "grid", -1)
    upward, downward = pack_y(*fields, low_x, high_x)
    low_y, high_y = shift(upward, "mark", 1), shift(downward, "mark", -1)

    picked = pick_bricks(asked, velocity)
    bricks = lax.all_to_all(picked, "mark", 0, 0, tiled=True)
    marker_visc, moments = marker_work(
        block_counts, positions, start_visc, marker_dens, bricks, upward
    )
    gathered = lax.all_to_all(moments, "mark", 0, 0, tiled=True)
    velocity_next, pressure_next = all_sweeps(*fields, low_x, high_x, low_y, high_y)
    visc_next, dens_next = settle(asked, gathered, cell_visc, cell_dens)
    return velocity_next, pressure_next, visc_next, dens_next, marker_visc


def solution(mesh):
    in_specs = (
        P(None, "grid", "mark", None),
        P("grid", "mark", None),
        P("grid", "mark", None),
        P("grid", "mark", None),
        P(("grid", "mark"), None),
        P(("grid", "mark"), None),
        P(("grid", "mark"), None, None, None),
        P(("grid", "mark"), None, None),
        P(("grid", "mark"), None, None),
    )
    out_specs = (
        P(None, "grid", "mark", None),
        P("grid", "mark", None),
        P("grid", "mark", None),
        P("grid", "mark", None),
        P(("grid", "mark"), None, None),
    )
    return jax.shard_map(
        per_device, mesh=mesh, in_specs=in_specs, out_specs=out_specs, check_vma=False
    )
```

```python
import functools

import jax
import jax.numpy as jnp
import numpy as np
from jax import lax
from jax.experimental import pallas as pl
from jax.experimental.pallas import tpu as pltpu
from jax.sharding import PartitionSpec as P

SWEEPS = 4
RELAX = 0.6
PRESSURE_RATE = 0.25
GRAVITY = 1.0
STRAIN_SCALE = 0.5

BX, BY, BZ = 4, 4, 8
PLANE = BX * BY
ROWS = 3 * PLANE
LANES = 128
GROUP = LANES // BZ
HALF = 8
SUBLANES = 8

f32, bf16 = jnp.float32, jnp.bfloat16


def vmem_limit(mib):
    return pltpu.CompilerParams(vmem_limit_bytes=mib * 1024 * 1024)


def cost(microseconds):
    return pl.CostEstimate(
        flops=int(microseconds * 1.15e9), bytes_accessed=0, transcendentals=0
    )


def place_of(brick):
    return lax.shift_right_logical(brick, GROUP.bit_length() - 1), (brick & (GROUP - 1)) * BZ


def pick_body(asked, vel, out, table):
    size_x, size_y, size_z = vel.shape[1:]
    bricks_y, halves = size_y // BY, size_z // LANES

    def repack(block_x, carry):
        for block_y in range(bricks_y):
            for half in range(halves):
                place = (block_x * bricks_y + block_y) * halves + half
                for c in range(3):
                    for i in range(BX):
                        row = (c * BX + i) * BY
                        table[place, row : row + BY, :] = vel[
                            c,
                            block_x * BX + i,
                            block_y * BY : (block_y + 1) * BY,
                            half * LANES : (half + 1) * LANES,
                        ]
        return carry

    lax.fori_loop(0, size_x // BX, repack, 0)
    groups = out.shape[1]
    lane_slot = lax.broadcasted_iota(jnp.int32, (ROWS, LANES), 1) // BZ

    def one_group(step, carry):
        device, group = step // groups, step % groups
        packed = jnp.zeros((ROWS, LANES), f32)
        for slot in range(GROUP):
            place, lane = place_of(asked[device, group * GROUP + slot])
            rolled = pltpu.roll(table[place], (BZ * slot - lane) & (LANES - 1), 1)
            packed = jnp.where(lane_slot == slot, rolled, packed)
        out[device, group] = packed
        return carry

    lax.fori_loop(0, out.shape[0] * groups, one_group, 0)


def pick_bricks(asked, velocity):
    devices, slots = asked.shape
    size_x, size_y, size_z = velocity.shape[1:]
    places = (size_x // BX) * (size_y // BY) * (size_z // LANES)
    return pl.pallas_call(
        pick_body,
        out_shape=jax.ShapeDtypeStruct((devices, slots // GROUP, ROWS, LANES), f32),
        in_specs=[
            pl.BlockSpec(memory_space=pltpu.SMEM),
            pl.BlockSpec(memory_space=pltpu.VMEM),
        ],
        out_specs=pl.BlockSpec(memory_space=pltpu.VMEM),
        scratch_shapes=[pltpu.VMEM((places, ROWS, LANES), f32)],
        compiler_params=vmem_limit(24),
        cost_estimate=cost(25),
        name="pick_bricks",
    )(asked, velocity)


def permutations():
    inside = BZ * HALF
    spread = np.zeros((2, 2, LANES, 4 * inside), np.float32)
    gather = np.zeros((2, BY * inside, BY * LANES), np.float32)
    for half in range(2):
        for slot in range(HALF):
            for z in range(BZ):
                outer, inner = (half * HALF + slot) * BZ + z, z * HALF + slot
                for part in range(4):
                    spread[half, part // 2, outer, part * inside + inner] = 1
                for j in range(BY):
                    gather[half, j * inside + inner, j * LANES + outer] = 1
    return jnp.asarray(spread, bf16), jnp.asarray(gather, bf16)


def split(value):
    high = value.astype(bf16)
    return high, (value - high.astype(f32)).astype(bf16)


def add_all(values):
    return functools.reduce(jnp.add, values)


def axis_weights(fraction, cells):
    middle = (cells - 1) / 2
    base = jnp.exp(fraction * (2.0 * cells) - float(cells))
    powers = [None, base]
    for i in range(2, cells):
        powers.append(powers[i // 2] * powers[i - i // 2])
    factors = [float(np.exp(middle**2 - (i - middle) ** 2)) for i in range(cells)]
    bells = [None] + [powers[i] * factors[i] for i in range(1, cells)]
    scale = 1.0 / (add_all(bells[1:]) + factors[0])
    weights = [scale * factors[0]] + [bell * scale for bell in bells[1:]]
    mean = add_all(
        [
            (weights[cells - 1 - i] - weights[i]) * (2.0 * (middle - i))
            for i in range(cells // 2)
        ]
    )
    slopes = [w * (2.0 * (i - middle) - mean) for i, w in enumerate(weights)]
    return weights, slopes


def dot(a, b):
    return jnp.dot(a, b, preferred_element_type=f32)


def gradients(products, weights, markers):
    weight_x, slope_x, weight_y, slope_y = ([weights[4 * n + i] for i in range(4)] for n in range(4))
    grads = []
    for c in range(3):
        lines = [[], [], []]
        for i in range(BX):
            rows = [((c * BX + i) * BY + j) * HALF for j in range(BY)]
            still = [products[row : row + HALF, :markers] for row in rows]
            rising = [products[row : row + HALF, markers:] for row in rows]
            lines[0].append(slope_x[i] * add_all([w * t for w, t in zip(weight_y, still)]))
            lines[1].append(weight_x[i] * add_all([w * t for w, t in zip(slope_y, still)]))
            lines[2].append(weight_x[i] * add_all([w * t for w, t in zip(weight_y, rising)]))
        grads.append([add_all(line) for line in lines])
    return grads


def own_lanes():
    shape = (HALF, 4 * BZ * HALF)
    lane = lax.broadcasted_iota(jnp.int32, shape, 1)
    return (lane % HALF == lax.broadcasted_iota(jnp.int32, shape, 0)).astype(f32)


def first_stage(unit, ins, buffers):
    spread, _, places, _, _, brick = ins
    permuted, left, right, products, weights, _, planes_high, planes_low = buffers
    owner, part = unit
    markers = places.shape[-1]
    inside = BZ * HALF
    own = own_lanes()
    half = part & 1
    parts = split(brick[owner, lax.shift_right_logical(part, 1)])
    permuted[...] = dot(parts[0], spread[half, 0]) + dot(parts[1], spread[half, 1])
    weight_z, slope_z = axis_weights(places[owner, 2, part], BZ)
    for z in range(0, BZ, 2):
        for column, values in ((0, weight_z), (1, slope_z)):
            high, low = split(jnp.concatenate(values[z : z + 2], axis=0))
            columns = slice(column * markers, (column + 1) * markers)
            for n in range(4):
                begin = n * inside + z * HALF
                right[begin : begin + 2 * HALF, columns] = low if n % 2 else high
    for row in range(0, ROWS, 2):
        pair = [jnp.broadcast_to(permuted[r : r + 1, :], own.shape) * own for r in (row, row + 1)]
        left[row * HALF : (row + 2) * HALF, :] = jnp.concatenate(pair, axis=0).astype(bf16)
    products[...] = dot(left[...], right[...])
    weights_x = axis_weights(places[owner, 0, part], BX)
    weights_y = axis_weights(places[owner, 1, part], BY)
    for n, values in enumerate((*weights_x, *weights_y)):
        for i, value in enumerate(values):
            weights[4 * n + i] = value
    for j in range(BY):
        for z in range(0, BZ, 2):
            pair = [weights_y[0][j] * weight_z[z + k] for k in range(2)]
            rows = slice((j * BZ + z) * HALF, (j * BZ + z + 2) * HALF)
            high, low = split(jnp.concatenate(pair, axis=0))
            planes_high[rows, :] = high
            planes_low[rows, :] = low


def second_stage(unit, counts, ins, buffers, outs, sums):
    _, gather, places, start, dens, _ = ins
    visc_out, moments_out = outs
    _, _, _, products, weights, factors, planes_high, planes_low = buffers
    owner, part = unit
    markers = places.shape[-1]
    inside = BZ * HALF
    grads = gradients(products, weights, markers)
    normal = grads[0][0] ** 2 + grads[1][1] ** 2 + grads[2][2] ** 2
    shear_xy = 0.5 * (grads[0][1] + grads[1][0])
    shear_xz = 0.5 * (grads[0][2] + grads[2][0])
    shear_yz = 0.5 * (grads[1][2] + grads[2][1])
    invariant = 0.5 * normal + shear_xy**2 + shear_xz**2 + shear_yz**2
    third = jnp.log(1.0 + invariant * (1.0 / (STRAIN_SCALE * STRAIN_SCALE))) * (1.0 / 3.0)
    first = start[owner, part]
    slot = lax.broadcasted_iota(jnp.int32, first.shape, 0) + part * HALF
    live = slot < counts[0, owner]
    visc_out[owner, part] = jnp.where(live, first * jnp.exp(-third), 0.0)
    carried = (
        live.astype(f32),
        jnp.where(live, jnp.log(first) - third, 0.0),
        jnp.where(live, dens[owner, part], 0.0),
    )
    count = 3 * BX * HALF
    for c in range(3):
        for i in range(0, BX, 2):
            pair = [carried[c] * weights[i + k] for k in range(2)]
            row = (c * BX + i) * HALF
            high, low = split(jnp.concatenate(pair, axis=0))
            factors[row : row + 2 * HALF, :] = high
            factors[count + row : count + row + 2 * HALF, :] = low
    contract = (((1,), (1,)), ((), ()))
    both = lax.dot_general(factors[...], planes_high[...], contract, preferred_element_type=f32)
    rest = lax.dot_general(factors[:count], planes_low[...], contract, preferred_element_type=f32)
    total = both[:count] + both[count:] + rest
    chosen = total.reshape(3 * BX, HALF, BY * inside) * own_lanes()[None]
    high, low = split(jnp.sum(chosen, axis=1))
    sums[: 3 * BX, :] = high.astype(f32)
    sums[16 : 16 + 3 * BX, :] = low.astype(f32)
    moved = dot(sums[...].astype(bf16), gather[part & 1])
    moved = moved[: 3 * BX] + moved[16 : 16 + 3 * BX]
    group = lax.shift_right_logical(part, 1)
    for j in range(BY):
        rows = pl.ds(j, 3 * BX, stride=BY)
        before = moments_out[owner, group, rows, :]
        moments_out[owner, group, rows, :] = before + moved[:, j * LANES : (j + 1) * LANES]


def marker_body(counts, *refs):
    ins, outs, scratch = refs[:6], refs[7:9], refs[9:]
    units, sums, *buffers = scratch
    buffers = (buffers[0::2], buffers[1::2])
    visc_out, moments_out = outs
    owners, parts = visc_out.shape[:2]
    visc_out[...] = jnp.zeros_like(visc_out)
    moments_out[...] = jnp.zeros_like(moments_out)
    sums[...] = jnp.zeros_like(sums)

    def list_units(index, found):
        number, dead = found
        owner, part = index // parts, index % parts
        live = part * HALF < counts[0, owner]

        @pl.when(live)
        def _():
            units[2 * number] = owner
            units[2 * number + 1] = part

        return jnp.where(live, number + 1, number), jnp.where(live, dead, index)

    number, dead = lax.fori_loop(0, owners * parts, list_units, (0, 0))

    @pl.when(number % 2 == 1)
    def _():
        units[2 * number] = dead // parts
        units[2 * number + 1] = dead % parts

    pairs = (number + 1) // 2

    def unit(index):
        return units[2 * index], units[2 * index + 1]

    def first(index, buffer):
        first_stage(unit(index), ins, buffers[buffer])

    def second(index, buffer):
        second_stage(unit(index), counts, ins, buffers[buffer], outs, sums)

    def both(pair, carry):
        first(2 * pair, 0)
        first(2 * pair + 1, 1)
        second(2 * pair, 0)
        second(2 * pair + 1, 1)
        return carry

    lax.fori_loop(0, pairs, both, 0)


def marker_work(counts, positions, start_visc, marker_dens, bricks, after):
    owners, _, slots, markers = positions.shape
    groups, parts = slots // GROUP, slots // HALF
    spread, gather = permutations()
    width = 4 * BZ * HALF
    whole = pl.BlockSpec(memory_space=pltpu.VMEM)
    buffers = (
        pltpu.VMEM((ROWS, width), f32),
        pltpu.VMEM((ROWS * HALF, width), bf16),
        pltpu.VMEM((width, 2 * markers), bf16),
        pltpu.VMEM((ROWS * HALF, 2 * markers), f32),
        pltpu.VMEM((4 * 4, HALF, markers), f32),
        pltpu.VMEM((2 * 3 * BX * HALF, markers), bf16),
        pltpu.VMEM((BY * BZ * HALF, markers), bf16),
        pltpu.VMEM((BY * BZ * HALF, markers), bf16),
    )
    visc, moments = pl.pallas_call(
        marker_body,
        out_shape=(
            jax.ShapeDtypeStruct((owners, parts, HALF, markers), f32),
            jax.ShapeDtypeStruct((owners, groups, ROWS, LANES), f32),
        ),
        in_specs=[pl.BlockSpec(memory_space=pltpu.SMEM)]
        + [whole] * 6
        + [pl.BlockSpec(memory_space=pl.ANY)],
        out_specs=(whole, whole),
        scratch_shapes=[
            pltpu.SMEM((2 * (owners * parts + 1),), jnp.int32),
            pltpu.VMEM((32, BY * BZ * HALF), f32),
        ]
        + [buffer for buffer in buffers for _ in range(2)],
        compiler_params=vmem_limit(60),
        cost_estimate=cost(25),
        name="marker_work",
    )(
        counts,
        spread,
        gather,
        positions.reshape(owners, 3, parts, HALF, markers),
        start_visc.reshape(owners, parts, HALF, markers),
        marker_dens.reshape(owners, parts, HALF, markers),
        bricks,
        after,
    )
    return visc.reshape(owners, slots, markers), moments


def settle_body(asked, moments_in, visc_in, dens_in, visc_out, dens_out, *scratch):
    moments, visc, dens, done, *tables = scratch
    size_x, size_y, size_z = visc.shape
    copies = [
        pltpu.make_async_copy(there, here, done.at[n])
        for n, (there, here) in enumerate(
            ((moments_in, moments), (visc_in, visc), (dens_in, dens))
        )
    ]
    for copy in copies:
        copy.start()
    bricks_y, halves = size_y // BY, size_z // LANES
    for table in tables:
        table[...] = jnp.zeros_like(table)
    copies[0].wait()
    groups = moments.shape[1]
    lane_slot = lax.broadcasted_iota(jnp.int32, (ROWS, LANES), 1) // BZ

    def one_group(step, carry):
        device, group = step // groups, step % groups
        packed = moments[device, group]
        for slot in range(GROUP):
            table = tables[slot % len(tables)]
            place, lane = place_of(asked[device, group * GROUP + slot])
            piece = jnp.where(lane_slot == slot, packed, 0.0)
            piece = pltpu.roll(piece, (lane - BZ * slot) & (LANES - 1), 1)
            table[place] = table[place] + piece
        return carry

    lax.fori_loop(0, moments.shape[0] * groups, one_group, 0)
    copies[1].wait()
    copies[2].wait()

    def finish(block_x, carry):
        for block_y in range(0, bricks_y, 2):
            for half in range(halves):
                for i in range(BX):
                    here = (
                        block_x * BX + i,
                        slice(block_y * BY, (block_y + 2) * BY),
                        slice(half * LANES, (half + 1) * LANES),
                    )
                    sums = []
                    for c in range(3):
                        rows = slice((c * BX + i) * BY, (c * BX + i + 1) * BY)
                        places = [
                            (block_x * bricks_y + block_y + k) * halves + half for k in range(2)
                        ]
                        sums.append(
                            jnp.concatenate(
                                [add_all([t[place, rows, :] for t in tables]) for place in places]
                            )
                        )
                    scale = 1.0 / (sums[0] + 1.0)
                    visc_out[here] = jnp.exp((sums[1] + jnp.log(visc[here])) * scale)
                    dens_out[here] = (sums[2] + dens[here]) * scale
        return carry

    lax.fori_loop(0, size_x // BX, finish, 0)


def settle(asked, moments, cell_visc, cell_dens):
    size_x, size_y, size_z = cell_visc.shape
    places = (size_x // BX) * (size_y // BY) * (size_z // LANES)
    whole = pl.BlockSpec(memory_space=pltpu.VMEM)
    shape = jax.ShapeDtypeStruct(cell_visc.shape, f32)
    return pl.pallas_call(
        settle_body,
        out_shape=(shape, shape),
        in_specs=[pl.BlockSpec(memory_space=pltpu.SMEM)]
        + [pl.BlockSpec(memory_space=pl.ANY)] * 3,
        out_specs=(whole, whole),
        scratch_shapes=[
            pltpu.VMEM(moments.shape, f32),
            pltpu.VMEM(cell_visc.shape, f32),
            pltpu.VMEM(cell_visc.shape, f32),
            pltpu.SemaphoreType.DMA((3,)),
        ]
        + [pltpu.VMEM((places, ROWS, LANES), f32)] * 2,
        compiler_params=vmem_limit(24),
        cost_estimate=cost(7),
        name="settle",
    )(asked, moments, cell_visc, cell_dens)


def field_of(fields, index):
    return fields[0].at[index] if index < 3 else fields[index - 2]


def pack_x_body(*refs):
    ends, outs = refs[:8], refs[8:]
    for side in range(2):
        for f in range(6):
            outs[side][f] = field_of(ends[side::2], f)[...]


def pack_x(velocity, pressure, cell_visc, cell_dens):
    size_x, size_y, size_z = cell_visc.shape
    width = SWEEPS
    ends = (0, size_x // width - 1)
    vel = [
        pl.BlockSpec((3, width, size_y, size_z), lambda i, e=e: (0, e, 0, 0)) for e in ends
    ]
    block = [pl.BlockSpec((width, size_y, size_z), lambda i, e=e: (e, 0, 0)) for e in ends]
    whole = pl.BlockSpec((6, width, size_y, size_z), lambda i: (0, 0, 0, 0))
    shape = jax.ShapeDtypeStruct((6, width, size_y, size_z), f32)
    return pl.pallas_call(
        pack_x_body,
        grid=(1,),
        out_shape=(shape, shape),
        in_specs=vel + block * 3,
        out_specs=(whole, whole),
        compiler_params=vmem_limit(60),
        cost_estimate=cost(2),
        name="pack_x",
    )(velocity, velocity, pressure, pressure, cell_visc, cell_visc, cell_dens, cell_dens)


def corner_rows(field):
    found, width = [], SWEEPS
    per_field = width * (width - 1)
    for side in range(2):
        for far_x in range(1, width):
            for far_y in range(1, width - far_x + 1):
                flat = field * per_field + len(found)
                found.append((side, far_x, far_y, *divmod(flat, 6 * width)))
    return found


def pack_y_body(vel, pres, visc, dens, low_x, high_x, upward, downward):
    step_x, size_y, _ = pres.shape
    width = SWEEPS
    step = pl.program_id(0)
    planes = pl.ds(pl.multiple_of(step * step_x, step_x), step_x)
    for f in range(6):
        field = field_of((vel, pres, visc, dens), f)
        rows = slice(f * width, (f + 1) * width)
        upward[planes, rows, :] = field[:, size_y - width :, :]
        downward[planes, rows, :] = field[:, :width, :]

    @pl.when(step == 0)
    def _():
        size_x = pl.num_programs(0) * step_x
        for f in range(6):
            for side, far_x, far_y, plane, row in corner_rows(f):
                halo, at = (high_x, far_x - 1) if side else (low_x, width - far_x)
                upward[size_x + plane, row] = halo[f, at, size_y - far_y]
                downward[size_x + plane, row] = halo[f, at, far_y - 1]


def pack_y(velocity, pressure, cell_visc, cell_dens, low_x, high_x):
    size_x, size_y, size_z = cell_visc.shape
    step, width = 8, SWEEPS
    long_x = size_x + width - 1
    block = pl.BlockSpec((step, size_y, size_z), lambda i: (i, 0, 0))
    halo = pl.BlockSpec(low_x.shape, lambda i: (0, 0, 0, 0))
    face = pl.BlockSpec((long_x, 6 * width, size_z), lambda i: (0, 0, 0))
    shape = jax.ShapeDtypeStruct((long_x, 6 * width, size_z), f32)
    return pl.pallas_call(
        pack_y_body,
        grid=(size_x // step,),
        out_shape=(shape, shape),
        in_specs=[
            pl.BlockSpec((3, step, size_y, size_z), lambda i: (0, i, 0, 0)),
            block,
            block,
            block,
            halo,
            halo,
        ],
        out_specs=(face, face),
        compiler_params=vmem_limit(24),
        cost_estimate=cost(15),
        name="pack_y",
    )(velocity, pressure, cell_visc, cell_dens, low_x, high_x)


def sweep_body(vel, pres, visc, dens, low_x, high_x, low_y, high_y, vel_out, pres_out, *work):
    blocks, sides_x, sides_y, results, fields, coefs, relax, forcing, rate, done = work
    size_x, size_y, size_z = blocks.shape[1:]
    width = SWEEPS
    per, halves = fields.shape[1:3]
    long_y = size_y + 2 * width
    inputs = (
        (visc, blocks.at[4]),
        (vel, blocks.at[0:3]),
        (pres, blocks.at[3]),
        (dens, blocks.at[5]),
        (low_x, sides_x.at[0]),
        (high_x, sides_x.at[1]),
        (low_y, sides_y.at[0]),
        (high_y, sides_y.at[1]),
    )
    copies = [
        pltpu.make_async_copy(there, here, done.at[n]) for n, (there, here) in enumerate(inputs)
    ]
    for copy in copies:
        copy.start()

    def place(x, y, rows):
        return x % per, pl.ds(y * SUBLANES + x // per, rows, stride=SUBLANES)

    def put(field, x, y, rows, value):
        plane, lines = place(x, y, rows)
        for half in range(halves):
            fields[field, plane, half, lines, :] = value[:, half * LANES : (half + 1) * LANES]

    def own_planes(field, carry):
        for i in range(size_x):
            for y in range(0, size_y, SUBLANES):
                put(field, i + width, y + width, SUBLANES, blocks[field, i, y : y + SUBLANES, :])
        return carry

    def side_planes(field):
        rows = slice(field * width, (field + 1) * width)
        for side, begin in enumerate((0, width + size_x)):
            for i in range(width):
                for y in range(0, size_y, SUBLANES):
                    value = sides_x[side, field, i, y : y + SUBLANES, :]
                    put(field, begin + i, y + width, SUBLANES, value)
                for y in (0, width + size_y):
                    put(field, begin + i, y, width, jnp.zeros((width, size_z), f32))
        for side, begin in enumerate((0, width + size_y)):
            for i in range(size_x):
                put(field, i + width, begin, width, sides_y[side, i, rows, :])

    for copy in copies[:4]:
        copy.wait()
    lax.fori_loop(0, 6, own_planes, 0)
    for copy in copies[4:]:
        copy.wait()
    for field in range(6):
        side_planes(field)
        for side, far_x, far_y, plane, row in corner_rows(field):
            x = width + size_x - 1 + far_x if side else width - far_x
            for end, y in enumerate((width - far_y, width + size_y - 1 + far_y)):
                line = sides_y[end, size_x + plane, pl.ds(row, 1), :]
                put(field, x, y, 1, line)

    lane = lax.broadcasted_iota(jnp.int32, (SUBLANES, size_z), 1)
    not_last = (lane < size_z - 1).astype(f32)
    not_first = (lane > 0).astype(f32)

    def tile(y):
        return pl.ds(pl.multiple_of(y * SUBLANES, SUBLANES), SUBLANES)

    def take(field, plane, y):
        return jnp.concatenate(
            [fields[field, plane, half, tile(y), :] for half in range(halves)], axis=1
        )

    def store(field, plane, y, value):
        for half in range(halves):
            part = value[:, half * LANES : (half + 1) * LANES]
            fields[field, plane, half, tile(y), :] = part

    def up_x(field, plane, y):
        if plane < per - 1:
            return take(field, plane + 1, y)
        return pltpu.roll(take(field, 0, y), SUBLANES - 1, 0)

    def down_x(field, plane, y):
        if plane > 0:
            return take(field, plane - 1, y)
        return pltpu.roll(take(field, per - 1, y), 1, 0)

    def up_z(a):
        return pltpu.roll(a, size_z - 1, 1)

    def down_z(a):
        return pltpu.roll(a, 1, 1)

    def prepare(y, carry):
        for plane in range(per):
            here = take(4, plane, y)
            near = [
                up_x(4, plane, y),
                down_x(4, plane, y),
                take(4, plane, y + 1),
                take(4, plane, y - 1),
                up_z(here) * not_last,
                down_z(here) * not_first,
            ]
            links = [0.5 * (here + other) for other in near]
            scale = jnp.where(here > 0.0, RELAX / add_all(links), 0.0)
            links[4] = links[4] * not_last
            links[5] = links[5] * not_first
            for n in range(6):
                coefs[n, plane, tile(y), :] = links[n] * scale
            relax[plane, tile(y), :] = scale
            forcing[plane, tile(y), :] = take(5, plane, y) * (-GRAVITY * scale)
            rate[plane, tile(y), :] = PRESSURE_RATE * here
        return carry

    lax.fori_loop(1, long_y - 1, prepare, 0)

    for sweep in range(SWEEPS):
        old, new = (6, 0) if sweep % 2 else (0, 6)

        def one_row(y, carry, old=old, new=new):
            for plane in range(per):
                pressure = take(old + 3, plane, y)
                scale = relax[plane, tile(y), :]
                before = (
                    down_x(old + 3, plane, y),
                    take(old + 3, plane, y - 1),
                    down_z(pressure) * not_first,
                )
                divergence = None
                for c in range(3):
                    here = take(old + c, plane, y)
                    near = [
                        up_x(old + c, plane, y),
                        down_x(old + c, plane, y),
                        take(old + c, plane, y + 1),
                        take(old + c, plane, y - 1),
                        up_z(here),
                        down_z(here),
                    ]
                    total = (1.0 - RELAX) * here - scale * (pressure - before[c])
                    for n, other in enumerate(near):
                        total = total + coefs[n, plane, tile(y), :] * other
                    ahead = near[2 * c]
                    if c == 2:
                        total = total + forcing[plane, tile(y), :]
                        ahead = ahead * not_last
                    change = ahead - here
                    divergence = change if divergence is None else divergence + change
                    store(new + c, plane, y, total)
                pressed = pressure - rate[plane, tile(y), :] * divergence
                store(new + 3, plane, y, pressed)
            return carry

        lax.fori_loop(1 + sweep, long_y - 1 - sweep, one_row, 0)

    final = 6 if SWEEPS % 2 else 0
    outs = [vel_out.at[0], vel_out.at[1], vel_out.at[2], pres_out]
    sends = [
        pltpu.make_async_copy(results.at[n], out, done.at[n]) for n, out in enumerate(outs)
    ]
    for field, send in enumerate(sends):
        for i in range(size_x):
            for y in range(0, size_y, SUBLANES):
                plane, lines = place(i + width, y + width, SUBLANES)
                for half in range(halves):
                    results[
                        field, i, y : y + SUBLANES, half * LANES : (half + 1) * LANES
                    ] = fields[final + field, plane, half, lines, :]
        send.start()
    for send in sends:
        send.wait()


def all_sweeps(velocity, pressure, cell_visc, cell_dens, low_x, high_x, low_y, high_y):
    size_x, size_y, size_z = cell_visc.shape
    width = low_x.shape[1]
    per, rows = (size_x + 2 * width) // SUBLANES, (size_y + 2 * width) * SUBLANES
    block = (per, rows, size_z)
    anywhere = pl.BlockSpec(memory_space=pl.ANY)
    return pl.pallas_call(
        sweep_body,
        out_shape=(
            jax.ShapeDtypeStruct(velocity.shape, f32),
            jax.ShapeDtypeStruct(pressure.shape, f32),
        ),
        in_specs=[anywhere] * 8,
        out_specs=(anywhere, anywhere),
        scratch_shapes=[
            pltpu.VMEM((6,) + cell_visc.shape, f32),
            pltpu.VMEM((2,) + low_x.shape, f32),
            pltpu.VMEM((2,) + low_y.shape, f32),
            pltpu.VMEM((4,) + cell_visc.shape, f32),
            pltpu.VMEM((10, per, size_z // LANES, rows, LANES), f32),
            pltpu.VMEM((6,) + block, f32),
            pltpu.VMEM(block, f32),
            pltpu.VMEM(block, f32),
            pltpu.VMEM(block, f32),
            pltpu.SemaphoreType.DMA((8,)),
        ],
        compiler_params=vmem_limit(44),
        cost_estimate=cost(20),
        name="all_sweeps",
    )(velocity, pressure, cell_visc, cell_dens, low_x, high_x, low_y, high_y)


def shift(value, axis, step):
    size = lax.axis_size(axis)
    pairs = [(i, i + step) for i in range(size) if 0 <= i + step < size]
    return lax.ppermute(value, axis, pairs)


def per_device(
    velocity,
    pressure,
    cell_visc,
    cell_dens,
    block_brick,
    block_counts,
    positions,
    start_visc,
    marker_dens,
):
    asked = lax.all_to_all(block_brick, "mark", 0, 0, tiled=True)
    fields = (velocity, pressure, cell_visc, cell_dens)
    to_low, to_high = pack_x(*fields)
    low_x, high_x = shift(to_high, "grid", 1), shift(to_low, "grid", -1)
    upward, downward = pack_y(*fields, low_x, high_x)
    low_y, high_y = shift(upward, "mark", 1), shift(downward, "mark", -1)

    picked = pick_bricks(asked, velocity)
    bricks = lax.all_to_all(picked, "mark", 0, 0, tiled=True)
    marker_visc, moments = marker_work(
        block_counts, positions, start_visc, marker_dens, bricks, upward
    )
    gathered = lax.all_to_all(moments, "mark", 0, 0, tiled=True)
    velocity_next, pressure_next = all_sweeps(*fields, low_x, high_x, low_y, high_y)
    visc_next, dens_next = settle(asked, gathered, cell_visc, cell_dens)
    return velocity_next, pressure_next, visc_next, dens_next, marker_visc


def solution(mesh):
    in_specs = (
        P(None, "grid", "mark", None),
        P("grid", "mark", None),
        P("grid", "mark", None),
        P("grid", "mark", None),
        P(("grid", "mark"), None),
        P(("grid", "mark"), None),
        P(("grid", "mark"), None, None, None),
        P(("grid", "mark"), None, None),
        P(("grid", "mark"), None, None),
    )
    out_specs = (
        P(None, "grid", "mark", None),
        P("grid", "mark", None),
        P("grid", "mark", None),
        P("grid", "mark", None),
        P(("grid", "mark"), None, None),
    )
    return jax.shard_map(
        per_device, mesh=mesh, in_specs=in_specs, out_specs=out_specs, check_vma=False
    )
```

```python
import functools

import jax
import jax.numpy as jnp
import numpy as np
from jax import lax
from jax.experimental import pallas as pl
from jax.experimental.pallas import tpu as pltpu
from jax.sharding import PartitionSpec as P

SWEEPS = 4
RELAX = 0.6
PRESSURE_RATE = 0.25
GRAVITY = 1.0
STRAIN_SCALE = 0.5

BX, BY, BZ = 4, 4, 8
PLANE = BX * BY
ROWS = 3 * PLANE
LANES = 128
GROUP = LANES // BZ
HALF = 8
SUBLANES = 8

f32, bf16 = jnp.float32, jnp.bfloat16


def vmem_limit(mib):
    return pltpu.CompilerParams(vmem_limit_bytes=mib * 1024 * 1024)


def cost(microseconds):
    return pl.CostEstimate(
        flops=int(microseconds * 1.15e9), bytes_accessed=0, transcendentals=0
    )


def place_of(brick):
    return lax.shift_right_logical(brick, GROUP.bit_length() - 1), (brick & (GROUP - 1)) * BZ


def pick_body(asked, vel, out, table):
    size_x, size_y, size_z = vel.shape[1:]
    bricks_y, halves = size_y // BY, size_z // LANES

    def repack(block_x, carry):
        for block_y in range(bricks_y):
            for half in range(halves):
                place = (block_x * bricks_y + block_y) * halves + half
                for c in range(3):
                    for i in range(BX):
                        row = (c * BX + i) * BY
                        table[place, row : row + BY, :] = vel[
                            c,
                            block_x * BX + i,
                            block_y * BY : (block_y + 1) * BY,
                            half * LANES : (half + 1) * LANES,
                        ]
        return carry

    lax.fori_loop(0, size_x // BX, repack, 0)
    groups = out.shape[1]
    lane_slot = lax.broadcasted_iota(jnp.int32, (ROWS, LANES), 1) // BZ

    def one_group(step, carry):
        device, group = step // groups, step % groups
        packed = jnp.zeros((ROWS, LANES), f32)
        for slot in range(GROUP):
            place, lane = place_of(asked[device, group * GROUP + slot])
            rolled = pltpu.roll(table[place], (BZ * slot - lane) & (LANES - 1), 1)
            packed = jnp.where(lane_slot == slot, rolled, packed)
        out[device, group] = packed
        return carry

    lax.fori_loop(0, out.shape[0] * groups, one_group, 0)


def pick_bricks(asked, velocity):
    devices, slots = asked.shape
    size_x, size_y, size_z = velocity.shape[1:]
    places = (size_x // BX) * (size_y // BY) * (size_z // LANES)
    return pl.pallas_call(
        pick_body,
        out_shape=jax.ShapeDtypeStruct((devices, slots // GROUP, ROWS, LANES), f32),
        in_specs=[
            pl.BlockSpec(memory_space=pltpu.SMEM),
            pl.BlockSpec(memory_space=pltpu.VMEM),
        ],
        out_specs=pl.BlockSpec(memory_space=pltpu.VMEM),
        scratch_shapes=[pltpu.VMEM((places, ROWS, LANES), f32)],
        compiler_params=vmem_limit(24),
        cost_estimate=cost(25),
        name="pick_bricks",
    )(asked, velocity)


def permutations():
    inside = BZ * HALF
    spread = np.zeros((2, 2, LANES, 4 * inside), np.float32)
    gather = np.zeros((2 * BY * inside, BY * LANES), np.float32)
    for half in range(2):
        for slot in range(HALF):
            for z in range(BZ):
                outer, inner = (half * HALF + slot) * BZ + z, z * HALF + slot
                for part in range(4):
                    spread[half, part // 2, outer, part * inside + inner] = 1
                for j in range(BY):
                    gather[(half * BY + j) * inside + inner, j * LANES + outer] = 1
    return jnp.asarray(spread, bf16), jnp.asarray(gather, bf16)


def split(value):
    high = value.astype(bf16)
    return high, (value - high.astype(f32)).astype(bf16)


def add_all(values):
    return functools.reduce(jnp.add, values)


def axis_weights(fraction, cells):
    middle = (cells - 1) / 2
    base = jnp.exp(fraction * (2.0 * cells) - float(cells))
    powers = [None, base]
    for i in range(2, cells):
        powers.append(powers[i // 2] * powers[i - i // 2])
    factors = [float(np.exp(middle**2 - (i - middle) ** 2)) for i in range(cells)]
    bells = [None] + [powers[i] * factors[i] for i in range(1, cells)]
    scale = 1.0 / (add_all(bells[1:]) + factors[0])
    weights = [scale * factors[0]] + [bell * scale for bell in bells[1:]]
    mean = add_all(
        [
            (weights[cells - 1 - i] - weights[i]) * (2.0 * (middle - i))
            for i in range(cells // 2)
        ]
    )
    slopes = [w * (2.0 * (i - middle) - mean) for i, w in enumerate(weights)]
    return weights, slopes


def dot(a, b):
    return jnp.dot(a, b, preferred_element_type=f32)


def gradients(products, weights, markers):
    weight_x, slope_x, weight_y, slope_y = ([weights[4 * n + i] for i in range(4)] for n in range(4))
    grads = []
    for c in range(3):
        lines = [[], [], []]
        for i in range(BX):
            rows = [((c * BX + i) * BY + j) * HALF for j in range(BY)]
            still = [products[row : row + HALF, :markers] for row in rows]
            rising = [products[row : row + HALF, markers:] for row in rows]
            lines[0].append(slope_x[i] * add_all([w * t for w, t in zip(weight_y, still)]))
            lines[1].append(weight_x[i] * add_all([w * t for w, t in zip(slope_y, still)]))
            lines[2].append(weight_x[i] * add_all([w * t for w, t in zip(weight_y, rising)]))
        grads.append([add_all(line) for line in lines])
    return grads


def own_lanes():
    shape = (HALF, 4 * BZ * HALF)
    lane = lax.broadcasted_iota(jnp.int32, shape, 1)
    return (lane % HALF == lax.broadcasted_iota(jnp.int32, shape, 0)).astype(f32)


def marker_groups(groups, counts, ins, outs, buffers, sums):
    spread, gather, places, start, dens, brick = ins
    visc_out, moments_out = outs
    permuted, left, right, products, weights, factors, planes_high, planes_low = buffers
    markers = places.shape[-1]
    inside = BZ * HALF
    own = own_lanes()
    halves = [
        (owner, 2 * group + half, half, 2 * n + half)
        for n, (owner, group) in enumerate(groups)
        for half in range(2)
    ]
    parts = [split(brick[owner, group]) for owner, group in groups]
    for _, _, half, n in halves:
        high, low = parts[n // 2]
        permuted[n][...] = dot(high, spread[half, 0]) + dot(low, spread[half, 1])
    heights = []
    for owner, part, _, n in halves:
        weight_z, slope_z = axis_weights(places[owner, 2, part], BZ)
        heights.append(weight_z)
        for z in range(0, BZ, 2):
            for column, values in ((0, weight_z), (1, slope_z)):
                high, low = split(jnp.concatenate(values[z : z + 2], axis=0))
                columns = slice(column * markers, (column + 1) * markers)
                for k in range(4):
                    begin = k * inside + z * HALF
                    right[n][begin : begin + 2 * HALF, columns] = low if k % 2 else high
    for _, _, _, n in halves:
        for row in range(0, ROWS, 2):
            pair = [
                jnp.broadcast_to(permuted[n][r : r + 1, :], own.shape) * own for r in (row, row + 1)
            ]
            left[n][row * HALF : (row + 2) * HALF, :] = jnp.concatenate(pair, axis=0).astype(bf16)
    for _, _, _, n in halves:
        products[n][...] = dot(left[n][...], right[n][...])
    for owner, part, _, n in halves:
        weights_x = axis_weights(places[owner, 0, part], BX)
        weights_y = axis_weights(places[owner, 1, part], BY)
        for k, values in enumerate((*weights_x, *weights_y)):
            for i, value in enumerate(values):
                weights[n][4 * k + i] = value
        for j in range(BY):
            for z in range(0, BZ, 2):
                pair = [weights_y[0][j] * heights[n][z + k] for k in range(2)]
                rows = slice((j * BZ + z) * HALF, (j * BZ + z + 2) * HALF)
                high, low = split(jnp.concatenate(pair, axis=0))
                planes_high[n][rows, :] = high
                planes_low[n][rows, :] = low

    count = 3 * BX * HALF
    for owner, part, _, n in halves:
        grads = gradients(products[n], weights[n], markers)
        normal = grads[0][0] ** 2 + grads[1][1] ** 2 + grads[2][2] ** 2
        shear_xy = 0.5 * (grads[0][1] + grads[1][0])
        shear_xz = 0.5 * (grads[0][2] + grads[2][0])
        shear_yz = 0.5 * (grads[1][2] + grads[2][1])
        invariant = 0.5 * normal + shear_xy**2 + shear_xz**2 + shear_yz**2
        scaled = invariant * (1.0 / (STRAIN_SCALE * STRAIN_SCALE))
        third = jnp.log(1.0 + scaled) * (1.0 / 3.0)
        first = start[owner, part]
        slot = lax.broadcasted_iota(jnp.int32, first.shape, 0) + part * HALF
        live = slot < counts[0, owner]
        visc_out[owner, part] = jnp.where(live, first * jnp.exp(-third), 0.0)
        carried = (
            live.astype(f32),
            jnp.where(live, jnp.log(first) - third, 0.0),
            jnp.where(live, dens[owner, part], 0.0),
        )
        for c in range(3):
            for i in range(0, BX, 2):
                pair = [carried[c] * weights[n][i + k] for k in range(2)]
                row = (c * BX + i) * HALF
                high, low = split(jnp.concatenate(pair, axis=0))
                factors[n][row : row + 2 * HALF, :] = high
                factors[n][count + row : count + row + 2 * HALF, :] = low

    contract = (((1,), (1,)), ((), ()))
    found = []
    for _, _, _, n in halves:
        both = lax.dot_general(
            factors[n][...], planes_high[n][...], contract, preferred_element_type=f32
        )
        rest = lax.dot_general(
            factors[n][:count], planes_low[n][...], contract, preferred_element_type=f32
        )
        found.append((both, rest))
    for _, _, half, n in halves:
        both, rest = found[n]
        total = both[:count] + both[count:] + rest
        chosen = total.reshape(3 * BX, HALF, BY * inside) * own[None]
        high, low = split(jnp.sum(chosen, axis=1))
        columns = slice(half * BY * inside, (half + 1) * BY * inside)
        row = (n // 2) * 32
        sums[row : row + 3 * BX, columns] = high.astype(f32)
        sums[row + 16 : row + 16 + 3 * BX, columns] = low.astype(f32)
    moved = dot(sums[...].astype(bf16), gather[...])
    for n, (owner, group) in enumerate(groups):
        mine = moved[32 * n : 32 * n + 3 * BX] + moved[32 * n + 16 : 32 * n + 16 + 3 * BX]
        for j in range(BY):
            rows = pl.ds(j, 3 * BX, stride=BY)
            moments_out[owner, group, rows, :] = mine[:, j * LANES : (j + 1) * LANES]


TOGETHER = 2


def marker_body(counts, *refs):
    ins, outs, scratch = refs[:6], refs[7:9], refs[9:]
    listed, sums, *flat = scratch
    held = 2 * TOGETHER
    buffers = [flat[n * held : (n + 1) * held] for n in range(len(flat) // held)]
    visc_out, moments_out = outs
    owners, groups = moments_out.shape[:2]
    visc_out[...] = jnp.zeros_like(visc_out)
    moments_out[...] = jnp.zeros_like(moments_out)
    sums[...] = jnp.zeros_like(sums)

    def list_groups(index, number):
        owner, group = index // groups, index % groups
        live = group * GROUP < counts[0, owner]

        @pl.when(live)
        def _():
            for n in range(TOGETHER):
                listed[2 * (number + n)] = owner
                listed[2 * (number + n) + 1] = group

        return jnp.where(live, number + 1, number)

    number = lax.fori_loop(0, owners * groups, list_groups, 0)

    def step(index, carry):
        first = TOGETHER * index
        taken = [
            (listed[2 * (first + n)], listed[2 * (first + n) + 1]) for n in range(TOGETHER)
        ]
        marker_groups(taken, counts, ins, outs, buffers, sums)
        return carry

    lax.fori_loop(0, (number + TOGETHER - 1) // TOGETHER, step, 0)


def marker_work(counts, positions, start_visc, marker_dens, bricks, after):
    owners, _, slots, markers = positions.shape
    groups, parts = slots // GROUP, slots // HALF
    spread, gather = permutations()
    width = 4 * BZ * HALF
    whole = pl.BlockSpec(memory_space=pltpu.VMEM)
    buffers = (
        pltpu.VMEM((ROWS, width), f32),
        pltpu.VMEM((ROWS * HALF, width), bf16),
        pltpu.VMEM((width, 2 * markers), bf16),
        pltpu.VMEM((ROWS * HALF, 2 * markers), f32),
        pltpu.VMEM((4 * 4, HALF, markers), f32),
        pltpu.VMEM((2 * 3 * BX * HALF, markers), bf16),
        pltpu.VMEM((BY * BZ * HALF, markers), bf16),
        pltpu.VMEM((BY * BZ * HALF, markers), bf16),
    )
    visc, moments = pl.pallas_call(
        marker_body,
        out_shape=(
            jax.ShapeDtypeStruct((owners, parts, HALF, markers), f32),
            jax.ShapeDtypeStruct((owners, groups, ROWS, LANES), f32),
        ),
        in_specs=[pl.BlockSpec(memory_space=pltpu.SMEM)]
        + [whole] * 6
        + [pl.BlockSpec(memory_space=pl.ANY)],
        out_specs=(whole, whole),
        scratch_shapes=[
            pltpu.SMEM((2 * (owners * groups + TOGETHER),), jnp.int32),
            pltpu.VMEM((32 * TOGETHER, 2 * BY * BZ * HALF), f32),
        ]
        + [buffer for buffer in buffers for _ in range(2 * TOGETHER)],
        compiler_params=vmem_limit(60),
        cost_estimate=cost(25),
        name="marker_work",
    )(
        counts,
        spread,
        gather,
        positions.reshape(owners, 3, parts, HALF, markers),
        start_visc.reshape(owners, parts, HALF, markers),
        marker_dens.reshape(owners, parts, HALF, markers),
        bricks,
        after,
    )
    return visc.reshape(owners, slots, markers), moments


def settle_body(asked, moments_in, visc_in, dens_in, visc_out, dens_out, *scratch):
    moments, visc, dens, done, *tables = scratch
    size_x, size_y, size_z = visc.shape
    copies = [
        pltpu.make_async_copy(there, here, done.at[n])
        for n, (there, here) in enumerate(
            ((moments_in, moments), (visc_in, visc), (dens_in, dens))
        )
    ]
    for copy in copies:
        copy.start()
    bricks_y, halves = size_y // BY, size_z // LANES
    for table in tables:
        table[...] = jnp.zeros_like(table)
    copies[0].wait()
    groups = moments.shape[1]
    lane_slot = lax.broadcasted_iota(jnp.int32, (ROWS, LANES), 1) // BZ

    def one_group(step, carry):
        device, group = step // groups, step % groups
        packed = moments[device, group]
        for slot in range(GROUP):
            table = tables[slot % len(tables)]
            place, lane = place_of(asked[device, group * GROUP + slot])
            piece = jnp.where(lane_slot == slot, packed, 0.0)
            piece = pltpu.roll(piece, (lane - BZ * slot) & (LANES - 1), 1)
            table[place] = table[place] + piece
        return carry

    lax.fori_loop(0, moments.shape[0] * groups, one_group, 0)
    copies[1].wait()
    copies[2].wait()

    def finish(block_x, carry):
        for block_y in range(0, bricks_y, 2):
            for half in range(halves):
                for i in range(BX):
                    here = (
                        block_x * BX + i,
                        slice(block_y * BY, (block_y + 2) * BY),
                        slice(half * LANES, (half + 1) * LANES),
                    )
                    sums = []
                    for c in range(3):
                        rows = slice((c * BX + i) * BY, (c * BX + i + 1) * BY)
                        places = [
                            (block_x * bricks_y + block_y + k) * halves + half for k in range(2)
                        ]
                        sums.append(
                            jnp.concatenate(
                                [add_all([t[place, rows, :] for t in tables]) for place in places]
                            )
                        )
                    scale = 1.0 / (sums[0] + 1.0)
                    visc_out[here] = jnp.exp((sums[1] + jnp.log(visc[here])) * scale)
                    dens_out[here] = (sums[2] + dens[here]) * scale
        return carry

    lax.fori_loop(0, size_x // BX, finish, 0)


def settle(asked, moments, cell_visc, cell_dens):
    size_x, size_y, size_z = cell_visc.shape
    places = (size_x // BX) * (size_y // BY) * (size_z // LANES)
    whole = pl.BlockSpec(memory_space=pltpu.VMEM)
    shape = jax.ShapeDtypeStruct(cell_visc.shape, f32)
    return pl.pallas_call(
        settle_body,
        out_shape=(shape, shape),
        in_specs=[pl.BlockSpec(memory_space=pltpu.SMEM)]
        + [pl.BlockSpec(memory_space=pl.ANY)]
        + [pl.BlockSpec(memory_space=pltpu.HBM)] * 2,
        out_specs=(whole, whole),
        scratch_shapes=[
            pltpu.VMEM(moments.shape, f32),
            pltpu.VMEM(cell_visc.shape, f32),
            pltpu.VMEM(cell_visc.shape, f32),
            pltpu.SemaphoreType.DMA((3,)),
        ]
        + [pltpu.VMEM((places, ROWS, LANES), f32)] * 2,
        compiler_params=vmem_limit(60),
        cost_estimate=cost(7),
        name="settle",
    )(asked, moments, cell_visc, cell_dens)


def field_of(fields, index):
    return fields[0].at[index] if index < 3 else fields[index - 2]


def pack_x_body(*refs):
    ends, outs = refs[:8], refs[8:]
    for side in range(2):
        for f in range(6):
            outs[side][f] = field_of(ends[side::2], f)[...]


def pack_x(velocity, pressure, cell_visc, cell_dens):
    size_x, size_y, size_z = cell_visc.shape
    width = SWEEPS
    ends = (0, size_x // width - 1)
    vel = [
        pl.BlockSpec((3, width, size_y, size_z), lambda i, e=e: (0, e, 0, 0)) for e in ends
    ]
    block = [pl.BlockSpec((width, size_y, size_z), lambda i, e=e: (e, 0, 0)) for e in ends]
    whole = pl.BlockSpec((6, width, size_y, size_z), lambda i: (0, 0, 0, 0))
    shape = jax.ShapeDtypeStruct((6, width, size_y, size_z), f32)
    return pl.pallas_call(
        pack_x_body,
        grid=(1,),
        out_shape=(shape, shape),
        in_specs=vel + block * 3,
        out_specs=(whole, whole),
        compiler_params=vmem_limit(60),
        cost_estimate=cost(2),
        name="pack_x",
    )(velocity, velocity, pressure, pressure, cell_visc, cell_visc, cell_dens, cell_dens)


def corner_rows(field):
    found, width = [], SWEEPS
    per_field = width * (width - 1)
    for side in range(2):
        for far_x in range(1, width):
            for far_y in range(1, width - far_x + 1):
                flat = field * per_field + len(found)
                found.append((side, far_x, far_y, *divmod(flat, 6 * width)))
    return found


def pack_y_body(vel, pres, visc, dens, low_x, high_x, upward, downward):
    step_x, size_y, _ = pres.shape
    width = SWEEPS
    step = pl.program_id(0)
    planes = pl.ds(pl.multiple_of(step * step_x, step_x), step_x)
    for f in range(6):
        field = field_of((vel, pres, visc, dens), f)
        rows = slice(f * width, (f + 1) * width)
        upward[planes, rows, :] = field[:, size_y - width :, :]
        downward[planes, rows, :] = field[:, :width, :]

    @pl.when(step == 0)
    def _():
        size_x = pl.num_programs(0) * step_x
        for f in range(6):
            for side, far_x, far_y, plane, row in corner_rows(f):
                halo, at = (high_x, far_x - 1) if side else (low_x, width - far_x)
                upward[size_x + plane, row] = halo[f, at, size_y - far_y]
                downward[size_x + plane, row] = halo[f, at, far_y - 1]


def pack_y(velocity, pressure, cell_visc, cell_dens, low_x, high_x):
    size_x, size_y, size_z = cell_visc.shape
    step, width = 8, SWEEPS
    long_x = size_x + width - 1
    block = pl.BlockSpec((step, size_y, size_z), lambda i: (i, 0, 0))
    halo = pl.BlockSpec(low_x.shape, lambda i: (0, 0, 0, 0))
    face = pl.BlockSpec((long_x, 6 * width, size_z), lambda i: (0, 0, 0))
    shape = jax.ShapeDtypeStruct((long_x, 6 * width, size_z), f32)
    return pl.pallas_call(
        pack_y_body,
        grid=(size_x // step,),
        out_shape=(shape, shape),
        in_specs=[
            pl.BlockSpec((3, step, size_y, size_z), lambda i: (0, i, 0, 0)),
            block,
            block,
            block,
            halo,
            halo,
        ],
        out_specs=(face, face),
        compiler_params=vmem_limit(24),
        cost_estimate=cost(15),
        name="pack_y",
    )(velocity, pressure, cell_visc, cell_dens, low_x, high_x)


def sweep_body(vel, pres, visc, dens, low_x, high_x, low_y, high_y, vel_out, pres_out, *work):
    blocks, sides_x, sides_y, results, even, odd, cells, coefs, relax, forcing, rate, done = work
    size_x, size_y, size_z = blocks.shape[1:]
    width = SWEEPS
    per, halves = even.shape[1:3]
    long_y = size_y + 2 * width
    inputs = (
        (visc, blocks.at[4]),
        (vel, blocks.at[0:3]),
        (pres, blocks.at[3]),
        (dens, blocks.at[5]),
        (low_x, sides_x.at[0]),
        (high_x, sides_x.at[1]),
        (low_y, sides_y.at[0]),
        (high_y, sides_y.at[1]),
    )
    copies = [
        pltpu.make_async_copy(there, here, done.at[n]) for n, (there, here) in enumerate(inputs)
    ]
    for copy in copies:
        copy.start()

    def place(x, y, rows):
        return x % per, pl.ds(y * SUBLANES + x // per, rows, stride=SUBLANES)

    def put(field, x, y, rows, value):
        plane, lines = place(x, y, rows)
        target = even.at[field] if field < 4 else cells.at[field - 4]
        for half in range(halves):
            target[plane, half, lines, :] = value[:, half * LANES : (half + 1) * LANES]

    def own_planes(field):
        for i in range(size_x):
            for y in range(0, size_y, SUBLANES):
                put(field, i + width, y + width, SUBLANES, blocks[field, i, y : y + SUBLANES, :])

    def side_planes(field):
        rows = slice(field * width, (field + 1) * width)
        for side, begin in enumerate((0, width + size_x)):
            for i in range(width):
                for y in range(0, size_y, SUBLANES):
                    value = sides_x[side, field, i, y : y + SUBLANES, :]
                    put(field, begin + i, y + width, SUBLANES, value)
                for y in (0, width + size_y):
                    put(field, begin + i, y, width, jnp.zeros((width, size_z), f32))
        for side, begin in enumerate((0, width + size_y)):
            for i in range(size_x):
                put(field, i + width, begin, width, sides_y[side, i, rows, :])

    for copy, held in zip(copies, ((4,), (0, 1, 2), (3,), (5,))):
        copy.wait()
        for field in held:
            own_planes(field)
    for copy in copies[4:]:
        copy.wait()
    for field in range(6):
        side_planes(field)
        for side, far_x, far_y, plane, row in corner_rows(field):
            x = width + size_x - 1 + far_x if side else width - far_x
            for end, y in enumerate((width - far_y, width + size_y - 1 + far_y)):
                line = sides_y[end, size_x + plane, pl.ds(row, 1), :]
                put(field, x, y, 1, line)

    lane = lax.broadcasted_iota(jnp.int32, (SUBLANES, size_z), 1)
    not_last = (lane < size_z - 1).astype(f32)
    not_first = (lane > 0).astype(f32)

    def tile(y):
        return pl.ds(pl.multiple_of(y * SUBLANES, SUBLANES), SUBLANES)

    def take(field, plane, y):
        return jnp.concatenate(
            [field[plane, half, tile(y), :] for half in range(halves)], axis=1
        )

    def store(field, plane, y, value):
        for half in range(halves):
            field[plane, half, tile(y), :] = value[:, half * LANES : (half + 1) * LANES]

    def up_x(field, plane, y):
        if plane < per - 1:
            return take(field, plane + 1, y)
        return pltpu.roll(take(field, 0, y), SUBLANES - 1, 0)

    def down_x(field, plane, y):
        if plane > 0:
            return take(field, plane - 1, y)
        return pltpu.roll(take(field, per - 1, y), 1, 0)

    def up_z(a):
        return pltpu.roll(a, size_z - 1, 1)

    def down_z(a):
        return pltpu.roll(a, 1, 1)

    def prepare(y, carry):
        visc, dens = cells.at[0], cells.at[1]
        for plane in range(per):
            here = take(visc, plane, y)
            near = [
                up_x(visc, plane, y),
                down_x(visc, plane, y),
                take(visc, plane, y + 1),
                take(visc, plane, y - 1),
                up_z(here) * not_last,
                down_z(here) * not_first,
            ]
            links = [0.5 * (here + other) for other in near]
            scale = jnp.where(here > 0.0, RELAX / add_all(links), 0.0)
            links[4] = links[4] * not_last
            links[5] = links[5] * not_first
            for n in range(6):
                coefs[n, plane, tile(y), :] = links[n] * scale
            relax[plane, tile(y), :] = scale
            forcing[plane, tile(y), :] = take(dens, plane, y) * (-GRAVITY * scale)
            rate[plane, tile(y), :] = PRESSURE_RATE * here
        return carry

    lax.fori_loop(1, long_y - 1, prepare, 0, unroll=2)

    for sweep in range(SWEEPS):
        old, new = (odd, even) if sweep % 2 else (even, odd)

        def one_row(y, carry, old=old, new=new):
            for plane in range(per):
                links = [coefs[n, plane, tile(y), :] for n in range(6)]
                scale = relax[plane, tile(y), :]
                pressure = take(old.at[3], plane, y)
                before = (
                    down_x(old.at[3], plane, y),
                    take(old.at[3], plane, y - 1),
                    down_z(pressure) * not_first,
                )
                changes = []
                for c in range(3):
                    field = old.at[c]
                    here = take(field, plane, y)
                    near = [
                        up_x(field, plane, y),
                        down_x(field, plane, y),
                        take(field, plane, y + 1),
                        take(field, plane, y - 1),
                        up_z(here),
                        down_z(here),
                    ]
                    terms = [link * other for link, other in zip(links, near)]
                    total = (terms[0] + terms[1]) + (terms[2] + terms[3])
                    total = total + (terms[4] + terms[5])
                    rest = (1.0 - RELAX) * here - scale * (pressure - before[c])
                    ahead = near[2 * c]
                    if c == 2:
                        rest = rest + forcing[plane, tile(y), :]
                        ahead = ahead * not_last
                    changes.append(ahead - here)
                    store(new.at[c], plane, y, total + rest)
                pressed = pressure - rate[plane, tile(y), :] * add_all(changes)
                store(new.at[3], plane, y, pressed)
            return carry

        lax.fori_loop(1 + sweep, long_y - 1 - sweep, one_row, 0, unroll=2)

    final = odd if SWEEPS % 2 else even
    outs = [vel_out.at[0], vel_out.at[1], vel_out.at[2], pres_out]
    sends = [
        pltpu.make_async_copy(results.at[n], out, done.at[n]) for n, out in enumerate(outs)
    ]
    for field, send in enumerate(sends):
        for i in range(size_x):
            for y in range(0, size_y, SUBLANES):
                plane, lines = place(i + width, y + width, SUBLANES)
                for half in range(halves):
                    results[
                        field, i, y : y + SUBLANES, half * LANES : (half + 1) * LANES
                    ] = final[field, plane, half, lines, :]
        send.start()
    for send in sends:
        send.wait()


def all_sweeps(velocity, pressure, cell_visc, cell_dens, low_x, high_x, low_y, high_y):
    size_x, size_y, size_z = cell_visc.shape
    width = low_x.shape[1]
    per, rows = (size_x + 2 * width) // SUBLANES, (size_y + 2 * width) * SUBLANES
    block = (per, rows, size_z)
    anywhere = pl.BlockSpec(memory_space=pl.ANY)
    in_hbm = pl.BlockSpec(memory_space=pltpu.HBM)
    return pl.pallas_call(
        sweep_body,
        out_shape=(
            jax.ShapeDtypeStruct(velocity.shape, f32),
            jax.ShapeDtypeStruct(pressure.shape, f32),
        ),
        in_specs=[in_hbm] * 4 + [anywhere] * 4,
        out_specs=(anywhere, anywhere),
        scratch_shapes=[
            pltpu.VMEM((6,) + cell_visc.shape, f32),
            pltpu.VMEM((2,) + low_x.shape, f32),
            pltpu.VMEM((2,) + low_y.shape, f32),
            pltpu.VMEM((4,) + cell_visc.shape, f32),
            pltpu.VMEM((4, per, size_z // LANES, rows, LANES), f32),
            pltpu.VMEM((4, per, size_z // LANES, rows, LANES), f32),
            pltpu.VMEM((2, per, size_z // LANES, rows, LANES), f32),
            pltpu.VMEM((6,) + block, f32),
            pltpu.VMEM(block, f32),
            pltpu.VMEM(block, f32),
            pltpu.VMEM(block, f32),
            pltpu.SemaphoreType.DMA((8,)),
        ],
        compiler_params=vmem_limit(44),
        cost_estimate=cost(20),
        name="all_sweeps",
    )(velocity, pressure, cell_visc, cell_dens, low_x, high_x, low_y, high_y)


def shift(value, axis, step):
    size = lax.axis_size(axis)
    pairs = [(i, i + step) for i in range(size) if 0 <= i + step < size]
    return lax.ppermute(value, axis, pairs)


def per_device(
    velocity,
    pressure,
    cell_visc,
    cell_dens,
    block_brick,
    block_counts,
    positions,
    start_visc,
    marker_dens,
):
    asked = lax.all_to_all(block_brick, "mark", 0, 0, tiled=True)
    fields = (velocity, pressure, cell_visc, cell_dens)
    to_low, to_high = pack_x(*fields)
    low_x, high_x = shift(to_high, "grid", 1), shift(to_low, "grid", -1)
    upward, downward = pack_y(*fields, low_x, high_x)
    low_y, high_y = shift(upward, "mark", 1), shift(downward, "mark", -1)

    picked = pick_bricks(asked, velocity)
    bricks = lax.all_to_all(picked, "mark", 0, 0, tiled=True)
    marker_visc, moments = marker_work(
        block_counts, positions, start_visc, marker_dens, bricks, upward
    )
    gathered = lax.all_to_all(moments, "mark", 0, 0, tiled=True)
    velocity_next, pressure_next = all_sweeps(*fields, low_x, high_x, low_y, high_y)
    visc_next, dens_next = settle(asked, gathered, cell_visc, cell_dens)
    return velocity_next, pressure_next, visc_next, dens_next, marker_visc


def solution(mesh):
    in_specs = (
        P(None, "grid", "mark", None),
        P("grid", "mark", None),
        P("grid", "mark", None),
        P("grid", "mark", None),
        P(("grid", "mark"), None),
        P(("grid", "mark"), None),
        P(("grid", "mark"), None, None, None),
        P(("grid", "mark"), None, None),
        P(("grid", "mark"), None, None),
    )
    out_specs = (
        P(None, "grid", "mark", None),
        P("grid", "mark", None),
        P("grid", "mark", None),
        P("grid", "mark", None),
        P(("grid", "mark"), None, None),
    )
    return jax.shard_map(
        per_device, mesh=mesh, in_specs=in_specs, out_specs=out_specs, check_vma=False
    )
```

```python
import functools

import jax
import jax.numpy as jnp
import numpy as np
from jax import lax
from jax.experimental import pallas as pl
from jax.experimental.pallas import tpu as pltpu
from jax.sharding import PartitionSpec as P

SWEEPS = 4
RELAX = 0.6
PRESSURE_RATE = 0.25
GRAVITY = 1.0
STRAIN_SCALE = 0.5

BX, BY, BZ = 4, 4, 8
PLANE = BX * BY
ROWS = 3 * PLANE
LANES = 128
GROUP = LANES // BZ
HALF = 8
SUBLANES = 8

f32, bf16 = jnp.float32, jnp.bfloat16


def vmem_limit(mib):
    return pltpu.CompilerParams(vmem_limit_bytes=mib * 1024 * 1024)


def cost(microseconds):
    return pl.CostEstimate(
        flops=int(microseconds * 1.15e9), bytes_accessed=0, transcendentals=0
    )


def place_of(brick):
    return lax.shift_right_logical(brick, GROUP.bit_length() - 1), (brick & (GROUP - 1)) * BZ


def pick_body(asked, vel, out, table):
    size_x, size_y, size_z = vel.shape[1:]
    bricks_y, halves = size_y // BY, size_z // LANES

    def repack(block_x, carry):
        for block_y in range(bricks_y):
            for half in range(halves):
                place = (block_x * bricks_y + block_y) * halves + half
                for c in range(3):
                    for i in range(BX):
                        row = (c * BX + i) * BY
                        table[place, row : row + BY, :] = vel[
                            c,
                            block_x * BX + i,
                            block_y * BY : (block_y + 1) * BY,
                            half * LANES : (half + 1) * LANES,
                        ]
        return carry

    lax.fori_loop(0, size_x // BX, repack, 0)
    groups = out.shape[1]
    lane_slot = lax.broadcasted_iota(jnp.int32, (ROWS, LANES), 1) // BZ

    def one_group(step, carry):
        device, group = step // groups, step % groups
        packed = jnp.zeros((ROWS, LANES), f32)
        for slot in range(GROUP):
            place, lane = place_of(asked[device, group * GROUP + slot])
            rolled = pltpu.roll(table[place], (BZ * slot - lane) & (LANES - 1), 1)
            packed = jnp.where(lane_slot == slot, rolled, packed)
        out[device, group] = packed
        return carry

    lax.fori_loop(0, out.shape[0] * groups, one_group, 0)


def pick_bricks(asked, velocity):
    devices, slots = asked.shape
    size_x, size_y, size_z = velocity.shape[1:]
    places = (size_x // BX) * (size_y // BY) * (size_z // LANES)
    return pl.pallas_call(
        pick_body,
        out_shape=jax.ShapeDtypeStruct((devices, slots // GROUP, ROWS, LANES), f32),
        in_specs=[
            pl.BlockSpec(memory_space=pltpu.SMEM),
            pl.BlockSpec(memory_space=pltpu.VMEM),
        ],
        out_specs=pl.BlockSpec(memory_space=pltpu.VMEM),
        scratch_shapes=[pltpu.VMEM((places, ROWS, LANES), f32)],
        compiler_params=vmem_limit(24),
        cost_estimate=cost(25),
        name="pick_bricks",
    )(asked, velocity)


def permutations():
    inside = BZ * HALF
    spread = np.zeros((2, 2, LANES, 4 * inside), np.float32)
    gather = np.zeros((2 * BY * inside, BY * LANES), np.float32)
    for half in range(2):
        for slot in range(HALF):
            for z in range(BZ):
                outer, inner = (half * HALF + slot) * BZ + z, z * HALF + slot
                for part in range(4):
                    spread[half, part // 2, outer, part * inside + inner] = 1
                for j in range(BY):
                    gather[(half * BY + j) * inside + inner, j * LANES + outer] = 1
    return jnp.asarray(spread, bf16), jnp.asarray(gather, bf16)


def split(value):
    high = value.astype(bf16)
    return high, (value - high.astype(f32)).astype(bf16)


def add_all(values):
    return functools.reduce(jnp.add, values)


def axis_weights(fraction, cells):
    middle = (cells - 1) / 2
    base = jnp.exp(fraction * (2.0 * cells) - float(cells))
    powers = [None, base]
    for i in range(2, cells):
        powers.append(powers[i // 2] * powers[i - i // 2])
    factors = [float(np.exp(middle**2 - (i - middle) ** 2)) for i in range(cells)]
    bells = [None] + [powers[i] * factors[i] for i in range(1, cells)]
    scale = 1.0 / (add_all(bells[1:]) + factors[0])
    weights = [scale * factors[0]] + [bell * scale for bell in bells[1:]]
    mean = add_all(
        [
            (weights[cells - 1 - i] - weights[i]) * (2.0 * (middle - i))
            for i in range(cells // 2)
        ]
    )
    slopes = [w * (2.0 * (i - middle) - mean) for i, w in enumerate(weights)]
    return weights, slopes


def dot(a, b):
    return jnp.dot(a, b, preferred_element_type=f32)


def gradients(products, weights, markers):
    weight_x, slope_x, weight_y, slope_y = ([weights[4 * n + i] for i in range(4)] for n in range(4))
    grads = []
    for c in range(3):
        lines = [[], [], []]
        for i in range(BX):
            rows = [((c * BX + i) * BY + j) * HALF for j in range(BY)]
            still = [products[row : row + HALF, :markers] for row in rows]
            rising = [products[row : row + HALF, markers:] for row in rows]
            lines[0].append(slope_x[i] * add_all([w * t for w, t in zip(weight_y, still)]))
            lines[1].append(weight_x[i] * add_all([w * t for w, t in zip(slope_y, still)]))
            lines[2].append(weight_x[i] * add_all([w * t for w, t in zip(weight_y, rising)]))
        grads.append([add_all(line) for line in lines])
    return grads


def own_lanes():
    shape = (HALF, 4 * BZ * HALF)
    lane = lax.broadcasted_iota(jnp.int32, shape, 1)
    return (lane % HALF == lax.broadcasted_iota(jnp.int32, shape, 0)).astype(f32)


def marker_groups(groups, counts, ins, outs, buffers, sums):
    spread, gather, places, start, dens, brick = ins
    visc_out, moments_out = outs
    permuted, left, right, products, weights, factors, planes_high, planes_low = buffers
    markers = places.shape[-1]
    inside = BZ * HALF
    own = own_lanes()
    halves = [
        (owner, 2 * group + half, half, 2 * n + half)
        for n, (owner, group) in enumerate(groups)
        for half in range(2)
    ]
    parts = [split(brick[owner, group]) for owner, group in groups]
    for _, _, half, n in halves:
        high, low = parts[n // 2]
        permuted[n][...] = dot(high, spread[half, 0]) + dot(low, spread[half, 1])
    heights = []
    for owner, part, _, n in halves:
        weight_z, slope_z = axis_weights(places[owner, 2, part], BZ)
        heights.append(weight_z)
        for z in range(0, BZ, 2):
            for column, values in ((0, weight_z), (1, slope_z)):
                high, low = split(jnp.concatenate(values[z : z + 2], axis=0))
                columns = slice(column * markers, (column + 1) * markers)
                for k in range(4):
                    begin = k * inside + z * HALF
                    right[n][begin : begin + 2 * HALF, columns] = low if k % 2 else high
    for _, _, _, n in halves:
        for row in range(0, ROWS, 2):
            pair = [
                jnp.broadcast_to(permuted[n][r : r + 1, :], own.shape) * own for r in (row, row + 1)
            ]
            left[n][row * HALF : (row + 2) * HALF, :] = jnp.concatenate(pair, axis=0).astype(bf16)
    for _, _, _, n in halves:
        products[n][...] = dot(left[n][...], right[n][...])
    for owner, part, _, n in halves:
        weights_x = axis_weights(places[owner, 0, part], BX)
        weights_y = axis_weights(places[owner, 1, part], BY)
        for k, values in enumerate((*weights_x, *weights_y)):
            for i, value in enumerate(values):
                weights[n][4 * k + i] = value
        for j in range(BY):
            for z in range(0, BZ, 2):
                pair = [weights_y[0][j] * heights[n][z + k] for k in range(2)]
                rows = slice((j * BZ + z) * HALF, (j * BZ + z + 2) * HALF)
                high, low = split(jnp.concatenate(pair, axis=0))
                planes_high[n][rows, :] = high
                planes_low[n][rows, :] = low

    count = 3 * BX * HALF
    for owner, part, _, n in halves:
        grads = gradients(products[n], weights[n], markers)
        normal = grads[0][0] ** 2 + grads[1][1] ** 2 + grads[2][2] ** 2
        shear_xy = 0.5 * (grads[0][1] + grads[1][0])
        shear_xz = 0.5 * (grads[0][2] + grads[2][0])
        shear_yz = 0.5 * (grads[1][2] + grads[2][1])
        invariant = 0.5 * normal + shear_xy**2 + shear_xz**2 + shear_yz**2
        scaled = invariant * (1.0 / (STRAIN_SCALE * STRAIN_SCALE))
        third = jnp.log(1.0 + scaled) * (1.0 / 3.0)
        first = start[owner, part]
        slot = lax.broadcasted_iota(jnp.int32, first.shape, 0) + part * HALF
        live = slot < counts[0, owner]
        visc_out[owner, part] = jnp.where(live, first * jnp.exp(-third), 0.0)
        carried = (
            live.astype(f32),
            jnp.where(live, jnp.log(first) - third, 0.0),
            jnp.where(live, dens[owner, part], 0.0),
        )
        for c in range(3):
            for i in range(0, BX, 2):
                pair = [carried[c] * weights[n][i + k] for k in range(2)]
                row = (c * BX + i) * HALF
                high, low = split(jnp.concatenate(pair, axis=0))
                factors[n][row : row + 2 * HALF, :] = high
                factors[n][count + row : count + row + 2 * HALF, :] = low

    contract = (((1,), (1,)), ((), ()))
    found = []
    for _, _, _, n in halves:
        both = lax.dot_general(
            factors[n][...], planes_high[n][...], contract, preferred_element_type=f32
        )
        rest = lax.dot_general(
            factors[n][:count], planes_low[n][...], contract, preferred_element_type=f32
        )
        found.append((both, rest))
    for _, _, half, n in halves:
        both, rest = found[n]
        total = both[:count] + both[count:] + rest
        chosen = total.reshape(3 * BX, HALF, BY * inside) * own[None]
        high, low = split(jnp.sum(chosen, axis=1))
        columns = slice(half * BY * inside, (half + 1) * BY * inside)
        row = (n // 2) * 32
        sums[row : row + 3 * BX, columns] = high.astype(f32)
        sums[row + 16 : row + 16 + 3 * BX, columns] = low.astype(f32)
    moved = dot(sums[...].astype(bf16), gather[...])
    for n, (owner, group) in enumerate(groups):
        mine = moved[32 * n : 32 * n + 3 * BX] + moved[32 * n + 16 : 32 * n + 16 + 3 * BX]
        for j in range(BY):
            rows = pl.ds(j, 3 * BX, stride=BY)
            moments_out[owner, group, rows, :] = mine[:, j * LANES : (j + 1) * LANES]


TOGETHER = 2


def marker_body(counts, *refs):
    ins, outs, scratch = refs[:6], refs[7:9], refs[9:]
    listed, sums, *flat = scratch
    held = 2 * TOGETHER
    buffers = [flat[n * held : (n + 1) * held] for n in range(len(flat) // held)]
    visc_out, moments_out = outs
    owners, groups = moments_out.shape[:2]
    visc_out[...] = jnp.zeros_like(visc_out)
    moments_out[...] = jnp.zeros_like(moments_out)
    sums[...] = jnp.zeros_like(sums)

    def list_groups(index, number):
        owner, group = index // groups, index % groups
        live = group * GROUP < counts[0, owner]

        @pl.when(live)
        def _():
            for n in range(TOGETHER):
                listed[2 * (number + n)] = owner
                listed[2 * (number + n) + 1] = group

        return jnp.where(live, number + 1, number)

    number = lax.fori_loop(0, owners * groups, list_groups, 0)

    def step(index, carry):
        first = TOGETHER * index
        taken = [
            (listed[2 * (first + n)], listed[2 * (first + n) + 1]) for n in range(TOGETHER)
        ]
        marker_groups(taken, counts, ins, outs, buffers, sums)
        return carry

    lax.fori_loop(0, (number + TOGETHER - 1) // TOGETHER, step, 0)


def marker_work(counts, positions, start_visc, marker_dens, bricks, after):
    owners, _, slots, markers = positions.shape
    groups, parts = slots // GROUP, slots // HALF
    spread, gather = permutations()
    width = 4 * BZ * HALF
    whole = pl.BlockSpec(memory_space=pltpu.VMEM)
    buffers = (
        pltpu.VMEM((ROWS, width), f32),
        pltpu.VMEM((ROWS * HALF, width), bf16),
        pltpu.VMEM((width, 2 * markers), bf16),
        pltpu.VMEM((ROWS * HALF, 2 * markers), f32),
        pltpu.VMEM((4 * 4, HALF, markers), f32),
        pltpu.VMEM((2 * 3 * BX * HALF, markers), bf16),
        pltpu.VMEM((BY * BZ * HALF, markers), bf16),
        pltpu.VMEM((BY * BZ * HALF, markers), bf16),
    )
    visc, moments = pl.pallas_call(
        marker_body,
        out_shape=(
            jax.ShapeDtypeStruct((owners, parts, HALF, markers), f32),
            jax.ShapeDtypeStruct((owners, groups, ROWS, LANES), f32),
        ),
        in_specs=[pl.BlockSpec(memory_space=pltpu.SMEM)]
        + [whole] * 6
        + [pl.BlockSpec(memory_space=pl.ANY)],
        out_specs=(whole, whole),
        scratch_shapes=[
            pltpu.SMEM((2 * (owners * groups + TOGETHER),), jnp.int32),
            pltpu.VMEM((32 * TOGETHER, 2 * BY * BZ * HALF), f32),
        ]
        + [buffer for buffer in buffers for _ in range(2 * TOGETHER)],
        compiler_params=vmem_limit(32),
        cost_estimate=cost(25),
        name="marker_work",
    )(
        counts,
        spread,
        gather,
        positions.reshape(owners, 3, parts, HALF, markers),
        start_visc.reshape(owners, parts, HALF, markers),
        marker_dens.reshape(owners, parts, HALF, markers),
        bricks,
        after,
    )
    return visc.reshape(owners, slots, markers), moments


def settle_body(asked, moments_in, visc_in, dens_in, visc_out, dens_out, *scratch):
    moments, visc, dens, done, *tables = scratch
    size_x, size_y, size_z = visc.shape
    copies = [
        pltpu.make_async_copy(there, here, done.at[n])
        for n, (there, here) in enumerate(
            ((moments_in, moments), (visc_in, visc), (dens_in, dens))
        )
    ]
    for copy in copies:
        copy.start()
    bricks_y, halves = size_y // BY, size_z // LANES
    for table in tables:
        table[...] = jnp.zeros_like(table)
    copies[0].wait()
    groups = moments.shape[1]
    lane_slot = lax.broadcasted_iota(jnp.int32, (ROWS, LANES), 1) // BZ

    def one_group(step, carry):
        device, group = step // groups, step % groups
        packed = moments[device, group]
        for slot in range(GROUP):
            table = tables[slot % len(tables)]
            place, lane = place_of(asked[device, group * GROUP + slot])
            piece = jnp.where(lane_slot == slot, packed, 0.0)
            piece = pltpu.roll(piece, (lane - BZ * slot) & (LANES - 1), 1)
            table[place] = table[place] + piece
        return carry

    lax.fori_loop(0, moments.shape[0] * groups, one_group, 0)
    copies[1].wait()
    copies[2].wait()

    def finish(block_x, carry):
        for block_y in range(0, bricks_y, 2):
            for half in range(halves):
                for i in range(BX):
                    here = (
                        block_x * BX + i,
                        slice(block_y * BY, (block_y + 2) * BY),
                        slice(half * LANES, (half + 1) * LANES),
                    )
                    sums = []
                    for c in range(3):
                        rows = slice((c * BX + i) * BY, (c * BX + i + 1) * BY)
                        places = [
                            (block_x * bricks_y + block_y + k) * halves + half for k in range(2)
                        ]
                        sums.append(
                            jnp.concatenate(
                                [add_all([t[place, rows, :] for t in tables]) for place in places]
                            )
                        )
                    scale = 1.0 / (sums[0] + 1.0)
                    visc_out[here] = jnp.exp((sums[1] + jnp.log(visc[here])) * scale)
                    dens_out[here] = (sums[2] + dens[here]) * scale
        return carry

    lax.fori_loop(0, size_x // BX, finish, 0)


def settle(asked, moments, cell_visc, cell_dens):
    size_x, size_y, size_z = cell_visc.shape
    places = (size_x // BX) * (size_y // BY) * (size_z // LANES)
    whole = pl.BlockSpec(memory_space=pltpu.VMEM)
    shape = jax.ShapeDtypeStruct(cell_visc.shape, f32)
    return pl.pallas_call(
        settle_body,
        out_shape=(shape, shape),
        in_specs=[pl.BlockSpec(memory_space=pltpu.SMEM)]
        + [pl.BlockSpec(memory_space=pl.ANY)] * 3,
        out_specs=(whole, whole),
        scratch_shapes=[
            pltpu.VMEM(moments.shape, f32),
            pltpu.VMEM(cell_visc.shape, f32),
            pltpu.VMEM(cell_visc.shape, f32),
            pltpu.SemaphoreType.DMA((3,)),
        ]
        + [pltpu.VMEM((places, ROWS, LANES), f32)] * 2,
        compiler_params=vmem_limit(24),
        cost_estimate=cost(7),
        name="settle",
    )(asked, moments, cell_visc, cell_dens)


def field_of(fields, index):
    return fields[0].at[index] if index < 3 else fields[index - 2]


def pack_x_body(*refs):
    ends, outs = refs[:8], refs[8:]
    for side in range(2):
        for f in range(6):
            outs[side][f] = field_of(ends[side::2], f)[...]


def pack_x(velocity, pressure, cell_visc, cell_dens):
    size_x, size_y, size_z = cell_visc.shape
    width = SWEEPS
    ends = (0, size_x // width - 1)
    vel = [
        pl.BlockSpec((3, width, size_y, size_z), lambda i, e=e: (0, e, 0, 0)) for e in ends
    ]
    block = [pl.BlockSpec((width, size_y, size_z), lambda i, e=e: (e, 0, 0)) for e in ends]
    whole = pl.BlockSpec((6, width, size_y, size_z), lambda i: (0, 0, 0, 0))
    shape = jax.ShapeDtypeStruct((6, width, size_y, size_z), f32)
    return pl.pallas_call(
        pack_x_body,
        grid=(1,),
        out_shape=(shape, shape),
        in_specs=vel + block * 3,
        out_specs=(whole, whole),
        compiler_params=vmem_limit(60),
        cost_estimate=cost(2),
        name="pack_x",
    )(velocity, velocity, pressure, pressure, cell_visc, cell_visc, cell_dens, cell_dens)


def corner_rows(upward, size_x):
    width = SWEEPS
    spare = (5 * width,) if upward else (4 * width - 1, 6 * width - 1)
    places = [(plane, row) for plane in range(size_x) for row in spare]
    found = []
    for field in range(6):
        for side in range(2):
            near = field == 5 or (field == 3 and side == 1 and not upward)
            reach = width - 1 if near else width
            for far_x in range(1, width):
                for far_y in range(1, reach - far_x + 1):
                    found.append((field, side, far_x, far_y))
    more = max(0, len(found) - len(places))
    places += [(size_x + n // (6 * width), n % (6 * width)) for n in range(more)]
    return [cell + at for cell, at in zip(found, places)], size_x + -(-more // (6 * width))


def pack_y_body(size_x, vel, pres, visc, dens, low_x, high_x, upward, downward):
    step_x, size_y, _ = pres.shape
    width = SWEEPS
    step = pl.program_id(0)
    planes = pl.ds(pl.multiple_of(step * step_x, step_x), step_x)
    for f in range(6):
        field = field_of((vel, pres, visc, dens), f)
        rows = slice(f * width, (f + 1) * width)
        upward[planes, rows, :] = field[:, size_y - width :, :]
        downward[planes, rows, :] = field[:, :width, :]

    @pl.when(step == pl.num_programs(0) - 1)
    def _():
        for up, face in ((True, upward), (False, downward)):
            for f, side, far_x, far_y, plane, row in corner_rows(up, size_x)[0]:
                halo, at = (high_x, far_x - 1) if side else (low_x, width - far_x)
                face[plane, row] = halo[f, at, size_y - far_y if up else far_y - 1]


def pack_y(velocity, pressure, cell_visc, cell_dens, low_x, high_x):
    size_x, size_y, size_z = cell_visc.shape
    step = 8
    block = pl.BlockSpec((step, size_y, size_z), lambda i: (i, 0, 0))
    halo = pl.BlockSpec(low_x.shape, lambda i: (0, 0, 0, 0))
    shapes = [(corner_rows(up, size_x)[1], 6 * SWEEPS, size_z) for up in (True, False)]
    return pl.pallas_call(
        functools.partial(pack_y_body, size_x),
        grid=(size_x // step,),
        out_shape=tuple(jax.ShapeDtypeStruct(shape, f32) for shape in shapes),
        in_specs=[
            pl.BlockSpec((3, step, size_y, size_z), lambda i: (0, i, 0, 0)),
            block,
            block,
            block,
            halo,
            halo,
        ],
        out_specs=tuple(pl.BlockSpec(shape, lambda i: (0, 0, 0)) for shape in shapes),
        compiler_params=vmem_limit(24),
        cost_estimate=cost(15),
        name="pack_y",
    )(velocity, pressure, cell_visc, cell_dens, low_x, high_x)


def place(per, x, y, rows):
    return x % per, pl.ds(y * SUBLANES + x // per, rows, stride=SUBLANES)


def put(target, x, y, rows, value):
    per, halves = target.shape[:2]
    plane, lines = place(per, x, y, rows)
    for half in range(halves):
        target[plane, half, lines, :] = value[:, half * LANES : (half + 1) * LANES]


def tile(y):
    if isinstance(y, int):
        return pl.ds(y * SUBLANES, SUBLANES)
    return pl.ds(pl.multiple_of(y * SUBLANES, SUBLANES), SUBLANES)


def row_work(cells, coefs, relax, forcing, rate):
    per, halves = cells.shape[1:3]
    size_z = halves * LANES
    lane = lax.broadcasted_iota(jnp.int32, (SUBLANES, size_z), 1)
    not_last = (lane < size_z - 1).astype(f32)
    not_first = (lane > 0).astype(f32)

    def take(field, plane, y):
        return jnp.concatenate([field[plane, half, tile(y), :] for half in range(halves)], axis=1)

    def store(field, plane, y, value):
        for half in range(halves):
            field[plane, half, tile(y), :] = value[:, half * LANES : (half + 1) * LANES]

    def up_x(field, plane, y):
        if plane < per - 1:
            return take(field, plane + 1, y)
        return pltpu.roll(take(field, 0, y), SUBLANES - 1, 0)

    def down_x(field, plane, y):
        if plane > 0:
            return take(field, plane - 1, y)
        return pltpu.roll(take(field, per - 1, y), 1, 0)

    def up_z(a):
        return pltpu.roll(a, size_z - 1, 1)

    def down_z(a):
        return pltpu.roll(a, 1, 1)

    def prepare(y):
        visc, dens = cells.at[0], cells.at[1]
        for plane in range(per):
            here = take(visc, plane, y)
            near = [
                up_x(visc, plane, y),
                down_x(visc, plane, y),
                take(visc, plane, y + 1),
                take(visc, plane, y - 1),
                up_z(here) * not_last,
                down_z(here) * not_first,
            ]
            links = [0.5 * (here + other) for other in near]
            scale = jnp.where(here > 0.0, RELAX / add_all(links), 0.0)
            links[4] = links[4] * not_last
            links[5] = links[5] * not_first
            for n in range(6):
                coefs[n, plane, tile(y), :] = links[n] * scale
            relax[plane, tile(y), :] = scale
            forcing[plane, tile(y), :] = take(dens, plane, y) * (-GRAVITY * scale)
            rate[plane, tile(y), :] = PRESSURE_RATE * here

    def sweep(y, old, new):
        for plane in range(per):
            links = [coefs[n, plane, tile(y), :] for n in range(6)]
            scale = relax[plane, tile(y), :]
            pressure = take(old.at[3], plane, y)
            before = (
                down_x(old.at[3], plane, y),
                take(old.at[3], plane, y - 1),
                down_z(pressure) * not_first,
            )
            changes = []
            for c in range(3):
                field = old.at[c]
                here = take(field, plane, y)
                near = [
                    up_x(field, plane, y),
                    down_x(field, plane, y),
                    take(field, plane, y + 1),
                    take(field, plane, y - 1),
                    up_z(here),
                    down_z(here),
                ]
                terms = [link * other for link, other in zip(links, near)]
                total = (terms[0] + terms[1]) + (terms[2] + terms[3])
                total = total + (terms[4] + terms[5])
                rest = (1.0 - RELAX) * here - scale * (pressure - before[c])
                ahead = near[2 * c]
                if c == 2:
                    rest = rest + forcing[plane, tile(y), :]
                    ahead = ahead * not_last
                changes.append(ahead - here)
                store(new.at[c], plane, y, total + rest)
            pressed = pressure - rate[plane, tile(y), :] * add_all(changes)
            store(new.at[3], plane, y, pressed)

    return prepare, sweep


def kept_rows(size_y):
    width = SWEEPS
    return (
        ((width, size_y),),
        ((width + 1, width), (size_y - 1, width)),
        ((width, width + 1), (size_y - 1, width + 1)),
    )


def kept_copies(pairs, size_y, done):
    copies = []
    for (source, target), strips in zip(pairs, kept_rows(size_y)):
        for begin, rows in strips:
            span = (slice(None),) * 3 + (pl.ds(begin * SUBLANES, rows * SUBLANES),)
            copies.append(
                pltpu.make_async_copy(source.at[span], target.at[span], done.at[len(copies)])
            )
    return copies


def inner_body(vel, pres, visc, dens, low_x, high_x, _, even_out, odd_out, cells_out, *work):
    blocks, sides_x, even, odd, cells, coefs, relax, forcing, rate, done = work
    size_x, size_y, size_z = blocks.shape[1:]
    width = SWEEPS
    inputs = (
        (visc, blocks.at[4], (4,)),
        (vel, blocks.at[0:3], (0, 1, 2)),
        (pres, blocks.at[3], (3,)),
        (dens, blocks.at[5], (5,)),
        (low_x, sides_x.at[0], ()),
        (high_x, sides_x.at[1], ()),
    )
    copies = [
        pltpu.make_async_copy(there, here, done.at[n]) for n, (there, here, _) in enumerate(inputs)
    ]
    for copy in copies:
        copy.start()
    targets = [even.at[n] for n in range(4)] + [cells.at[n] for n in range(2)]
    for copy, (_, _, held) in zip(copies, inputs):
        copy.wait()
        for f in held:
            for i in range(size_x):
                for y in range(0, size_y, SUBLANES):
                    value = blocks[f, i, y : y + SUBLANES, :]
                    put(targets[f], i + width, y + width, SUBLANES, value)
    for side, begin in enumerate((0, width + size_x)):
        for f in range(6):
            for i in range(width):
                for y in range(0, size_y, SUBLANES):
                    value = sides_x[side, f, i, y : y + SUBLANES, :]
                    put(targets[f], begin + i, y + width, SUBLANES, value)

    prepare, sweep = row_work(cells, coefs, relax, forcing, rate)

    def prepare_row(y, carry):
        prepare(y)
        return carry

    first, last = width + 1, width + size_y - 1
    lax.fori_loop(first, last, prepare_row, 0, unroll=2)
    for step in range(SWEEPS):
        old, new = (odd, even) if step % 2 else (even, odd)

        def sweep_row(y, carry, old=old, new=new):
            sweep(y, old, new)
            return carry

        lax.fori_loop(first + step, last - step, sweep_row, 0, unroll=2)
    sends = kept_copies(((even, even_out), (odd, odd_out), (cells, cells_out)), size_y, done)
    for send in sends:
        send.start()
    for send in sends:
        send.wait()


def inner_sweeps(velocity, pressure, cell_visc, cell_dens, low_x, high_x, after):
    size_x, size_y, size_z = cell_visc.shape
    width = low_x.shape[1]
    per, rows = (size_x + 2 * width) // SUBLANES, (size_y + 2 * width) * SUBLANES
    block, cut = (per, rows, size_z), (per, size_z // LANES, rows, LANES)
    shapes = [(4,) + cut, (4,) + cut, (2,) + cut]
    anywhere = pl.BlockSpec(memory_space=pl.ANY)
    return pl.pallas_call(
        inner_body,
        out_shape=tuple(jax.ShapeDtypeStruct(shape, f32) for shape in shapes),
        in_specs=[anywhere] * 7,
        out_specs=(anywhere,) * 3,
        scratch_shapes=[
            pltpu.VMEM((6,) + cell_visc.shape, f32),
            pltpu.VMEM((2,) + low_x.shape, f32),
        ]
        + [pltpu.VMEM(shape, f32) for shape in shapes]
        + [
            pltpu.VMEM((6,) + block, f32),
            pltpu.VMEM(block, f32),
            pltpu.VMEM(block, f32),
            pltpu.VMEM(block, f32),
            pltpu.SemaphoreType.DMA((6,)),
        ],
        compiler_params=vmem_limit(40),
        cost_estimate=cost(25),
        name="inner_sweeps",
    )(velocity, pressure, cell_visc, cell_dens, low_x, high_x, after)


def edge_body(even_in, odd_in, cells_in, low_y, high_y, vel_out, pres_out, *work):
    from_low, from_high, results, even, odd, cells, coefs, relax, forcing, rate, done, more = work
    size_x, size_y, size_z = results.shape[1:]
    width = SWEEPS
    long_y = size_y + 2 * width
    halos = [
        pltpu.make_async_copy(low_y, from_low, more.at[0]),
        pltpu.make_async_copy(high_y, from_high, more.at[1]),
    ]
    kept = kept_copies(((even_in, even), (odd_in, odd), (cells_in, cells)), size_y, done)
    for copy in (*halos, *kept[3:], *kept[:3]):
        copy.start()
    targets = [even.at[n] for n in range(4)] + [cells.at[n] for n in range(2)]
    for target in targets:
        for x in (*range(width), *range(width + size_x, size_x + 2 * width)):
            for y in (0, width + size_y):
                put(target, x, y, width, jnp.zeros((width, size_z), f32))
    for up, halo, copy, begin in (
        (True, from_low, halos[0], 0),
        (False, from_high, halos[1], width + size_y),
    ):
        copy.wait()
        for f, target in enumerate(targets):
            rows = slice(f * width, (f + 1) * width)
            for i in range(size_x):
                put(target, i + width, begin, width, halo[i, rows, :])
        for f, side, far_x, far_y, plane, row in corner_rows(up, size_x)[0]:
            x = width + size_x - 1 + far_x if side else width - far_x
            y = width - far_y if up else width + size_y - 1 + far_y
            put(targets[f], x, y, 1, halo[plane, row : row + 1, :])
    for copy in kept:
        copy.wait()

    prepare, sweep = row_work(cells, coefs, relax, forcing, rate)

    def prepare_rows(n, carry):
        prepare(1 + n)
        prepare(long_y - 2 * width + n)
        return carry

    lax.fori_loop(0, 2 * width - 1, prepare_rows, 0)
    for step in range(SWEEPS):
        old, new = (odd, even) if step % 2 else (even, odd)

        def sweep_rows(n, carry, old=old, new=new, step=step):
            sweep(1 + step + n, old, new)
            sweep(width + size_y - 1 - step + n, old, new)
            return carry

        lax.fori_loop(0, width, sweep_rows, 0)

    final = odd if SWEEPS % 2 else even
    outs = [vel_out.at[0], vel_out.at[1], vel_out.at[2], pres_out]
    sends = [pltpu.make_async_copy(results.at[n], out, done.at[n]) for n, out in enumerate(outs)]
    per, halves = even.shape[1:3]
    for field, send in enumerate(sends):
        for i in range(size_x):
            for y in range(0, size_y, SUBLANES):
                plane, lines = place(per, i + width, y + width, SUBLANES)
                for half in range(halves):
                    columns = slice(half * LANES, (half + 1) * LANES)
                    results[field, i, y : y + SUBLANES, columns] = final[
                        field, plane, half, lines, :
                    ]
        send.start()
    for send in sends:
        send.wait()


def edge_sweeps(even, odd, cells, low_y, high_y, size_x, size_y):
    per, halves, rows = even.shape[1:4]
    size_z = halves * LANES
    block = (per, rows, size_z)
    anywhere = pl.BlockSpec(memory_space=pl.ANY)
    return pl.pallas_call(
        edge_body,
        out_shape=(
            jax.ShapeDtypeStruct((3, size_x, size_y, size_z), f32),
            jax.ShapeDtypeStruct((size_x, size_y, size_z), f32),
        ),
        in_specs=[anywhere] * 5,
        out_specs=(anywhere,) * 2,
        scratch_shapes=[
            pltpu.VMEM(low_y.shape, f32),
            pltpu.VMEM(high_y.shape, f32),
            pltpu.VMEM((4, size_x, size_y, size_z), f32),
            pltpu.VMEM(even.shape, f32),
            pltpu.VMEM(odd.shape, f32),
            pltpu.VMEM(cells.shape, f32),
            pltpu.VMEM((6,) + block, f32),
            pltpu.VMEM(block, f32),
            pltpu.VMEM(block, f32),
            pltpu.VMEM(block, f32),
            pltpu.SemaphoreType.DMA((5,)),
            pltpu.SemaphoreType.DMA((2,)),
        ],
        compiler_params=vmem_limit(40),
        cost_estimate=cost(1),
        name="edge_sweeps",
    )(even, odd, cells, low_y, high_y)


def shift(value, axis, step):
    size = lax.axis_size(axis)
    pairs = [(i, i + step) for i in range(size) if 0 <= i + step < size]
    return lax.ppermute(value, axis, pairs)


def per_device(
    velocity,
    pressure,
    cell_visc,
    cell_dens,
    block_brick,
    block_counts,
    positions,
    start_visc,
    marker_dens,
):
    asked = lax.all_to_all(block_brick, "mark", 0, 0, tiled=True)
    fields = (velocity, pressure, cell_visc, cell_dens)
    to_low, to_high = pack_x(*fields)
    low_x, high_x = shift(to_high, "grid", 1), shift(to_low, "grid", -1)
    upward, downward = pack_y(*fields, low_x, high_x)
    low_y, high_y = shift(upward, "mark", 1), shift(downward, "mark", -1)

    picked = pick_bricks(asked, velocity)
    bricks = lax.all_to_all(picked, "mark", 0, 0, tiled=True)
    marker_visc, moments = marker_work(
        block_counts, positions, start_visc, marker_dens, bricks, upward
    )
    gathered = lax.all_to_all(moments, "mark", 0, 0, tiled=True)
    state = inner_sweeps(*fields, low_x, high_x, moments)
    velocity_next, pressure_next = edge_sweeps(*state, low_y, high_y, *pressure.shape[:2])
    visc_next, dens_next = settle(asked, gathered, cell_visc, cell_dens)
    return velocity_next, pressure_next, visc_next, dens_next, marker_visc


def solution(mesh):
    in_specs = (
        P(None, "grid", "mark", None),
        P("grid", "mark", None),
        P("grid", "mark", None),
        P("grid", "mark", None),
        P(("grid", "mark"), None),
        P(("grid", "mark"), None),
        P(("grid", "mark"), None, None, None),
        P(("grid", "mark"), None, None),
        P(("grid", "mark"), None, None),
    )
    out_specs = (
        P(None, "grid", "mark", None),
        P("grid", "mark", None),
        P("grid", "mark", None),
        P("grid", "mark", None),
        P(("grid", "mark"), None, None),
    )
    return jax.shard_map(
        per_device, mesh=mesh, in_specs=in_specs, out_specs=out_specs, check_vma=False
    )
```

```python
import functools

import jax
import jax.numpy as jnp
import numpy as np
from jax import lax
from jax.experimental import pallas as pl
from jax.experimental.pallas import tpu as pltpu
from jax.sharding import PartitionSpec as P

SWEEPS = 4
RELAX = 0.6
PRESSURE_RATE = 0.25
GRAVITY = 1.0
STRAIN_SCALE = 0.5

BX, BY, BZ = 4, 4, 8
PLANE = BX * BY
ROWS = 3 * PLANE
LANES = 128
GROUP = LANES // BZ
HALF = 8
SUBLANES = 8

f32, bf16 = jnp.float32, jnp.bfloat16


def vmem_limit(mib):
    return pltpu.CompilerParams(vmem_limit_bytes=mib * 1024 * 1024)


def cost(microseconds):
    return pl.CostEstimate(
        flops=int(microseconds * 1.15e9), bytes_accessed=0, transcendentals=0
    )


def place_of(brick):
    return lax.shift_right_logical(brick, GROUP.bit_length() - 1), (brick & (GROUP - 1)) * BZ


def pick_body(asked, vel, out, table):
    size_x, size_y, size_z = vel.shape[1:]
    bricks_y, halves = size_y // BY, size_z // LANES

    def repack(block_x, carry):
        for block_y in range(bricks_y):
            for half in range(halves):
                place = (block_x * bricks_y + block_y) * halves + half
                for c in range(3):
                    for i in range(BX):
                        row = (c * BX + i) * BY
                        table[place, row : row + BY, :] = vel[
                            c,
                            block_x * BX + i,
                            block_y * BY : (block_y + 1) * BY,
                            half * LANES : (half + 1) * LANES,
                        ]
        return carry

    lax.fori_loop(0, size_x // BX, repack, 0)
    groups = out.shape[1]
    lane_slot = lax.broadcasted_iota(jnp.int32, (ROWS, LANES), 1) // BZ

    def one_group(step, carry):
        device, group = step // groups, step % groups
        packed = jnp.zeros((ROWS, LANES), f32)
        for slot in range(GROUP):
            place, lane = place_of(asked[device, group * GROUP + slot])
            rolled = pltpu.roll(table[place], (BZ * slot - lane) & (LANES - 1), 1)
            packed = jnp.where(lane_slot == slot, rolled, packed)
        out[device, group] = packed
        return carry

    lax.fori_loop(0, out.shape[0] * groups, one_group, 0)


def pick_bricks(asked, velocity):
    devices, slots = asked.shape
    size_x, size_y, size_z = velocity.shape[1:]
    places = (size_x // BX) * (size_y // BY) * (size_z // LANES)
    return pl.pallas_call(
        pick_body,
        out_shape=jax.ShapeDtypeStruct((devices, slots // GROUP, ROWS, LANES), f32),
        in_specs=[
            pl.BlockSpec(memory_space=pltpu.SMEM),
            pl.BlockSpec(memory_space=pltpu.VMEM),
        ],
        out_specs=pl.BlockSpec(memory_space=pltpu.VMEM),
        scratch_shapes=[pltpu.VMEM((places, ROWS, LANES), f32)],
        compiler_params=vmem_limit(24),
        cost_estimate=cost(25),
        name="pick_bricks",
    )(asked, velocity)


def permutations():
    inside = BZ * HALF
    spread = np.zeros((2, 2, LANES, 4 * inside), np.float32)
    gather = np.zeros((2 * BY * inside, BY * LANES), np.float32)
    for half in range(2):
        for slot in range(HALF):
            for z in range(BZ):
                outer, inner = (half * HALF + slot) * BZ + z, z * HALF + slot
                for part in range(4):
                    spread[half, part // 2, outer, part * inside + inner] = 1
                for j in range(BY):
                    gather[(half * BY + j) * inside + inner, j * LANES + outer] = 1
    return jnp.asarray(spread, bf16), jnp.asarray(gather, bf16)


def split(value):
    high = value.astype(bf16)
    return high, (value - high.astype(f32)).astype(bf16)


def add_all(values):
    return functools.reduce(jnp.add, values)


def axis_weights(fraction, cells):
    middle = (cells - 1) / 2
    base = jnp.exp(fraction * (2.0 * cells) - float(cells))
    powers = [None, base]
    for i in range(2, cells):
        powers.append(powers[i // 2] * powers[i - i // 2])
    factors = [float(np.exp(middle**2 - (i - middle) ** 2)) for i in range(cells)]
    bells = [None] + [powers[i] * factors[i] for i in range(1, cells)]
    scale = 1.0 / (add_all(bells[1:]) + factors[0])
    weights = [scale * factors[0]] + [bell * scale for bell in bells[1:]]
    mean = add_all(
        [
            (weights[cells - 1 - i] - weights[i]) * (2.0 * (middle - i))
            for i in range(cells // 2)
        ]
    )
    slopes = [w * (2.0 * (i - middle) - mean) for i, w in enumerate(weights)]
    return weights, slopes


def dot(a, b):
    return jnp.dot(a, b, preferred_element_type=f32)


def gradients(products, weights, markers):
    weight_x, slope_x, weight_y, slope_y = ([weights[4 * n + i] for i in range(4)] for n in range(4))
    grads = []
    for c in range(3):
        lines = [[], [], []]
        for i in range(BX):
            rows = [((c * BX + i) * BY + j) * HALF for j in range(BY)]
            still = [products[row : row + HALF, :markers] for row in rows]
            rising = [products[row : row + HALF, markers:] for row in rows]
            lines[0].append(slope_x[i] * add_all([w * t for w, t in zip(weight_y, still)]))
            lines[1].append(weight_x[i] * add_all([w * t for w, t in zip(slope_y, still)]))
            lines[2].append(weight_x[i] * add_all([w * t for w, t in zip(weight_y, rising)]))
        grads.append([add_all(line) for line in lines])
    return grads


def own_lanes():
    shape = (HALF, 4 * BZ * HALF)
    lane = lax.broadcasted_iota(jnp.int32, shape, 1)
    return (lane % HALF == lax.broadcasted_iota(jnp.int32, shape, 0)).astype(f32)


def marker_groups(groups, counts, ins, outs, buffers, sums):
    spread, gather, places, start, dens, brick = ins
    visc_out, moments_out = outs
    permuted, left, right, products, weights, factors, planes_high, planes_low = buffers
    markers = places.shape[-1]
    inside = BZ * HALF
    own = own_lanes()
    halves = [
        (owner, 2 * group + half, half, 2 * n + half)
        for n, (owner, group) in enumerate(groups)
        for half in range(2)
    ]
    parts = [split(brick[owner, group]) for owner, group in groups]
    for _, _, half, n in halves:
        high, low = parts[n // 2]
        permuted[n][...] = dot(high, spread[half, 0]) + dot(low, spread[half, 1])
    heights = []
    for owner, part, _, n in halves:
        weight_z, slope_z = axis_weights(places[owner, 2, part], BZ)
        heights.append(weight_z)
        for z in range(0, BZ, 2):
            for column, values in ((0, weight_z), (1, slope_z)):
                high, low = split(jnp.concatenate(values[z : z + 2], axis=0))
                columns = slice(column * markers, (column + 1) * markers)
                for k in range(4):
                    begin = k * inside + z * HALF
                    right[n][begin : begin + 2 * HALF, columns] = low if k % 2 else high
    for _, _, _, n in halves:
        for row in range(0, ROWS, 2):
            pair = [
                jnp.broadcast_to(permuted[n][r : r + 1, :], own.shape) * own for r in (row, row + 1)
            ]
            left[n][row * HALF : (row + 2) * HALF, :] = jnp.concatenate(pair, axis=0).astype(bf16)
    for _, _, _, n in halves:
        products[n][...] = dot(left[n][...], right[n][...])
    for owner, part, _, n in halves:
        weights_x = axis_weights(places[owner, 0, part], BX)
        weights_y = axis_weights(places[owner, 1, part], BY)
        for k, values in enumerate((*weights_x, *weights_y)):
            for i, value in enumerate(values):
                weights[n][4 * k + i] = value
        for j in range(BY):
            for z in range(0, BZ, 2):
                pair = [weights_y[0][j] * heights[n][z + k] for k in range(2)]
                rows = slice((j * BZ + z) * HALF, (j * BZ + z + 2) * HALF)
                high, low = split(jnp.concatenate(pair, axis=0))
                planes_high[n][rows, :] = high
                planes_low[n][rows, :] = low

    count = 3 * BX * HALF
    for owner, part, _, n in halves:
        grads = gradients(products[n], weights[n], markers)
        normal = grads[0][0] ** 2 + grads[1][1] ** 2 + grads[2][2] ** 2
        shear_xy = 0.5 * (grads[0][1] + grads[1][0])
        shear_xz = 0.5 * (grads[0][2] + grads[2][0])
        shear_yz = 0.5 * (grads[1][2] + grads[2][1])
        invariant = 0.5 * normal + shear_xy**2 + shear_xz**2 + shear_yz**2
        scaled = invariant * (1.0 / (STRAIN_SCALE * STRAIN_SCALE))
        third = jnp.log(1.0 + scaled) * (1.0 / 3.0)
        first = start[owner, part]
        slot = lax.broadcasted_iota(jnp.int32, first.shape, 0) + part * HALF
        live = slot < counts[0, owner]
        visc_out[owner, part] = jnp.where(live, first * jnp.exp(-third), 0.0)
        carried = (
            live.astype(f32),
            jnp.where(live, jnp.log(first) - third, 0.0),
            jnp.where(live, dens[owner, part], 0.0),
        )
        for c in range(3):
            for i in range(0, BX, 2):
                pair = [carried[c] * weights[n][i + k] for k in range(2)]
                row = (c * BX + i) * HALF
                high, low = split(jnp.concatenate(pair, axis=0))
                factors[n][row : row + 2 * HALF, :] = high
                factors[n][count + row : count + row + 2 * HALF, :] = low

    contract = (((1,), (1,)), ((), ()))
    found = []
    for _, _, _, n in halves:
        both = lax.dot_general(
            factors[n][...], planes_high[n][...], contract, preferred_element_type=f32
        )
        rest = lax.dot_general(
            factors[n][:count], planes_low[n][...], contract, preferred_element_type=f32
        )
        found.append((both, rest))
    for _, _, half, n in halves:
        both, rest = found[n]
        total = both[:count] + both[count:] + rest
        chosen = total.reshape(3 * BX, HALF, BY * inside) * own[None]
        high, low = split(jnp.sum(chosen, axis=1))
        columns = slice(half * BY * inside, (half + 1) * BY * inside)
        row = (n // 2) * 32
        sums[row : row + 3 * BX, columns] = high.astype(f32)
        sums[row + 16 : row + 16 + 3 * BX, columns] = low.astype(f32)
    moved = dot(sums[...].astype(bf16), gather[...])
    for n, (owner, group) in enumerate(groups):
        mine = moved[32 * n : 32 * n + 3 * BX] + moved[32 * n + 16 : 32 * n + 16 + 3 * BX]
        for j in range(BY):
            rows = pl.ds(j, 3 * BX, stride=BY)
            moments_out[owner, group, rows, :] = mine[:, j * LANES : (j + 1) * LANES]


TOGETHER = 2


def marker_body(counts, *refs):
    ins, outs, scratch = refs[:6], refs[7:9], refs[9:]
    listed, sums, *flat = scratch
    held = 2 * TOGETHER
    buffers = [flat[n * held : (n + 1) * held] for n in range(len(flat) // held)]
    visc_out, moments_out = outs
    owners, groups = moments_out.shape[:2]
    visc_out[...] = jnp.zeros_like(visc_out)
    moments_out[...] = jnp.zeros_like(moments_out)
    sums[...] = jnp.zeros_like(sums)

    def list_groups(index, number):
        owner, group = index // groups, index % groups
        live = group * GROUP < counts[0, owner]

        @pl.when(live)
        def _():
            for n in range(TOGETHER):
                listed[2 * (number + n)] = owner
                listed[2 * (number + n) + 1] = group

        return jnp.where(live, number + 1, number)

    number = lax.fori_loop(0, owners * groups, list_groups, 0)

    def step(index, carry):
        first = TOGETHER * index
        taken = [
            (listed[2 * (first + n)], listed[2 * (first + n) + 1]) for n in range(TOGETHER)
        ]
        marker_groups(taken, counts, ins, outs, buffers, sums)
        return carry

    lax.fori_loop(0, (number + TOGETHER - 1) // TOGETHER, step, 0)


def marker_work(counts, positions, start_visc, marker_dens, bricks, after):
    owners, _, slots, markers = positions.shape
    groups, parts = slots // GROUP, slots // HALF
    spread, gather = permutations()
    width = 4 * BZ * HALF
    whole = pl.BlockSpec(memory_space=pltpu.VMEM)
    buffers = (
        pltpu.VMEM((ROWS, width), f32),
        pltpu.VMEM((ROWS * HALF, width), bf16),
        pltpu.VMEM((width, 2 * markers), bf16),
        pltpu.VMEM((ROWS * HALF, 2 * markers), f32),
        pltpu.VMEM((4 * 4, HALF, markers), f32),
        pltpu.VMEM((2 * 3 * BX * HALF, markers), bf16),
        pltpu.VMEM((BY * BZ * HALF, markers), bf16),
        pltpu.VMEM((BY * BZ * HALF, markers), bf16),
    )
    visc, moments = pl.pallas_call(
        marker_body,
        out_shape=(
            jax.ShapeDtypeStruct((owners, parts, HALF, markers), f32),
            jax.ShapeDtypeStruct((owners, groups, ROWS, LANES), f32),
        ),
        in_specs=[pl.BlockSpec(memory_space=pltpu.SMEM)]
        + [whole] * 6
        + [pl.BlockSpec(memory_space=pl.ANY)],
        out_specs=(whole, whole),
        scratch_shapes=[
            pltpu.SMEM((2 * (owners * groups + TOGETHER),), jnp.int32),
            pltpu.VMEM((32 * TOGETHER, 2 * BY * BZ * HALF), f32),
        ]
        + [buffer for buffer in buffers for _ in range(2 * TOGETHER)],
        compiler_params=vmem_limit(60),
        cost_estimate=cost(25),
        name="marker_work",
    )(
        counts,
        spread,
        gather,
        positions.reshape(owners, 3, parts, HALF, markers),
        start_visc.reshape(owners, parts, HALF, markers),
        marker_dens.reshape(owners, parts, HALF, markers),
        bricks,
        after,
    )
    return visc.reshape(owners, slots, markers), moments


def settle_body(asked, moments_in, visc_in, dens_in, visc_out, dens_out, *scratch):
    moments, visc, dens, done, *tables = scratch
    size_x, size_y, size_z = visc.shape
    copies = [
        pltpu.make_async_copy(there, here, done.at[n])
        for n, (there, here) in enumerate(
            ((moments_in, moments), (visc_in, visc), (dens_in, dens))
        )
    ]
    for copy in copies:
        copy.start()
    bricks_y, halves = size_y // BY, size_z // LANES
    for table in tables:
        table[...] = jnp.zeros_like(table)
    copies[0].wait()
    groups = moments.shape[1]
    lane_slot = lax.broadcasted_iota(jnp.int32, (ROWS, LANES), 1) // BZ

    def one_group(step, carry):
        device, group = step // groups, step % groups
        packed = moments[device, group]
        for slot in range(GROUP):
            table = tables[slot % len(tables)]
            place, lane = place_of(asked[device, group * GROUP + slot])
            piece = jnp.where(lane_slot == slot, packed, 0.0)
            piece = pltpu.roll(piece, (lane - BZ * slot) & (LANES - 1), 1)
            table[place] = table[place] + piece
        return carry

    lax.fori_loop(0, moments.shape[0] * groups, one_group, 0)
    copies[1].wait()
    copies[2].wait()

    def finish(block_x, carry):
        for block_y in range(0, bricks_y, 2):
            for half in range(halves):
                for i in range(BX):
                    here = (
                        block_x * BX + i,
                        slice(block_y * BY, (block_y + 2) * BY),
                        slice(half * LANES, (half + 1) * LANES),
                    )
                    sums = []
                    for c in range(3):
                        rows = slice((c * BX + i) * BY, (c * BX + i + 1) * BY)
                        places = [
                            (block_x * bricks_y + block_y + k) * halves + half for k in range(2)
                        ]
                        sums.append(
                            jnp.concatenate(
                                [add_all([t[place, rows, :] for t in tables]) for place in places]
                            )
                        )
                    scale = 1.0 / (sums[0] + 1.0)
                    visc_out[here] = jnp.exp((sums[1] + jnp.log(visc[here])) * scale)
                    dens_out[here] = (sums[2] + dens[here]) * scale
        return carry

    lax.fori_loop(0, size_x // BX, finish, 0)


def settle(asked, moments, cell_visc, cell_dens):
    size_x, size_y, size_z = cell_visc.shape
    places = (size_x // BX) * (size_y // BY) * (size_z // LANES)
    whole = pl.BlockSpec(memory_space=pltpu.VMEM)
    shape = jax.ShapeDtypeStruct(cell_visc.shape, f32)
    return pl.pallas_call(
        settle_body,
        out_shape=(shape, shape),
        in_specs=[pl.BlockSpec(memory_space=pltpu.SMEM)]
        + [pl.BlockSpec(memory_space=pl.ANY)] * 3,
        out_specs=(whole, whole),
        scratch_shapes=[
            pltpu.VMEM(moments.shape, f32),
            pltpu.VMEM(cell_visc.shape, f32),
            pltpu.VMEM(cell_visc.shape, f32),
            pltpu.SemaphoreType.DMA((3,)),
        ]
        + [pltpu.VMEM((places, ROWS, LANES), f32)] * 2,
        compiler_params=vmem_limit(60),
        cost_estimate=cost(7),
        name="settle",
    )(asked, moments, cell_visc, cell_dens)


def field_of(fields, index):
    return fields[0].at[index] if index < 3 else fields[index - 2]


def pack_x_body(vel, pres, visc, dens, to_low, to_high, done):
    width = SWEEPS
    copies = []
    for begin, out in ((0, to_low), (pres.shape[0] - width, to_high)):
        planes = pl.ds(begin, width)
        for n, field in enumerate((pres, visc, dens)):
            copies.append((field.at[planes], out.at[3 + n]))
        copies.append((vel.at[:, planes], out.at[0:3]))
    copies = [pltpu.make_async_copy(*pair, done.at[n]) for n, pair in enumerate(copies)]
    for copy in copies:
        copy.start()
    for copy in copies:
        copy.wait()


def pack_x(velocity, pressure, cell_visc, cell_dens):
    _, size_y, size_z = cell_visc.shape
    anywhere = pl.BlockSpec(memory_space=pl.ANY)
    shape = jax.ShapeDtypeStruct((6, SWEEPS, size_y, size_z), f32)
    return pl.pallas_call(
        pack_x_body,
        out_shape=(shape, shape),
        in_specs=[anywhere] * 4,
        out_specs=(anywhere, anywhere),
        scratch_shapes=[pltpu.SemaphoreType.DMA((8,))],
        compiler_params=vmem_limit(60),
        cost_estimate=cost(2),
        name="pack_x",
    )(velocity, pressure, cell_visc, cell_dens)


def corner_rows(upward, size_x):
    width = SWEEPS
    spare = (5 * width,) if upward else (4 * width - 1, 6 * width - 1)
    places = [(plane, row) for plane in range(size_x) for row in spare]
    found = []
    for field in range(6):
        for side in range(2):
            near = field == 5 or (field == 3 and side == 1 and not upward)
            reach = width - 1 if near else width
            for far_x in range(1, width):
                for far_y in range(1, reach - far_x + 1):
                    found.append((field, side, far_x, far_y))
    more = max(0, len(found) - len(places))
    places += [(size_x + n // (6 * width), n % (6 * width)) for n in range(more)]
    return [cell + at for cell, at in zip(found, places)], size_x + -(-more // (6 * width))


def pack_y_body(size_x, vel, pres, visc, dens, low_x, high_x, upward, downward):
    step_x, size_y, _ = pres.shape
    width = SWEEPS
    step = pl.program_id(0)
    planes = pl.ds(pl.multiple_of(step * step_x, step_x), step_x)
    for f in range(6):
        field = field_of((vel, pres, visc, dens), f)
        rows = slice(f * width, (f + 1) * width)
        upward[planes, rows, :] = field[:, size_y - width :, :]
        downward[planes, rows, :] = field[:, :width, :]

    @pl.when(step == pl.num_programs(0) - 1)
    def _():
        for up, face in ((True, upward), (False, downward)):
            for f, side, far_x, far_y, plane, row in corner_rows(up, size_x)[0]:
                halo, at = (high_x, far_x - 1) if side else (low_x, width - far_x)
                face[plane, row] = halo[f, at, size_y - far_y if up else far_y - 1]


def pack_y(velocity, pressure, cell_visc, cell_dens, low_x, high_x):
    size_x, size_y, size_z = cell_visc.shape
    step = 8
    block = pl.BlockSpec((step, size_y, size_z), lambda i: (i, 0, 0))
    halo = pl.BlockSpec(low_x.shape, lambda i: (0, 0, 0, 0))
    shapes = [(corner_rows(up, size_x)[1], 6 * SWEEPS, size_z) for up in (True, False)]
    return pl.pallas_call(
        functools.partial(pack_y_body, size_x),
        grid=(size_x // step,),
        out_shape=tuple(jax.ShapeDtypeStruct(shape, f32) for shape in shapes),
        in_specs=[
            pl.BlockSpec((3, step, size_y, size_z), lambda i: (0, i, 0, 0)),
            block,
            block,
            block,
            halo,
            halo,
        ],
        out_specs=tuple(pl.BlockSpec(shape, lambda i: (0, 0, 0)) for shape in shapes),
        compiler_params=vmem_limit(60),
        cost_estimate=cost(15),
        name="pack_y",
    )(velocity, pressure, cell_visc, cell_dens, low_x, high_x)


def place(per, x, y, rows):
    return x % per, pl.ds(y * SUBLANES + x // per, rows, stride=SUBLANES)


def put(target, x, y, rows, value):
    per, halves = target.shape[:2]
    plane, lines = place(per, x, y, rows)
    for half in range(halves):
        target[plane, half, lines, :] = value[:, half * LANES : (half + 1) * LANES]


def tile(y):
    if isinstance(y, int):
        return pl.ds(y * SUBLANES, SUBLANES)
    return pl.ds(pl.multiple_of(y * SUBLANES, SUBLANES), SUBLANES)


def row_work(cells, coefs, relax, forcing, rate):
    per, halves = cells.shape[1:3]
    lane = lax.broadcasted_iota(jnp.int32, (SUBLANES, LANES), 1)
    at_first, at_last = lane == 0, lane == LANES - 1

    def take(field, plane, y):
        return jnp.concatenate([field[plane, half, tile(y), :] for half in range(halves)], axis=1)

    def store(field, plane, y, value):
        for half in range(halves):
            field[plane, half, tile(y), :] = value[:, half * LANES : (half + 1) * LANES]

    def up_x(field, plane, y):
        if plane < per - 1:
            return take(field, plane + 1, y)
        return pltpu.roll(take(field, 0, y), SUBLANES - 1, 0)

    def down_x(field, plane, y):
        if plane > 0:
            return take(field, plane - 1, y)
        return pltpu.roll(take(field, per - 1, y), 1, 0)

    def rolled(a, shift):
        return [
            pltpu.roll(a[:, half * LANES : (half + 1) * LANES], shift, 1) for half in range(halves)
        ]

    def up_z(a):
        parts = rolled(a, LANES - 1)
        after = parts[1:] + [jnp.zeros_like(parts[0])]
        return jnp.concatenate([jnp.where(at_last, n, p) for p, n in zip(parts, after)], axis=1)

    def down_z(a):
        parts = rolled(a, 1)
        before = [jnp.zeros_like(parts[0])] + parts[:-1]
        return jnp.concatenate([jnp.where(at_first, b, p) for p, b in zip(parts, before)], axis=1)

    def prepare(y):
        visc, dens = cells.at[0], cells.at[1]
        for plane in range(per):
            here = take(visc, plane, y)
            near = [
                up_x(visc, plane, y),
                down_x(visc, plane, y),
                take(visc, plane, y + 1),
                take(visc, plane, y - 1),
                up_z(here),
                down_z(here),
            ]
            links = [0.5 * (here + other) for other in near]
            scale = jnp.where(here > 0.0, RELAX / add_all(links), 0.0)
            for n in range(6):
                coefs[n, plane, tile(y), :] = links[n] * scale
            relax[plane, tile(y), :] = scale
            forcing[plane, tile(y), :] = take(dens, plane, y) * (-GRAVITY * scale)
            rate[plane, tile(y), :] = PRESSURE_RATE * here

    def sweep(y, old, new):
        for plane in range(per):
            links = [coefs[n, plane, tile(y), :] for n in range(6)]
            scale = relax[plane, tile(y), :]
            pressure = take(old.at[3], plane, y)
            before = (
                down_x(old.at[3], plane, y),
                take(old.at[3], plane, y - 1),
                down_z(pressure),
            )
            changes = []
            for c in range(3):
                field = old.at[c]
                here = take(field, plane, y)
                near = [
                    up_x(field, plane, y),
                    down_x(field, plane, y),
                    take(field, plane, y + 1),
                    take(field, plane, y - 1),
                    up_z(here),
                    down_z(here),
                ]
                terms = [link * other for link, other in zip(links, near)]
                total = (terms[0] + terms[1]) + (terms[2] + terms[3])
                total = total + (terms[4] + terms[5])
                rest = (1.0 - RELAX) * here - scale * (pressure - before[c])
                if c == 2:
                    rest = rest + forcing[plane, tile(y), :]
                changes.append(near[2 * c] - here)
                store(new.at[c], plane, y, total + rest)
            pressed = pressure - rate[plane, tile(y), :] * add_all(changes)
            store(new.at[3], plane, y, pressed)

    return prepare, sweep


def kept_rows(size_y):
    width = SWEEPS
    return (
        ((width, size_y),),
        ((width + 1, width), (size_y - 1, width)),
        ((width, width + 1), (size_y - 1, width + 1)),
    )


def kept_copies(pairs, size_y, done):
    copies = []
    for (source, target), strips in zip(pairs, kept_rows(size_y)):
        for begin, rows in strips:
            span = (slice(None),) * 3 + (pl.ds(begin * SUBLANES, rows * SUBLANES),)
            copies.append(
                pltpu.make_async_copy(source.at[span], target.at[span], done.at[len(copies)])
            )
    return copies


def inner_body(vel, pres, visc, dens, low_x, high_x, _, even_out, odd_out, cells_out, *work):
    blocks, sides_x, even, odd, cells, coefs, relax, forcing, rate, done = work
    size_x, size_y, size_z = blocks.shape[1:]
    width = SWEEPS
    inputs = (
        (visc, blocks.at[4], (4,)),
        (vel, blocks.at[0:3], (0, 1, 2)),
        (pres, blocks.at[3], (3,)),
        (dens, blocks.at[5], (5,)),
        (low_x, sides_x.at[0], ()),
        (high_x, sides_x.at[1], ()),
    )
    copies = [
        pltpu.make_async_copy(there, here, done.at[n]) for n, (there, here, _) in enumerate(inputs)
    ]
    for copy in copies:
        copy.start()
    targets = [even.at[n] for n in range(4)] + [cells.at[n] for n in range(2)]
    for copy, (_, _, held) in zip(copies, inputs):
        copy.wait()
        for f in held:
            for i in range(size_x):
                for y in range(0, size_y, SUBLANES):
                    value = blocks[f, i, y : y + SUBLANES, :]
                    put(targets[f], i + width, y + width, SUBLANES, value)
    for side, begin in enumerate((0, width + size_x)):
        for f in range(6):
            for i in range(width):
                for y in range(0, size_y, SUBLANES):
                    value = sides_x[side, f, i, y : y + SUBLANES, :]
                    put(targets[f], begin + i, y + width, SUBLANES, value)

    prepare, sweep = row_work(cells, coefs, relax, forcing, rate)

    def prepare_row(y, carry):
        prepare(y)
        return carry

    first, last = width + 1, width + size_y - 1
    lax.fori_loop(first, last, prepare_row, 0, unroll=2)
    for step in range(SWEEPS):
        old, new = (odd, even) if step % 2 else (even, odd)

        def sweep_row(y, carry, old=old, new=new):
            sweep(y, old, new)
            return carry

        lax.fori_loop(first + step, last - step, sweep_row, 0, unroll=2)
    sends = kept_copies(((even, even_out), (odd, odd_out), (cells, cells_out)), size_y, done)
    for send in sends:
        send.start()
    for send in sends:
        send.wait()


def inner_sweeps(velocity, pressure, cell_visc, cell_dens, low_x, high_x, after):
    size_x, size_y, size_z = cell_visc.shape
    width = low_x.shape[1]
    per, rows = (size_x + 2 * width) // SUBLANES, (size_y + 2 * width) * SUBLANES
    block, cut = (per, rows, size_z), (per, size_z // LANES, rows, LANES)
    shapes = [(4,) + cut, (4,) + cut, (2,) + cut]
    anywhere = pl.BlockSpec(memory_space=pl.ANY)
    return pl.pallas_call(
        inner_body,
        out_shape=tuple(jax.ShapeDtypeStruct(shape, f32) for shape in shapes),
        in_specs=[anywhere] * 7,
        out_specs=(anywhere,) * 3,
        scratch_shapes=[
            pltpu.VMEM((6,) + cell_visc.shape, f32),
            pltpu.VMEM((2,) + low_x.shape, f32),
        ]
        + [pltpu.VMEM(shape, f32) for shape in shapes]
        + [
            pltpu.VMEM((6,) + block, f32),
            pltpu.VMEM(block, f32),
            pltpu.VMEM(block, f32),
            pltpu.VMEM(block, f32),
            pltpu.SemaphoreType.DMA((6,)),
        ],
        compiler_params=vmem_limit(60),
        cost_estimate=cost(25),
        name="inner_sweeps",
    )(velocity, pressure, cell_visc, cell_dens, low_x, high_x, after)


def edge_body(even_in, odd_in, cells_in, low_y, high_y, vel_out, pres_out, *work):
    from_low, from_high, results, even, odd, cells, coefs, relax, forcing, rate, done, more = work
    size_x, size_y, size_z = results.shape[1:]
    width = SWEEPS
    long_y = size_y + 2 * width
    halos = [
        pltpu.make_async_copy(low_y, from_low, more.at[0]),
        pltpu.make_async_copy(high_y, from_high, more.at[1]),
    ]
    kept = kept_copies(((even_in, even), (odd_in, odd), (cells_in, cells)), size_y, done)
    for copy in (*halos, *kept[3:], *kept[:3]):
        copy.start()
    targets = [even.at[n] for n in range(4)] + [cells.at[n] for n in range(2)]
    for target in targets:
        for x in (*range(width), *range(width + size_x, size_x + 2 * width)):
            for y in (0, width + size_y):
                put(target, x, y, width, jnp.zeros((width, size_z), f32))
    for up, halo, copy, begin in (
        (True, from_low, halos[0], 0),
        (False, from_high, halos[1], width + size_y),
    ):
        copy.wait()
        for f, target in enumerate(targets):
            rows = slice(f * width, (f + 1) * width)
            for i in range(size_x):
                put(target, i + width, begin, width, halo[i, rows, :])
        for f, side, far_x, far_y, plane, row in corner_rows(up, size_x)[0]:
            x = width + size_x - 1 + far_x if side else width - far_x
            y = width - far_y if up else width + size_y - 1 + far_y
            put(targets[f], x, y, 1, halo[plane, row : row + 1, :])
    for copy in kept:
        copy.wait()

    prepare, sweep = row_work(cells, coefs, relax, forcing, rate)

    def prepare_rows(n, carry):
        prepare(1 + n)
        prepare(long_y - 2 * width + n)
        return carry

    lax.fori_loop(0, 2 * width - 1, prepare_rows, 0)
    for step in range(SWEEPS):
        old, new = (odd, even) if step % 2 else (even, odd)

        def sweep_rows(n, carry, old=old, new=new, step=step):
            sweep(1 + step + n, old, new)
            sweep(width + size_y - 1 - step + n, old, new)
            return carry

        lax.fori_loop(0, width, sweep_rows, 0)

    final = odd if SWEEPS % 2 else even
    outs = [vel_out.at[0], vel_out.at[1], vel_out.at[2], pres_out]
    sends = [pltpu.make_async_copy(results.at[n], out, done.at[n]) for n, out in enumerate(outs)]
    per, halves = even.shape[1:3]
    for field, send in enumerate(sends):
        for i in range(size_x):
            for y in range(0, size_y, SUBLANES):
                plane, lines = place(per, i + width, y + width, SUBLANES)
                for half in range(halves):
                    columns = slice(half * LANES, (half + 1) * LANES)
                    results[field, i, y : y + SUBLANES, columns] = final[
                        field, plane, half, lines, :
                    ]
        send.start()
    for send in sends:
        send.wait()


def edge_sweeps(even, odd, cells, low_y, high_y, size_x, size_y):
    per, halves, rows = even.shape[1:4]
    size_z = halves * LANES
    block = (per, rows, size_z)
    anywhere = pl.BlockSpec(memory_space=pl.ANY)
    return pl.pallas_call(
        edge_body,
        out_shape=(
            jax.ShapeDtypeStruct((3, size_x, size_y, size_z), f32),
            jax.ShapeDtypeStruct((size_x, size_y, size_z), f32),
        ),
        in_specs=[anywhere] * 5,
        out_specs=(anywhere,) * 2,
        scratch_shapes=[
            pltpu.VMEM(low_y.shape, f32),
            pltpu.VMEM(high_y.shape, f32),
            pltpu.VMEM((4, size_x, size_y, size_z), f32),
            pltpu.VMEM(even.shape, f32),
            pltpu.VMEM(odd.shape, f32),
            pltpu.VMEM(cells.shape, f32),
            pltpu.VMEM((6,) + block, f32),
            pltpu.VMEM(block, f32),
            pltpu.VMEM(block, f32),
            pltpu.VMEM(block, f32),
            pltpu.SemaphoreType.DMA((5,)),
            pltpu.SemaphoreType.DMA((2,)),
        ],
        compiler_params=vmem_limit(40),
        cost_estimate=cost(1),
        name="edge_sweeps",
    )(even, odd, cells, low_y, high_y)


def shift(value, axis, step):
    size = lax.axis_size(axis)
    pairs = [(i, i + step) for i in range(size) if 0 <= i + step < size]
    return lax.ppermute(value, axis, pairs)


def per_device(
    velocity,
    pressure,
    cell_visc,
    cell_dens,
    block_brick,
    block_counts,
    positions,
    start_visc,
    marker_dens,
):
    asked = lax.all_to_all(block_brick, "mark", 0, 0, tiled=True)
    fields = (velocity, pressure, cell_visc, cell_dens)
    to_low, to_high = pack_x(*fields)
    low_x, high_x = shift(to_high, "grid", 1), shift(to_low, "grid", -1)
    upward, downward = pack_y(*fields, low_x, high_x)
    low_y, high_y = shift(upward, "mark", 1), shift(downward, "mark", -1)

    picked = pick_bricks(asked, velocity)
    bricks = lax.all_to_all(picked, "mark", 0, 0, tiled=True)
    marker_visc, moments = marker_work(
        block_counts, positions, start_visc, marker_dens, bricks, upward
    )
    gathered = lax.all_to_all(moments, "mark", 0, 0, tiled=True)
    state = inner_sweeps(*fields, low_x, high_x, moments)
    velocity_next, pressure_next = edge_sweeps(*state, low_y, high_y, *pressure.shape[:2])
    visc_next, dens_next = settle(asked, gathered, cell_visc, cell_dens)
    return velocity_next, pressure_next, visc_next, dens_next, marker_visc


def solution(mesh):
    in_specs = (
        P(None, "grid", "mark", None),
        P("grid", "mark", None),
        P("grid", "mark", None),
        P("grid", "mark", None),
        P(("grid", "mark"), None),
        P(("grid", "mark"), None),
        P(("grid", "mark"), None, None, None),
        P(("grid", "mark"), None, None),
        P(("grid", "mark"), None, None),
    )
    out_specs = (
        P(None, "grid", "mark", None),
        P("grid", "mark", None),
        P("grid", "mark", None),
        P("grid", "mark", None),
        P(("grid", "mark"), None, None),
    )
    return jax.shard_map(
        per_device, mesh=mesh, in_specs=in_specs, out_specs=out_specs, check_vma=False
    )
```

```python
import functools

import jax
import jax.numpy as jnp
import numpy as np
from jax import lax
from jax.experimental import pallas as pl
from jax.experimental.pallas import tpu as pltpu
from jax.sharding import PartitionSpec as P

SWEEPS = 4
RELAX = 0.6
PRESSURE_RATE = 0.25
GRAVITY = 1.0
STRAIN_SCALE = 0.5

BX, BY, BZ = 4, 4, 8
PLANE = BX * BY
ROWS = 3 * PLANE
LANES = 128
GROUP = LANES // BZ
HALF = 8
SUBLANES = 8

f32, bf16 = jnp.float32, jnp.bfloat16


def vmem_limit(mib):
    return pltpu.CompilerParams(vmem_limit_bytes=mib * 1024 * 1024)


def cost(microseconds):
    return pl.CostEstimate(
        flops=int(microseconds * 1.15e9), bytes_accessed=0, transcendentals=0
    )


def place_of(brick):
    return lax.shift_right_logical(brick, GROUP.bit_length() - 1), (brick & (GROUP - 1)) * BZ


def pick_body(asked, vel, out, table):
    size_x, size_y, size_z = vel.shape[1:]
    bricks_y, halves = size_y // BY, size_z // LANES

    def repack(block_x, carry):
        for block_y in range(bricks_y):
            for half in range(halves):
                place = (block_x * bricks_y + block_y) * halves + half
                for c in range(3):
                    for i in range(BX):
                        row = (c * BX + i) * BY
                        table[place, row : row + BY, :] = vel[
                            c,
                            block_x * BX + i,
                            block_y * BY : (block_y + 1) * BY,
                            half * LANES : (half + 1) * LANES,
                        ]
        return carry

    lax.fori_loop(0, size_x // BX, repack, 0)
    groups = out.shape[1]
    lane_slot = lax.broadcasted_iota(jnp.int32, (ROWS, LANES), 1) // BZ

    def one_group(step, carry):
        device, group = step // groups, step % groups
        packed = jnp.zeros((ROWS, LANES), f32)
        for slot in range(GROUP):
            place, lane = place_of(asked[device, group * GROUP + slot])
            rolled = pltpu.roll(table[place], (BZ * slot - lane) & (LANES - 1), 1)
            packed = jnp.where(lane_slot == slot, rolled, packed)
        out[device, group] = packed
        return carry

    lax.fori_loop(0, out.shape[0] * groups, one_group, 0)


def pick_bricks(asked, velocity):
    devices, slots = asked.shape
    size_x, size_y, size_z = velocity.shape[1:]
    places = (size_x // BX) * (size_y // BY) * (size_z // LANES)
    return pl.pallas_call(
        pick_body,
        out_shape=jax.ShapeDtypeStruct((devices, slots // GROUP, ROWS, LANES), f32),
        in_specs=[
            pl.BlockSpec(memory_space=pltpu.SMEM),
            pl.BlockSpec(memory_space=pltpu.VMEM),
        ],
        out_specs=pl.BlockSpec(memory_space=pltpu.VMEM),
        scratch_shapes=[pltpu.VMEM((places, ROWS, LANES), f32)],
        compiler_params=vmem_limit(24),
        cost_estimate=cost(25),
        name="pick_bricks",
    )(asked, velocity)


def permutations():
    inside = BZ * HALF
    spread = np.zeros((2, 2, LANES, 4 * inside), np.float32)
    gather = np.zeros((2 * BY * inside, BY * LANES), np.float32)
    for half in range(2):
        for slot in range(HALF):
            for z in range(BZ):
                outer, inner = (half * HALF + slot) * BZ + z, z * HALF + slot
                for part in range(4):
                    spread[half, part // 2, outer, part * inside + inner] = 1
                for j in range(BY):
                    gather[(half * BY + j) * inside + inner, j * LANES + outer] = 1
    return jnp.asarray(spread, bf16), jnp.asarray(gather, bf16)


def split(value):
    high = value.astype(bf16)
    return high, (value - high.astype(f32)).astype(bf16)


def add_all(values):
    return functools.reduce(jnp.add, values)


def axis_weights(fraction, cells):
    middle = (cells - 1) / 2
    base = jnp.exp(fraction * (2.0 * cells) - float(cells))
    powers = [None, base]
    for i in range(2, cells):
        powers.append(powers[i // 2] * powers[i - i // 2])
    factors = [float(np.exp(middle**2 - (i - middle) ** 2)) for i in range(cells)]
    bells = [None] + [powers[i] * factors[i] for i in range(1, cells)]
    scale = 1.0 / (add_all(bells[1:]) + factors[0])
    weights = [scale * factors[0]] + [bell * scale for bell in bells[1:]]
    mean = add_all(
        [
            (weights[cells - 1 - i] - weights[i]) * (2.0 * (middle - i))
            for i in range(cells // 2)
        ]
    )
    slopes = [w * (2.0 * (i - middle) - mean) for i, w in enumerate(weights)]
    return weights, slopes


def dot(a, b):
    return jnp.dot(a, b, preferred_element_type=f32)


def gradients(products, weights, markers):
    weight_x, slope_x, weight_y, slope_y = ([weights[4 * n + i] for i in range(4)] for n in range(4))
    grads = []
    for c in range(3):
        lines = [[], [], []]
        for i in range(BX):
            rows = [((c * BX + i) * BY + j) * HALF for j in range(BY)]
            still = [products[row : row + HALF, :markers] for row in rows]
            rising = [products[row : row + HALF, markers:] for row in rows]
            lines[0].append(slope_x[i] * add_all([w * t for w, t in zip(weight_y, still)]))
            lines[1].append(weight_x[i] * add_all([w * t for w, t in zip(slope_y, still)]))
            lines[2].append(weight_x[i] * add_all([w * t for w, t in zip(weight_y, rising)]))
        grads.append([add_all(line) for line in lines])
    return grads


def own_lanes():
    shape = (HALF, 4 * BZ * HALF)
    lane = lax.broadcasted_iota(jnp.int32, shape, 1)
    return (lane % HALF == lax.broadcasted_iota(jnp.int32, shape, 0)).astype(f32)


def marker_groups(groups, counts, ins, outs, buffers, sums):
    spread, gather, places, start, dens, brick = ins
    visc_out, moments_out = outs
    permuted, left, right, products, weights, factors, planes_high, planes_low = buffers
    markers = places.shape[-1]
    inside = BZ * HALF
    own = own_lanes()
    halves = [
        (owner, 2 * group + half, half, 2 * n + half)
        for n, (owner, group) in enumerate(groups)
        for half in range(2)
    ]
    parts = [split(brick[owner, group]) for owner, group in groups]
    for _, _, half, n in halves:
        high, low = parts[n // 2]
        permuted[n][...] = dot(high, spread[half, 0]) + dot(low, spread[half, 1])
    heights = []
    for owner, part, _, n in halves:
        weight_z, slope_z = axis_weights(places[owner, 2, part], BZ)
        heights.append(weight_z)
        for z in range(0, BZ, 2):
            for column, values in ((0, weight_z), (1, slope_z)):
                high, low = split(jnp.concatenate(values[z : z + 2], axis=0))
                columns = slice(column * markers, (column + 1) * markers)
                for k in range(4):
                    begin = k * inside + z * HALF
                    right[n][begin : begin + 2 * HALF, columns] = low if k % 2 else high
    for _, _, _, n in halves:
        for row in range(0, ROWS, 2):
            pair = [
                jnp.broadcast_to(permuted[n][r : r + 1, :], own.shape) * own for r in (row, row + 1)
            ]
            left[n][row * HALF : (row + 2) * HALF, :] = jnp.concatenate(pair, axis=0).astype(bf16)
    for _, _, _, n in halves:
        products[n][...] = dot(left[n][...], right[n][...])
    for owner, part, _, n in halves:
        weights_x = axis_weights(places[owner, 0, part], BX)
        weights_y = axis_weights(places[owner, 1, part], BY)
        for k, values in enumerate((*weights_x, *weights_y)):
            for i, value in enumerate(values):
                weights[n][4 * k + i] = value
        for j in range(BY):
            for z in range(0, BZ, 2):
                pair = [weights_y[0][j] * heights[n][z + k] for k in range(2)]
                rows = slice((j * BZ + z) * HALF, (j * BZ + z + 2) * HALF)
                high, low = split(jnp.concatenate(pair, axis=0))
                planes_high[n][rows, :] = high
                planes_low[n][rows, :] = low

    count = 3 * BX * HALF
    for owner, part, _, n in halves:
        grads = gradients(products[n], weights[n], markers)
        normal = grads[0][0] ** 2 + grads[1][1] ** 2 + grads[2][2] ** 2
        shear_xy = 0.5 * (grads[0][1] + grads[1][0])
        shear_xz = 0.5 * (grads[0][2] + grads[2][0])
        shear_yz = 0.5 * (grads[1][2] + grads[2][1])
        invariant = 0.5 * normal + shear_xy**2 + shear_xz**2 + shear_yz**2
        scaled = invariant * (1.0 / (STRAIN_SCALE * STRAIN_SCALE))
        third = jnp.log(1.0 + scaled) * (1.0 / 3.0)
        first = start[owner, part]
        slot = lax.broadcasted_iota(jnp.int32, first.shape, 0) + part * HALF
        live = slot < counts[0, owner]
        visc_out[owner, part] = jnp.where(live, first * jnp.exp(-third), 0.0)
        carried = (
            live.astype(f32),
            jnp.where(live, jnp.log(first) - third, 0.0),
            jnp.where(live, dens[owner, part], 0.0),
        )
        for c in range(3):
            for i in range(0, BX, 2):
                pair = [carried[c] * weights[n][i + k] for k in range(2)]
                row = (c * BX + i) * HALF
                high, low = split(jnp.concatenate(pair, axis=0))
                factors[n][row : row + 2 * HALF, :] = high
                factors[n][count + row : count + row + 2 * HALF, :] = low

    contract = (((1,), (1,)), ((), ()))
    found = []
    for _, _, _, n in halves:
        both = lax.dot_general(
            factors[n][...], planes_high[n][...], contract, preferred_element_type=f32
        )
        rest = lax.dot_general(
            factors[n][:count], planes_low[n][...], contract, preferred_element_type=f32
        )
        found.append((both, rest))
    for _, _, half, n in halves:
        both, rest = found[n]
        total = both[:count] + both[count:] + rest
        chosen = total.reshape(3 * BX, HALF, BY * inside) * own[None]
        high, low = split(jnp.sum(chosen, axis=1))
        columns = slice(half * BY * inside, (half + 1) * BY * inside)
        row = (n // 2) * 32
        sums[row : row + 3 * BX, columns] = high.astype(f32)
        sums[row + 16 : row + 16 + 3 * BX, columns] = low.astype(f32)
    moved = dot(sums[...].astype(bf16), gather[...])
    for n, (owner, group) in enumerate(groups):
        mine = moved[32 * n : 32 * n + 3 * BX] + moved[32 * n + 16 : 32 * n + 16 + 3 * BX]
        for j in range(BY):
            rows = pl.ds(j, 3 * BX, stride=BY)
            moments_out[owner, group, rows, :] = mine[:, j * LANES : (j + 1) * LANES]


TOGETHER = 2


def marker_body(counts, *refs):
    ins, outs, scratch = refs[:6], refs[7:9], refs[9:]
    listed, sums, *flat = scratch
    held = 2 * TOGETHER
    buffers = [flat[n * held : (n + 1) * held] for n in range(len(flat) // held)]
    visc_out, moments_out = outs
    owners, groups = moments_out.shape[:2]
    visc_out[...] = jnp.zeros_like(visc_out)
    moments_out[...] = jnp.zeros_like(moments_out)
    sums[...] = jnp.zeros_like(sums)

    def list_groups(index, number):
        owner, group = index // groups, index % groups
        live = group * GROUP < counts[0, owner]

        @pl.when(live)
        def _():
            for n in range(TOGETHER):
                listed[2 * (number + n)] = owner
                listed[2 * (number + n) + 1] = group

        return jnp.where(live, number + 1, number)

    number = lax.fori_loop(0, owners * groups, list_groups, 0)

    def step(index, carry):
        first = TOGETHER * index
        taken = [
            (listed[2 * (first + n)], listed[2 * (first + n) + 1]) for n in range(TOGETHER)
        ]
        marker_groups(taken, counts, ins, outs, buffers, sums)
        return carry

    lax.fori_loop(0, (number + TOGETHER - 1) // TOGETHER, step, 0)


def marker_work(counts, positions, start_visc, marker_dens, bricks, after):
    owners, _, slots, markers = positions.shape
    groups, parts = slots // GROUP, slots // HALF
    spread, gather = permutations()
    width = 4 * BZ * HALF
    whole = pl.BlockSpec(memory_space=pltpu.VMEM)
    buffers = (
        pltpu.VMEM((ROWS, width), f32),
        pltpu.VMEM((ROWS * HALF, width), bf16),
        pltpu.VMEM((width, 2 * markers), bf16),
        pltpu.VMEM((ROWS * HALF, 2 * markers), f32),
        pltpu.VMEM((4 * 4, HALF, markers), f32),
        pltpu.VMEM((2 * 3 * BX * HALF, markers), bf16),
        pltpu.VMEM((BY * BZ * HALF, markers), bf16),
        pltpu.VMEM((BY * BZ * HALF, markers), bf16),
    )
    visc, moments = pl.pallas_call(
        marker_body,
        out_shape=(
            jax.ShapeDtypeStruct((owners, parts, HALF, markers), f32),
            jax.ShapeDtypeStruct((owners, groups, ROWS, LANES), f32),
        ),
        in_specs=[pl.BlockSpec(memory_space=pltpu.SMEM)]
        + [whole] * 6
        + [pl.BlockSpec(memory_space=pl.ANY)],
        out_specs=(whole, whole),
        scratch_shapes=[
            pltpu.SMEM((2 * (owners * groups + TOGETHER),), jnp.int32),
            pltpu.VMEM((32 * TOGETHER, 2 * BY * BZ * HALF), f32),
        ]
        + [buffer for buffer in buffers for _ in range(2 * TOGETHER)],
        compiler_params=vmem_limit(60),
        cost_estimate=cost(25),
        name="marker_work",
    )(
        counts,
        spread,
        gather,
        positions.reshape(owners, 3, parts, HALF, markers),
        start_visc.reshape(owners, parts, HALF, markers),
        marker_dens.reshape(owners, parts, HALF, markers),
        bricks,
        after,
    )
    return visc.reshape(owners, slots, markers), moments


def settle_body(asked, moments_in, visc_in, dens_in, visc_out, dens_out, *scratch):
    moments, visc, dens, done, *tables = scratch
    size_x, size_y, size_z = visc.shape
    copies = [
        pltpu.make_async_copy(there, here, done.at[n])
        for n, (there, here) in enumerate(
            ((moments_in, moments), (visc_in, visc), (dens_in, dens))
        )
    ]
    for copy in copies:
        copy.start()
    bricks_y, halves = size_y // BY, size_z // LANES
    for table in tables:
        table[...] = jnp.zeros_like(table)
    copies[0].wait()
    groups = moments.shape[1]
    lane_slot = lax.broadcasted_iota(jnp.int32, (ROWS, LANES), 1) // BZ

    def one_group(step, carry):
        device, group = step // groups, step % groups
        packed = moments[device, group]
        for slot in range(GROUP):
            table = tables[slot % len(tables)]
            place, lane = place_of(asked[device, group * GROUP + slot])
            piece = jnp.where(lane_slot == slot, packed, 0.0)
            piece = pltpu.roll(piece, (lane - BZ * slot) & (LANES - 1), 1)
            table[place] = table[place] + piece
        return carry

    lax.fori_loop(0, moments.shape[0] * groups, one_group, 0)
    copies[1].wait()
    copies[2].wait()

    def finish(block_x, carry):
        for block_y in range(0, bricks_y, 2):
            for half in range(halves):
                for i in range(BX):
                    here = (
                        block_x * BX + i,
                        slice(block_y * BY, (block_y + 2) * BY),
                        slice(half * LANES, (half + 1) * LANES),
                    )
                    sums = []
                    for c in range(3):
                        rows = slice((c * BX + i) * BY, (c * BX + i + 1) * BY)
                        places = [
                            (block_x * bricks_y + block_y + k) * halves + half for k in range(2)
                        ]
                        sums.append(
                            jnp.concatenate(
                                [add_all([t[place, rows, :] for t in tables]) for place in places]
                            )
                        )
                    scale = 1.0 / (sums[0] + 1.0)
                    visc_out[here] = jnp.exp((sums[1] + jnp.log(visc[here])) * scale)
                    dens_out[here] = (sums[2] + dens[here]) * scale
        return carry

    lax.fori_loop(0, size_x // BX, finish, 0)


def settle(asked, moments, cell_visc, cell_dens):
    size_x, size_y, size_z = cell_visc.shape
    places = (size_x // BX) * (size_y // BY) * (size_z // LANES)
    whole = pl.BlockSpec(memory_space=pltpu.VMEM)
    shape = jax.ShapeDtypeStruct(cell_visc.shape, f32)
    return pl.pallas_call(
        settle_body,
        out_shape=(shape, shape),
        in_specs=[pl.BlockSpec(memory_space=pltpu.SMEM)]
        + [pl.BlockSpec(memory_space=pl.ANY)] * 3,
        out_specs=(whole, whole),
        scratch_shapes=[
            pltpu.VMEM(moments.shape, f32),
            pltpu.VMEM(cell_visc.shape, f32),
            pltpu.VMEM(cell_visc.shape, f32),
            pltpu.SemaphoreType.DMA((3,)),
        ]
        + [pltpu.VMEM((places, ROWS, LANES), f32)] * 2,
        compiler_params=vmem_limit(24),
        cost_estimate=cost(7),
        name="settle",
    )(asked, moments, cell_visc, cell_dens)


def field_of(fields, index):
    return fields[0].at[index] if index < 3 else fields[index - 2]


def pack_x_body(*refs):
    ends, outs = refs[:8], refs[8:]
    for side in range(2):
        for f in range(6):
            outs[side][f] = field_of(ends[side::2], f)[...]


def pack_x(velocity, pressure, cell_visc, cell_dens):
    size_x, size_y, size_z = cell_visc.shape
    width = SWEEPS
    ends = (0, size_x // width - 1)
    vel = [
        pl.BlockSpec((3, width, size_y, size_z), lambda i, e=e: (0, e, 0, 0)) for e in ends
    ]
    block = [pl.BlockSpec((width, size_y, size_z), lambda i, e=e: (e, 0, 0)) for e in ends]
    whole = pl.BlockSpec((6, width, size_y, size_z), lambda i: (0, 0, 0, 0))
    shape = jax.ShapeDtypeStruct((6, width, size_y, size_z), f32)
    return pl.pallas_call(
        pack_x_body,
        grid=(1,),
        out_shape=(shape, shape),
        in_specs=vel + block * 3,
        out_specs=(whole, whole),
        compiler_params=vmem_limit(60),
        cost_estimate=cost(2),
        name="pack_x",
    )(velocity, velocity, pressure, pressure, cell_visc, cell_visc, cell_dens, cell_dens)


def corner_rows(upward, size_x):
    width = SWEEPS
    spare = (5 * width,) if upward else (4 * width - 1, 6 * width - 1)
    places = [(plane, row) for plane in range(size_x) for row in spare]
    found = []
    for field in range(6):
        for side in range(2):
            near = field == 5 or (field == 3 and side == 1 and not upward)
            reach = width - 1 if near else width
            for far_x in range(1, width):
                for far_y in range(1, reach - far_x + 1):
                    found.append((field, side, far_x, far_y))
    more = max(0, len(found) - len(places))
    places += [(size_x + n // (6 * width), n % (6 * width)) for n in range(more)]
    return [cell + at for cell, at in zip(found, places)], size_x + -(-more // (6 * width))


def pack_y_body(size_x, vel, pres, visc, dens, low_x, high_x, upward, downward):
    step_x, size_y, _ = pres.shape
    width = SWEEPS
    step = pl.program_id(0)
    planes = pl.ds(pl.multiple_of(step * step_x, step_x), step_x)
    for f in range(6):
        field = field_of((vel, pres, visc, dens), f)
        rows = slice(f * width, (f + 1) * width)
        upward[planes, rows, :] = field[:, size_y - width :, :]
        downward[planes, rows, :] = field[:, :width, :]

    @pl.when(step == pl.num_programs(0) - 1)
    def _():
        for up, face in ((True, upward), (False, downward)):
            for f, side, far_x, far_y, plane, row in corner_rows(up, size_x)[0]:
                halo, at = (high_x, far_x - 1) if side else (low_x, width - far_x)
                face[plane, row] = halo[f, at, size_y - far_y if up else far_y - 1]


def pack_y(velocity, pressure, cell_visc, cell_dens, low_x, high_x):
    size_x, size_y, size_z = cell_visc.shape
    step = 8
    block = pl.BlockSpec((step, size_y, size_z), lambda i: (i, 0, 0))
    halo = pl.BlockSpec(low_x.shape, lambda i: (0, 0, 0, 0))
    shapes = [(corner_rows(up, size_x)[1], 6 * SWEEPS, size_z) for up in (True, False)]
    return pl.pallas_call(
        functools.partial(pack_y_body, size_x),
        grid=(size_x // step,),
        out_shape=tuple(jax.ShapeDtypeStruct(shape, f32) for shape in shapes),
        in_specs=[
            pl.BlockSpec((3, step, size_y, size_z), lambda i: (0, i, 0, 0)),
            block,
            block,
            block,
            halo,
            halo,
        ],
        out_specs=tuple(pl.BlockSpec(shape, lambda i: (0, 0, 0)) for shape in shapes),
        compiler_params=vmem_limit(24),
        cost_estimate=cost(15),
        name="pack_y",
    )(velocity, pressure, cell_visc, cell_dens, low_x, high_x)


def place(per, x, y, rows):
    return x % per, pl.ds(y * SUBLANES + x // per, rows, stride=SUBLANES)


def put(target, x, y, rows, value):
    per, halves = target.shape[:2]
    plane, lines = place(per, x, y, rows)
    for half in range(halves):
        target[plane, half, lines, :] = value[:, half * LANES : (half + 1) * LANES]


def tile(y):
    if isinstance(y, int):
        return pl.ds(y * SUBLANES, SUBLANES)
    return pl.ds(pl.multiple_of(y * SUBLANES, SUBLANES), SUBLANES)


def row_work(cells, coefs, relax, forcing, rate):
    per, halves = cells.shape[1:3]
    lane = lax.broadcasted_iota(jnp.int32, (SUBLANES, LANES), 1)
    at_first, at_last = lane == 0, lane == LANES - 1

    def take(field, plane, y):
        return jnp.concatenate([field[plane, half, tile(y), :] for half in range(halves)], axis=1)

    def store(field, plane, y, value):
        for half in range(halves):
            field[plane, half, tile(y), :] = value[:, half * LANES : (half + 1) * LANES]

    def up_x(field, plane, y):
        if plane < per - 1:
            return take(field, plane + 1, y)
        return pltpu.roll(take(field, 0, y), SUBLANES - 1, 0)

    def down_x(field, plane, y):
        if plane > 0:
            return take(field, plane - 1, y)
        return pltpu.roll(take(field, per - 1, y), 1, 0)

    def rolled(a, shift):
        return [
            pltpu.roll(a[:, half * LANES : (half + 1) * LANES], shift, 1) for half in range(halves)
        ]

    def up_z(a):
        parts = rolled(a, LANES - 1)
        after = parts[1:] + [jnp.zeros_like(parts[0])]
        return jnp.concatenate([jnp.where(at_last, n, p) for p, n in zip(parts, after)], axis=1)

    def down_z(a):
        parts = rolled(a, 1)
        before = [jnp.zeros_like(parts[0])] + parts[:-1]
        return jnp.concatenate([jnp.where(at_first, b, p) for p, b in zip(parts, before)], axis=1)

    def prepare(y):
        visc, dens = cells.at[0], cells.at[1]
        for plane in range(per):
            here = take(visc, plane, y)
            near = [
                up_x(visc, plane, y),
                down_x(visc, plane, y),
                take(visc, plane, y + 1),
                take(visc, plane, y - 1),
                up_z(here),
                down_z(here),
            ]
            links = [0.5 * (here + other) for other in near]
            scale = jnp.where(here > 0.0, RELAX / add_all(links), 0.0)
            for n in range(6):
                coefs[n, plane, tile(y), :] = links[n] * scale
            relax[plane, tile(y), :] = scale
            forcing[plane, tile(y), :] = take(dens, plane, y) * (-GRAVITY * scale)
            rate[plane, tile(y), :] = PRESSURE_RATE * here

    def sweep(y, old, new):
        for plane in range(per):
            links = [coefs[n, plane, tile(y), :] for n in range(6)]
            scale = relax[plane, tile(y), :]
            pressure = take(old.at[3], plane, y)
            before = (
                down_x(old.at[3], plane, y),
                take(old.at[3], plane, y - 1),
                down_z(pressure),
            )
            changes = []
            for c in range(3):
                field = old.at[c]
                here = take(field, plane, y)
                near = [
                    up_x(field, plane, y),
                    down_x(field, plane, y),
                    take(field, plane, y + 1),
                    take(field, plane, y - 1),
                    up_z(here),
                    down_z(here),
                ]
                terms = [link * other for link, other in zip(links, near)]
                total = (terms[0] + terms[1]) + (terms[2] + terms[3])
                total = total + (terms[4] + terms[5])
                rest = (1.0 - RELAX) * here - scale * (pressure - before[c])
                if c == 2:
                    rest = rest + forcing[plane, tile(y), :]
                changes.append(near[2 * c] - here)
                store(new.at[c], plane, y, total + rest)
            pressed = pressure - rate[plane, tile(y), :] * add_all(changes)
            store(new.at[3], plane, y, pressed)

    return prepare, sweep


def kept_rows(size_y):
    width = SWEEPS
    return (
        ((width, size_y),),
        ((width + 1, width), (size_y - 1, width)),
        ((width, width + 1), (size_y - 1, width + 1)),
    )


def kept_copies(pairs, size_y, done):
    copies = []
    for (source, target), strips in zip(pairs, kept_rows(size_y)):
        for begin, rows in strips:
            span = (slice(None),) * 3 + (pl.ds(begin * SUBLANES, rows * SUBLANES),)
            copies.append(
                pltpu.make_async_copy(source.at[span], target.at[span], done.at[len(copies)])
            )
    return copies


def inner_body(vel, pres, visc, dens, low_x, high_x, _, even_out, odd_out, cells_out, *work):
    blocks, sides_x, even, odd, cells, coefs, relax, forcing, rate, done = work
    size_x, size_y, size_z = blocks.shape[1:]
    width = SWEEPS
    inputs = (
        (visc, blocks.at[4], (4,)),
        (vel, blocks.at[0:3], (0, 1, 2)),
        (pres, blocks.at[3], (3,)),
        (dens, blocks.at[5], (5,)),
        (low_x, sides_x.at[0], ()),
        (high_x, sides_x.at[1], ()),
    )
    copies = [
        pltpu.make_async_copy(there, here, done.at[n]) for n, (there, here, _) in enumerate(inputs)
    ]
    for copy in copies:
        copy.start()
    targets = [even.at[n] for n in range(4)] + [cells.at[n] for n in range(2)]
    for copy, (_, _, held) in zip(copies, inputs):
        copy.wait()
        for f in held:
            for i in range(size_x):
                for y in range(0, size_y, SUBLANES):
                    value = blocks[f, i, y : y + SUBLANES, :]
                    put(targets[f], i + width, y + width, SUBLANES, value)
    for side, begin in enumerate((0, width + size_x)):
        for f in range(6):
            for i in range(width):
                for y in range(0, size_y, SUBLANES):
                    value = sides_x[side, f, i, y : y + SUBLANES, :]
                    put(targets[f], begin + i, y + width, SUBLANES, value)

    prepare, sweep = row_work(cells, coefs, relax, forcing, rate)

    def prepare_row(y, carry):
        prepare(y)
        return carry

    first, last = width + 1, width + size_y - 1
    lax.fori_loop(first, last, prepare_row, 0, unroll=2)
    for step in range(SWEEPS):
        old, new = (odd, even) if step % 2 else (even, odd)

        def sweep_row(y, carry, old=old, new=new):
            sweep(y, old, new)
            return carry

        lax.fori_loop(first + step, last - step, sweep_row, 0, unroll=2)
    sends = kept_copies(((even, even_out), (odd, odd_out), (cells, cells_out)), size_y, done)
    for send in sends:
        send.start()
    for send in sends:
        send.wait()


def inner_sweeps(velocity, pressure, cell_visc, cell_dens, low_x, high_x, after):
    size_x, size_y, size_z = cell_visc.shape
    width = low_x.shape[1]
    per, rows = (size_x + 2 * width) // SUBLANES, (size_y + 2 * width) * SUBLANES
    block, cut = (per, rows, size_z), (per, size_z // LANES, rows, LANES)
    shapes = [(4,) + cut, (4,) + cut, (2,) + cut]
    anywhere = pl.BlockSpec(memory_space=pl.ANY)
    return pl.pallas_call(
        inner_body,
        out_shape=tuple(jax.ShapeDtypeStruct(shape, f32) for shape in shapes),
        in_specs=[anywhere] * 7,
        out_specs=(anywhere,) * 3,
        scratch_shapes=[
            pltpu.VMEM((6,) + cell_visc.shape, f32),
            pltpu.VMEM((2,) + low_x.shape, f32),
        ]
        + [pltpu.VMEM(shape, f32) for shape in shapes]
        + [
            pltpu.VMEM((6,) + block, f32),
            pltpu.VMEM(block, f32),
            pltpu.VMEM(block, f32),
            pltpu.VMEM(block, f32),
            pltpu.SemaphoreType.DMA((6,)),
        ],
        compiler_params=vmem_limit(40),
        cost_estimate=cost(25),
        name="inner_sweeps",
    )(velocity, pressure, cell_visc, cell_dens, low_x, high_x, after)


def edge_body(even_in, odd_in, cells_in, low_y, high_y, vel_out, pres_out, *work):
    from_low, from_high, results, even, odd, cells, coefs, relax, forcing, rate, done, more = work
    size_x, size_y, size_z = results.shape[1:]
    width = SWEEPS
    long_y = size_y + 2 * width
    halos = [
        pltpu.make_async_copy(low_y, from_low, more.at[0]),
        pltpu.make_async_copy(high_y, from_high, more.at[1]),
    ]
    kept = kept_copies(((even_in, even), (odd_in, odd), (cells_in, cells)), size_y, done)
    for copy in (*halos, *kept[3:], *kept[:3]):
        copy.start()
    targets = [even.at[n] for n in range(4)] + [cells.at[n] for n in range(2)]
    for target in targets:
        for x in (*range(width), *range(width + size_x, size_x + 2 * width)):
            for y in (0, width + size_y):
                put(target, x, y, width, jnp.zeros((width, size_z), f32))
    for up, halo, copy, begin in (
        (True, from_low, halos[0], 0),
        (False, from_high, halos[1], width + size_y),
    ):
        copy.wait()
        for f, target in enumerate(targets):
            rows = slice(f * width, (f + 1) * width)
            for i in range(size_x):
                put(target, i + width, begin, width, halo[i, rows, :])
        for f, side, far_x, far_y, plane, row in corner_rows(up, size_x)[0]:
            x = width + size_x - 1 + far_x if side else width - far_x
            y = width - far_y if up else width + size_y - 1 + far_y
            put(targets[f], x, y, 1, halo[plane, row : row + 1, :])
    for copy in kept:
        copy.wait()

    prepare, sweep = row_work(cells, coefs, relax, forcing, rate)

    def prepare_rows(n, carry):
        prepare(1 + n)
        prepare(long_y - 2 * width + n)
        return carry

    lax.fori_loop(0, 2 * width - 1, prepare_rows, 0)
    for step in range(SWEEPS):
        old, new = (odd, even) if step % 2 else (even, odd)

        def sweep_rows(n, carry, old=old, new=new, step=step):
            sweep(1 + step + n, old, new)
            sweep(width + size_y - 1 - step + n, old, new)
            return carry

        lax.fori_loop(0, width, sweep_rows, 0)

    final = odd if SWEEPS % 2 else even
    outs = [vel_out.at[0], vel_out.at[1], vel_out.at[2], pres_out]
    sends = [pltpu.make_async_copy(results.at[n], out, done.at[n]) for n, out in enumerate(outs)]
    per, halves = even.shape[1:3]
    for field, send in enumerate(sends):
        for i in range(size_x):
            for y in range(0, size_y, SUBLANES):
                plane, lines = place(per, i + width, y + width, SUBLANES)
                for half in range(halves):
                    columns = slice(half * LANES, (half + 1) * LANES)
                    results[field, i, y : y + SUBLANES, columns] = final[
                        field, plane, half, lines, :
                    ]
        send.start()
    for send in sends:
        send.wait()


def edge_sweeps(even, odd, cells, low_y, high_y, size_x, size_y):
    per, halves, rows = even.shape[1:4]
    size_z = halves * LANES
    block = (per, rows, size_z)
    anywhere = pl.BlockSpec(memory_space=pl.ANY)
    return pl.pallas_call(
        edge_body,
        out_shape=(
            jax.ShapeDtypeStruct((3, size_x, size_y, size_z), f32),
            jax.ShapeDtypeStruct((size_x, size_y, size_z), f32),
        ),
        in_specs=[anywhere] * 5,
        out_specs=(anywhere,) * 2,
        scratch_shapes=[
            pltpu.VMEM(low_y.shape, f32),
            pltpu.VMEM(high_y.shape, f32),
            pltpu.VMEM((4, size_x, size_y, size_z), f32),
            pltpu.VMEM(even.shape, f32),
            pltpu.VMEM(odd.shape, f32),
            pltpu.VMEM(cells.shape, f32),
            pltpu.VMEM((6,) + block, f32),
            pltpu.VMEM(block, f32),
            pltpu.VMEM(block, f32),
            pltpu.VMEM(block, f32),
            pltpu.SemaphoreType.DMA((5,)),
            pltpu.SemaphoreType.DMA((2,)),
        ],
        compiler_params=vmem_limit(40),
        cost_estimate=cost(1),
        name="edge_sweeps",
    )(even, odd, cells, low_y, high_y)


def shift(value, axis, step):
    size = lax.axis_size(axis)
    pairs = [(i, i + step) for i in range(size) if 0 <= i + step < size]
    return lax.ppermute(value, axis, pairs)


def per_device(
    velocity,
    pressure,
    cell_visc,
    cell_dens,
    block_brick,
    block_counts,
    positions,
    start_visc,
    marker_dens,
):
    asked = lax.all_to_all(block_brick, "mark", 0, 0, tiled=True)
    fields = (velocity, pressure, cell_visc, cell_dens)
    to_low, to_high = pack_x(*fields)
    low_x, high_x = shift(to_high, "grid", 1), shift(to_low, "grid", -1)
    upward, downward = pack_y(*fields, low_x, high_x)
    low_y, high_y = shift(upward, "mark", 1), shift(downward, "mark", -1)

    picked = pick_bricks(asked, velocity)
    bricks = lax.all_to_all(picked, "mark", 0, 0, tiled=True)
    marker_visc, moments = marker_work(
        block_counts, positions, start_visc, marker_dens, bricks, upward
    )
    gathered = lax.all_to_all(moments, "mark", 0, 0, tiled=True)
    state = inner_sweeps(*fields, low_x, high_x, moments)
    velocity_next, pressure_next = edge_sweeps(*state, low_y, high_y, *pressure.shape[:2])
    visc_next, dens_next = settle(asked, gathered, cell_visc, cell_dens)
    return velocity_next, pressure_next, visc_next, dens_next, marker_visc


def solution(mesh):
    in_specs = (
        P(None, "grid", "mark", None),
        P("grid", "mark", None),
        P("grid", "mark", None),
        P("grid", "mark", None),
        P(("grid", "mark"), None),
        P(("grid", "mark"), None),
        P(("grid", "mark"), None, None, None),
        P(("grid", "mark"), None, None),
        P(("grid", "mark"), None, None),
    )
    out_specs = (
        P(None, "grid", "mark", None),
        P("grid", "mark", None),
        P("grid", "mark", None),
        P("grid", "mark", None),
        P(("grid", "mark"), None, None),
    )
    return jax.shard_map(
        per_device, mesh=mesh, in_specs=in_specs, out_specs=out_specs, check_vma=False
    )
```

```python
import functools

import jax
import jax.numpy as jnp
import numpy as np
from jax import lax
from jax.experimental import pallas as pl
from jax.experimental.pallas import tpu as pltpu
from jax.sharding import PartitionSpec as P

SWEEPS = 4
RELAX = 0.6
PRESSURE_RATE = 0.25
GRAVITY = 1.0
STRAIN_SCALE = 0.5

BX, BY, BZ = 4, 4, 8
PLANE = BX * BY
ROWS = 3 * PLANE
LANES = 128
GROUP = LANES // BZ
HALF = 8
SUBLANES = 8

f32, bf16 = jnp.float32, jnp.bfloat16


def vmem_limit(mib):
    return pltpu.CompilerParams(vmem_limit_bytes=mib * 1024 * 1024)


def in_hbm(*arrays):
    return [pltpu.with_memory_space_constraint(array, pltpu.HBM) for array in arrays]


def cost(microseconds):
    return pl.CostEstimate(
        flops=int(microseconds * 1.15e9), bytes_accessed=0, transcendentals=0
    )


def place_of(brick):
    return lax.shift_right_logical(brick, GROUP.bit_length() - 1), (brick & (GROUP - 1)) * BZ


def pick_body(asked, vel, out, table):
    size_x, size_y, size_z = vel.shape[1:]
    bricks_y, halves = size_y // BY, size_z // LANES

    def repack(block_x, carry):
        for block_y in range(bricks_y):
            for half in range(halves):
                place = (block_x * bricks_y + block_y) * halves + half
                for c in range(3):
                    for i in range(BX):
                        row = (c * BX + i) * BY
                        table[place, row : row + BY, :] = vel[
                            c,
                            block_x * BX + i,
                            block_y * BY : (block_y + 1) * BY,
                            half * LANES : (half + 1) * LANES,
                        ]
        return carry

    lax.fori_loop(0, size_x // BX, repack, 0)
    groups = out.shape[1]
    lane_slot = lax.broadcasted_iota(jnp.int32, (ROWS, LANES), 1) // BZ

    def one_group(step, carry):
        device, group = step // groups, step % groups
        packed = jnp.zeros((ROWS, LANES), f32)
        for slot in range(GROUP):
            place, lane = place_of(asked[device, group * GROUP + slot])
            rolled = pltpu.roll(table[place], (BZ * slot - lane) & (LANES - 1), 1)
            packed = jnp.where(lane_slot == slot, rolled, packed)
        out[device, group] = packed
        return carry

    lax.fori_loop(0, out.shape[0] * groups, one_group, 0)


def pick_bricks(asked, velocity):
    devices, slots = asked.shape
    size_x, size_y, size_z = velocity.shape[1:]
    places = (size_x // BX) * (size_y // BY) * (size_z // LANES)
    return pl.pallas_call(
        pick_body,
        out_shape=jax.ShapeDtypeStruct((devices, slots // GROUP, ROWS, LANES), f32),
        in_specs=[
            pl.BlockSpec(memory_space=pltpu.SMEM),
            pl.BlockSpec(memory_space=pltpu.VMEM),
        ],
        out_specs=pl.BlockSpec(memory_space=pltpu.VMEM),
        scratch_shapes=[pltpu.VMEM((places, ROWS, LANES), f32)],
        compiler_params=vmem_limit(24),
        cost_estimate=cost(25),
        name="pick_bricks",
    )(asked, velocity)


def permutations():
    inside = BZ * HALF
    spread = np.zeros((2, 2, LANES, 4 * inside), np.float32)
    gather = np.zeros((2 * BY * inside, BY * LANES), np.float32)
    for half in range(2):
        for slot in range(HALF):
            for z in range(BZ):
                outer, inner = (half * HALF + slot) * BZ + z, z * HALF + slot
                for part in range(4):
                    spread[half, part // 2, outer, part * inside + inner] = 1
                for j in range(BY):
                    gather[(half * BY + j) * inside + inner, j * LANES + outer] = 1
    return jnp.asarray(spread, bf16), jnp.asarray(gather, bf16)


def split(value):
    high = value.astype(bf16)
    return high, (value - high.astype(f32)).astype(bf16)


def add_all(values):
    return functools.reduce(jnp.add, values)


def axis_weights(fraction, cells):
    middle = (cells - 1) / 2
    base = jnp.exp(fraction * (2.0 * cells) - float(cells))
    powers = [None, base]
    for i in range(2, cells):
        powers.append(powers[i // 2] * powers[i - i // 2])
    factors = [float(np.exp(middle**2 - (i - middle) ** 2)) for i in range(cells)]
    bells = [None] + [powers[i] * factors[i] for i in range(1, cells)]
    scale = 1.0 / (add_all(bells[1:]) + factors[0])
    weights = [scale * factors[0]] + [bell * scale for bell in bells[1:]]
    mean = add_all(
        [
            (weights[cells - 1 - i] - weights[i]) * (2.0 * (middle - i))
            for i in range(cells // 2)
        ]
    )
    slopes = [w * (2.0 * (i - middle) - mean) for i, w in enumerate(weights)]
    return weights, slopes


def dot(a, b):
    return jnp.dot(a, b, preferred_element_type=f32)


def gradients(products, weights, markers):
    weight_x, slope_x, weight_y, slope_y = ([weights[4 * n + i] for i in range(4)] for n in range(4))
    grads = []
    for c in range(3):
        lines = [[], [], []]
        for i in range(BX):
            rows = [((c * BX + i) * BY + j) * HALF for j in range(BY)]
            still = [products[row : row + HALF, :markers] for row in rows]
            rising = [products[row : row + HALF, markers:] for row in rows]
            lines[0].append(slope_x[i] * add_all([w * t for w, t in zip(weight_y, still)]))
            lines[1].append(weight_x[i] * add_all([w * t for w, t in zip(slope_y, still)]))
            lines[2].append(weight_x[i] * add_all([w * t for w, t in zip(weight_y, rising)]))
        grads.append([add_all(line) for line in lines])
    return grads


def own_lanes():
    shape = (HALF, 4 * BZ * HALF)
    lane = lax.broadcasted_iota(jnp.int32, shape, 1)
    return (lane % HALF == lax.broadcasted_iota(jnp.int32, shape, 0)).astype(f32)


def marker_groups(groups, counts, ins, outs, buffers, sums):
    spread, gather, places, start, dens, brick = ins
    visc_out, moments_out = outs
    permuted, left, right, products, weights, factors, planes_high, planes_low = buffers
    markers = places.shape[-1]
    inside = BZ * HALF
    own = own_lanes()
    halves = [
        (owner, 2 * group + half, half, 2 * n + half)
        for n, (owner, group) in enumerate(groups)
        for half in range(2)
    ]
    parts = [split(brick[owner, group]) for owner, group in groups]
    for _, _, half, n in halves:
        high, low = parts[n // 2]
        permuted[n][...] = dot(high, spread[half, 0]) + dot(low, spread[half, 1])
    heights = []
    for owner, part, _, n in halves:
        weight_z, slope_z = axis_weights(places[owner, 2, part], BZ)
        heights.append(weight_z)
        for z in range(0, BZ, 2):
            for column, values in ((0, weight_z), (1, slope_z)):
                high, low = split(jnp.concatenate(values[z : z + 2], axis=0))
                columns = slice(column * markers, (column + 1) * markers)
                for k in range(4):
                    begin = k * inside + z * HALF
                    right[n][begin : begin + 2 * HALF, columns] = low if k % 2 else high
    for _, _, _, n in halves:
        for row in range(0, ROWS, 2):
            pair = [
                jnp.broadcast_to(permuted[n][r : r + 1, :], own.shape) * own for r in (row, row + 1)
            ]
            left[n][row * HALF : (row + 2) * HALF, :] = jnp.concatenate(pair, axis=0).astype(bf16)
    for _, _, _, n in halves:
        products[n][...] = dot(left[n][...], right[n][...])
    for owner, part, _, n in halves:
        weights_x = axis_weights(places[owner, 0, part], BX)
        weights_y = axis_weights(places[owner, 1, part], BY)
        for k, values in enumerate((*weights_x, *weights_y)):
            for i, value in enumerate(values):
                weights[n][4 * k + i] = value
        for j in range(BY):
            for z in range(0, BZ, 2):
                pair = [weights_y[0][j] * heights[n][z + k] for k in range(2)]
                rows = slice((j * BZ + z) * HALF, (j * BZ + z + 2) * HALF)
                high, low = split(jnp.concatenate(pair, axis=0))
                planes_high[n][rows, :] = high
                planes_low[n][rows, :] = low

    count = 3 * BX * HALF
    for owner, part, _, n in halves:
        grads = gradients(products[n], weights[n], markers)
        normal = grads[0][0] ** 2 + grads[1][1] ** 2 + grads[2][2] ** 2
        shear_xy = 0.5 * (grads[0][1] + grads[1][0])
        shear_xz = 0.5 * (grads[0][2] + grads[2][0])
        shear_yz = 0.5 * (grads[1][2] + grads[2][1])
        invariant = 0.5 * normal + shear_xy**2 + shear_xz**2 + shear_yz**2
        scaled = invariant * (1.0 / (STRAIN_SCALE * STRAIN_SCALE))
        third = jnp.log(1.0 + scaled) * (1.0 / 3.0)
        first = start[owner, part]
        slot = lax.broadcasted_iota(jnp.int32, first.shape, 0) + part * HALF
        live = slot < counts[0, owner]
        visc_out[owner, part] = jnp.where(live, first * jnp.exp(-third), 0.0)
        carried = (
            live.astype(f32),
            jnp.where(live, jnp.log(first) - third, 0.0),
            jnp.where(live, dens[owner, part], 0.0),
        )
        for c in range(3):
            for i in range(0, BX, 2):
                pair = [carried[c] * weights[n][i + k] for k in range(2)]
                row = (c * BX + i) * HALF
                high, low = split(jnp.concatenate(pair, axis=0))
                factors[n][row : row + 2 * HALF, :] = high
                factors[n][count + row : count + row + 2 * HALF, :] = low

    contract = (((1,), (1,)), ((), ()))
    found = []
    for _, _, _, n in halves:
        both = lax.dot_general(
            factors[n][...], planes_high[n][...], contract, preferred_element_type=f32
        )
        rest = lax.dot_general(
            factors[n][:count], planes_low[n][...], contract, preferred_element_type=f32
        )
        found.append((both, rest))
    for _, _, half, n in halves:
        both, rest = found[n]
        total = both[:count] + both[count:] + rest
        chosen = total.reshape(3 * BX, HALF, BY * inside) * own[None]
        high, low = split(jnp.sum(chosen, axis=1))
        columns = slice(half * BY * inside, (half + 1) * BY * inside)
        row = (n // 2) * 32
        sums[row : row + 3 * BX, columns] = high.astype(f32)
        sums[row + 16 : row + 16 + 3 * BX, columns] = low.astype(f32)
    moved = dot(sums[...].astype(bf16), gather[...])
    for n, (owner, group) in enumerate(groups):
        mine = moved[32 * n : 32 * n + 3 * BX] + moved[32 * n + 16 : 32 * n + 16 + 3 * BX]
        for j in range(BY):
            rows = pl.ds(j, 3 * BX, stride=BY)
            moments_out[owner, group, rows, :] = mine[:, j * LANES : (j + 1) * LANES]


TOGETHER = 2


def marker_body(counts, *refs):
    ins, outs, scratch = refs[:6], refs[7:9], refs[9:]
    listed, sums, *flat = scratch
    held = 2 * TOGETHER
    buffers = [flat[n * held : (n + 1) * held] for n in range(len(flat) // held)]
    visc_out, moments_out = outs
    owners, groups = moments_out.shape[:2]
    visc_out[...] = jnp.zeros_like(visc_out)
    moments_out[...] = jnp.zeros_like(moments_out)
    sums[...] = jnp.zeros_like(sums)

    def list_groups(index, number):
        owner, group = index // groups, index % groups
        live = group * GROUP < counts[0, owner]

        @pl.when(live)
        def _():
            for n in range(TOGETHER):
                listed[2 * (number + n)] = owner
                listed[2 * (number + n) + 1] = group

        return jnp.where(live, number + 1, number)

    number = lax.fori_loop(0, owners * groups, list_groups, 0)

    def step(index, carry):
        first = TOGETHER * index
        taken = [
            (listed[2 * (first + n)], listed[2 * (first + n) + 1]) for n in range(TOGETHER)
        ]
        marker_groups(taken, counts, ins, outs, buffers, sums)
        return carry

    lax.fori_loop(0, (number + TOGETHER - 1) // TOGETHER, step, 0)


def marker_work(counts, positions, start_visc, marker_dens, bricks, after):
    owners, _, slots, markers = positions.shape
    groups, parts = slots // GROUP, slots // HALF
    spread, gather = permutations()
    width = 4 * BZ * HALF
    whole = pl.BlockSpec(memory_space=pltpu.VMEM)
    buffers = (
        pltpu.VMEM((ROWS, width), f32),
        pltpu.VMEM((ROWS * HALF, width), bf16),
        pltpu.VMEM((width, 2 * markers), bf16),
        pltpu.VMEM((ROWS * HALF, 2 * markers), f32),
        pltpu.VMEM((4 * 4, HALF, markers), f32),
        pltpu.VMEM((2 * 3 * BX * HALF, markers), bf16),
        pltpu.VMEM((BY * BZ * HALF, markers), bf16),
        pltpu.VMEM((BY * BZ * HALF, markers), bf16),
    )
    visc, moments = pl.pallas_call(
        marker_body,
        out_shape=(
            jax.ShapeDtypeStruct((owners, parts, HALF, markers), f32),
            jax.ShapeDtypeStruct((owners, groups, ROWS, LANES), f32),
        ),
        in_specs=[pl.BlockSpec(memory_space=pltpu.SMEM)]
        + [whole] * 6
        + [pl.BlockSpec(memory_space=pl.ANY)],
        out_specs=(whole, whole),
        scratch_shapes=[
            pltpu.SMEM((2 * (owners * groups + TOGETHER),), jnp.int32),
            pltpu.VMEM((32 * TOGETHER, 2 * BY * BZ * HALF), f32),
        ]
        + [buffer for buffer in buffers for _ in range(2 * TOGETHER)],
        compiler_params=vmem_limit(40),
        cost_estimate=cost(25),
        name="marker_work",
    )(
        counts,
        *in_hbm(
            spread,
            gather,
            positions.reshape(owners, 3, parts, HALF, markers),
            start_visc.reshape(owners, parts, HALF, markers),
            marker_dens.reshape(owners, parts, HALF, markers),
            bricks,
        ),
        after,
    )
    return visc.reshape(owners, slots, markers), moments


def settle_body(asked, moments_in, visc_in, dens_in, visc_out, dens_out, *scratch):
    moments, visc, dens, done, *tables = scratch
    size_x, size_y, size_z = visc.shape
    copies = [
        pltpu.make_async_copy(there, here, done.at[n])
        for n, (there, here) in enumerate(
            ((moments_in, moments), (visc_in, visc), (dens_in, dens))
        )
    ]
    for copy in copies:
        copy.start()
    bricks_y, halves = size_y // BY, size_z // LANES
    for table in tables:
        table[...] = jnp.zeros_like(table)
    copies[0].wait()
    groups = moments.shape[1]
    lane_slot = lax.broadcasted_iota(jnp.int32, (ROWS, LANES), 1) // BZ

    def one_group(step, carry):
        device, group = step // groups, step % groups
        packed = moments[device, group]
        for slot in range(GROUP):
            table = tables[slot % len(tables)]
            place, lane = place_of(asked[device, group * GROUP + slot])
            piece = jnp.where(lane_slot == slot, packed, 0.0)
            piece = pltpu.roll(piece, (lane - BZ * slot) & (LANES - 1), 1)
            table[place] = table[place] + piece
        return carry

    lax.fori_loop(0, moments.shape[0] * groups, one_group, 0)
    copies[1].wait()
    copies[2].wait()

    def finish(block_x, carry):
        for block_y in range(0, bricks_y, 2):
            for half in range(halves):
                for i in range(BX):
                    here = (
                        block_x * BX + i,
                        slice(block_y * BY, (block_y + 2) * BY),
                        slice(half * LANES, (half + 1) * LANES),
                    )
                    sums = []
                    for c in range(3):
                        rows = slice((c * BX + i) * BY, (c * BX + i + 1) * BY)
                        places = [
                            (block_x * bricks_y + block_y + k) * halves + half for k in range(2)
                        ]
                        sums.append(
                            jnp.concatenate(
                                [add_all([t[place, rows, :] for t in tables]) for place in places]
                            )
                        )
                    scale = 1.0 / (sums[0] + 1.0)
                    visc_out[here] = jnp.exp((sums[1] + jnp.log(visc[here])) * scale)
                    dens_out[here] = (sums[2] + dens[here]) * scale
        return carry

    lax.fori_loop(0, size_x // BX, finish, 0)


def settle(asked, moments, cell_visc, cell_dens):
    size_x, size_y, size_z = cell_visc.shape
    places = (size_x // BX) * (size_y // BY) * (size_z // LANES)
    whole = pl.BlockSpec(memory_space=pltpu.VMEM)
    shape = jax.ShapeDtypeStruct(cell_visc.shape, f32)
    return pl.pallas_call(
        settle_body,
        out_shape=(shape, shape),
        in_specs=[pl.BlockSpec(memory_space=pltpu.SMEM)]
        + [pl.BlockSpec(memory_space=pl.ANY)] * 3,
        out_specs=(whole, whole),
        scratch_shapes=[
            pltpu.VMEM(moments.shape, f32),
            pltpu.VMEM(cell_visc.shape, f32),
            pltpu.VMEM(cell_visc.shape, f32),
            pltpu.SemaphoreType.DMA((3,)),
        ]
        + [pltpu.VMEM((places, ROWS, LANES), f32)] * 2,
        compiler_params=vmem_limit(24),
        cost_estimate=cost(7),
        name="settle",
    )(asked, *in_hbm(moments, cell_visc, cell_dens))


def field_of(fields, index):
    return fields[0].at[index] if index < 3 else fields[index - 2]


def pack_x_body(*refs):
    ends, outs = refs[:8], refs[8:]
    for side in range(2):
        for f in range(6):
            outs[side][f] = field_of(ends[side::2], f)[...]


def pack_x(velocity, pressure, cell_visc, cell_dens):
    size_x, size_y, size_z = cell_visc.shape
    width = SWEEPS
    ends = (0, size_x // width - 1)
    vel = [
        pl.BlockSpec((3, width, size_y, size_z), lambda i, e=e: (0, e, 0, 0)) for e in ends
    ]
    block = [pl.BlockSpec((width, size_y, size_z), lambda i, e=e: (e, 0, 0)) for e in ends]
    whole = pl.BlockSpec((6, width, size_y, size_z), lambda i: (0, 0, 0, 0))
    shape = jax.ShapeDtypeStruct((6, width, size_y, size_z), f32)
    return pl.pallas_call(
        pack_x_body,
        grid=(1,),
        out_shape=(shape, shape),
        in_specs=vel + block * 3,
        out_specs=(whole, whole),
        compiler_params=vmem_limit(60),
        cost_estimate=cost(2),
        name="pack_x",
    )(velocity, velocity, pressure, pressure, cell_visc, cell_visc, cell_dens, cell_dens)


def corner_rows(upward, size_x):
    width = SWEEPS
    spare = (5 * width,) if upward else (4 * width - 1, 6 * width - 1)
    places = [(plane, row) for plane in range(size_x) for row in spare]
    found = []
    for field in range(6):
        for side in range(2):
            near = field == 5 or (field == 3 and side == 1 and not upward)
            reach = width - 1 if near else width
            for far_x in range(1, width):
                for far_y in range(1, reach - far_x + 1):
                    found.append((field, side, far_x, far_y))
    more = max(0, len(found) - len(places))
    places += [(size_x + n // (6 * width), n % (6 * width)) for n in range(more)]
    return [cell + at for cell, at in zip(found, places)], size_x + -(-more // (6 * width))


def pack_y_body(size_x, vel, pres, visc, dens, low_x, high_x, upward, downward):
    step_x, size_y, _ = pres.shape
    width = SWEEPS
    step = pl.program_id(0)
    planes = pl.ds(pl.multiple_of(step * step_x, step_x), step_x)
    for f in range(6):
        field = field_of((vel, pres, visc, dens), f)
        rows = slice(f * width, (f + 1) * width)
        upward[planes, rows, :] = field[:, size_y - width :, :]
        downward[planes, rows, :] = field[:, :width, :]

    @pl.when(step == pl.num_programs(0) - 1)
    def _():
        for up, face in ((True, upward), (False, downward)):
            for f, side, far_x, far_y, plane, row in corner_rows(up, size_x)[0]:
                halo, at = (high_x, far_x - 1) if side else (low_x, width - far_x)
                face[plane, row] = halo[f, at, size_y - far_y if up else far_y - 1]


def pack_y(velocity, pressure, cell_visc, cell_dens, low_x, high_x):
    size_x, size_y, size_z = cell_visc.shape
    step = 8
    block = pl.BlockSpec((step, size_y, size_z), lambda i: (i, 0, 0))
    halo = pl.BlockSpec(low_x.shape, lambda i: (0, 0, 0, 0))
    shapes = [(corner_rows(up, size_x)[1], 6 * SWEEPS, size_z) for up in (True, False)]
    return pl.pallas_call(
        functools.partial(pack_y_body, size_x),
        grid=(size_x // step,),
        out_shape=tuple(jax.ShapeDtypeStruct(shape, f32) for shape in shapes),
        in_specs=[
            pl.BlockSpec((3, step, size_y, size_z), lambda i: (0, i, 0, 0)),
            block,
            block,
            block,
            halo,
            halo,
        ],
        out_specs=tuple(pl.BlockSpec(shape, lambda i: (0, 0, 0)) for shape in shapes),
        compiler_params=vmem_limit(24),
        cost_estimate=cost(15),
        name="pack_y",
    )(*in_hbm(velocity, pressure, cell_visc, cell_dens), low_x, high_x)


def place(per, x, y, rows):
    return x % per, pl.ds(y * SUBLANES + x // per, rows, stride=SUBLANES)


def put(target, x, y, rows, value):
    per, halves = target.shape[:2]
    plane, lines = place(per, x, y, rows)
    for half in range(halves):
        target[plane, half, lines, :] = value[:, half * LANES : (half + 1) * LANES]


def tile(y):
    if isinstance(y, int):
        return pl.ds(y * SUBLANES, SUBLANES)
    return pl.ds(pl.multiple_of(y * SUBLANES, SUBLANES), SUBLANES)


def row_work(cells, coefs, relax, forcing, rate):
    per, halves = cells.shape[1:3]
    lane = lax.broadcasted_iota(jnp.int32, (SUBLANES, LANES), 1)
    at_first, at_last = lane == 0, lane == LANES - 1

    def take(field, plane, y):
        return jnp.concatenate([field[plane, half, tile(y), :] for half in range(halves)], axis=1)

    def store(field, plane, y, value):
        for half in range(halves):
            field[plane, half, tile(y), :] = value[:, half * LANES : (half + 1) * LANES]

    def up_x(field, plane, y):
        if plane < per - 1:
            return take(field, plane + 1, y)
        return pltpu.roll(take(field, 0, y), SUBLANES - 1, 0)

    def down_x(field, plane, y):
        if plane > 0:
            return take(field, plane - 1, y)
        return pltpu.roll(take(field, per - 1, y), 1, 0)

    def rolled(a, shift):
        return [
            pltpu.roll(a[:, half * LANES : (half + 1) * LANES], shift, 1) for half in range(halves)
        ]

    def up_z(a):
        parts = rolled(a, LANES - 1)
        after = parts[1:] + [jnp.zeros_like(parts[0])]
        return jnp.concatenate([jnp.where(at_last, n, p) for p, n in zip(parts, after)], axis=1)

    def down_z(a):
        parts = rolled(a, 1)
        before = [jnp.zeros_like(parts[0])] + parts[:-1]
        return jnp.concatenate([jnp.where(at_first, b, p) for p, b in zip(parts, before)], axis=1)

    def prepare(y):
        visc, dens = cells.at[0], cells.at[1]
        for plane in range(per):
            here = take(visc, plane, y)
            near = [
                up_x(visc, plane, y),
                down_x(visc, plane, y),
                take(visc, plane, y + 1),
                take(visc, plane, y - 1),
                up_z(here),
                down_z(here),
            ]
            links = [0.5 * (here + other) for other in near]
            scale = jnp.where(here > 0.0, RELAX / add_all(links), 0.0)
            for n in range(6):
                coefs[n, plane, tile(y), :] = links[n] * scale
            relax[plane, tile(y), :] = scale
            forcing[plane, tile(y), :] = take(dens, plane, y) * (-GRAVITY * scale)
            rate[plane, tile(y), :] = PRESSURE_RATE * here

    def sweep(y, old, new):
        for plane in range(per):
            links = [coefs[n, plane, tile(y), :] for n in range(6)]
            scale = relax[plane, tile(y), :]
            pressure = take(old.at[3], plane, y)
            before = (
                down_x(old.at[3], plane, y),
                take(old.at[3], plane, y - 1),
                down_z(pressure),
            )
            changes = []
            for c in range(3):
                field = old.at[c]
                here = take(field, plane, y)
                near = [
                    up_x(field, plane, y),
                    down_x(field, plane, y),
                    take(field, plane, y + 1),
                    take(field, plane, y - 1),
                    up_z(here),
                    down_z(here),
                ]
                terms = [link * other for link, other in zip(links, near)]
                total = (terms[0] + terms[1]) + (terms[2] + terms[3])
                total = total + (terms[4] + terms[5])
                rest = (1.0 - RELAX) * here - scale * (pressure - before[c])
                if c == 2:
                    rest = rest + forcing[plane, tile(y), :]
                changes.append(near[2 * c] - here)
                store(new.at[c], plane, y, total + rest)
            pressed = pressure - rate[plane, tile(y), :] * add_all(changes)
            store(new.at[3], plane, y, pressed)

    return prepare, sweep


def kept_rows(size_y):
    width = SWEEPS
    return (
        ((width, size_y),),
        ((width + 1, width), (size_y - 1, width)),
        ((width, width + 1), (size_y - 1, width + 1)),
    )


def kept_copies(pairs, size_y, done):
    copies = []
    for (source, target), strips in zip(pairs, kept_rows(size_y)):
        for begin, rows in strips:
            span = (slice(None),) * 3 + (pl.ds(begin * SUBLANES, rows * SUBLANES),)
            copies.append(
                pltpu.make_async_copy(source.at[span], target.at[span], done.at[len(copies)])
            )
    return copies


def inner_body(vel, pres, visc, dens, low_x, high_x, _, even_out, odd_out, cells_out, *work):
    blocks, sides_x, even, odd, cells, coefs, relax, forcing, rate, done = work
    size_x, size_y, size_z = blocks.shape[1:]
    width = SWEEPS
    inputs = (
        (visc, blocks.at[4], (4,)),
        (vel, blocks.at[0:3], (0, 1, 2)),
        (pres, blocks.at[3], (3,)),
        (dens, blocks.at[5], (5,)),
        (low_x, sides_x.at[0], ()),
        (high_x, sides_x.at[1], ()),
    )
    copies = [
        pltpu.make_async_copy(there, here, done.at[n]) for n, (there, here, _) in enumerate(inputs)
    ]
    for copy in copies:
        copy.start()
    targets = [even.at[n] for n in range(4)] + [cells.at[n] for n in range(2)]
    for copy, (_, _, held) in zip(copies, inputs):
        copy.wait()
        for f in held:
            for i in range(size_x):
                for y in range(0, size_y, SUBLANES):
                    value = blocks[f, i, y : y + SUBLANES, :]
                    put(targets[f], i + width, y + width, SUBLANES, value)
    for side, begin in enumerate((0, width + size_x)):
        for f in range(6):
            for i in range(width):
                for y in range(0, size_y, SUBLANES):
                    value = sides_x[side, f, i, y : y + SUBLANES, :]
                    put(targets[f], begin + i, y + width, SUBLANES, value)

    prepare, sweep = row_work(cells, coefs, relax, forcing, rate)

    def prepare_row(y, carry):
        prepare(y)
        return carry

    first, last = width + 1, width + size_y - 1
    lax.fori_loop(first, last, prepare_row, 0, unroll=2)
    for step in range(SWEEPS):
        old, new = (odd, even) if step % 2 else (even, odd)

        def sweep_row(y, carry, old=old, new=new):
            sweep(y, old, new)
            return carry

        lax.fori_loop(first + step, last - step, sweep_row, 0, unroll=2)
    sends = kept_copies(((even, even_out), (odd, odd_out), (cells, cells_out)), size_y, done)
    for send in sends:
        send.start()
    for send in sends:
        send.wait()


def inner_sweeps(velocity, pressure, cell_visc, cell_dens, low_x, high_x, after):
    size_x, size_y, size_z = cell_visc.shape
    width = low_x.shape[1]
    per, rows = (size_x + 2 * width) // SUBLANES, (size_y + 2 * width) * SUBLANES
    block, cut = (per, rows, size_z), (per, size_z // LANES, rows, LANES)
    shapes = [(4,) + cut, (4,) + cut, (2,) + cut]
    anywhere = pl.BlockSpec(memory_space=pl.ANY)
    return pl.pallas_call(
        inner_body,
        out_shape=tuple(jax.ShapeDtypeStruct(shape, f32) for shape in shapes),
        in_specs=[anywhere] * 7,
        out_specs=(anywhere,) * 3,
        scratch_shapes=[
            pltpu.VMEM((6,) + cell_visc.shape, f32),
            pltpu.VMEM((2,) + low_x.shape, f32),
        ]
        + [pltpu.VMEM(shape, f32) for shape in shapes]
        + [
            pltpu.VMEM((6,) + block, f32),
            pltpu.VMEM(block, f32),
            pltpu.VMEM(block, f32),
            pltpu.VMEM(block, f32),
            pltpu.SemaphoreType.DMA((6,)),
        ],
        compiler_params=vmem_limit(40),
        cost_estimate=cost(25),
        name="inner_sweeps",
    )(*in_hbm(velocity, pressure, cell_visc, cell_dens), low_x, high_x, after)


def edge_body(even_in, odd_in, cells_in, low_y, high_y, vel_out, pres_out, *work):
    from_low, from_high, results, even, odd, cells, coefs, relax, forcing, rate, done, more = work
    size_x, size_y, size_z = results.shape[1:]
    width = SWEEPS
    long_y = size_y + 2 * width
    halos = [
        pltpu.make_async_copy(low_y, from_low, more.at[0]),
        pltpu.make_async_copy(high_y, from_high, more.at[1]),
    ]
    kept = kept_copies(((even_in, even), (odd_in, odd), (cells_in, cells)), size_y, done)
    for copy in (*halos, *kept[3:], *kept[:3]):
        copy.start()
    targets = [even.at[n] for n in range(4)] + [cells.at[n] for n in range(2)]
    for target in targets:
        for x in (*range(width), *range(width + size_x, size_x + 2 * width)):
            for y in (0, width + size_y):
                put(target, x, y, width, jnp.zeros((width, size_z), f32))
    for up, halo, copy, begin in (
        (True, from_low, halos[0], 0),
        (False, from_high, halos[1], width + size_y),
    ):
        copy.wait()
        for f, target in enumerate(targets):
            rows = slice(f * width, (f + 1) * width)
            for i in range(size_x):
                put(target, i + width, begin, width, halo[i, rows, :])
        for f, side, far_x, far_y, plane, row in corner_rows(up, size_x)[0]:
            x = width + size_x - 1 + far_x if side else width - far_x
            y = width - far_y if up else width + size_y - 1 + far_y
            put(targets[f], x, y, 1, halo[plane, row : row + 1, :])
    for copy in kept:
        copy.wait()

    prepare, sweep = row_work(cells, coefs, relax, forcing, rate)

    def prepare_rows(n, carry):
        prepare(1 + n)
        prepare(long_y - 2 * width + n)
        return carry

    lax.fori_loop(0, 2 * width - 1, prepare_rows, 0)
    for step in range(SWEEPS):
        old, new = (odd, even) if step % 2 else (even, odd)

        def sweep_rows(n, carry, old=old, new=new, step=step):
            sweep(1 + step + n, old, new)
            sweep(width + size_y - 1 - step + n, old, new)
            return carry

        lax.fori_loop(0, width, sweep_rows, 0)

    final = odd if SWEEPS % 2 else even
    outs = [vel_out.at[0], vel_out.at[1], vel_out.at[2], pres_out]
    sends = [pltpu.make_async_copy(results.at[n], out, done.at[n]) for n, out in enumerate(outs)]
    per, halves = even.shape[1:3]
    for field, send in enumerate(sends):
        for i in range(size_x):
            for y in range(0, size_y, SUBLANES):
                plane, lines = place(per, i + width, y + width, SUBLANES)
                for half in range(halves):
                    columns = slice(half * LANES, (half + 1) * LANES)
                    results[field, i, y : y + SUBLANES, columns] = final[
                        field, plane, half, lines, :
                    ]
        send.start()
    for send in sends:
        send.wait()


def edge_sweeps(even, odd, cells, low_y, high_y, size_x, size_y):
    per, halves, rows = even.shape[1:4]
    size_z = halves * LANES
    block = (per, rows, size_z)
    anywhere = pl.BlockSpec(memory_space=pl.ANY)
    return pl.pallas_call(
        edge_body,
        out_shape=(
            jax.ShapeDtypeStruct((3, size_x, size_y, size_z), f32),
            jax.ShapeDtypeStruct((size_x, size_y, size_z), f32),
        ),
        in_specs=[anywhere] * 5,
        out_specs=(anywhere,) * 2,
        scratch_shapes=[
            pltpu.VMEM(low_y.shape, f32),
            pltpu.VMEM(high_y.shape, f32),
            pltpu.VMEM((4, size_x, size_y, size_z), f32),
            pltpu.VMEM(even.shape, f32),
            pltpu.VMEM(odd.shape, f32),
            pltpu.VMEM(cells.shape, f32),
            pltpu.VMEM((6,) + block, f32),
            pltpu.VMEM(block, f32),
            pltpu.VMEM(block, f32),
            pltpu.VMEM(block, f32),
            pltpu.SemaphoreType.DMA((5,)),
            pltpu.SemaphoreType.DMA((2,)),
        ],
        compiler_params=vmem_limit(40),
        cost_estimate=cost(1),
        name="edge_sweeps",
    )(even, odd, cells, low_y, high_y)


def shift(value, axis, step):
    size = lax.axis_size(axis)
    pairs = [(i, i + step) for i in range(size) if 0 <= i + step < size]
    return lax.ppermute(value, axis, pairs)


def per_device(
    velocity,
    pressure,
    cell_visc,
    cell_dens,
    block_brick,
    block_counts,
    positions,
    start_visc,
    marker_dens,
):
    asked = lax.all_to_all(block_brick, "mark", 0, 0, tiled=True)
    fields = (velocity, pressure, cell_visc, cell_dens)
    to_low, to_high = pack_x(*fields)
    low_x, high_x = shift(to_high, "grid", 1), shift(to_low, "grid", -1)
    upward, downward = pack_y(*fields, low_x, high_x)
    low_y, high_y = shift(upward, "mark", 1), shift(downward, "mark", -1)

    picked = pick_bricks(asked, velocity)
    bricks = lax.all_to_all(picked, "mark", 0, 0, tiled=True)
    marker_visc, moments = marker_work(
        block_counts, positions, start_visc, marker_dens, bricks, upward
    )
    gathered = lax.all_to_all(moments, "mark", 0, 0, tiled=True)
    state = inner_sweeps(*fields, low_x, high_x, moments)
    velocity_next, pressure_next = edge_sweeps(*state, low_y, high_y, *pressure.shape[:2])
    visc_next, dens_next = settle(asked, gathered, cell_visc, cell_dens)
    return velocity_next, pressure_next, visc_next, dens_next, marker_visc


def solution(mesh):
    in_specs = (
        P(None, "grid", "mark", None),
        P("grid", "mark", None),
        P("grid", "mark", None),
        P("grid", "mark", None),
        P(("grid", "mark"), None),
        P(("grid", "mark"), None),
        P(("grid", "mark"), None, None, None),
        P(("grid", "mark"), None, None),
        P(("grid", "mark"), None, None),
    )
    out_specs = (
        P(None, "grid", "mark", None),
        P("grid", "mark", None),
        P("grid", "mark", None),
        P("grid", "mark", None),
        P(("grid", "mark"), None, None),
    )
    return jax.shard_map(
        per_device, mesh=mesh, in_specs=in_specs, out_specs=out_specs, check_vma=False
    )
```

```python
import functools

import jax
import jax.numpy as jnp
import numpy as np
from jax import lax
from jax.experimental import pallas as pl
from jax.experimental.pallas import tpu as pltpu
from jax.sharding import PartitionSpec as P

SWEEPS = 4
RELAX = 0.6
PRESSURE_RATE = 0.25
GRAVITY = 1.0
STRAIN_SCALE = 0.5

BX, BY, BZ = 4, 4, 8
PLANE = BX * BY
ROWS = 3 * PLANE
LANES = 128
GROUP = LANES // BZ
HALF = 8
SUBLANES = 8

f32, bf16 = jnp.float32, jnp.bfloat16


def vmem_limit(mib):
    return pltpu.CompilerParams(vmem_limit_bytes=mib * 1024 * 1024)


def in_hbm(*arrays):
    return [pltpu.with_memory_space_constraint(array, pltpu.HBM) for array in arrays]


def cost(microseconds):
    return pl.CostEstimate(
        flops=int(microseconds * 1.15e9), bytes_accessed=0, transcendentals=0
    )


def place_of(brick):
    return lax.shift_right_logical(brick, GROUP.bit_length() - 1), (brick & (GROUP - 1)) * BZ


def pick_body(asked, vel, out, table):
    size_x, size_y, size_z = vel.shape[1:]
    bricks_y, halves = size_y // BY, size_z // LANES

    def repack(block_x, carry):
        for block_y in range(bricks_y):
            for half in range(halves):
                place = (block_x * bricks_y + block_y) * halves + half
                for c in range(3):
                    for i in range(BX):
                        row = (c * BX + i) * BY
                        table[place, row : row + BY, :] = vel[
                            c,
                            block_x * BX + i,
                            block_y * BY : (block_y + 1) * BY,
                            half * LANES : (half + 1) * LANES,
                        ]
        return carry

    lax.fori_loop(0, size_x // BX, repack, 0)
    groups = out.shape[1]
    lane_slot = lax.broadcasted_iota(jnp.int32, (ROWS, LANES), 1) // BZ

    def one_group(step, carry):
        device, group = step // groups, step % groups
        packed = jnp.zeros((ROWS, LANES), f32)
        for slot in range(GROUP):
            place, lane = place_of(asked[device, group * GROUP + slot])
            rolled = pltpu.roll(table[place], (BZ * slot - lane) & (LANES - 1), 1)
            packed = jnp.where(lane_slot == slot, rolled, packed)
        out[device, group] = packed
        return carry

    lax.fori_loop(0, out.shape[0] * groups, one_group, 0)


def pick_bricks(asked, velocity):
    devices, slots = asked.shape
    size_x, size_y, size_z = velocity.shape[1:]
    places = (size_x // BX) * (size_y // BY) * (size_z // LANES)
    return pl.pallas_call(
        pick_body,
        out_shape=jax.ShapeDtypeStruct((devices, slots // GROUP, ROWS, LANES), f32),
        in_specs=[
            pl.BlockSpec(memory_space=pltpu.SMEM),
            pl.BlockSpec(memory_space=pltpu.VMEM),
        ],
        out_specs=pl.BlockSpec(memory_space=pltpu.VMEM),
        scratch_shapes=[pltpu.VMEM((places, ROWS, LANES), f32)],
        compiler_params=vmem_limit(24),
        cost_estimate=cost(25),
        name="pick_bricks",
    )(asked, velocity)


def permutations():
    inside = BZ * HALF
    spread = np.zeros((2, 2, LANES, 4 * inside), np.float32)
    gather = np.zeros((2 * BY * inside, BY * LANES), np.float32)
    for half in range(2):
        for slot in range(HALF):
            for z in range(BZ):
                outer, inner = (half * HALF + slot) * BZ + z, z * HALF + slot
                for part in range(4):
                    spread[half, part // 2, outer, part * inside + inner] = 1
                for j in range(BY):
                    gather[(half * BY + j) * inside + inner, j * LANES + outer] = 1
    return jnp.asarray(spread, bf16), jnp.asarray(gather, bf16)


def split(value):
    high = value.astype(bf16)
    return high, (value - high.astype(f32)).astype(bf16)


def add_all(values):
    return functools.reduce(jnp.add, values)


def axis_weights(fraction, cells):
    middle = (cells - 1) / 2
    base = jnp.exp(fraction * (2.0 * cells) - float(cells))
    powers = [None, base]
    for i in range(2, cells):
        powers.append(powers[i // 2] * powers[i - i // 2])
    factors = [float(np.exp(middle**2 - (i - middle) ** 2)) for i in range(cells)]
    bells = [None] + [powers[i] * factors[i] for i in range(1, cells)]
    scale = 1.0 / (add_all(bells[1:]) + factors[0])
    weights = [scale * factors[0]] + [bell * scale for bell in bells[1:]]
    mean = add_all(
        [
            (weights[cells - 1 - i] - weights[i]) * (2.0 * (middle - i))
            for i in range(cells // 2)
        ]
    )
    slopes = [w * (2.0 * (i - middle) - mean) for i, w in enumerate(weights)]
    return weights, slopes


def dot(a, b):
    return jnp.dot(a, b, preferred_element_type=f32)


def gradients(products, weights, markers):
    weight_x, slope_x, weight_y, slope_y = ([weights[4 * n + i] for i in range(4)] for n in range(4))
    grads = []
    for c in range(3):
        lines = [[], [], []]
        for i in range(BX):
            rows = [((c * BX + i) * BY + j) * HALF for j in range(BY)]
            still = [products[row : row + HALF, :markers] for row in rows]
            rising = [products[row : row + HALF, markers:] for row in rows]
            lines[0].append(slope_x[i] * add_all([w * t for w, t in zip(weight_y, still)]))
            lines[1].append(weight_x[i] * add_all([w * t for w, t in zip(slope_y, still)]))
            lines[2].append(weight_x[i] * add_all([w * t for w, t in zip(weight_y, rising)]))
        grads.append([add_all(line) for line in lines])
    return grads


def own_lanes():
    shape = (HALF, 4 * BZ * HALF)
    lane = lax.broadcasted_iota(jnp.int32, shape, 1)
    return (lane % HALF == lax.broadcasted_iota(jnp.int32, shape, 0)).astype(f32)


def marker_groups(groups, counts, ins, outs, buffers, sums):
    spread, gather, places, start, dens, brick = ins
    visc_out, moments_out = outs
    permuted, left, right, products, weights, factors, planes = buffers
    markers = places.shape[-1]
    inside = BZ * HALF
    own = own_lanes()
    halves = [
        (owner, 2 * group + half, half, 2 * n + half)
        for n, (owner, group) in enumerate(groups)
        for half in range(2)
    ]
    parts = [split(brick[owner, group]) for owner, group in groups]
    for _, _, half, n in halves:
        high, low = parts[n // 2]
        permuted[n][...] = dot(high, spread[half, 0]) + dot(low, spread[half, 1])
    for owner, part, _, n in halves:
        weight_z, slope_z = axis_weights(places[owner, 2, part], BZ)
        for z in range(0, BZ, 2):
            for column, values in ((0, weight_z), (1, slope_z)):
                high, low = split(jnp.concatenate(values[z : z + 2], axis=0))
                columns = slice(column * markers, (column + 1) * markers)
                for k in range(4):
                    begin = k * inside + z * HALF
                    right[n][begin : begin + 2 * HALF, columns] = low if k % 2 else high
        for row in range(0, ROWS, 2):
            pair = [
                jnp.broadcast_to(permuted[n][r : r + 1, :], own.shape) * own for r in (row, row + 1)
            ]
            left[n][row * HALF : (row + 2) * HALF, :] = jnp.concatenate(pair, axis=0).astype(bf16)
        products[n][...] = dot(left[n][...], right[n][...])
        weights_x = axis_weights(places[owner, 0, part], BX)
        weights_y = axis_weights(places[owner, 1, part], BY)
        for k, values in enumerate((*weights_x, *weights_y)):
            for i, value in enumerate(values):
                weights[n][4 * k + i] = value
        for j in range(BY):
            for z in range(0, BZ, 2):
                pair = [weights_y[0][j] * weight_z[z + k] for k in range(2)]
                rows = slice((j * BZ + z) * HALF, (j * BZ + z + 2) * HALF)
                high, low = split(jnp.concatenate(pair, axis=0))
                planes[n][rows, :markers] = high
                planes[n][rows, markers:] = low

    contract = (((1,), (1,)), ((), ()))
    found = []
    for owner, part, _, n in halves:
        grads = gradients(products[n], weights[n], markers)
        normal = grads[0][0] ** 2 + grads[1][1] ** 2 + grads[2][2] ** 2
        shear_xy = 0.5 * (grads[0][1] + grads[1][0])
        shear_xz = 0.5 * (grads[0][2] + grads[2][0])
        shear_yz = 0.5 * (grads[1][2] + grads[2][1])
        invariant = 0.5 * normal + shear_xy**2 + shear_xz**2 + shear_yz**2
        scaled = invariant * (1.0 / (STRAIN_SCALE * STRAIN_SCALE))
        third = jnp.log(1.0 + scaled) * (1.0 / 3.0)
        first = start[owner, part]
        slot = lax.broadcasted_iota(jnp.int32, first.shape, 0) + part * HALF
        live = slot < counts[0, owner]
        visc_out[owner, part] = jnp.where(live, first * jnp.exp(-third), 0.0)
        carried = (
            live.astype(f32),
            jnp.where(live, jnp.log(first) - third, 0.0),
            jnp.where(live, dens[owner, part], 0.0),
        )
        for c in range(3):
            for i in range(0, BX, 2):
                pair = [carried[c] * weights[n][i + k] for k in range(2)]
                row = (c * BX + i) * HALF
                high, low = split(jnp.concatenate(pair, axis=0))
                rows = slice(row, row + 2 * HALF)
                factors[n][rows, :markers] = high
                factors[n][rows, markers : 2 * markers] = high
                factors[n][rows, 2 * markers :] = low

        both = lax.dot_general(
            factors[n][:, : 2 * markers], planes[n][...], contract, preferred_element_type=f32
        )
        rest = lax.dot_general(
            factors[n][:, 2 * markers :],
            planes[n][:, :markers],
            contract,
            preferred_element_type=f32,
        )
        found.append(both + rest)
    for _, _, half, n in halves:
        chosen = found[n].reshape(3 * BX, HALF, BY * inside) * own[None]
        high, low = split(jnp.sum(chosen, axis=1))
        columns = slice(half * BY * inside, (half + 1) * BY * inside)
        row = (n // 2) * 32
        sums[row : row + 3 * BX, columns] = high.astype(f32)
        sums[row + 16 : row + 16 + 3 * BX, columns] = low.astype(f32)
    moved = dot(sums[...].astype(bf16), gather[...])
    for n, (owner, group) in enumerate(groups):
        mine = moved[32 * n : 32 * n + 3 * BX] + moved[32 * n + 16 : 32 * n + 16 + 3 * BX]
        for j in range(BY):
            rows = pl.ds(j, 3 * BX, stride=BY)
            moments_out[owner, group, rows, :] = mine[:, j * LANES : (j + 1) * LANES]


TOGETHER = 2


def marker_body(counts, *refs):
    ins, outs, scratch = refs[:6], refs[7:9], refs[9:]
    listed, sums, *flat = scratch
    held = 2 * TOGETHER
    buffers = [flat[n * held : (n + 1) * held] for n in range(len(flat) // held)]
    visc_out, moments_out = outs
    owners, groups = moments_out.shape[:2]
    visc_out[...] = jnp.zeros_like(visc_out)
    moments_out[...] = jnp.zeros_like(moments_out)
    sums[...] = jnp.zeros_like(sums)

    def list_groups(index, number):
        owner, group = index // groups, index % groups
        live = group * GROUP < counts[0, owner]

        @pl.when(live)
        def _():
            for n in range(TOGETHER):
                listed[2 * (number + n)] = owner
                listed[2 * (number + n) + 1] = group

        return jnp.where(live, number + 1, number)

    number = lax.fori_loop(0, owners * groups, list_groups, 0)

    def step(index, carry):
        first = TOGETHER * index
        taken = [
            (listed[2 * (first + n)], listed[2 * (first + n) + 1]) for n in range(TOGETHER)
        ]
        marker_groups(taken, counts, ins, outs, buffers, sums)
        return carry

    lax.fori_loop(0, (number + TOGETHER - 1) // TOGETHER, step, 0)


def marker_work(counts, positions, start_visc, marker_dens, bricks, after):
    owners, _, slots, markers = positions.shape
    groups, parts = slots // GROUP, slots // HALF
    spread, gather = permutations()
    width = 4 * BZ * HALF
    whole = pl.BlockSpec(memory_space=pltpu.VMEM)
    buffers = (
        pltpu.VMEM((ROWS, width), f32),
        pltpu.VMEM((ROWS * HALF, width), bf16),
        pltpu.VMEM((width, 2 * markers), bf16),
        pltpu.VMEM((ROWS * HALF, 2 * markers), f32),
        pltpu.VMEM((4 * 4, HALF, markers), f32),
        pltpu.VMEM((3 * BX * HALF, 3 * markers), bf16),
        pltpu.VMEM((BY * BZ * HALF, 2 * markers), bf16),
    )
    visc, moments = pl.pallas_call(
        marker_body,
        out_shape=(
            jax.ShapeDtypeStruct((owners, parts, HALF, markers), f32),
            jax.ShapeDtypeStruct((owners, groups, ROWS, LANES), f32),
        ),
        in_specs=[pl.BlockSpec(memory_space=pltpu.SMEM)]
        + [whole] * 6
        + [pl.BlockSpec(memory_space=pl.ANY)],
        out_specs=(whole, whole),
        scratch_shapes=[
            pltpu.SMEM((2 * (owners * groups + TOGETHER),), jnp.int32),
            pltpu.VMEM((32 * TOGETHER, 2 * BY * BZ * HALF), f32),
        ]
        + [buffer for buffer in buffers for _ in range(2 * TOGETHER)],
        compiler_params=vmem_limit(40),
        cost_estimate=cost(25),
        name="marker_work",
    )(
        counts,
        *in_hbm(
            spread,
            gather,
            positions.reshape(owners, 3, parts, HALF, markers),
            start_visc.reshape(owners, parts, HALF, markers),
            marker_dens.reshape(owners, parts, HALF, markers),
            bricks,
        ),
        after,
    )
    return visc.reshape(owners, slots, markers), moments


def settle_body(asked, moments_in, visc_in, dens_in, visc_out, dens_out, *scratch):
    moments, visc, dens, done, *tables = scratch
    size_x, size_y, size_z = visc.shape
    copies = [
        pltpu.make_async_copy(there, here, done.at[n])
        for n, (there, here) in enumerate(
            ((moments_in, moments), (visc_in, visc), (dens_in, dens))
        )
    ]
    for copy in copies:
        copy.start()
    bricks_y, halves = size_y // BY, size_z // LANES
    for table in tables:
        table[...] = jnp.zeros_like(table)
    copies[0].wait()
    groups = moments.shape[1]
    lane_slot = lax.broadcasted_iota(jnp.int32, (ROWS, LANES), 1) // BZ

    def one_group(step, carry):
        device, group = step // groups, step % groups
        packed = moments[device, group]
        for slot in range(GROUP):
            table = tables[slot % len(tables)]
            place, lane = place_of(asked[device, group * GROUP + slot])
            piece = jnp.where(lane_slot == slot, packed, 0.0)
            piece = pltpu.roll(piece, (lane - BZ * slot) & (LANES - 1), 1)
            table[place] = table[place] + piece
        return carry

    lax.fori_loop(0, moments.shape[0] * groups, one_group, 0)
    copies[1].wait()
    copies[2].wait()

    def finish(block_x, carry):
        for block_y in range(0, bricks_y, 2):
            for half in range(halves):
                for i in range(BX):
                    here = (
                        block_x * BX + i,
                        slice(block_y * BY, (block_y + 2) * BY),
                        slice(half * LANES, (half + 1) * LANES),
                    )
                    sums = []
                    for c in range(3):
                        rows = slice((c * BX + i) * BY, (c * BX + i + 1) * BY)
                        places = [
                            (block_x * bricks_y + block_y + k) * halves + half for k in range(2)
                        ]
                        sums.append(
                            jnp.concatenate(
                                [add_all([t[place, rows, :] for t in tables]) for place in places]
                            )
                        )
                    scale = 1.0 / (sums[0] + 1.0)
                    visc_out[here] = jnp.exp((sums[1] + jnp.log(visc[here])) * scale)
                    dens_out[here] = (sums[2] + dens[here]) * scale
        return carry

    lax.fori_loop(0, size_x // BX, finish, 0)


def settle(asked, moments, cell_visc, cell_dens):
    size_x, size_y, size_z = cell_visc.shape
    places = (size_x // BX) * (size_y // BY) * (size_z // LANES)
    whole = pl.BlockSpec(memory_space=pltpu.VMEM)
    shape = jax.ShapeDtypeStruct(cell_visc.shape, f32)
    return pl.pallas_call(
        settle_body,
        out_shape=(shape, shape),
        in_specs=[pl.BlockSpec(memory_space=pltpu.SMEM)]
        + [pl.BlockSpec(memory_space=pl.ANY)] * 3,
        out_specs=(whole, whole),
        scratch_shapes=[
            pltpu.VMEM(moments.shape, f32),
            pltpu.VMEM(cell_visc.shape, f32),
            pltpu.VMEM(cell_visc.shape, f32),
            pltpu.SemaphoreType.DMA((3,)),
        ]
        + [pltpu.VMEM((places, ROWS, LANES), f32)] * 2,
        compiler_params=vmem_limit(24),
        cost_estimate=cost(7),
        name="settle",
    )(asked, *in_hbm(moments, cell_visc, cell_dens))


def field_of(fields, index):
    return fields[0].at[index] if index < 3 else fields[index - 2]


def pack_x_body(*refs):
    ends, outs = refs[:8], refs[8:]
    for side in range(2):
        for f in range(6):
            outs[side][f] = field_of(ends[side::2], f)[...]


def pack_x(velocity, pressure, cell_visc, cell_dens):
    size_x, size_y, size_z = cell_visc.shape
    width = SWEEPS
    ends = (0, size_x // width - 1)
    vel = [
        pl.BlockSpec((3, width, size_y, size_z), lambda i, e=e: (0, e, 0, 0)) for e in ends
    ]
    block = [pl.BlockSpec((width, size_y, size_z), lambda i, e=e: (e, 0, 0)) for e in ends]
    whole = pl.BlockSpec((6, width, size_y, size_z), lambda i: (0, 0, 0, 0))
    shape = jax.ShapeDtypeStruct((6, width, size_y, size_z), f32)
    return pl.pallas_call(
        pack_x_body,
        grid=(1,),
        out_shape=(shape, shape),
        in_specs=vel + block * 3,
        out_specs=(whole, whole),
        compiler_params=vmem_limit(60),
        cost_estimate=cost(2),
        name="pack_x",
    )(velocity, velocity, pressure, pressure, cell_visc, cell_visc, cell_dens, cell_dens)


def corner_rows(upward, size_x):
    width = SWEEPS
    spare = (5 * width,) if upward else (4 * width - 1, 6 * width - 1)
    places = [(plane, row) for plane in range(size_x) for row in spare]
    found = []
    for field in range(6):
        for side in range(2):
            near = field == 5 or (field == 3 and side == 1 and not upward)
            reach = width - 1 if near else width
            for far_x in range(1, width):
                for far_y in range(1, reach - far_x + 1):
                    found.append((field, side, far_x, far_y))
    more = max(0, len(found) - len(places))
    places += [(size_x + n // (6 * width), n % (6 * width)) for n in range(more)]
    return [cell + at for cell, at in zip(found, places)], size_x + -(-more // (6 * width))


def pack_y_body(size_x, vel, pres, visc, dens, low_x, high_x, upward, downward):
    step_x, size_y, _ = pres.shape
    width = SWEEPS
    step = pl.program_id(0)
    planes = pl.ds(pl.multiple_of(step * step_x, step_x), step_x)
    for f in range(6):
        field = field_of((vel, pres, visc, dens), f)
        rows = slice(f * width, (f + 1) * width)
        upward[planes, rows, :] = field[:, size_y - width :, :]
        downward[planes, rows, :] = field[:, :width, :]

    @pl.when(step == pl.num_programs(0) - 1)
    def _():
        for up, face in ((True, upward), (False, downward)):
            for f, side, far_x, far_y, plane, row in corner_rows(up, size_x)[0]:
                halo, at = (high_x, far_x - 1) if side else (low_x, width - far_x)
                face[plane, row] = halo[f, at, size_y - far_y if up else far_y - 1]


def pack_y(velocity, pressure, cell_visc, cell_dens, low_x, high_x):
    size_x, size_y, size_z = cell_visc.shape
    step = 8
    block = pl.BlockSpec((step, size_y, size_z), lambda i: (i, 0, 0))
    halo = pl.BlockSpec(low_x.shape, lambda i: (0, 0, 0, 0))
    shapes = [(corner_rows(up, size_x)[1], 6 * SWEEPS, size_z) for up in (True, False)]
    return pl.pallas_call(
        functools.partial(pack_y_body, size_x),
        grid=(size_x // step,),
        out_shape=tuple(jax.ShapeDtypeStruct(shape, f32) for shape in shapes),
        in_specs=[
            pl.BlockSpec((3, step, size_y, size_z), lambda i: (0, i, 0, 0)),
            block,
            block,
            block,
            halo,
            halo,
        ],
        out_specs=tuple(pl.BlockSpec(shape, lambda i: (0, 0, 0)) for shape in shapes),
        compiler_params=vmem_limit(24),
        cost_estimate=cost(15),
        name="pack_y",
    )(*in_hbm(velocity, pressure, cell_visc, cell_dens, low_x, high_x))


def place(per, x, y, rows):
    return x % per, pl.ds(y * SUBLANES + x // per, rows, stride=SUBLANES)


def put(target, x, y, rows, value):
    per, halves = target.shape[:2]
    plane, lines = place(per, x, y, rows)
    for half in range(halves):
        target[plane, half, lines, :] = value[:, half * LANES : (half + 1) * LANES]


def tile(y):
    if isinstance(y, int):
        return pl.ds(y * SUBLANES, SUBLANES)
    return pl.ds(pl.multiple_of(y * SUBLANES, SUBLANES), SUBLANES)


def row_work(cells, coefs, relax, forcing, rate):
    per, halves = cells.shape[1:3]
    lane = lax.broadcasted_iota(jnp.int32, (SUBLANES, LANES), 1)
    at_first, at_last = lane == 0, lane == LANES - 1

    def take(field, plane, y):
        return jnp.concatenate([field[plane, half, tile(y), :] for half in range(halves)], axis=1)

    def store(field, plane, y, value):
        for half in range(halves):
            field[plane, half, tile(y), :] = value[:, half * LANES : (half + 1) * LANES]

    def up_x(field, plane, y):
        if plane < per - 1:
            return take(field, plane + 1, y)
        return pltpu.roll(take(field, 0, y), SUBLANES - 1, 0)

    def down_x(field, plane, y):
        if plane > 0:
            return take(field, plane - 1, y)
        return pltpu.roll(take(field, per - 1, y), 1, 0)

    def rolled(a, shift):
        return [
            pltpu.roll(a[:, half * LANES : (half + 1) * LANES], shift, 1) for half in range(halves)
        ]

    def up_z(a):
        parts = rolled(a, LANES - 1)
        after = parts[1:] + [jnp.zeros_like(parts[0])]
        return jnp.concatenate([jnp.where(at_last, n, p) for p, n in zip(parts, after)], axis=1)

    def down_z(a):
        parts = rolled(a, 1)
        before = [jnp.zeros_like(parts[0])] + parts[:-1]
        return jnp.concatenate([jnp.where(at_first, b, p) for p, b in zip(parts, before)], axis=1)

    def prepare(y):
        visc, dens = cells.at[0], cells.at[1]
        for plane in range(per):
            here = take(visc, plane, y)
            near = [
                up_x(visc, plane, y),
                down_x(visc, plane, y),
                take(visc, plane, y + 1),
                take(visc, plane, y - 1),
                up_z(here),
                down_z(here),
            ]
            links = [0.5 * (here + other) for other in near]
            scale = jnp.where(here > 0.0, RELAX / add_all(links), 0.0)
            for n in range(6):
                coefs[n, plane, tile(y), :] = links[n] * scale
            relax[plane, tile(y), :] = scale
            forcing[plane, tile(y), :] = take(dens, plane, y) * (-GRAVITY * scale)
            rate[plane, tile(y), :] = PRESSURE_RATE * here

    def sweep(y, old, new, results=None):
        def keep(field, plane, value):
            if results is None:
                store(new.at[field], plane, y, value)
                return
            size_y = results.shape[2] // (per * SUBLANES)
            begin = plane * size_y + y - SWEEPS
            rows = pl.ds(begin, SUBLANES, stride=per * size_y)
            for half in range(halves):
                results[field, half, rows, :] = value[:, half * LANES : (half + 1) * LANES]

        for plane in range(per):
            links = [coefs[n, plane, tile(y), :] for n in range(6)]
            scale = relax[plane, tile(y), :]
            pressure = take(old.at[3], plane, y)
            before = (
                down_x(old.at[3], plane, y),
                take(old.at[3], plane, y - 1),
                down_z(pressure),
            )
            changes = []
            for c in range(3):
                field = old.at[c]
                here = take(field, plane, y)
                near = [
                    up_x(field, plane, y),
                    down_x(field, plane, y),
                    take(field, plane, y + 1),
                    take(field, plane, y - 1),
                    up_z(here),
                    down_z(here),
                ]
                terms = [link * other for link, other in zip(links, near)]
                total = (terms[0] + terms[1]) + (terms[2] + terms[3])
                total = total + (terms[4] + terms[5])
                rest = (1.0 - RELAX) * here - scale * (pressure - before[c])
                if c == 2:
                    rest = rest + forcing[plane, tile(y), :]
                changes.append(near[2 * c] - here)
                keep(c, plane, total + rest)
            pressed = pressure - rate[plane, tile(y), :] * add_all(changes)
            keep(3, plane, pressed)

    return prepare, sweep


def kept_rows(size_y):
    width = SWEEPS
    return (
        ((width, width), (size_y, width)),
        ((width + 1, width), (size_y - 1, width)),
        ((width, width + 1), (size_y - 1, width + 1)),
    )


def kept_copies(pairs, size_y, done):
    copies = []
    for (source, target), strips in zip(pairs, kept_rows(size_y)):
        for begin, rows in strips:
            span = (slice(None),) * 3 + (pl.ds(begin * SUBLANES, rows * SUBLANES),)
            copies.append(
                pltpu.make_async_copy(source.at[span], target.at[span], done.at[len(copies)])
            )
    return copies


def inner_body(vel, pres, visc, dens, low_x, high_x, _, *refs):
    even_out, odd_out, cells_out, results_out, *work = refs
    blocks, sides_x, even, odd, cells, results, coefs, relax, forcing, rate, done = work
    size_x, size_y, size_z = blocks.shape[1:]
    width = SWEEPS
    inputs = (
        (visc, blocks.at[4], (4,)),
        (vel, blocks.at[0:3], (0, 1, 2)),
        (pres, blocks.at[3], (3,)),
        (dens, blocks.at[5], (5,)),
        (low_x, sides_x.at[0], ()),
        (high_x, sides_x.at[1], ()),
    )
    copies = [
        pltpu.make_async_copy(there, here, done.at[n]) for n, (there, here, _) in enumerate(inputs)
    ]
    for copy in copies:
        copy.start()
    targets = [even.at[n] for n in range(4)] + [cells.at[n] for n in range(2)]
    for copy, (_, _, held) in zip(copies, inputs):
        copy.wait()
        for f in held:
            for i in range(size_x):
                for y in range(0, size_y, SUBLANES):
                    value = blocks[f, i, y : y + SUBLANES, :]
                    put(targets[f], i + width, y + width, SUBLANES, value)
    for side, begin in enumerate((0, width + size_x)):
        for f in range(6):
            for i in range(width):
                for y in range(0, size_y, SUBLANES):
                    value = sides_x[side, f, i, y : y + SUBLANES, :]
                    put(targets[f], begin + i, y + width, SUBLANES, value)

    prepare, sweep = row_work(cells, coefs, relax, forcing, rate)

    def prepare_row(y, carry):
        prepare(y)
        return carry

    first, last = width + 1, width + size_y - 1
    lax.fori_loop(first, last, prepare_row, 0, unroll=2)
    for step in range(SWEEPS):
        old, new = (odd, even) if step % 2 else (even, odd)

        last_one = results if step == SWEEPS - 1 else None

        def sweep_row(y, carry, old=old, new=new, results=last_one):
            sweep(y, old, new, results)
            return carry

        lax.fori_loop(first + step, last - step, sweep_row, 0, unroll=2)
    sends = kept_copies(((even, even_out), (odd, odd_out), (cells, cells_out)), size_y, done)
    sends.append(pltpu.make_async_copy(results, results_out, done.at[len(sends)]))
    for send in sends:
        send.start()
    for send in sends:
        send.wait()


def inner_sweeps(velocity, pressure, cell_visc, cell_dens, low_x, high_x, after):
    size_x, size_y, size_z = cell_visc.shape
    width = low_x.shape[1]
    per, rows = (size_x + 2 * width) // SUBLANES, (size_y + 2 * width) * SUBLANES
    block, cut = (per, rows, size_z), (per, size_z // LANES, rows, LANES)
    shapes = [(4,) + cut, (4,) + cut, (2,) + cut]
    shapes.append((4, size_z // LANES, (size_x + 2 * width) * size_y, LANES))
    anywhere = pl.BlockSpec(memory_space=pl.ANY)
    return pl.pallas_call(
        inner_body,
        out_shape=tuple(jax.ShapeDtypeStruct(shape, f32) for shape in shapes),
        in_specs=[anywhere] * 7,
        out_specs=(anywhere,) * 4,
        scratch_shapes=[
            pltpu.VMEM((6,) + cell_visc.shape, f32),
            pltpu.VMEM((2,) + low_x.shape, f32),
        ]
        + [pltpu.VMEM(shape, f32) for shape in shapes]
        + [
            pltpu.VMEM((6,) + block, f32),
            pltpu.VMEM(block, f32),
            pltpu.VMEM(block, f32),
            pltpu.VMEM(block, f32),
            pltpu.SemaphoreType.DMA((7,)),
        ],
        compiler_params=vmem_limit(40),
        cost_estimate=cost(25),
        name="inner_sweeps",
    )(*in_hbm(velocity, pressure, cell_visc, cell_dens, low_x, high_x), after)


def edge_body(size_x, even_in, odd_in, cells_in, results_in, low_y, high_y, vel_out, pres_out, *work):
    from_low, from_high, results, even, odd, cells, coefs, relax, forcing, rate, done, more = work
    width = SWEEPS
    halves, long_y = even.shape[2], even.shape[3] // SUBLANES
    size_y, size_z = long_y - 2 * width, halves * LANES
    halos = [
        pltpu.make_async_copy(low_y, from_low, more.at[0]),
        pltpu.make_async_copy(high_y, from_high, more.at[1]),
    ]
    kept = kept_copies(((even_in, even), (odd_in, odd), (cells_in, cells)), size_y, done)
    inner = pltpu.make_async_copy(results_in, results, more.at[2])
    for copy in (*halos, *kept, inner):
        copy.start()
    targets = [even.at[n] for n in range(4)] + [cells.at[n] for n in range(2)]
    for target in targets:
        for x in (*range(width), *range(width + size_x, size_x + 2 * width)):
            for y in (0, width + size_y):
                put(target, x, y, width, jnp.zeros((width, size_z), f32))
    for up, halo, copy, begin in (
        (True, from_low, halos[0], 0),
        (False, from_high, halos[1], width + size_y),
    ):
        copy.wait()
        for f, target in enumerate(targets):
            rows = slice(f * width, (f + 1) * width)
            for i in range(size_x):
                put(target, i + width, begin, width, halo[i, rows, :])
        for f, side, far_x, far_y, plane, row in corner_rows(up, size_x)[0]:
            x = width + size_x - 1 + far_x if side else width - far_x
            y = width - far_y if up else width + size_y - 1 + far_y
            put(targets[f], x, y, 1, halo[plane, row : row + 1, :])
    for copy in kept:
        copy.wait()

    prepare, sweep = row_work(cells, coefs, relax, forcing, rate)

    def prepare_rows(n, carry):
        prepare(1 + n)
        prepare(long_y - 2 * width + n)
        return carry

    lax.fori_loop(0, 2 * width - 1, prepare_rows, 0)
    for step in range(SWEEPS):
        old, new = (odd, even) if step % 2 else (even, odd)

        last_one = None
        if step == SWEEPS - 1:
            last_one = results
            inner.wait()

        def sweep_rows(n, carry, old=old, new=new, step=step, results=last_one):
            sweep(1 + step + n, old, new, results)
            sweep(width + size_y - 1 - step + n, old, new, results)
            return carry

        lax.fori_loop(0, width, sweep_rows, 0)

    own = pl.ds(width * size_y, size_x * size_y)
    sends = []
    for field, out in enumerate([vel_out.at[0], vel_out.at[1], vel_out.at[2], pres_out]):
        for half in range(halves):
            columns = pl.ds(half * LANES, LANES)
            done_one = done.at[len(sends)]
            sends.append(
                pltpu.make_async_copy(results.at[field, half, own], out.at[:, columns], done_one)
            )
    for send in sends:
        send.start()
    for send in sends:
        send.wait()


def edge_sweeps(even, odd, cells, results, low_y, high_y, size_x, size_y):
    per, halves, rows = even.shape[1:4]
    size_z = halves * LANES
    block = (per, rows, size_z)
    anywhere = pl.BlockSpec(memory_space=pl.ANY)
    velocity, pressure = pl.pallas_call(
        functools.partial(edge_body, size_x),
        out_shape=(
            jax.ShapeDtypeStruct((3, size_x * size_y, size_z), f32),
            jax.ShapeDtypeStruct((size_x * size_y, size_z), f32),
        ),
        in_specs=[anywhere] * 6,
        out_specs=(anywhere,) * 2,
        scratch_shapes=[
            pltpu.VMEM(low_y.shape, f32),
            pltpu.VMEM(high_y.shape, f32),
            pltpu.VMEM(results.shape, f32),
            pltpu.VMEM(even.shape, f32),
            pltpu.VMEM(odd.shape, f32),
            pltpu.VMEM(cells.shape, f32),
            pltpu.VMEM((6,) + block, f32),
            pltpu.VMEM(block, f32),
            pltpu.VMEM(block, f32),
            pltpu.VMEM(block, f32),
            pltpu.SemaphoreType.DMA((8,)),
            pltpu.SemaphoreType.DMA((3,)),
        ],
        compiler_params=vmem_limit(40),
        cost_estimate=cost(1),
        name="edge_sweeps",
    )(even, odd, cells, results, low_y, high_y)
    return (
        velocity.reshape(3, size_x, size_y, size_z),
        pressure.reshape(size_x, size_y, size_z),
    )


def shift(value, axis, step):
    size = lax.axis_size(axis)
    pairs = [(i, i + step) for i in range(size) if 0 <= i + step < size]
    return lax.ppermute(value, axis, pairs)


def per_device(
    velocity,
    pressure,
    cell_visc,
    cell_dens,
    block_brick,
    block_counts,
    positions,
    start_visc,
    marker_dens,
):
    asked = lax.all_to_all(block_brick, "mark", 0, 0, tiled=True)
    fields = (velocity, pressure, cell_visc, cell_dens)
    to_low, to_high = pack_x(*fields)
    low_x, high_x = shift(to_high, "grid", 1), shift(to_low, "grid", -1)
    upward, downward = pack_y(*fields, low_x, high_x)
    low_y, high_y = shift(upward, "mark", 1), shift(downward, "mark", -1)

    picked = pick_bricks(asked, velocity)
    bricks = lax.all_to_all(picked, "mark", 0, 0, tiled=True)
    marker_visc, moments = marker_work(
        block_counts, positions, start_visc, marker_dens, bricks, upward
    )
    gathered = lax.all_to_all(moments, "mark", 0, 0, tiled=True)
    state = inner_sweeps(*fields, low_x, high_x, moments)
    velocity_next, pressure_next = edge_sweeps(*state, low_y, high_y, *pressure.shape[:2])
    visc_next, dens_next = settle(asked, gathered, cell_visc, cell_dens)
    return velocity_next, pressure_next, visc_next, dens_next, marker_visc


def solution(mesh):
    in_specs = (
        P(None, "grid", "mark", None),
        P("grid", "mark", None),
        P("grid", "mark", None),
        P("grid", "mark", None),
        P(("grid", "mark"), None),
        P(("grid", "mark"), None),
        P(("grid", "mark"), None, None, None),
        P(("grid", "mark"), None, None),
        P(("grid", "mark"), None, None),
    )
    out_specs = (
        P(None, "grid", "mark", None),
        P("grid", "mark", None),
        P("grid", "mark", None),
        P("grid", "mark", None),
        P(("grid", "mark"), None, None),
    )
    return jax.shard_map(
        per_device, mesh=mesh, in_specs=in_specs, out_specs=out_specs, check_vma=False
    )
```

```python
import functools

import jax
import jax.numpy as jnp
import numpy as np
from jax import lax
from jax.experimental import pallas as pl
from jax.experimental.pallas import tpu as pltpu
from jax.sharding import PartitionSpec as P

SWEEPS = 4
RELAX = 0.6
PRESSURE_RATE = 0.25
GRAVITY = 1.0
STRAIN_SCALE = 0.5

BX, BY, BZ = 4, 4, 8
PLANE = BX * BY
ROWS = 3 * PLANE
LANES = 128
GROUP = LANES // BZ
HALF = 8
SUBLANES = 8

f32, bf16 = jnp.float32, jnp.bfloat16


def vmem_limit(mib):
    return pltpu.CompilerParams(vmem_limit_bytes=mib * 1024 * 1024)


def in_hbm(*arrays):
    return [pltpu.with_memory_space_constraint(array, pltpu.HBM) for array in arrays]


def cost(microseconds):
    return pl.CostEstimate(
        flops=int(microseconds * 1.15e9), bytes_accessed=0, transcendentals=0
    )


def place_of(brick):
    return lax.shift_right_logical(brick, GROUP.bit_length() - 1), (brick & (GROUP - 1)) * BZ


def pick_body(asked, vel, out, table):
    size_x, size_y, size_z = vel.shape[1:]
    bricks_y, halves = size_y // BY, size_z // LANES

    def repack(block_x, carry):
        for block_y in range(bricks_y):
            for half in range(halves):
                place = (block_x * bricks_y + block_y) * halves + half
                for c in range(3):
                    for i in range(BX):
                        row = (c * BX + i) * BY
                        table[place, row : row + BY, :] = vel[
                            c,
                            block_x * BX + i,
                            block_y * BY : (block_y + 1) * BY,
                            half * LANES : (half + 1) * LANES,
                        ]
        return carry

    lax.fori_loop(0, size_x // BX, repack, 0)
    groups = out.shape[1]
    lane_slot = lax.broadcasted_iota(jnp.int32, (ROWS, LANES), 1) // BZ

    def one_group(step, carry):
        device, group = step // groups, step % groups
        packed = jnp.zeros((ROWS, LANES), f32)
        for slot in range(GROUP):
            place, lane = place_of(asked[device, group * GROUP + slot])
            rolled = pltpu.roll(table[place], (BZ * slot - lane) & (LANES - 1), 1)
            packed = jnp.where(lane_slot == slot, rolled, packed)
        out[device, group] = packed
        return carry

    lax.fori_loop(0, out.shape[0] * groups, one_group, 0)


def pick_bricks(asked, velocity):
    devices, slots = asked.shape
    size_x, size_y, size_z = velocity.shape[1:]
    places = (size_x // BX) * (size_y // BY) * (size_z // LANES)
    return pl.pallas_call(
        pick_body,
        out_shape=jax.ShapeDtypeStruct((devices, slots // GROUP, ROWS, LANES), f32),
        in_specs=[
            pl.BlockSpec(memory_space=pltpu.SMEM),
            pl.BlockSpec(memory_space=pltpu.VMEM),
        ],
        out_specs=pl.BlockSpec(memory_space=pltpu.VMEM),
        scratch_shapes=[pltpu.VMEM((places, ROWS, LANES), f32)],
        compiler_params=vmem_limit(24),
        cost_estimate=cost(25),
        name="pick_bricks",
    )(asked, velocity)


def permutations():
    inside = BZ * HALF
    spread = np.zeros((2, 2, LANES, 4 * inside), np.float32)
    gather = np.zeros((2 * BY * inside, BY * LANES), np.float32)
    for half in range(2):
        for slot in range(HALF):
            for z in range(BZ):
                outer, inner = (half * HALF + slot) * BZ + z, z * HALF + slot
                for part in range(4):
                    spread[half, part // 2, outer, part * inside + inner] = 1
                for j in range(BY):
                    gather[(half * BY + j) * inside + inner, j * LANES + outer] = 1
    return jnp.asarray(spread, bf16), jnp.asarray(gather, bf16)


def split(value):
    high = value.astype(bf16)
    return high, (value - high.astype(f32)).astype(bf16)


def add_all(values):
    return functools.reduce(jnp.add, values)


def axis_weights(fraction, cells):
    middle = (cells - 1) / 2
    base = jnp.exp(fraction * (2.0 * cells) - float(cells))
    powers = [None, base]
    for i in range(2, cells):
        powers.append(powers[i // 2] * powers[i - i // 2])
    factors = [float(np.exp(middle**2 - (i - middle) ** 2)) for i in range(cells)]
    bells = [None] + [powers[i] * factors[i] for i in range(1, cells)]
    scale = 1.0 / (add_all(bells[1:]) + factors[0])
    weights = [scale * factors[0]] + [bell * scale for bell in bells[1:]]
    mean = add_all(
        [
            (weights[cells - 1 - i] - weights[i]) * (2.0 * (middle - i))
            for i in range(cells // 2)
        ]
    )
    slopes = [w * (2.0 * (i - middle) - mean) for i, w in enumerate(weights)]
    return weights, slopes


def dot(a, b):
    return jnp.dot(a, b, preferred_element_type=f32)


def gradients(products, weights, markers):
    weight_x, slope_x, weight_y, slope_y = ([weights[4 * n + i] for i in range(4)] for n in range(4))
    grads = []
    for c in range(3):
        lines = [[], [], []]
        for i in range(BX):
            rows = [((c * BX + i) * BY + j) * HALF for j in range(BY)]
            still = [products[row : row + HALF, :markers] for row in rows]
            rising = [products[row : row + HALF, markers:] for row in rows]
            lines[0].append(slope_x[i] * add_all([w * t for w, t in zip(weight_y, still)]))
            lines[1].append(weight_x[i] * add_all([w * t for w, t in zip(slope_y, still)]))
            lines[2].append(weight_x[i] * add_all([w * t for w, t in zip(weight_y, rising)]))
        grads.append([add_all(line) for line in lines])
    return grads


def own_lanes():
    shape = (HALF, 4 * BZ * HALF)
    lane = lax.broadcasted_iota(jnp.int32, shape, 1)
    return (lane % HALF == lax.broadcasted_iota(jnp.int32, shape, 0)).astype(f32)


def marker_groups(groups, counts, ins, outs, buffers, sums):
    spread, gather, places, start, dens, brick = ins
    visc_out, moments_out = outs
    permuted, left, right, products, weights, factors, planes_high, planes_low = buffers
    markers = places.shape[-1]
    inside = BZ * HALF
    own = own_lanes()
    halves = [
        (owner, 2 * group + half, half, 2 * n + half)
        for n, (owner, group) in enumerate(groups)
        for half in range(2)
    ]
    parts = [split(brick[owner, group]) for owner, group in groups]
    for _, _, half, n in halves:
        high, low = parts[n // 2]
        permuted[n][...] = dot(high, spread[half, 0]) + dot(low, spread[half, 1])
    heights = []
    for owner, part, _, n in halves:
        weight_z, slope_z = axis_weights(places[owner, 2, part], BZ)
        heights.append(weight_z)
        for z in range(0, BZ, 2):
            for column, values in ((0, weight_z), (1, slope_z)):
                high, low = split(jnp.concatenate(values[z : z + 2], axis=0))
                columns = slice(column * markers, (column + 1) * markers)
                for k in range(4):
                    begin = k * inside + z * HALF
                    right[n][begin : begin + 2 * HALF, columns] = low if k % 2 else high
    for _, _, _, n in halves:
        for row in range(0, ROWS, 2):
            pair = [
                jnp.broadcast_to(permuted[n][r : r + 1, :], own.shape) * own for r in (row, row + 1)
            ]
            left[n][row * HALF : (row + 2) * HALF, :] = jnp.concatenate(pair, axis=0).astype(bf16)
    for _, _, _, n in halves:
        products[n][...] = dot(left[n][...], right[n][...])
    for owner, part, _, n in halves:
        weights_x = axis_weights(places[owner, 0, part], BX)
        weights_y = axis_weights(places[owner, 1, part], BY)
        for k, values in enumerate((*weights_x, *weights_y)):
            for i, value in enumerate(values):
                weights[n][4 * k + i] = value
        for j in range(BY):
            for z in range(0, BZ, 2):
                pair = [weights_y[0][j] * heights[n][z + k] for k in range(2)]
                rows = slice((j * BZ + z) * HALF, (j * BZ + z + 2) * HALF)
                high, low = split(jnp.concatenate(pair, axis=0))
                planes_high[n][rows, :] = high
                planes_low[n][rows, :] = low

    count = 3 * BX * HALF
    for owner, part, _, n in halves:
        grads = gradients(products[n], weights[n], markers)
        normal = grads[0][0] ** 2 + grads[1][1] ** 2 + grads[2][2] ** 2
        shear_xy = 0.5 * (grads[0][1] + grads[1][0])
        shear_xz = 0.5 * (grads[0][2] + grads[2][0])
        shear_yz = 0.5 * (grads[1][2] + grads[2][1])
        invariant = 0.5 * normal + shear_xy**2 + shear_xz**2 + shear_yz**2
        scaled = invariant * (1.0 / (STRAIN_SCALE * STRAIN_SCALE))
        third = jnp.log(1.0 + scaled) * (1.0 / 3.0)
        first = start[owner, part]
        slot = lax.broadcasted_iota(jnp.int32, first.shape, 0) + part * HALF
        live = slot < counts[0, owner]
        visc_out[owner, part] = jnp.where(live, first * jnp.exp(-third), 0.0)
        carried = (
            live.astype(f32),
            jnp.where(live, jnp.log(first) - third, 0.0),
            jnp.where(live, dens[owner, part], 0.0),
        )
        for c in range(3):
            for i in range(0, BX, 2):
                pair = [carried[c] * weights[n][i + k] for k in range(2)]
                row = (c * BX + i) * HALF
                high, low = split(jnp.concatenate(pair, axis=0))
                factors[n][row : row + 2 * HALF, :] = high
                factors[n][count + row : count + row + 2 * HALF, :] = low

    contract = (((1,), (1,)), ((), ()))
    found = []
    for _, _, _, n in halves:
        both = lax.dot_general(
            factors[n][...], planes_high[n][...], contract, preferred_element_type=f32
        )
        rest = lax.dot_general(
            factors[n][:count], planes_low[n][...], contract, preferred_element_type=f32
        )
        found.append((both, rest))
    for _, _, half, n in halves:
        both, rest = found[n]
        total = both[:count] + both[count:] + rest
        chosen = total.reshape(3 * BX, HALF, BY * inside) * own[None]
        high, low = split(jnp.sum(chosen, axis=1))
        columns = slice(half * BY * inside, (half + 1) * BY * inside)
        row = (n // 2) * 32
        sums[row : row + 3 * BX, columns] = high.astype(f32)
        sums[row + 16 : row + 16 + 3 * BX, columns] = low.astype(f32)
    moved = dot(sums[...].astype(bf16), gather[...])
    for n, (owner, group) in enumerate(groups):
        mine = moved[32 * n : 32 * n + 3 * BX] + moved[32 * n + 16 : 32 * n + 16 + 3 * BX]
        for j in range(BY):
            rows = pl.ds(j, 3 * BX, stride=BY)
            moments_out[owner, group, rows, :] = mine[:, j * LANES : (j + 1) * LANES]


TOGETHER = 2


def marker_body(counts, *refs):
    ins, outs, scratch = refs[:6], refs[6:8], refs[8:]
    listed, sums, *flat = scratch
    held = 2 * TOGETHER
    buffers = [flat[n * held : (n + 1) * held] for n in range(len(flat) // held)]
    visc_out, moments_out = outs
    owners, groups = moments_out.shape[:2]
    visc_out[...] = jnp.zeros_like(visc_out)
    moments_out[...] = jnp.zeros_like(moments_out)
    sums[...] = jnp.zeros_like(sums)

    def list_groups(index, number):
        owner, group = index // groups, index % groups
        live = group * GROUP < counts[0, owner]

        @pl.when(live)
        def _():
            for n in range(TOGETHER):
                listed[2 * (number + n)] = owner
                listed[2 * (number + n) + 1] = group

        return jnp.where(live, number + 1, number)

    number = lax.fori_loop(0, owners * groups, list_groups, 0)

    def step(index, carry):
        first = TOGETHER * index
        taken = [
            (listed[2 * (first + n)], listed[2 * (first + n) + 1]) for n in range(TOGETHER)
        ]
        marker_groups(taken, counts, ins, outs, buffers, sums)
        return carry

    lax.fori_loop(0, (number + TOGETHER - 1) // TOGETHER, step, 0)


def by_halves(positions, start_visc, marker_dens):
    owners, _, slots, markers = positions.shape
    parts = slots // HALF
    return (
        positions.reshape(owners, 3, parts, HALF, markers),
        start_visc.reshape(owners, parts, HALF, markers),
        marker_dens.reshape(owners, parts, HALF, markers),
    )


def marker_work(counts, positions, start_visc, marker_dens, bricks):
    owners, _, parts, _, markers = positions.shape
    slots = parts * HALF
    groups = slots // GROUP
    spread, gather = permutations()
    width = 4 * BZ * HALF
    whole = pl.BlockSpec(memory_space=pltpu.VMEM)
    buffers = (
        pltpu.VMEM((ROWS, width), f32),
        pltpu.VMEM((ROWS * HALF, width), bf16),
        pltpu.VMEM((width, 2 * markers), bf16),
        pltpu.VMEM((ROWS * HALF, 2 * markers), f32),
        pltpu.VMEM((4 * 4, HALF, markers), f32),
        pltpu.VMEM((2 * 3 * BX * HALF, markers), bf16),
        pltpu.VMEM((BY * BZ * HALF, markers), bf16),
        pltpu.VMEM((BY * BZ * HALF, markers), bf16),
    )
    visc, moments = pl.pallas_call(
        marker_body,
        out_shape=(
            jax.ShapeDtypeStruct((owners, parts, HALF, markers), f32),
            jax.ShapeDtypeStruct((owners, groups, ROWS, LANES), f32),
        ),
        in_specs=[pl.BlockSpec(memory_space=pltpu.SMEM)]
        + [whole] * 6,
        out_specs=(whole, whole),
        scratch_shapes=[
            pltpu.SMEM((2 * (owners * groups + TOGETHER),), jnp.int32),
            pltpu.VMEM((32 * TOGETHER, 2 * BY * BZ * HALF), f32),
        ]
        + [buffer for buffer in buffers for _ in range(2 * TOGETHER)],
        compiler_params=vmem_limit(40),
        cost_estimate=cost(25),
        name="marker_work",
    )(
        counts,
        *in_hbm(spread, gather),
        *[
            pltpu.with_memory_space_constraint(array, pltpu.VMEM)
            for array in (positions, start_visc, marker_dens)
        ],
        *in_hbm(bricks),
    )
    return visc.reshape(owners, slots, markers), moments


def settle_body(asked, moments_in, visc_in, dens_in, visc_out, dens_out, *scratch):
    moments, visc, dens, done, *tables = scratch
    size_x, size_y, size_z = visc.shape
    copies = [
        pltpu.make_async_copy(there, here, done.at[n])
        for n, (there, here) in enumerate(
            ((moments_in, moments), (visc_in, visc), (dens_in, dens))
        )
    ]
    for copy in copies:
        copy.start()
    bricks_y, halves = size_y // BY, size_z // LANES
    for table in tables:
        table[...] = jnp.zeros_like(table)
    copies[0].wait()
    groups = moments.shape[1]
    lane_slot = lax.broadcasted_iota(jnp.int32, (ROWS, LANES), 1) // BZ

    def one_group(step, carry):
        device, group = step // groups, step % groups
        packed = moments[device, group]
        for slot in range(GROUP):
            table = tables[slot % len(tables)]
            place, lane = place_of(asked[device, group * GROUP + slot])
            piece = jnp.where(lane_slot == slot, packed, 0.0)
            piece = pltpu.roll(piece, (lane - BZ * slot) & (LANES - 1), 1)
            table[place] = table[place] + piece
        return carry

    lax.fori_loop(0, moments.shape[0] * groups, one_group, 0)
    copies[1].wait()
    copies[2].wait()

    def finish(block_x, carry):
        for block_y in range(0, bricks_y, 2):
            for half in range(halves):
                for i in range(BX):
                    here = (
                        block_x * BX + i,
                        slice(block_y * BY, (block_y + 2) * BY),
                        slice(half * LANES, (half + 1) * LANES),
                    )
                    sums = []
                    for c in range(3):
                        rows = slice((c * BX + i) * BY, (c * BX + i + 1) * BY)
                        places = [
                            (block_x * bricks_y + block_y + k) * halves + half for k in range(2)
                        ]
                        sums.append(
                            jnp.concatenate(
                                [add_all([t[place, rows, :] for t in tables]) for place in places]
                            )
                        )
                    scale = 1.0 / (sums[0] + 1.0)
                    visc_out[here] = jnp.exp((sums[1] + jnp.log(visc[here])) * scale)
                    dens_out[here] = (sums[2] + dens[here]) * scale
        return carry

    lax.fori_loop(0, size_x // BX, finish, 0)


def settle(asked, moments, cell_visc, cell_dens):
    size_x, size_y, size_z = cell_visc.shape
    places = (size_x // BX) * (size_y // BY) * (size_z // LANES)
    whole = pl.BlockSpec(memory_space=pltpu.VMEM)
    shape = jax.ShapeDtypeStruct(cell_visc.shape, f32)
    return pl.pallas_call(
        settle_body,
        out_shape=(shape, shape),
        in_specs=[pl.BlockSpec(memory_space=pltpu.SMEM)]
        + [pl.BlockSpec(memory_space=pl.ANY)] * 3,
        out_specs=(whole, whole),
        scratch_shapes=[
            pltpu.VMEM(moments.shape, f32),
            pltpu.VMEM(cell_visc.shape, f32),
            pltpu.VMEM(cell_visc.shape, f32),
            pltpu.SemaphoreType.DMA((3,)),
        ]
        + [pltpu.VMEM((places, ROWS, LANES), f32)] * 2,
        compiler_params=vmem_limit(24),
        cost_estimate=cost(7),
        name="settle",
    )(asked, *in_hbm(moments, cell_visc, cell_dens))


def field_of(fields, index):
    return fields[0].at[index] if index < 3 else fields[index - 2]


def pack_x_body(*refs):
    ends, outs = refs[:8], refs[8:]
    for side in range(2):
        for f in range(6):
            outs[side][f] = field_of(ends[side::2], f)[...]


def pack_x(velocity, pressure, cell_visc, cell_dens):
    size_x, size_y, size_z = cell_visc.shape
    width = SWEEPS
    ends = (0, size_x // width - 1)
    vel = [
        pl.BlockSpec((3, width, size_y, size_z), lambda i, e=e: (0, e, 0, 0)) for e in ends
    ]
    block = [pl.BlockSpec((width, size_y, size_z), lambda i, e=e: (e, 0, 0)) for e in ends]
    whole = pl.BlockSpec((6, width, size_y, size_z), lambda i: (0, 0, 0, 0))
    shape = jax.ShapeDtypeStruct((6, width, size_y, size_z), f32)
    return pl.pallas_call(
        pack_x_body,
        grid=(1,),
        out_shape=(shape, shape),
        in_specs=vel + block * 3,
        out_specs=(whole, whole),
        compiler_params=vmem_limit(60),
        cost_estimate=cost(2),
        name="pack_x",
    )(velocity, velocity, pressure, pressure, cell_visc, cell_visc, cell_dens, cell_dens)


def corner_rows(upward, size_x):
    width = SWEEPS
    spare = (5 * width,) if upward else (4 * width - 1, 6 * width - 1)
    places = [(plane, row) for plane in range(size_x) for row in spare]
    found = []
    for field in range(6):
        for side in range(2):
            near = field == 5 or (field == 3 and side == 1 and not upward)
            reach = width - 1 if near else width
            for far_x in range(1, width):
                for far_y in range(1, reach - far_x + 1):
                    found.append((field, side, far_x, far_y))
    more = max(0, len(found) - len(places))
    places += [(size_x + n // (6 * width), n % (6 * width)) for n in range(more)]
    return [cell + at for cell, at in zip(found, places)], size_x + -(-more // (6 * width))


def pack_y_body(size_x, vel, pres, visc, dens, low_x, high_x, *refs):
    sources, (upward, downward), targets, done = refs[:3], refs[3:5], refs[5:8], refs[8]
    fetches = [
        pltpu.make_async_copy(source, target, done.at[n])
        for n, (source, target) in enumerate(zip(sources, targets))
    ]

    @pl.when(pl.program_id(0) == 0)
    def _():
        for fetch in fetches:
            fetch.start()

    step_x, size_y, _ = pres.shape
    width = SWEEPS
    step = pl.program_id(0)
    planes = pl.ds(pl.multiple_of(step * step_x, step_x), step_x)
    for f in range(6):
        field = field_of((vel, pres, visc, dens), f)
        rows = slice(f * width, (f + 1) * width)
        upward[planes, rows, :] = field[:, size_y - width :, :]
        downward[planes, rows, :] = field[:, :width, :]

    @pl.when(step == pl.num_programs(0) - 1)
    def _():
        for up, face in ((True, upward), (False, downward)):
            for f, side, far_x, far_y, plane, row in corner_rows(up, size_x)[0]:
                halo, at = (high_x, far_x - 1) if side else (low_x, width - far_x)
                face[plane, row] = halo[f, at, size_y - far_y if up else far_y - 1]
        for fetch in fetches:
            fetch.wait()


def pack_y(velocity, pressure, cell_visc, cell_dens, low_x, high_x, *fetched):
    size_x, size_y, size_z = cell_visc.shape
    step = 8
    block = pl.BlockSpec((step, size_y, size_z), lambda i: (i, 0, 0))
    halo = pl.BlockSpec(low_x.shape, lambda i: (0, 0, 0, 0))
    anywhere = pl.BlockSpec(memory_space=pl.ANY)
    shapes = [(corner_rows(up, size_x)[1], 6 * SWEEPS, size_z) for up in (True, False)]
    return pl.pallas_call(
        functools.partial(pack_y_body, size_x),
        grid=(size_x // step,),
        out_shape=tuple(jax.ShapeDtypeStruct(shape, f32) for shape in shapes)
        + tuple(pltpu.VMEM(array.shape, f32) for array in fetched),
        in_specs=[
            pl.BlockSpec((3, step, size_y, size_z), lambda i: (0, i, 0, 0)),
            block,
            block,
            block,
            halo,
            halo,
        ]
        + [anywhere] * len(fetched),
        out_specs=tuple(pl.BlockSpec(shape, lambda i: (0, 0, 0)) for shape in shapes)
        + (anywhere,) * len(fetched),
        scratch_shapes=[pltpu.SemaphoreType.DMA((3,))],
        compiler_params=vmem_limit(24),
        cost_estimate=cost(15),
        name="pack_y",
    )(*in_hbm(velocity, pressure, cell_visc, cell_dens, low_x, high_x, *fetched))


def place(per, x, y, rows):
    return x % per, pl.ds(y * SUBLANES + x // per, rows, stride=SUBLANES)


def put(target, x, y, rows, value):
    per, halves = target.shape[:2]
    plane, lines = place(per, x, y, rows)
    for half in range(halves):
        target[plane, half, lines, :] = value[:, half * LANES : (half + 1) * LANES]


def tile(y):
    if isinstance(y, int):
        return pl.ds(y * SUBLANES, SUBLANES)
    return pl.ds(pl.multiple_of(y * SUBLANES, SUBLANES), SUBLANES)


def row_work(cells, coefs, relax, forcing, rate):
    per, halves = cells.shape[1:3]
    lane = lax.broadcasted_iota(jnp.int32, (SUBLANES, LANES), 1)
    at_first, at_last = lane == 0, lane == LANES - 1

    def take(field, plane, y):
        return jnp.concatenate([field[plane, half, tile(y), :] for half in range(halves)], axis=1)

    def store(field, plane, y, value):
        for half in range(halves):
            field[plane, half, tile(y), :] = value[:, half * LANES : (half + 1) * LANES]

    def up_x(field, plane, y):
        if plane < per - 1:
            return take(field, plane + 1, y)
        return pltpu.roll(take(field, 0, y), SUBLANES - 1, 0)

    def down_x(field, plane, y):
        if plane > 0:
            return take(field, plane - 1, y)
        return pltpu.roll(take(field, per - 1, y), 1, 0)

    def rolled(a, shift):
        return [
            pltpu.roll(a[:, half * LANES : (half + 1) * LANES], shift, 1) for half in range(halves)
        ]

    def up_z(a):
        parts = rolled(a, LANES - 1)
        after = parts[1:] + [jnp.zeros_like(parts[0])]
        return jnp.concatenate([jnp.where(at_last, n, p) for p, n in zip(parts, after)], axis=1)

    def down_z(a):
        parts = rolled(a, 1)
        before = [jnp.zeros_like(parts[0])] + parts[:-1]
        return jnp.concatenate([jnp.where(at_first, b, p) for p, b in zip(parts, before)], axis=1)

    def prepare(y):
        visc, dens = cells.at[0], cells.at[1]
        for plane in range(per):
            here = take(visc, plane, y)
            near = [
                up_x(visc, plane, y),
                down_x(visc, plane, y),
                take(visc, plane, y + 1),
                take(visc, plane, y - 1),
                up_z(here),
                down_z(here),
            ]
            links = [0.5 * (here + other) for other in near]
            scale = jnp.where(here > 0.0, RELAX / add_all(links), 0.0)
            for n in range(6):
                coefs[n, plane, tile(y), :] = links[n] * scale
            relax[plane, tile(y), :] = scale
            forcing[plane, tile(y), :] = take(dens, plane, y) * (-GRAVITY * scale)
            rate[plane, tile(y), :] = PRESSURE_RATE * here

    def sweep(y, old, new):
        for plane in range(per):
            links = [coefs[n, plane, tile(y), :] for n in range(6)]
            scale = relax[plane, tile(y), :]
            pressure = take(old.at[3], plane, y)
            before = (
                down_x(old.at[3], plane, y),
                take(old.at[3], plane, y - 1),
                down_z(pressure),
            )
            changes = []
            for c in range(3):
                field = old.at[c]
                here = take(field, plane, y)
                near = [
                    up_x(field, plane, y),
                    down_x(field, plane, y),
                    take(field, plane, y + 1),
                    take(field, plane, y - 1),
                    up_z(here),
                    down_z(here),
                ]
                terms = [link * other for link, other in zip(links, near)]
                total = (terms[0] + terms[1]) + (terms[2] + terms[3])
                total = total + (terms[4] + terms[5])
                rest = (1.0 - RELAX) * here - scale * (pressure - before[c])
                if c == 2:
                    rest = rest + forcing[plane, tile(y), :]
                changes.append(near[2 * c] - here)
                store(new.at[c], plane, y, total + rest)
            pressed = pressure - rate[plane, tile(y), :] * add_all(changes)
            store(new.at[3], plane, y, pressed)

    return prepare, sweep


def kept_rows(size_y):
    width = SWEEPS
    return (
        ((width, size_y),),
        ((width + 1, width), (size_y - 1, width)),
        ((width, width + 1), (size_y - 1, width + 1)),
    )


def kept_copies(pairs, size_y, done):
    copies = []
    for (source, target), strips in zip(pairs, kept_rows(size_y)):
        for begin, rows in strips:
            span = (slice(None),) * 3 + (pl.ds(begin * SUBLANES, rows * SUBLANES),)
            copies.append(
                pltpu.make_async_copy(source.at[span], target.at[span], done.at[len(copies)])
            )
    return copies


def inner_body(vel, pres, visc, dens, low_x, high_x, _, even_out, odd_out, cells_out, *work):
    blocks, sides_x, even, odd, cells, coefs, relax, forcing, rate, done = work
    size_x, size_y, size_z = blocks.shape[1:]
    width = SWEEPS
    inputs = (
        (visc, blocks.at[4], (4,)),
        (vel, blocks.at[0:3], (0, 1, 2)),
        (pres, blocks.at[3], (3,)),
        (dens, blocks.at[5], (5,)),
        (low_x, sides_x.at[0], ()),
        (high_x, sides_x.at[1], ()),
    )
    copies = [
        pltpu.make_async_copy(there, here, done.at[n]) for n, (there, here, _) in enumerate(inputs)
    ]
    for copy in copies:
        copy.start()
    targets = [even.at[n] for n in range(4)] + [cells.at[n] for n in range(2)]
    for copy, (_, _, held) in zip(copies, inputs):
        copy.wait()
        for f in held:
            for i in range(size_x):
                for y in range(0, size_y, SUBLANES):
                    value = blocks[f, i, y : y + SUBLANES, :]
                    put(targets[f], i + width, y + width, SUBLANES, value)
    for side, begin in enumerate((0, width + size_x)):
        for f in range(6):
            for i in range(width):
                for y in range(0, size_y, SUBLANES):
                    value = sides_x[side, f, i, y : y + SUBLANES, :]
                    put(targets[f], begin + i, y + width, SUBLANES, value)

    prepare, sweep = row_work(cells, coefs, relax, forcing, rate)

    def prepare_row(y, carry):
        prepare(y)
        return carry

    first, last = width + 1, width + size_y - 1
    lax.fori_loop(first, last, prepare_row, 0, unroll=2)
    for step in range(SWEEPS):
        old, new = (odd, even) if step % 2 else (even, odd)

        def sweep_row(y, carry, old=old, new=new):
            sweep(y, old, new)
            return carry

        lax.fori_loop(first + step, last - step, sweep_row, 0, unroll=2)
    sends = kept_copies(((even, even_out), (odd, odd_out), (cells, cells_out)), size_y, done)
    for send in sends:
        send.start()
    for send in sends:
        send.wait()


def inner_sweeps(velocity, pressure, cell_visc, cell_dens, low_x, high_x, after):
    size_x, size_y, size_z = cell_visc.shape
    width = low_x.shape[1]
    per, rows = (size_x + 2 * width) // SUBLANES, (size_y + 2 * width) * SUBLANES
    block, cut = (per, rows, size_z), (per, size_z // LANES, rows, LANES)
    shapes = [(4,) + cut, (4,) + cut, (2,) + cut]
    anywhere = pl.BlockSpec(memory_space=pl.ANY)
    return pl.pallas_call(
        inner_body,
        out_shape=tuple(jax.ShapeDtypeStruct(shape, f32) for shape in shapes),
        in_specs=[anywhere] * 7,
        out_specs=(anywhere,) * 3,
        scratch_shapes=[
            pltpu.VMEM((6,) + cell_visc.shape, f32),
            pltpu.VMEM((2,) + low_x.shape, f32),
        ]
        + [pltpu.VMEM(shape, f32) for shape in shapes]
        + [
            pltpu.VMEM((6,) + block, f32),
            pltpu.VMEM(block, f32),
            pltpu.VMEM(block, f32),
            pltpu.VMEM(block, f32),
            pltpu.SemaphoreType.DMA((6,)),
        ],
        compiler_params=vmem_limit(40),
        cost_estimate=cost(25),
        name="inner_sweeps",
    )(*in_hbm(velocity, pressure, cell_visc, cell_dens, low_x, high_x), after)


def edge_body(even_in, odd_in, cells_in, low_y, high_y, vel_out, pres_out, *work):
    from_low, from_high, results, even, odd, cells, coefs, relax, forcing, rate, done, more = work
    size_x, size_y, size_z = results.shape[1:]
    width = SWEEPS
    long_y = size_y + 2 * width
    halos = [
        pltpu.make_async_copy(low_y, from_low, more.at[0]),
        pltpu.make_async_copy(high_y, from_high, more.at[1]),
    ]
    kept = kept_copies(((even_in, even), (odd_in, odd), (cells_in, cells)), size_y, done)
    for copy in (*halos, *kept[3:], *kept[:3]):
        copy.start()
    targets = [even.at[n] for n in range(4)] + [cells.at[n] for n in range(2)]
    for target in targets:
        for x in (*range(width), *range(width + size_x, size_x + 2 * width)):
            for y in (0, width + size_y):
                put(target, x, y, width, jnp.zeros((width, size_z), f32))
    for up, halo, copy, begin in (
        (True, from_low, halos[0], 0),
        (False, from_high, halos[1], width + size_y),
    ):
        copy.wait()
        for f, target in enumerate(targets):
            rows = slice(f * width, (f + 1) * width)
            for i in range(size_x):
                put(target, i + width, begin, width, halo[i, rows, :])
        for f, side, far_x, far_y, plane, row in corner_rows(up, size_x)[0]:
            x = width + size_x - 1 + far_x if side else width - far_x
            y = width - far_y if up else width + size_y - 1 + far_y
            put(targets[f], x, y, 1, halo[plane, row : row + 1, :])
    for copy in kept:
        copy.wait()

    prepare, sweep = row_work(cells, coefs, relax, forcing, rate)

    def prepare_rows(n, carry):
        prepare(1 + n)
        prepare(long_y - 2 * width + n)
        return carry

    lax.fori_loop(0, 2 * width - 1, prepare_rows, 0)
    for step in range(SWEEPS):
        old, new = (odd, even) if step % 2 else (even, odd)

        def sweep_rows(n, carry, old=old, new=new, step=step):
            sweep(1 + step + n, old, new)
            sweep(width + size_y - 1 - step + n, old, new)
            return carry

        lax.fori_loop(0, width, sweep_rows, 0)

    final = odd if SWEEPS % 2 else even
    outs = [vel_out.at[0], vel_out.at[1], vel_out.at[2], pres_out]
    sends = [pltpu.make_async_copy(results.at[n], out, done.at[n]) for n, out in enumerate(outs)]
    per, halves = even.shape[1:3]
    for field, send in enumerate(sends):
        for i in range(size_x):
            for y in range(0, size_y, SUBLANES):
                plane, lines = place(per, i + width, y + width, SUBLANES)
                for half in range(halves):
                    columns = slice(half * LANES, (half + 1) * LANES)
                    results[field, i, y : y + SUBLANES, columns] = final[
                        field, plane, half, lines, :
                    ]
        send.start()
    for send in sends:
        send.wait()


def edge_sweeps(even, odd, cells, low_y, high_y, size_x, size_y):
    per, halves, rows = even.shape[1:4]
    size_z = halves * LANES
    block = (per, rows, size_z)
    anywhere = pl.BlockSpec(memory_space=pl.ANY)
    return pl.pallas_call(
        edge_body,
        out_shape=(
            jax.ShapeDtypeStruct((3, size_x, size_y, size_z), f32),
            jax.ShapeDtypeStruct((size_x, size_y, size_z), f32),
        ),
        in_specs=[anywhere] * 5,
        out_specs=(anywhere,) * 2,
        scratch_shapes=[
            pltpu.VMEM(low_y.shape, f32),
            pltpu.VMEM(high_y.shape, f32),
            pltpu.VMEM((4, size_x, size_y, size_z), f32),
            pltpu.VMEM(even.shape, f32),
            pltpu.VMEM(odd.shape, f32),
            pltpu.VMEM(cells.shape, f32),
            pltpu.VMEM((6,) + block, f32),
            pltpu.VMEM(block, f32),
            pltpu.VMEM(block, f32),
            pltpu.VMEM(block, f32),
            pltpu.SemaphoreType.DMA((5,)),
            pltpu.SemaphoreType.DMA((2,)),
        ],
        compiler_params=vmem_limit(40),
        cost_estimate=cost(1),
        name="edge_sweeps",
    )(even, odd, cells, low_y, high_y)


def shift(value, axis, step):
    size = lax.axis_size(axis)
    pairs = [(i, i + step) for i in range(size) if 0 <= i + step < size]
    return lax.ppermute(value, axis, pairs)


def per_device(
    velocity,
    pressure,
    cell_visc,
    cell_dens,
    block_brick,
    block_counts,
    positions,
    start_visc,
    marker_dens,
):
    asked = lax.all_to_all(block_brick, "mark", 0, 0, tiled=True)
    fields = (velocity, pressure, cell_visc, cell_dens)
    to_low, to_high = pack_x(*fields)
    low_x, high_x = shift(to_high, "grid", 1), shift(to_low, "grid", -1)
    marker_data = by_halves(positions, start_visc, marker_dens)
    upward, downward, *marker_data = pack_y(*fields, low_x, high_x, *marker_data)
    low_y, high_y = shift(upward, "mark", 1), shift(downward, "mark", -1)

    picked = pick_bricks(asked, velocity)
    bricks = lax.all_to_all(picked, "mark", 0, 0, tiled=True)
    marker_visc, moments = marker_work(block_counts, *marker_data, bricks)
    gathered = lax.all_to_all(moments, "mark", 0, 0, tiled=True)
    state = inner_sweeps(*fields, low_x, high_x, moments)
    velocity_next, pressure_next = edge_sweeps(*state, low_y, high_y, *pressure.shape[:2])
    visc_next, dens_next = settle(asked, gathered, cell_visc, cell_dens)
    return velocity_next, pressure_next, visc_next, dens_next, marker_visc


def solution(mesh):
    in_specs = (
        P(None, "grid", "mark", None),
        P("grid", "mark", None),
        P("grid", "mark", None),
        P("grid", "mark", None),
        P(("grid", "mark"), None),
        P(("grid", "mark"), None),
        P(("grid", "mark"), None, None, None),
        P(("grid", "mark"), None, None),
        P(("grid", "mark"), None, None),
    )
    out_specs = (
        P(None, "grid", "mark", None),
        P("grid", "mark", None),
        P("grid", "mark", None),
        P("grid", "mark", None),
        P(("grid", "mark"), None, None),
    )
    return jax.shard_map(
        per_device, mesh=mesh, in_specs=in_specs, out_specs=out_specs, check_vma=False
    )
```

```python
import functools

import jax
import jax.numpy as jnp
import numpy as np
from jax import lax
from jax.experimental import pallas as pl
from jax.experimental.pallas import tpu as pltpu
from jax.sharding import PartitionSpec as P

SWEEPS = 4
RELAX = 0.6
PRESSURE_RATE = 0.25
GRAVITY = 1.0
STRAIN_SCALE = 0.5

BX, BY, BZ = 4, 4, 8
PLANE = BX * BY
ROWS = 3 * PLANE
LANES = 128
GROUP = LANES // BZ
HALF = 8
SUBLANES = 8

f32, bf16 = jnp.float32, jnp.bfloat16


def vmem_limit(mib):
    return pltpu.CompilerParams(vmem_limit_bytes=mib * 1024 * 1024)


def in_hbm(*arrays):
    return [pltpu.with_memory_space_constraint(array, pltpu.HBM) for array in arrays]


def cost(microseconds):
    return pl.CostEstimate(
        flops=int(microseconds * 1.15e9), bytes_accessed=0, transcendentals=0
    )


def place_of(brick):
    return lax.shift_right_logical(brick, GROUP.bit_length() - 1), (brick & (GROUP - 1)) * BZ


def pick_body(asked, vel, out, table):
    size_x, size_y, size_z = vel.shape[1:]
    bricks_y, halves = size_y // BY, size_z // LANES

    def repack(block_x, carry):
        for block_y in range(bricks_y):
            for half in range(halves):
                place = (block_x * bricks_y + block_y) * halves + half
                for c in range(3):
                    for i in range(BX):
                        row = (c * BX + i) * BY
                        table[place, row : row + BY, :] = vel[
                            c,
                            block_x * BX + i,
                            block_y * BY : (block_y + 1) * BY,
                            half * LANES : (half + 1) * LANES,
                        ]
        return carry

    lax.fori_loop(0, size_x // BX, repack, 0)
    groups = out.shape[1]
    lane_slot = lax.broadcasted_iota(jnp.int32, (ROWS, LANES), 1) // BZ

    def one_group(step, carry):
        device, group = step // groups, step % groups
        packed = jnp.zeros((ROWS, LANES), f32)
        for slot in range(GROUP):
            place, lane = place_of(asked[device, group * GROUP + slot])
            rolled = pltpu.roll(table[place], (BZ * slot - lane) & (LANES - 1), 1)
            packed = jnp.where(lane_slot == slot, rolled, packed)
        out[device, group] = packed
        return carry

    lax.fori_loop(0, out.shape[0] * groups, one_group, 0)


def pick_bricks(asked, velocity):
    devices, slots = asked.shape
    size_x, size_y, size_z = velocity.shape[1:]
    places = (size_x // BX) * (size_y // BY) * (size_z // LANES)
    return pl.pallas_call(
        pick_body,
        out_shape=jax.ShapeDtypeStruct((devices, slots // GROUP, ROWS, LANES), f32),
        in_specs=[
            pl.BlockSpec(memory_space=pltpu.SMEM),
            pl.BlockSpec(memory_space=pltpu.VMEM),
        ],
        out_specs=pl.BlockSpec(memory_space=pltpu.VMEM),
        scratch_shapes=[pltpu.VMEM((places, ROWS, LANES), f32)],
        compiler_params=vmem_limit(24),
        cost_estimate=cost(25),
        name="pick_bricks",
    )(asked, velocity)


def permutations():
    inside = BZ * HALF
    spread = np.zeros((2, 2, LANES, 4 * inside), np.float32)
    gather = np.zeros((2 * BY * inside, BY * LANES), np.float32)
    for half in range(2):
        for slot in range(HALF):
            for z in range(BZ):
                outer, inner = (half * HALF + slot) * BZ + z, z * HALF + slot
                for part in range(4):
                    spread[half, part // 2, outer, part * inside + inner] = 1
                for j in range(BY):
                    gather[(half * BY + j) * inside + inner, j * LANES + outer] = 1
    return jnp.asarray(spread, bf16), jnp.asarray(gather, bf16)


def split(value):
    high = value.astype(bf16)
    return high, (value - high.astype(f32)).astype(bf16)


def add_all(values):
    return functools.reduce(jnp.add, values)


def axis_weights(fraction, cells):
    middle = (cells - 1) / 2
    base = jnp.exp(fraction * (2.0 * cells) - float(cells))
    powers = [None, base]
    for i in range(2, cells):
        powers.append(powers[i // 2] * powers[i - i // 2])
    factors = [float(np.exp(middle**2 - (i - middle) ** 2)) for i in range(cells)]
    bells = [None] + [powers[i] * factors[i] for i in range(1, cells)]
    scale = 1.0 / (add_all(bells[1:]) + factors[0])
    weights = [scale * factors[0]] + [bell * scale for bell in bells[1:]]
    mean = add_all(
        [
            (weights[cells - 1 - i] - weights[i]) * (2.0 * (middle - i))
            for i in range(cells // 2)
        ]
    )
    slopes = [w * (2.0 * (i - middle) - mean) for i, w in enumerate(weights)]
    return weights, slopes


def dot(a, b):
    return jnp.dot(a, b, preferred_element_type=f32)


def gradients(products, weights, markers):
    weight_x, slope_x, weight_y, slope_y = ([weights[4 * n + i] for i in range(4)] for n in range(4))
    grads = []
    for c in range(3):
        lines = [[], [], []]
        for i in range(BX):
            rows = [((c * BX + i) * BY + j) * HALF for j in range(BY)]
            still = [products[row : row + HALF, :markers] for row in rows]
            rising = [products[row : row + HALF, markers:] for row in rows]
            lines[0].append(slope_x[i] * add_all([w * t for w, t in zip(weight_y, still)]))
            lines[1].append(weight_x[i] * add_all([w * t for w, t in zip(slope_y, still)]))
            lines[2].append(weight_x[i] * add_all([w * t for w, t in zip(weight_y, rising)]))
        grads.append([add_all(line) for line in lines])
    return grads


def own_lanes():
    shape = (HALF, 4 * BZ * HALF)
    lane = lax.broadcasted_iota(jnp.int32, shape, 1)
    return (lane % HALF == lax.broadcasted_iota(jnp.int32, shape, 0)).astype(f32)


def marker_groups(groups, counts, ins, outs, buffers, sums):
    spread, gather, places, start, dens, brick = ins
    visc_out, moments_out = outs
    permuted, left, right, products, weights, factors, planes_high, planes_low = buffers
    markers = places.shape[-1]
    inside = BZ * HALF
    own = own_lanes()
    halves = [
        (owner, 2 * group + half, half, 2 * n + half)
        for n, (owner, group) in enumerate(groups)
        for half in range(2)
    ]
    parts = [split(brick[owner, group]) for owner, group in groups]
    for _, _, half, n in halves:
        high, low = parts[n // 2]
        permuted[n][...] = dot(high, spread[half, 0]) + dot(low, spread[half, 1])
    heights = []
    for owner, part, _, n in halves:
        weight_z, slope_z = axis_weights(places[owner, 2, part], BZ)
        heights.append(weight_z)
        for z in range(0, BZ, 2):
            for column, values in ((0, weight_z), (1, slope_z)):
                high, low = split(jnp.concatenate(values[z : z + 2], axis=0))
                columns = slice(column * markers, (column + 1) * markers)
                for k in range(4):
                    begin = k * inside + z * HALF
                    right[n][begin : begin + 2 * HALF, columns] = low if k % 2 else high
    for _, _, _, n in halves:
        for row in range(0, ROWS, 2):
            pair = [
                jnp.broadcast_to(permuted[n][r : r + 1, :], own.shape) * own for r in (row, row + 1)
            ]
            left[n][row * HALF : (row + 2) * HALF, :] = jnp.concatenate(pair, axis=0).astype(bf16)
    for _, _, _, n in halves:
        products[n][...] = dot(left[n][...], right[n][...])
    for owner, part, _, n in halves:
        weights_x = axis_weights(places[owner, 0, part], BX)
        weights_y = axis_weights(places[owner, 1, part], BY)
        for k, values in enumerate((*weights_x, *weights_y)):
            for i, value in enumerate(values):
                weights[n][4 * k + i] = value
        for j in range(BY):
            for z in range(0, BZ, 2):
                pair = [weights_y[0][j] * heights[n][z + k] for k in range(2)]
                rows = slice((j * BZ + z) * HALF, (j * BZ + z + 2) * HALF)
                high, low = split(jnp.concatenate(pair, axis=0))
                planes_high[n][rows, :] = high
                planes_low[n][rows, :] = low

    count = 3 * BX * HALF
    for owner, part, _, n in halves:
        grads = gradients(products[n], weights[n], markers)
        normal = grads[0][0] ** 2 + grads[1][1] ** 2 + grads[2][2] ** 2
        shear_xy = 0.5 * (grads[0][1] + grads[1][0])
        shear_xz = 0.5 * (grads[0][2] + grads[2][0])
        shear_yz = 0.5 * (grads[1][2] + grads[2][1])
        invariant = 0.5 * normal + shear_xy**2 + shear_xz**2 + shear_yz**2
        scaled = invariant * (1.0 / (STRAIN_SCALE * STRAIN_SCALE))
        third = jnp.log(1.0 + scaled) * (1.0 / 3.0)
        first = start[owner, part]
        slot = lax.broadcasted_iota(jnp.int32, first.shape, 0) + part * HALF
        live = slot < counts[0, owner]
        visc_out[owner, part] = jnp.where(live, first * jnp.exp(-third), 0.0)
        carried = (
            live.astype(f32),
            jnp.where(live, jnp.log(first) - third, 0.0),
            jnp.where(live, dens[owner, part], 0.0),
        )
        for c in range(3):
            for i in range(0, BX, 2):
                pair = [carried[c] * weights[n][i + k] for k in range(2)]
                row = (c * BX + i) * HALF
                high, low = split(jnp.concatenate(pair, axis=0))
                factors[n][row : row + 2 * HALF, :] = high
                factors[n][count + row : count + row + 2 * HALF, :] = low

    contract = (((1,), (1,)), ((), ()))
    found = []
    for _, _, _, n in halves:
        both = lax.dot_general(
            factors[n][...], planes_high[n][...], contract, preferred_element_type=f32
        )
        rest = lax.dot_general(
            factors[n][:count], planes_low[n][...], contract, preferred_element_type=f32
        )
        found.append((both, rest))
    for _, _, half, n in halves:
        both, rest = found[n]
        total = both[:count] + both[count:] + rest
        chosen = total.reshape(3 * BX, HALF, BY * inside) * own[None]
        high, low = split(jnp.sum(chosen, axis=1))
        columns = slice(half * BY * inside, (half + 1) * BY * inside)
        row = (n // 2) * 32
        sums[row : row + 3 * BX, columns] = high.astype(f32)
        sums[row + 16 : row + 16 + 3 * BX, columns] = low.astype(f32)
    moved = dot(sums[...].astype(bf16), gather[...])
    for n, (owner, group) in enumerate(groups):
        mine = moved[32 * n : 32 * n + 3 * BX] + moved[32 * n + 16 : 32 * n + 16 + 3 * BX]
        for j in range(BY):
            rows = pl.ds(j, 3 * BX, stride=BY)
            moments_out[owner, group, rows, :] = mine[:, j * LANES : (j + 1) * LANES]


TOGETHER = 3


def marker_body(counts, *refs):
    ins, outs, scratch = refs[:6], refs[7:9], refs[9:]
    listed, sums, *flat = scratch
    held = 2 * TOGETHER
    buffers = [flat[n * held : (n + 1) * held] for n in range(len(flat) // held)]
    visc_out, moments_out = outs
    owners, groups = moments_out.shape[:2]
    visc_out[...] = jnp.zeros_like(visc_out)
    moments_out[...] = jnp.zeros_like(moments_out)
    sums[...] = jnp.zeros_like(sums)

    def list_groups(index, number):
        owner, group = index // groups, index % groups
        live = group * GROUP < counts[0, owner]

        @pl.when(live)
        def _():
            for n in range(TOGETHER):
                listed[2 * (number + n)] = owner
                listed[2 * (number + n) + 1] = group

        return jnp.where(live, number + 1, number)

    number = lax.fori_loop(0, owners * groups, list_groups, 0)

    def step(index, carry):
        first = TOGETHER * index
        taken = [
            (listed[2 * (first + n)], listed[2 * (first + n) + 1]) for n in range(TOGETHER)
        ]
        marker_groups(taken, counts, ins, outs, buffers, sums)
        return carry

    lax.fori_loop(0, (number + TOGETHER - 1) // TOGETHER, step, 0)


def marker_work(counts, positions, start_visc, marker_dens, bricks, after):
    owners, _, slots, markers = positions.shape
    groups, parts = slots // GROUP, slots // HALF
    spread, gather = permutations()
    width = 4 * BZ * HALF
    whole = pl.BlockSpec(memory_space=pltpu.VMEM)
    buffers = (
        pltpu.VMEM((ROWS, width), f32),
        pltpu.VMEM((ROWS * HALF, width), bf16),
        pltpu.VMEM((width, 2 * markers), bf16),
        pltpu.VMEM((ROWS * HALF, 2 * markers), f32),
        pltpu.VMEM((4 * 4, HALF, markers), f32),
        pltpu.VMEM((2 * 3 * BX * HALF, markers), bf16),
        pltpu.VMEM((BY * BZ * HALF, markers), bf16),
        pltpu.VMEM((BY * BZ * HALF, markers), bf16),
    )
    visc, moments = pl.pallas_call(
        marker_body,
        out_shape=(
            jax.ShapeDtypeStruct((owners, parts, HALF, markers), f32),
            jax.ShapeDtypeStruct((owners, groups, ROWS, LANES), f32),
        ),
        in_specs=[pl.BlockSpec(memory_space=pltpu.SMEM)]
        + [whole] * 6
        + [pl.BlockSpec(memory_space=pl.ANY)],
        out_specs=(whole, whole),
        scratch_shapes=[
            pltpu.SMEM((2 * (owners * groups + TOGETHER),), jnp.int32),
            pltpu.VMEM((32 * TOGETHER, 2 * BY * BZ * HALF), f32),
        ]
        + [buffer for buffer in buffers for _ in range(2 * TOGETHER)],
        compiler_params=vmem_limit(40),
        cost_estimate=cost(25),
        name="marker_work",
    )(
        counts,
        *in_hbm(
            spread,
            gather,
            positions.reshape(owners, 3, parts, HALF, markers),
            start_visc.reshape(owners, parts, HALF, markers),
            marker_dens.reshape(owners, parts, HALF, markers),
            bricks,
        ),
        after,
    )
    return visc.reshape(owners, slots, markers), moments


def settle_body(asked, moments_in, visc_in, dens_in, visc_out, dens_out, *scratch):
    moments, visc, dens, done, *tables = scratch
    size_x, size_y, size_z = visc.shape
    copies = [
        pltpu.make_async_copy(there, here, done.at[n])
        for n, (there, here) in enumerate(
            ((moments_in, moments), (visc_in, visc), (dens_in, dens))
        )
    ]
    for copy in copies:
        copy.start()
    bricks_y, halves = size_y // BY, size_z // LANES
    for table in tables:
        table[...] = jnp.zeros_like(table)
    copies[0].wait()
    groups = moments.shape[1]
    lane_slot = lax.broadcasted_iota(jnp.int32, (ROWS, LANES), 1) // BZ

    def one_group(step, carry):
        device, group = step // groups, step % groups
        packed = moments[device, group]
        for slot in range(GROUP):
            table = tables[slot % len(tables)]
            place, lane = place_of(asked[device, group * GROUP + slot])
            piece = jnp.where(lane_slot == slot, packed, 0.0)
            piece = pltpu.roll(piece, (lane - BZ * slot) & (LANES - 1), 1)
            table[place] = table[place] + piece
        return carry

    lax.fori_loop(0, moments.shape[0] * groups, one_group, 0)
    copies[1].wait()
    copies[2].wait()

    def finish(block_x, carry):
        for block_y in range(0, bricks_y, 2):
            for half in range(halves):
                for i in range(BX):
                    here = (
                        block_x * BX + i,
                        slice(block_y * BY, (block_y + 2) * BY),
                        slice(half * LANES, (half + 1) * LANES),
                    )
                    sums = []
                    for c in range(3):
                        rows = slice((c * BX + i) * BY, (c * BX + i + 1) * BY)
                        places = [
                            (block_x * bricks_y + block_y + k) * halves + half for k in range(2)
                        ]
                        sums.append(
                            jnp.concatenate(
                                [add_all([t[place, rows, :] for t in tables]) for place in places]
                            )
                        )
                    scale = 1.0 / (sums[0] + 1.0)
                    visc_out[here] = jnp.exp((sums[1] + jnp.log(visc[here])) * scale)
                    dens_out[here] = (sums[2] + dens[here]) * scale
        return carry

    lax.fori_loop(0, size_x // BX, finish, 0)


def settle(asked, moments, cell_visc, cell_dens):
    size_x, size_y, size_z = cell_visc.shape
    places = (size_x // BX) * (size_y // BY) * (size_z // LANES)
    whole = pl.BlockSpec(memory_space=pltpu.VMEM)
    shape = jax.ShapeDtypeStruct(cell_visc.shape, f32)
    return pl.pallas_call(
        settle_body,
        out_shape=(shape, shape),
        in_specs=[pl.BlockSpec(memory_space=pltpu.SMEM)]
        + [pl.BlockSpec(memory_space=pl.ANY)] * 3,
        out_specs=(whole, whole),
        scratch_shapes=[
            pltpu.VMEM(moments.shape, f32),
            pltpu.VMEM(cell_visc.shape, f32),
            pltpu.VMEM(cell_visc.shape, f32),
            pltpu.SemaphoreType.DMA((3,)),
        ]
        + [pltpu.VMEM((places, ROWS, LANES), f32)],
        compiler_params=vmem_limit(24),
        cost_estimate=cost(7),
        name="settle",
    )(asked, *in_hbm(moments, cell_visc, cell_dens))


def field_of(fields, index):
    return fields[0].at[index] if index < 3 else fields[index - 2]


def pack_x_body(*refs):
    ends, outs = refs[:8], refs[8:]
    for side in range(2):
        for f in range(6):
            outs[side][f] = field_of(ends[side::2], f)[...]


def pack_x(velocity, pressure, cell_visc, cell_dens):
    size_x, size_y, size_z = cell_visc.shape
    width = SWEEPS
    ends = (0, size_x // width - 1)
    vel = [
        pl.BlockSpec((3, width, size_y, size_z), lambda i, e=e: (0, e, 0, 0)) for e in ends
    ]
    block = [pl.BlockSpec((width, size_y, size_z), lambda i, e=e: (e, 0, 0)) for e in ends]
    whole = pl.BlockSpec((6, width, size_y, size_z), lambda i: (0, 0, 0, 0))
    shape = jax.ShapeDtypeStruct((6, width, size_y, size_z), f32)
    return pl.pallas_call(
        pack_x_body,
        grid=(1,),
        out_shape=(shape, shape),
        in_specs=vel + block * 3,
        out_specs=(whole, whole),
        compiler_params=vmem_limit(60),
        cost_estimate=cost(2),
        name="pack_x",
    )(velocity, velocity, pressure, pressure, cell_visc, cell_visc, cell_dens, cell_dens)


def corner_rows(upward, size_x):
    width = SWEEPS
    spare = (5 * width,) if upward else (4 * width - 1, 6 * width - 1)
    places = [(plane, row) for plane in range(size_x) for row in spare]
    found = []
    for field in range(6):
        for side in range(2):
            near = field == 5 or (field == 3 and side == 1 and not upward)
            reach = width - 1 if near else width
            for far_x in range(1, width):
                for far_y in range(1, reach - far_x + 1):
                    found.append((field, side, far_x, far_y))
    more = max(0, len(found) - len(places))
    places += [(size_x + n // (6 * width), n % (6 * width)) for n in range(more)]
    return [cell + at for cell, at in zip(found, places)], size_x + -(-more // (6 * width))


def pack_y_body(size_x, vel, pres, visc, dens, low_x, high_x, upward, downward):
    step_x, size_y, _ = pres.shape
    width = SWEEPS
    step = pl.program_id(0)
    planes = pl.ds(pl.multiple_of(step * step_x, step_x), step_x)
    for f in range(6):
        field = field_of((vel, pres, visc, dens), f)
        rows = slice(f * width, (f + 1) * width)
        upward[planes, rows, :] = field[:, size_y - width :, :]
        downward[planes, rows, :] = field[:, :width, :]

    @pl.when(step == pl.num_programs(0) - 1)
    def _():
        for up, face in ((True, upward), (False, downward)):
            for f, side, far_x, far_y, plane, row in corner_rows(up, size_x)[0]:
                halo, at = (high_x, far_x - 1) if side else (low_x, width - far_x)
                face[plane, row] = halo[f, at, size_y - far_y if up else far_y - 1]


def pack_y(velocity, pressure, cell_visc, cell_dens, low_x, high_x):
    size_x, size_y, size_z = cell_visc.shape
    step = 8
    block = pl.BlockSpec((step, size_y, size_z), lambda i: (i, 0, 0))
    halo = pl.BlockSpec(low_x.shape, lambda i: (0, 0, 0, 0))
    shapes = [(corner_rows(up, size_x)[1], 6 * SWEEPS, size_z) for up in (True, False)]
    return pl.pallas_call(
        functools.partial(pack_y_body, size_x),
        grid=(size_x // step,),
        out_shape=tuple(jax.ShapeDtypeStruct(shape, f32) for shape in shapes),
        in_specs=[
            pl.BlockSpec((3, step, size_y, size_z), lambda i: (0, i, 0, 0)),
            block,
            block,
            block,
            halo,
            halo,
        ],
        out_specs=tuple(pl.BlockSpec(shape, lambda i: (0, 0, 0)) for shape in shapes),
        compiler_params=vmem_limit(24),
        cost_estimate=cost(15),
        name="pack_y",
    )(*in_hbm(velocity, pressure, cell_visc, cell_dens, low_x, high_x))


def place(per, x, y, rows):
    return x % per, pl.ds(y * SUBLANES + x // per, rows, stride=SUBLANES)


def put(target, x, y, rows, value):
    per, halves = target.shape[:2]
    plane, lines = place(per, x, y, rows)
    for half in range(halves):
        target[plane, half, lines, :] = value[:, half * LANES : (half + 1) * LANES]


def tile(y):
    if isinstance(y, int):
        return pl.ds(y * SUBLANES, SUBLANES)
    return pl.ds(pl.multiple_of(y * SUBLANES, SUBLANES), SUBLANES)


def row_work(cells, coefs, relax, forcing, rate):
    per, halves = cells.shape[1:3]
    lane = lax.broadcasted_iota(jnp.int32, (SUBLANES, LANES), 1)
    at_first, at_last = lane == 0, lane == LANES - 1

    def take(field, plane, y):
        return jnp.concatenate([field[plane, half, tile(y), :] for half in range(halves)], axis=1)

    def store(field, plane, y, value):
        for half in range(halves):
            field[plane, half, tile(y), :] = value[:, half * LANES : (half + 1) * LANES]

    def up_x(field, plane, y):
        if plane < per - 1:
            return take(field, plane + 1, y)
        return pltpu.roll(take(field, 0, y), SUBLANES - 1, 0)

    def down_x(field, plane, y):
        if plane > 0:
            return take(field, plane - 1, y)
        return pltpu.roll(take(field, per - 1, y), 1, 0)

    def rolled(a, shift):
        return [
            pltpu.roll(a[:, half * LANES : (half + 1) * LANES], shift, 1) for half in range(halves)
        ]

    def up_z(a):
        parts = rolled(a, LANES - 1)
        after = parts[1:] + [jnp.zeros_like(parts[0])]
        return jnp.concatenate([jnp.where(at_last, n, p) for p, n in zip(parts, after)], axis=1)

    def down_z(a):
        parts = rolled(a, 1)
        before = [jnp.zeros_like(parts[0])] + parts[:-1]
        return jnp.concatenate([jnp.where(at_first, b, p) for p, b in zip(parts, before)], axis=1)

    def prepare(y):
        visc, dens = cells.at[0], cells.at[1]
        for plane in range(per):
            here = take(visc, plane, y)
            near = [
                up_x(visc, plane, y),
                down_x(visc, plane, y),
                take(visc, plane, y + 1),
                take(visc, plane, y - 1),
                up_z(here),
                down_z(here),
            ]
            links = [0.5 * (here + other) for other in near]
            scale = jnp.where(here > 0.0, RELAX / add_all(links), 0.0)
            for n in range(6):
                coefs[n, plane, tile(y), :] = links[n] * scale
            relax[plane, tile(y), :] = scale
            forcing[plane, tile(y), :] = take(dens, plane, y) * (-GRAVITY * scale)
            rate[plane, tile(y), :] = PRESSURE_RATE * here

    def sweep(y, old, new):
        for plane in range(per):
            links = [coefs[n, plane, tile(y), :] for n in range(6)]
            scale = relax[plane, tile(y), :]
            pressure = take(old.at[3], plane, y)
            before = (
                down_x(old.at[3], plane, y),
                take(old.at[3], plane, y - 1),
                down_z(pressure),
            )
            changes = []
            for c in range(3):
                field = old.at[c]
                here = take(field, plane, y)
                near = [
                    up_x(field, plane, y),
                    down_x(field, plane, y),
                    take(field, plane, y + 1),
                    take(field, plane, y - 1),
                    up_z(here),
                    down_z(here),
                ]
                terms = [link * other for link, other in zip(links, near)]
                total = (terms[0] + terms[1]) + (terms[2] + terms[3])
                total = total + (terms[4] + terms[5])
                rest = (1.0 - RELAX) * here - scale * (pressure - before[c])
                if c == 2:
                    rest = rest + forcing[plane, tile(y), :]
                changes.append(near[2 * c] - here)
                store(new.at[c], plane, y, total + rest)
            pressed = pressure - rate[plane, tile(y), :] * add_all(changes)
            store(new.at[3], plane, y, pressed)

    return prepare, sweep


def kept_rows(size_y):
    width = SWEEPS
    return (
        ((width, size_y),),
        ((width + 1, width), (size_y - 1, width)),
        ((width, width + 1), (size_y - 1, width + 1)),
    )


def kept_copies(pairs, size_y, done):
    copies = []
    for (source, target), strips in zip(pairs, kept_rows(size_y)):
        for begin, rows in strips:
            span = (slice(None),) * 3 + (pl.ds(begin * SUBLANES, rows * SUBLANES),)
            copies.append(
                pltpu.make_async_copy(source.at[span], target.at[span], done.at[len(copies)])
            )
    return copies


def inner_body(vel, pres, visc, dens, low_x, high_x, _, even_out, odd_out, cells_out, *work):
    blocks, sides_x, even, odd, cells, coefs, relax, forcing, rate, done = work
    size_x, size_y, size_z = blocks.shape[1:]
    width = SWEEPS
    inputs = (
        (visc, blocks.at[4], (4,)),
        (vel, blocks.at[0:3], (0, 1, 2)),
        (pres, blocks.at[3], (3,)),
        (dens, blocks.at[5], (5,)),
        (low_x, sides_x.at[0], ()),
        (high_x, sides_x.at[1], ()),
    )
    copies = [
        pltpu.make_async_copy(there, here, done.at[n]) for n, (there, here, _) in enumerate(inputs)
    ]
    for copy in copies:
        copy.start()
    targets = [even.at[n] for n in range(4)] + [cells.at[n] for n in range(2)]
    for copy, (_, _, held) in zip(copies, inputs):
        copy.wait()
        for f in held:
            for i in range(size_x):
                for y in range(0, size_y, SUBLANES):
                    value = blocks[f, i, y : y + SUBLANES, :]
                    put(targets[f], i + width, y + width, SUBLANES, value)
    for side, begin in enumerate((0, width + size_x)):
        for f in range(6):
            for i in range(width):
                for y in range(0, size_y, SUBLANES):
                    value = sides_x[side, f, i, y : y + SUBLANES, :]
                    put(targets[f], begin + i, y + width, SUBLANES, value)

    prepare, sweep = row_work(cells, coefs, relax, forcing, rate)

    def prepare_row(y, carry):
        prepare(y)
        return carry

    first, last = width + 1, width + size_y - 1
    lax.fori_loop(first, last, prepare_row, 0, unroll=2)
    for step in range(SWEEPS):
        old, new = (odd, even) if step % 2 else (even, odd)

        def sweep_row(y, carry, old=old, new=new):
            sweep(y, old, new)
            return carry

        lax.fori_loop(first + step, last - step, sweep_row, 0, unroll=2)
    sends = kept_copies(((even, even_out), (odd, odd_out), (cells, cells_out)), size_y, done)
    for send in sends:
        send.start()
    for send in sends:
        send.wait()


def inner_sweeps(velocity, pressure, cell_visc, cell_dens, low_x, high_x, after):
    size_x, size_y, size_z = cell_visc.shape
    width = low_x.shape[1]
    per, rows = (size_x + 2 * width) // SUBLANES, (size_y + 2 * width) * SUBLANES
    block, cut = (per, rows, size_z), (per, size_z // LANES, rows, LANES)
    shapes = [(4,) + cut, (4,) + cut, (2,) + cut]
    anywhere = pl.BlockSpec(memory_space=pl.ANY)
    return pl.pallas_call(
        inner_body,
        out_shape=tuple(jax.ShapeDtypeStruct(shape, f32) for shape in shapes),
        in_specs=[anywhere] * 7,
        out_specs=(anywhere,) * 3,
        scratch_shapes=[
            pltpu.VMEM((6,) + cell_visc.shape, f32),
            pltpu.VMEM((2,) + low_x.shape, f32),
        ]
        + [pltpu.VMEM(shape, f32) for shape in shapes]
        + [
            pltpu.VMEM((6,) + block, f32),
            pltpu.VMEM(block, f32),
            pltpu.VMEM(block, f32),
            pltpu.VMEM(block, f32),
            pltpu.SemaphoreType.DMA((6,)),
        ],
        compiler_params=vmem_limit(40),
        cost_estimate=cost(25),
        name="inner_sweeps",
    )(*in_hbm(velocity, pressure, cell_visc, cell_dens, low_x, high_x), after)


def edge_body(even_in, odd_in, cells_in, low_y, high_y, vel_out, pres_out, *work):
    from_low, from_high, results, even, odd, cells, coefs, relax, forcing, rate, done, more = work
    size_x, size_y, size_z = results.shape[1:]
    width = SWEEPS
    long_y = size_y + 2 * width
    halos = [
        pltpu.make_async_copy(low_y, from_low, more.at[0]),
        pltpu.make_async_copy(high_y, from_high, more.at[1]),
    ]
    kept = kept_copies(((even_in, even), (odd_in, odd), (cells_in, cells)), size_y, done)
    for copy in (*halos, *kept[3:], *kept[:3]):
        copy.start()
    targets = [even.at[n] for n in range(4)] + [cells.at[n] for n in range(2)]
    for target in targets:
        for x in (*range(width), *range(width + size_x, size_x + 2 * width)):
            for y in (0, width + size_y):
                put(target, x, y, width, jnp.zeros((width, size_z), f32))
    for up, halo, copy, begin in (
        (True, from_low, halos[0], 0),
        (False, from_high, halos[1], width + size_y),
    ):
        copy.wait()
        for f, target in enumerate(targets):
            rows = slice(f * width, (f + 1) * width)
            for i in range(size_x):
                put(target, i + width, begin, width, halo[i, rows, :])
        for f, side, far_x, far_y, plane, row in corner_rows(up, size_x)[0]:
            x = width + size_x - 1 + far_x if side else width - far_x
            y = width - far_y if up else width + size_y - 1 + far_y
            put(targets[f], x, y, 1, halo[plane, row : row + 1, :])
    for copy in kept:
        copy.wait()

    prepare, sweep = row_work(cells, coefs, relax, forcing, rate)

    def prepare_rows(n, carry):
        prepare(1 + n)
        prepare(long_y - 2 * width + n)
        return carry

    lax.fori_loop(0, 2 * width - 1, prepare_rows, 0)
    for step in range(SWEEPS):
        old, new = (odd, even) if step % 2 else (even, odd)

        def sweep_rows(n, carry, old=old, new=new, step=step):
            sweep(1 + step + n, old, new)
            sweep(width + size_y - 1 - step + n, old, new)
            return carry

        lax.fori_loop(0, width, sweep_rows, 0)

    final = odd if SWEEPS % 2 else even
    outs = [vel_out.at[0], vel_out.at[1], vel_out.at[2], pres_out]
    sends = [pltpu.make_async_copy(results.at[n], out, done.at[n]) for n, out in enumerate(outs)]
    per, halves = even.shape[1:3]
    for field, send in enumerate(sends):
        for i in range(size_x):
            for y in range(0, size_y, SUBLANES):
                plane, lines = place(per, i + width, y + width, SUBLANES)
                for half in range(halves):
                    columns = slice(half * LANES, (half + 1) * LANES)
                    results[field, i, y : y + SUBLANES, columns] = final[
                        field, plane, half, lines, :
                    ]
        send.start()
    for send in sends:
        send.wait()


def edge_sweeps(even, odd, cells, low_y, high_y, size_x, size_y):
    per, halves, rows = even.shape[1:4]
    size_z = halves * LANES
    block = (per, rows, size_z)
    anywhere = pl.BlockSpec(memory_space=pl.ANY)
    return pl.pallas_call(
        edge_body,
        out_shape=(
            jax.ShapeDtypeStruct((3, size_x, size_y, size_z), f32),
            jax.ShapeDtypeStruct((size_x, size_y, size_z), f32),
        ),
        in_specs=[anywhere] * 5,
        out_specs=(anywhere,) * 2,
        scratch_shapes=[
            pltpu.VMEM(low_y.shape, f32),
            pltpu.VMEM(high_y.shape, f32),
            pltpu.VMEM((4, size_x, size_y, size_z), f32),
            pltpu.VMEM(even.shape, f32),
            pltpu.VMEM(odd.shape, f32),
            pltpu.VMEM(cells.shape, f32),
            pltpu.VMEM((6,) + block, f32),
            pltpu.VMEM(block, f32),
            pltpu.VMEM(block, f32),
            pltpu.VMEM(block, f32),
            pltpu.SemaphoreType.DMA((5,)),
            pltpu.SemaphoreType.DMA((2,)),
        ],
        compiler_params=vmem_limit(40),
        cost_estimate=cost(1),
        name="edge_sweeps",
    )(even, odd, cells, low_y, high_y)


def shift(value, axis, step):
    size = lax.axis_size(axis)
    pairs = [(i, i + step) for i in range(size) if 0 <= i + step < size]
    return lax.ppermute(value, axis, pairs)


def per_device(
    velocity,
    pressure,
    cell_visc,
    cell_dens,
    block_brick,
    block_counts,
    positions,
    start_visc,
    marker_dens,
):
    asked = lax.all_to_all(block_brick, "mark", 0, 0, tiled=True)
    fields = (velocity, pressure, cell_visc, cell_dens)
    to_low, to_high = pack_x(*fields)
    low_x, high_x = shift(to_high, "grid", 1), shift(to_low, "grid", -1)
    upward, downward = pack_y(*fields, low_x, high_x)
    low_y, high_y = shift(upward, "mark", 1), shift(downward, "mark", -1)

    picked = pick_bricks(asked, velocity)
    bricks = lax.all_to_all(picked, "mark", 0, 0, tiled=True)
    marker_visc, moments = marker_work(
        block_counts, positions, start_visc, marker_dens, bricks, upward
    )
    gathered = lax.all_to_all(moments, "mark", 0, 0, tiled=True)
    state = inner_sweeps(*fields, low_x, high_x, moments)
    velocity_next, pressure_next = edge_sweeps(*state, low_y, high_y, *pressure.shape[:2])
    visc_next, dens_next = settle(asked, gathered, cell_visc, cell_dens)
    return velocity_next, pressure_next, visc_next, dens_next, marker_visc


def solution(mesh):
    in_specs = (
        P(None, "grid", "mark", None),
        P("grid", "mark", None),
        P("grid", "mark", None),
        P("grid", "mark", None),
        P(("grid", "mark"), None),
        P(("grid", "mark"), None),
        P(("grid", "mark"), None, None, None),
        P(("grid", "mark"), None, None),
        P(("grid", "mark"), None, None),
    )
    out_specs = (
        P(None, "grid", "mark", None),
        P("grid", "mark", None),
        P("grid", "mark", None),
        P("grid", "mark", None),
        P(("grid", "mark"), None, None),
    )
    return jax.shard_map(
        per_device, mesh=mesh, in_specs=in_specs, out_specs=out_specs, check_vma=False
    )
```

```python
import functools

import jax
import jax.numpy as jnp
import numpy as np
from jax import lax
from jax.experimental import pallas as pl
from jax.experimental.pallas import tpu as pltpu
from jax.sharding import PartitionSpec as P

SWEEPS = 4
RELAX = 0.6
PRESSURE_RATE = 0.25
GRAVITY = 1.0
STRAIN_SCALE = 0.5

BX, BY, BZ = 4, 4, 8
PLANE = BX * BY
ROWS = 3 * PLANE
LANES = 128
GROUP = LANES // BZ
HALF = 8
SUBLANES = 8

f32, bf16 = jnp.float32, jnp.bfloat16


def vmem_limit(mib):
    return pltpu.CompilerParams(vmem_limit_bytes=mib * 1024 * 1024)


def in_hbm(*arrays):
    return [pltpu.with_memory_space_constraint(array, pltpu.HBM) for array in arrays]


def cost(microseconds):
    return pl.CostEstimate(
        flops=int(microseconds * 1.15e9), bytes_accessed=0, transcendentals=0
    )


def place_of(brick):
    return lax.shift_right_logical(brick, GROUP.bit_length() - 1), (brick & (GROUP - 1)) * BZ


def pick_body(asked, vel, out, table):
    size_x, size_y, size_z = vel.shape[1:]
    bricks_y, halves = size_y // BY, size_z // LANES

    def repack(block_x, carry):
        for block_y in range(bricks_y):
            for half in range(halves):
                place = (block_x * bricks_y + block_y) * halves + half
                for c in range(3):
                    for i in range(BX):
                        row = (c * BX + i) * BY
                        table[place, row : row + BY, :] = vel[
                            c,
                            block_x * BX + i,
                            block_y * BY : (block_y + 1) * BY,
                            half * LANES : (half + 1) * LANES,
                        ]
        return carry

    lax.fori_loop(0, size_x // BX, repack, 0)
    groups = out.shape[1]
    lane_slot = lax.broadcasted_iota(jnp.int32, (ROWS, LANES), 1) // BZ

    def one_group(step, carry):
        device, group = step // groups, step % groups
        packed = jnp.zeros((ROWS, LANES), f32)
        for slot in range(GROUP):
            place, lane = place_of(asked[device, group * GROUP + slot])
            rolled = pltpu.roll(table[place], (BZ * slot - lane) & (LANES - 1), 1)
            packed = jnp.where(lane_slot == slot, rolled, packed)
        out[device, group] = packed
        return carry

    lax.fori_loop(0, out.shape[0] * groups, one_group, 0)


def pick_bricks(asked, velocity):
    devices, slots = asked.shape
    size_x, size_y, size_z = velocity.shape[1:]
    places = (size_x // BX) * (size_y // BY) * (size_z // LANES)
    return pl.pallas_call(
        pick_body,
        out_shape=jax.ShapeDtypeStruct((devices, slots // GROUP, ROWS, LANES), f32),
        in_specs=[
            pl.BlockSpec(memory_space=pltpu.SMEM),
            pl.BlockSpec(memory_space=pltpu.VMEM),
        ],
        out_specs=pl.BlockSpec(memory_space=pltpu.VMEM),
        scratch_shapes=[pltpu.VMEM((places, ROWS, LANES), f32)],
        compiler_params=vmem_limit(24),
        cost_estimate=cost(25),
        name="pick_bricks",
    )(asked, velocity)


def permutations():
    inside = BZ * HALF
    spread = np.zeros((2, 2, LANES, 4 * inside), np.float32)
    gather = np.zeros((2 * BY * inside, BY * LANES), np.float32)
    for half in range(2):
        for slot in range(HALF):
            for z in range(BZ):
                outer, inner = (half * HALF + slot) * BZ + z, z * HALF + slot
                for part in range(4):
                    spread[half, part // 2, outer, part * inside + inner] = 1
                for j in range(BY):
                    gather[(half * BY + j) * inside + inner, j * LANES + outer] = 1
    return jnp.asarray(spread, bf16), jnp.asarray(gather, bf16)


def split(value):
    high = value.astype(bf16)
    return high, (value - high.astype(f32)).astype(bf16)


def add_all(values):
    return functools.reduce(jnp.add, values)


def axis_weights(fraction, cells):
    middle = (cells - 1) / 2
    base = jnp.exp(fraction * (2.0 * cells) - float(cells))
    powers = [None, base]
    for i in range(2, cells):
        powers.append(powers[i // 2] * powers[i - i // 2])
    factors = [float(np.exp(middle**2 - (i - middle) ** 2)) for i in range(cells)]
    bells = [None] + [powers[i] * factors[i] for i in range(1, cells)]
    scale = 1.0 / (add_all(bells[1:]) + factors[0])
    weights = [scale * factors[0]] + [bell * scale for bell in bells[1:]]
    mean = add_all(
        [
            (weights[cells - 1 - i] - weights[i]) * (2.0 * (middle - i))
            for i in range(cells // 2)
        ]
    )
    slopes = [w * (2.0 * (i - middle) - mean) for i, w in enumerate(weights)]
    return weights, slopes


def dot(a, b):
    return jnp.dot(a, b, preferred_element_type=f32)


def gradients(products, weights, markers):
    weight_x, slope_x, weight_y, slope_y = ([weights[4 * n + i] for i in range(4)] for n in range(4))
    grads = []
    for c in range(3):
        lines = [[], [], []]
        for i in range(BX):
            rows = [((c * BX + i) * BY + j) * HALF for j in range(BY)]
            still = [products[row : row + HALF, :markers] for row in rows]
            rising = [products[row : row + HALF, markers:] for row in rows]
            lines[0].append(slope_x[i] * add_all([w * t for w, t in zip(weight_y, still)]))
            lines[1].append(weight_x[i] * add_all([w * t for w, t in zip(slope_y, still)]))
            lines[2].append(weight_x[i] * add_all([w * t for w, t in zip(weight_y, rising)]))
        grads.append([add_all(line) for line in lines])
    return grads


def own_lanes():
    shape = (HALF, 4 * BZ * HALF)
    lane = lax.broadcasted_iota(jnp.int32, shape, 1)
    return (lane % HALF == lax.broadcasted_iota(jnp.int32, shape, 0)).astype(f32)


def marker_groups(groups, counts, ins, outs, buffers, sums):
    spread, gather, places, start, dens, brick = ins
    visc_out, moments_out = outs
    permuted, left, right, products, weights, factors, planes_high, planes_low = buffers
    markers = places.shape[-1]
    inside = BZ * HALF
    own = own_lanes()
    halves = [
        (owner, 2 * group + half, half, 2 * n + half)
        for n, (owner, group) in enumerate(groups)
        for half in range(2)
    ]
    parts = [split(brick[owner, group]) for owner, group in groups]
    for _, _, half, n in halves:
        high, low = parts[n // 2]
        permuted[n][...] = dot(high, spread[half, 0]) + dot(low, spread[half, 1])
    heights = []
    for owner, part, _, n in halves:
        weight_z, slope_z = axis_weights(places[owner, 2, part], BZ)
        heights.append(weight_z)
        for z in range(0, BZ, 2):
            for column, values in ((0, weight_z), (1, slope_z)):
                high, low = split(jnp.concatenate(values[z : z + 2], axis=0))
                columns = slice(column * markers, (column + 1) * markers)
                for k in range(4):
                    begin = k * inside + z * HALF
                    right[n][begin : begin + 2 * HALF, columns] = low if k % 2 else high
    for _, _, _, n in halves:
        for row in range(0, ROWS, 2):
            pair = [
                jnp.broadcast_to(permuted[n][r : r + 1, :], own.shape) * own for r in (row, row + 1)
            ]
            left[n][row * HALF : (row + 2) * HALF, :] = jnp.concatenate(pair, axis=0).astype(bf16)
    for _, _, _, n in halves:
        products[n][...] = dot(left[n][...], right[n][...])
    for owner, part, _, n in halves:
        weights_x = axis_weights(places[owner, 0, part], BX)
        weights_y = axis_weights(places[owner, 1, part], BY)
        for k, values in enumerate((*weights_x, *weights_y)):
            for i, value in enumerate(values):
                weights[n][4 * k + i] = value
        for j in range(BY):
            for z in range(0, BZ, 2):
                pair = [weights_y[0][j] * heights[n][z + k] for k in range(2)]
                rows = slice((j * BZ + z) * HALF, (j * BZ + z + 2) * HALF)
                high, low = split(jnp.concatenate(pair, axis=0))
                planes_high[n][rows, :] = high
                planes_low[n][rows, :] = low

    count = 3 * BX * HALF
    for owner, part, _, n in halves:
        grads = gradients(products[n], weights[n], markers)
        normal = grads[0][0] ** 2 + grads[1][1] ** 2 + grads[2][2] ** 2
        shear_xy = 0.5 * (grads[0][1] + grads[1][0])
        shear_xz = 0.5 * (grads[0][2] + grads[2][0])
        shear_yz = 0.5 * (grads[1][2] + grads[2][1])
        invariant = 0.5 * normal + shear_xy**2 + shear_xz**2 + shear_yz**2
        scaled = invariant * (1.0 / (STRAIN_SCALE * STRAIN_SCALE))
        third = jnp.log(1.0 + scaled) * (1.0 / 3.0)
        first = start[owner, part]
        slot = lax.broadcasted_iota(jnp.int32, first.shape, 0) + part * HALF
        live = slot < counts[0, owner]
        visc_out[owner, part] = jnp.where(live, first * jnp.exp(-third), 0.0)
        carried = (
            live.astype(f32),
            jnp.where(live, jnp.log(first) - third, 0.0),
            jnp.where(live, dens[owner, part], 0.0),
        )
        for c in range(3):
            for i in range(0, BX, 2):
                pair = [carried[c] * weights[n][i + k] for k in range(2)]
                row = (c * BX + i) * HALF
                high, low = split(jnp.concatenate(pair, axis=0))
                factors[n][row : row + 2 * HALF, :] = high
                factors[n][count + row : count + row + 2 * HALF, :] = low

    contract = (((1,), (1,)), ((), ()))
    found = []
    for _, _, _, n in halves:
        both = lax.dot_general(
            factors[n][...], planes_high[n][...], contract, preferred_element_type=f32
        )
        rest = lax.dot_general(
            factors[n][:count], planes_low[n][...], contract, preferred_element_type=f32
        )
        found.append((both, rest))
    for _, _, half, n in halves:
        both, rest = found[n]
        total = both[:count] + both[count:] + rest
        chosen = total.reshape(3 * BX, HALF, BY * inside) * own[None]
        high, low = split(jnp.sum(chosen, axis=1))
        columns = slice(half * BY * inside, (half + 1) * BY * inside)
        row = (n // 2) * 32
        sums[row : row + 3 * BX, columns] = high.astype(f32)
        sums[row + 16 : row + 16 + 3 * BX, columns] = low.astype(f32)
    moved = dot(sums[...].astype(bf16), gather[...])
    for n, (owner, group) in enumerate(groups):
        mine = moved[32 * n : 32 * n + 3 * BX] + moved[32 * n + 16 : 32 * n + 16 + 3 * BX]
        for j in range(BY):
            rows = pl.ds(j, 3 * BX, stride=BY)
            moments_out[owner, group, rows, :] = mine[:, j * LANES : (j + 1) * LANES]


TOGETHER = 3


def marker_body(counts, *refs):
    ins, outs, scratch = refs[:6], refs[7:9], refs[9:]
    listed, sums, *flat = scratch
    held = 2 * TOGETHER
    buffers = [flat[n * held : (n + 1) * held] for n in range(len(flat) // held)]
    visc_out, moments_out = outs
    owners, groups = moments_out.shape[:2]
    visc_out[...] = jnp.zeros_like(visc_out)
    moments_out[...] = jnp.zeros_like(moments_out)
    sums[...] = jnp.zeros_like(sums)

    def list_groups(index, number):
        owner, group = index // groups, index % groups
        live = group * GROUP < counts[0, owner]

        @pl.when(live)
        def _():
            for n in range(TOGETHER):
                listed[2 * (number + n)] = owner
                listed[2 * (number + n) + 1] = group

        return jnp.where(live, number + 1, number)

    number = lax.fori_loop(0, owners * groups, list_groups, 0)

    def step(index, carry):
        first = TOGETHER * index
        taken = [
            (listed[2 * (first + n)], listed[2 * (first + n) + 1]) for n in range(TOGETHER)
        ]
        marker_groups(taken, counts, ins, outs, buffers, sums)
        return carry

    lax.fori_loop(0, (number + TOGETHER - 1) // TOGETHER, step, 0)


def marker_work(counts, positions, start_visc, marker_dens, bricks, after):
    owners, _, slots, markers = positions.shape
    groups, parts = slots // GROUP, slots // HALF
    spread, gather = permutations()
    width = 4 * BZ * HALF
    whole = pl.BlockSpec(memory_space=pltpu.VMEM)
    buffers = (
        pltpu.VMEM((ROWS, width), f32),
        pltpu.VMEM((ROWS * HALF, width), bf16),
        pltpu.VMEM((width, 2 * markers), bf16),
        pltpu.VMEM((ROWS * HALF, 2 * markers), f32),
        pltpu.VMEM((4 * 4, HALF, markers), f32),
        pltpu.VMEM((2 * 3 * BX * HALF, markers), bf16),
        pltpu.VMEM((BY * BZ * HALF, markers), bf16),
        pltpu.VMEM((BY * BZ * HALF, markers), bf16),
    )
    visc, moments = pl.pallas_call(
        marker_body,
        out_shape=(
            jax.ShapeDtypeStruct((owners, parts, HALF, markers), f32),
            jax.ShapeDtypeStruct((owners, groups, ROWS, LANES), f32),
        ),
        in_specs=[pl.BlockSpec(memory_space=pltpu.SMEM)]
        + [whole] * 6
        + [pl.BlockSpec(memory_space=pl.ANY)],
        out_specs=(whole, whole),
        scratch_shapes=[
            pltpu.SMEM((2 * (owners * groups + TOGETHER),), jnp.int32),
            pltpu.VMEM((32 * TOGETHER, 2 * BY * BZ * HALF), f32),
        ]
        + [buffer for buffer in buffers for _ in range(2 * TOGETHER)],
        compiler_params=vmem_limit(40),
        cost_estimate=cost(25),
        name="marker_work",
    )(
        counts,
        *in_hbm(
            spread,
            gather,
            positions.reshape(owners, 3, parts, HALF, markers),
            start_visc.reshape(owners, parts, HALF, markers),
            marker_dens.reshape(owners, parts, HALF, markers),
            bricks,
        ),
        after,
    )
    return visc.reshape(owners, slots, markers), moments


def settle_body(asked, moments_in, visc_in, dens_in, visc_far, dens_far, *scratch):
    moments, visc, dens, visc_out, dens_out, done, sent, *tables = scratch
    size_x, size_y, size_z = visc.shape
    copies = [
        pltpu.make_async_copy(there, here, done.at[n])
        for n, (there, here) in enumerate(
            ((moments_in, moments), (visc_in, visc), (dens_in, dens))
        )
    ]
    for copy in copies:
        copy.start()
    bricks_y, halves = size_y // BY, size_z // LANES
    for table in tables:
        table[...] = jnp.zeros_like(table)
    copies[0].wait()
    groups = moments.shape[1]
    lane_slot = lax.broadcasted_iota(jnp.int32, (ROWS, LANES), 1) // BZ

    def one_group(step, carry):
        device, group = step // groups, step % groups
        packed = moments[device, group]
        for slot in range(GROUP):
            table = tables[slot % len(tables)]
            place, lane = place_of(asked[device, group * GROUP + slot])
            piece = jnp.where(lane_slot == slot, packed, 0.0)
            piece = pltpu.roll(piece, (lane - BZ * slot) & (LANES - 1), 1)
            table[place] = table[place] + piece
        return carry

    lax.fori_loop(0, moments.shape[0] * groups, one_group, 0)
    copies[1].wait()
    copies[2].wait()

    def sends(block_x):
        planes = pl.ds(block_x * BX, BX)
        return [
            pltpu.make_async_copy(here.at[planes], there.at[planes], sent.at[n, block_x])
            for n, (here, there) in enumerate(((visc_out, visc_far), (dens_out, dens_far)))
        ]

    def finish(block_x, carry):
        for block_y in range(0, bricks_y, 2):
            for half in range(halves):
                for i in range(BX):
                    here = (
                        block_x * BX + i,
                        slice(block_y * BY, (block_y + 2) * BY),
                        slice(half * LANES, (half + 1) * LANES),
                    )
                    sums = []
                    for c in range(3):
                        rows = slice((c * BX + i) * BY, (c * BX + i + 1) * BY)
                        places = [
                            (block_x * bricks_y + block_y + k) * halves + half for k in range(2)
                        ]
                        sums.append(
                            jnp.concatenate(
                                [add_all([t[place, rows, :] for t in tables]) for place in places]
                            )
                        )
                    scale = 1.0 / (sums[0] + 1.0)
                    visc_out[here] = jnp.exp((sums[1] + jnp.log(visc[here])) * scale)
                    dens_out[here] = (sums[2] + dens[here]) * scale
        for send in sends(block_x):
            send.start()
        return carry

    def drain(block_x, carry):
        for send in sends(block_x):
            send.wait()
        return carry

    lax.fori_loop(0, size_x // BX, finish, 0)
    lax.fori_loop(0, size_x // BX, drain, 0)


def settle(asked, moments, cell_visc, cell_dens):
    size_x, size_y, size_z = cell_visc.shape
    places = (size_x // BX) * (size_y // BY) * (size_z // LANES)
    shape = jax.ShapeDtypeStruct(cell_visc.shape, f32)
    return pl.pallas_call(
        settle_body,
        out_shape=(shape, shape),
        in_specs=[pl.BlockSpec(memory_space=pltpu.SMEM)]
        + [pl.BlockSpec(memory_space=pl.ANY)] * 3,
        out_specs=(pl.BlockSpec(memory_space=pl.ANY),) * 2,
        scratch_shapes=[
            pltpu.VMEM(moments.shape, f32),
            pltpu.VMEM(cell_visc.shape, f32),
            pltpu.VMEM(cell_visc.shape, f32),
            pltpu.VMEM(cell_visc.shape, f32),
            pltpu.VMEM(cell_visc.shape, f32),
            pltpu.SemaphoreType.DMA((3,)),
            pltpu.SemaphoreType.DMA((2, size_x // BX)),
        ]
        + [pltpu.VMEM((places, ROWS, LANES), f32)],
        compiler_params=vmem_limit(24),
        cost_estimate=cost(7),
        name="settle",
    )(asked, *in_hbm(moments, cell_visc, cell_dens))


def field_of(fields, index):
    return fields[0].at[index] if index < 3 else fields[index - 2]


def pack_x_body(*refs):
    ends, outs = refs[:8], refs[8:]
    for side in range(2):
        for f in range(6):
            outs[side][f] = field_of(ends[side::2], f)[...]


def pack_x(velocity, pressure, cell_visc, cell_dens):
    size_x, size_y, size_z = cell_visc.shape
    width = SWEEPS
    ends = (0, size_x // width - 1)
    vel = [
        pl.BlockSpec((3, width, size_y, size_z), lambda i, e=e: (0, e, 0, 0)) for e in ends
    ]
    block = [pl.BlockSpec((width, size_y, size_z), lambda i, e=e: (e, 0, 0)) for e in ends]
    whole = pl.BlockSpec((6, width, size_y, size_z), lambda i: (0, 0, 0, 0))
    shape = jax.ShapeDtypeStruct((6, width, size_y, size_z), f32)
    return pl.pallas_call(
        pack_x_body,
        grid=(1,),
        out_shape=(shape, shape),
        in_specs=vel + block * 3,
        out_specs=(whole, whole),
        compiler_params=vmem_limit(60),
        cost_estimate=cost(2),
        name="pack_x",
    )(velocity, velocity, pressure, pressure, cell_visc, cell_visc, cell_dens, cell_dens)


def corner_rows(upward, size_x):
    width = SWEEPS
    spare = (5 * width,) if upward else (4 * width - 1, 6 * width - 1)
    places = [(plane, row) for plane in range(size_x) for row in spare]
    found = []
    for field in range(6):
        for side in range(2):
            near = field == 5 or (field == 3 and side == 1 and not upward)
            reach = width - 1 if near else width
            for far_x in range(1, width):
                for far_y in range(1, reach - far_x + 1):
                    found.append((field, side, far_x, far_y))
    more = max(0, len(found) - len(places))
    places += [(size_x + n // (6 * width), n % (6 * width)) for n in range(more)]
    return [cell + at for cell, at in zip(found, places)], size_x + -(-more // (6 * width))


def pack_y_body(size_x, vel, pres, visc, dens, low_x, high_x, upward, downward):
    step_x, size_y, _ = pres.shape
    width = SWEEPS
    step = pl.program_id(0)
    planes = pl.ds(pl.multiple_of(step * step_x, step_x), step_x)
    for f in range(6):
        field = field_of((vel, pres, visc, dens), f)
        rows = slice(f * width, (f + 1) * width)
        upward[planes, rows, :] = field[:, size_y - width :, :]
        downward[planes, rows, :] = field[:, :width, :]

    @pl.when(step == pl.num_programs(0) - 1)
    def _():
        for up, face in ((True, upward), (False, downward)):
            for f, side, far_x, far_y, plane, row in corner_rows(up, size_x)[0]:
                halo, at = (high_x, far_x - 1) if side else (low_x, width - far_x)
                face[plane, row] = halo[f, at, size_y - far_y if up else far_y - 1]


def pack_y(velocity, pressure, cell_visc, cell_dens, low_x, high_x):
    size_x, size_y, size_z = cell_visc.shape
    step = 8
    block = pl.BlockSpec((step, size_y, size_z), lambda i: (i, 0, 0))
    halo = pl.BlockSpec(low_x.shape, lambda i: (0, 0, 0, 0))
    shapes = [(corner_rows(up, size_x)[1], 6 * SWEEPS, size_z) for up in (True, False)]
    return pl.pallas_call(
        functools.partial(pack_y_body, size_x),
        grid=(size_x // step,),
        out_shape=tuple(jax.ShapeDtypeStruct(shape, f32) for shape in shapes),
        in_specs=[
            pl.BlockSpec((3, step, size_y, size_z), lambda i: (0, i, 0, 0)),
            block,
            block,
            block,
            halo,
            halo,
        ],
        out_specs=tuple(pl.BlockSpec(shape, lambda i: (0, 0, 0)) for shape in shapes),
        compiler_params=vmem_limit(24),
        cost_estimate=cost(15),
        name="pack_y",
    )(*in_hbm(velocity, pressure, cell_visc, cell_dens, low_x, high_x))


def place(per, x, y, rows):
    return x % per, pl.ds(y * SUBLANES + x // per, rows, stride=SUBLANES)


def put(target, x, y, rows, value):
    per, halves = target.shape[:2]
    plane, lines = place(per, x, y, rows)
    for half in range(halves):
        target[plane, half, lines, :] = value[:, half * LANES : (half + 1) * LANES]


def tile(y):
    if isinstance(y, int):
        return pl.ds(y * SUBLANES, SUBLANES)
    return pl.ds(pl.multiple_of(y * SUBLANES, SUBLANES), SUBLANES)


def row_work(cells, coefs, relax, forcing, rate):
    per, halves = cells.shape[1:3]
    lane = lax.broadcasted_iota(jnp.int32, (SUBLANES, LANES), 1)
    at_first, at_last = lane == 0, lane == LANES - 1

    def take(field, plane, y):
        return jnp.concatenate([field[plane, half, tile(y), :] for half in range(halves)], axis=1)

    def store(field, plane, y, value):
        for half in range(halves):
            field[plane, half, tile(y), :] = value[:, half * LANES : (half + 1) * LANES]

    def up_x(field, plane, y):
        if plane < per - 1:
            return take(field, plane + 1, y)
        return pltpu.roll(take(field, 0, y), SUBLANES - 1, 0)

    def down_x(field, plane, y):
        if plane > 0:
            return take(field, plane - 1, y)
        return pltpu.roll(take(field, per - 1, y), 1, 0)

    def rolled(a, shift):
        return [
            pltpu.roll(a[:, half * LANES : (half + 1) * LANES], shift, 1) for half in range(halves)
        ]

    def up_z(a):
        parts = rolled(a, LANES - 1)
        after = parts[1:] + [jnp.zeros_like(parts[0])]
        return jnp.concatenate([jnp.where(at_last, n, p) for p, n in zip(parts, after)], axis=1)

    def down_z(a):
        parts = rolled(a, 1)
        before = [jnp.zeros_like(parts[0])] + parts[:-1]
        return jnp.concatenate([jnp.where(at_first, b, p) for p, b in zip(parts, before)], axis=1)

    def prepare(y):
        visc, dens = cells.at[0], cells.at[1]
        for plane in range(per):
            here = take(visc, plane, y)
            near = [
                up_x(visc, plane, y),
                down_x(visc, plane, y),
                take(visc, plane, y + 1),
                take(visc, plane, y - 1),
                up_z(here),
                down_z(here),
            ]
            links = [0.5 * (here + other) for other in near]
            scale = jnp.where(here > 0.0, RELAX / add_all(links), 0.0)
            for n in range(6):
                coefs[n, plane, tile(y), :] = links[n] * scale
            relax[plane, tile(y), :] = scale
            forcing[plane, tile(y), :] = take(dens, plane, y) * (-GRAVITY * scale)
            rate[plane, tile(y), :] = PRESSURE_RATE * here

    def sweep(y, old, new):
        for plane in range(per):
            links = [coefs[n, plane, tile(y), :] for n in range(6)]
            scale = relax[plane, tile(y), :]
            pressure = take(old.at[3], plane, y)
            before = (
                down_x(old.at[3], plane, y),
                take(old.at[3], plane, y - 1),
                down_z(pressure),
            )
            changes = []
            for c in range(3):
                field = old.at[c]
                here = take(field, plane, y)
                near = [
                    up_x(field, plane, y),
                    down_x(field, plane, y),
                    take(field, plane, y + 1),
                    take(field, plane, y - 1),
                    up_z(here),
                    down_z(here),
                ]
                terms = [link * other for link, other in zip(links, near)]
                total = (terms[0] + terms[1]) + (terms[2] + terms[3])
                total = total + (terms[4] + terms[5])
                rest = (1.0 - RELAX) * here - scale * (pressure - before[c])
                if c == 2:
                    rest = rest + forcing[plane, tile(y), :]
                changes.append(near[2 * c] - here)
                store(new.at[c], plane, y, total + rest)
            pressed = pressure - rate[plane, tile(y), :] * add_all(changes)
            store(new.at[3], plane, y, pressed)

    return prepare, sweep


def kept_rows(size_y):
    width = SWEEPS
    return (
        ((width, size_y),),
        ((width + 1, width), (size_y - 1, width)),
        ((width, width + 1), (size_y - 1, width + 1)),
    )


def kept_copies(pairs, size_y, done):
    copies = []
    for (source, target), strips in zip(pairs, kept_rows(size_y)):
        for begin, rows in strips:
            span = (slice(None),) * 3 + (pl.ds(begin * SUBLANES, rows * SUBLANES),)
            copies.append(
                pltpu.make_async_copy(source.at[span], target.at[span], done.at[len(copies)])
            )
    return copies


def inner_body(vel, pres, visc, dens, low_x, high_x, _, even_out, odd_out, cells_out, *work):
    blocks, sides_x, even, odd, cells, coefs, relax, forcing, rate, done, more = work
    size_x, size_y, size_z = blocks.shape[1:]
    width = SWEEPS
    inputs = (
        (visc, blocks.at[4]),
        (dens, blocks.at[5]),
        (low_x, sides_x.at[0]),
        (high_x, sides_x.at[1]),
        (vel, blocks.at[0:3]),
        (pres, blocks.at[3]),
    )
    copies = [
        pltpu.make_async_copy(there, here, done.at[n]) for n, (there, here) in enumerate(inputs)
    ]
    for copy in copies:
        copy.start()
    targets = [even.at[n] for n in range(4)] + [cells.at[n] for n in range(2)]

    def lay_out(f):
        for i in range(size_x):
            for y in range(0, size_y, SUBLANES):
                value = blocks[f, i, y : y + SUBLANES, :]
                put(targets[f], i + width, y + width, SUBLANES, value)
        for side, begin in enumerate((0, width + size_x)):
            for i in range(width):
                for y in range(0, size_y, SUBLANES):
                    value = sides_x[side, f, i, y : y + SUBLANES, :]
                    put(targets[f], begin + i, y + width, SUBLANES, value)

    for copy in copies[:4]:
        copy.wait()
    lay_out(4)
    lay_out(5)
    sends = kept_copies(((even, even_out), (odd, odd_out), (cells, cells_out)), size_y, more)
    for send in sends[3:]:
        send.start()

    prepare, sweep = row_work(cells, coefs, relax, forcing, rate)

    def prepare_row(y, carry):
        prepare(y)
        return carry

    first, last = width + 1, width + size_y - 1
    lax.fori_loop(first, last, prepare_row, 0, unroll=2)
    for copy in copies[4:]:
        copy.wait()
    for f in range(4):
        lay_out(f)
    early, late = (sends[1:3], sends[:1]) if SWEEPS % 2 == 0 else (sends[:1], sends[1:3])
    for step in range(SWEEPS):
        old, new = (odd, even) if step % 2 else (even, odd)
        if step == SWEEPS - 1:
            for send in early:
                send.start()

        def sweep_row(y, carry, old=old, new=new):
            sweep(y, old, new)
            return carry

        lax.fori_loop(first + step, last - step, sweep_row, 0, unroll=2)
    for send in late:
        send.start()
    for send in sends:
        send.wait()


def inner_sweeps(velocity, pressure, cell_visc, cell_dens, low_x, high_x, after):
    size_x, size_y, size_z = cell_visc.shape
    width = low_x.shape[1]
    per, rows = (size_x + 2 * width) // SUBLANES, (size_y + 2 * width) * SUBLANES
    block, cut = (per, rows, size_z), (per, size_z // LANES, rows, LANES)
    shapes = [(4,) + cut, (4,) + cut, (2,) + cut]
    anywhere = pl.BlockSpec(memory_space=pl.ANY)
    return pl.pallas_call(
        inner_body,
        out_shape=tuple(jax.ShapeDtypeStruct(shape, f32) for shape in shapes),
        in_specs=[anywhere] * 7,
        out_specs=(anywhere,) * 3,
        scratch_shapes=[
            pltpu.VMEM((6,) + cell_visc.shape, f32),
            pltpu.VMEM((2,) + low_x.shape, f32),
        ]
        + [pltpu.VMEM(shape, f32) for shape in shapes]
        + [
            pltpu.VMEM((6,) + block, f32),
            pltpu.VMEM(block, f32),
            pltpu.VMEM(block, f32),
            pltpu.VMEM(block, f32),
            pltpu.SemaphoreType.DMA((6,)),
            pltpu.SemaphoreType.DMA((5,)),
        ],
        compiler_params=vmem_limit(40),
        cost_estimate=cost(25),
        name="inner_sweeps",
    )(*in_hbm(velocity, pressure, cell_visc, cell_dens, low_x, high_x), after)


def edge_body(even_in, odd_in, cells_in, low_y, high_y, vel_out, pres_out, *work):
    from_low, from_high, results, even, odd, cells, coefs, relax, forcing, rate, done, more = work
    size_x, size_y, size_z = results.shape[1:]
    width = SWEEPS
    long_y = size_y + 2 * width
    halos = [
        pltpu.make_async_copy(low_y, from_low, more.at[0]),
        pltpu.make_async_copy(high_y, from_high, more.at[1]),
    ]
    kept = kept_copies(((even_in, even), (odd_in, odd), (cells_in, cells)), size_y, done)
    for copy in (*halos, *kept[3:], *kept[:3]):
        copy.start()
    targets = [even.at[n] for n in range(4)] + [cells.at[n] for n in range(2)]

    def lay_out(chosen):
        for f in chosen:
            for x in (*range(width), *range(width + size_x, size_x + 2 * width)):
                for y in (0, width + size_y):
                    put(targets[f], x, y, width, jnp.zeros((width, size_z), f32))
            rows = slice(f * width, (f + 1) * width)
            for halo, begin in ((from_low, 0), (from_high, width + size_y)):
                for i in range(size_x):
                    put(targets[f], i + width, begin, width, halo[i, rows, :])
        for up, halo in ((True, from_low), (False, from_high)):
            for f, side, far_x, far_y, plane, row in corner_rows(up, size_x)[0]:
                if f in chosen:
                    x = width + size_x - 1 + far_x if side else width - far_x
                    y = width - far_y if up else width + size_y - 1 + far_y
                    put(targets[f], x, y, 1, halo[plane, row : row + 1, :])

    for copy in halos:
        copy.wait()
    lay_out((4, 5))
    for copy in kept[3:]:
        copy.wait()

    prepare, sweep = row_work(cells, coefs, relax, forcing, rate)

    def prepare_rows(n, carry):
        prepare(1 + n)
        prepare(long_y - 2 * width + n)
        return carry

    lax.fori_loop(0, 2 * width - 1, prepare_rows, 0)
    lay_out((0, 1, 2, 3))
    for copy in kept[:3]:
        copy.wait()
    for step in range(SWEEPS):
        old, new = (odd, even) if step % 2 else (even, odd)

        def sweep_rows(n, carry, old=old, new=new, step=step):
            sweep(1 + step + n, old, new)
            sweep(width + size_y - 1 - step + n, old, new)
            return carry

        lax.fori_loop(0, width, sweep_rows, 0)

    final = odd if SWEEPS % 2 else even
    outs = [vel_out.at[0], vel_out.at[1], vel_out.at[2], pres_out]
    sends = [pltpu.make_async_copy(results.at[n], out, done.at[n]) for n, out in enumerate(outs)]
    per, halves = even.shape[1:3]
    for field, send in enumerate(sends):
        for i in range(size_x):
            for y in range(0, size_y, SUBLANES):
                plane, lines = place(per, i + width, y + width, SUBLANES)
                for half in range(halves):
                    columns = slice(half * LANES, (half + 1) * LANES)
                    results[field, i, y : y + SUBLANES, columns] = final[
                        field, plane, half, lines, :
                    ]
        send.start()
    for send in sends:
        send.wait()


def edge_sweeps(even, odd, cells, low_y, high_y, size_x, size_y):
    per, halves, rows = even.shape[1:4]
    size_z = halves * LANES
    block = (per, rows, size_z)
    anywhere = pl.BlockSpec(memory_space=pl.ANY)
    return pl.pallas_call(
        edge_body,
        out_shape=(
            jax.ShapeDtypeStruct((3, size_x, size_y, size_z), f32),
            jax.ShapeDtypeStruct((size_x, size_y, size_z), f32),
        ),
        in_specs=[anywhere] * 5,
        out_specs=(anywhere,) * 2,
        scratch_shapes=[
            pltpu.VMEM(low_y.shape, f32),
            pltpu.VMEM(high_y.shape, f32),
            pltpu.VMEM((4, size_x, size_y, size_z), f32),
            pltpu.VMEM(even.shape, f32),
            pltpu.VMEM(odd.shape, f32),
            pltpu.VMEM(cells.shape, f32),
            pltpu.VMEM((6,) + block, f32),
            pltpu.VMEM(block, f32),
            pltpu.VMEM(block, f32),
            pltpu.VMEM(block, f32),
            pltpu.SemaphoreType.DMA((5,)),
            pltpu.SemaphoreType.DMA((2,)),
        ],
        compiler_params=vmem_limit(40),
        cost_estimate=cost(1),
        name="edge_sweeps",
    )(even, odd, cells, low_y, high_y)


def shift(value, axis, step):
    size = lax.axis_size(axis)
    pairs = [(i, i + step) for i in range(size) if 0 <= i + step < size]
    return lax.ppermute(value, axis, pairs)


def per_device(
    velocity,
    pressure,
    cell_visc,
    cell_dens,
    block_brick,
    block_counts,
    positions,
    start_visc,
    marker_dens,
):
    asked = lax.all_to_all(block_brick, "mark", 0, 0, tiled=True)
    fields = (velocity, pressure, cell_visc, cell_dens)
    to_low, to_high = pack_x(*fields)
    low_x, high_x = shift(to_high, "grid", 1), shift(to_low, "grid", -1)
    upward, downward = pack_y(*fields, low_x, high_x)
    low_y, high_y = shift(upward, "mark", 1), shift(downward, "mark", -1)

    picked = pick_bricks(asked, velocity)
    bricks = lax.all_to_all(picked, "mark", 0, 0, tiled=True)
    marker_visc, moments = marker_work(
        block_counts, positions, start_visc, marker_dens, bricks, upward
    )
    gathered = lax.all_to_all(moments, "mark", 0, 0, tiled=True)
    state = inner_sweeps(*fields, low_x, high_x, moments)
    velocity_next, pressure_next = edge_sweeps(*state, low_y, high_y, *pressure.shape[:2])
    visc_next, dens_next = settle(asked, gathered, cell_visc, cell_dens)
    return velocity_next, pressure_next, visc_next, dens_next, marker_visc


def solution(mesh):
    in_specs = (
        P(None, "grid", "mark", None),
        P("grid", "mark", None),
        P("grid", "mark", None),
        P("grid", "mark", None),
        P(("grid", "mark"), None),
        P(("grid", "mark"), None),
        P(("grid", "mark"), None, None, None),
        P(("grid", "mark"), None, None),
        P(("grid", "mark"), None, None),
    )
    out_specs = (
        P(None, "grid", "mark", None),
        P("grid", "mark", None),
        P("grid", "mark", None),
        P("grid", "mark", None),
        P(("grid", "mark"), None, None),
    )
    return jax.shard_map(
        per_device, mesh=mesh, in_specs=in_specs, out_specs=out_specs, check_vma=False
    )
```

```python
import functools

import jax
import jax.numpy as jnp
import numpy as np
from jax import lax
from jax.experimental import pallas as pl
from jax.experimental.pallas import tpu as pltpu
from jax.sharding import PartitionSpec as P

SWEEPS = 4
RELAX = 0.6
PRESSURE_RATE = 0.25
GRAVITY = 1.0
STRAIN_SCALE = 0.5

BX, BY, BZ = 4, 4, 8
PLANE = BX * BY
ROWS = 3 * PLANE
LANES = 128
GROUP = LANES // BZ
HALF = 8
SUBLANES = 8

f32, bf16 = jnp.float32, jnp.bfloat16


def vmem_limit(mib):
    return pltpu.CompilerParams(vmem_limit_bytes=mib * 1024 * 1024)


def in_hbm(*arrays):
    return [pltpu.with_memory_space_constraint(array, pltpu.HBM) for array in arrays]


def cost(microseconds):
    return pl.CostEstimate(
        flops=int(microseconds * 1.15e9), bytes_accessed=0, transcendentals=0
    )


def place_of(brick):
    return lax.shift_right_logical(brick, GROUP.bit_length() - 1), (brick & (GROUP - 1)) * BZ


def pick_body(asked, vel, out, table):
    size_x, size_y, size_z = vel.shape[1:]
    bricks_y, halves = size_y // BY, size_z // LANES

    def repack(block_x, carry):
        for block_y in range(bricks_y):
            for half in range(halves):
                place = (block_x * bricks_y + block_y) * halves + half
                for c in range(3):
                    for i in range(BX):
                        row = (c * BX + i) * BY
                        table[place, row : row + BY, :] = vel[
                            c,
                            block_x * BX + i,
                            block_y * BY : (block_y + 1) * BY,
                            half * LANES : (half + 1) * LANES,
                        ]
        return carry

    lax.fori_loop(0, size_x // BX, repack, 0)
    groups = out.shape[1]
    lane_slot = lax.broadcasted_iota(jnp.int32, (ROWS, LANES), 1) // BZ

    def one_group(step, carry):
        device, group = step // groups, step % groups
        packed = jnp.zeros((ROWS, LANES), f32)
        for slot in range(GROUP):
            place, lane = place_of(asked[device, group * GROUP + slot])
            rolled = pltpu.roll(table[place], (BZ * slot - lane) & (LANES - 1), 1)
            packed = jnp.where(lane_slot == slot, rolled, packed)
        out[device, group] = packed
        return carry

    lax.fori_loop(0, out.shape[0] * groups, one_group, 0)


def pick_bricks(asked, velocity):
    devices, slots = asked.shape
    size_x, size_y, size_z = velocity.shape[1:]
    places = (size_x // BX) * (size_y // BY) * (size_z // LANES)
    return pl.pallas_call(
        pick_body,
        out_shape=jax.ShapeDtypeStruct((devices, slots // GROUP, ROWS, LANES), f32),
        in_specs=[
            pl.BlockSpec(memory_space=pltpu.SMEM),
            pl.BlockSpec(memory_space=pltpu.VMEM),
        ],
        out_specs=pl.BlockSpec(memory_space=pltpu.VMEM),
        scratch_shapes=[pltpu.VMEM((places, ROWS, LANES), f32)],
        compiler_params=vmem_limit(24),
        cost_estimate=cost(25),
        name="pick_bricks",
    )(asked, velocity)


def permutations():
    inside = BZ * HALF
    spread = np.zeros((2, 2, LANES, 4 * inside), np.float32)
    gather = np.zeros((2 * BY * inside, BY * LANES), np.float32)
    for half in range(2):
        for slot in range(HALF):
            for z in range(BZ):
                outer, inner = (half * HALF + slot) * BZ + z, z * HALF + slot
                for part in range(4):
                    spread[half, part // 2, outer, part * inside + inner] = 1
                for j in range(BY):
                    gather[(half * BY + j) * inside + inner, j * LANES + outer] = 1
    return jnp.asarray(spread, bf16), jnp.asarray(gather, bf16)


def split(value):
    high = value.astype(bf16)
    return high, (value - high.astype(f32)).astype(bf16)


def add_all(values):
    return functools.reduce(jnp.add, values)


def axis_weights(fraction, cells):
    middle = (cells - 1) / 2
    base = jnp.exp(fraction * (2.0 * cells) - float(cells))
    powers = [None, base]
    for i in range(2, cells):
        powers.append(powers[i // 2] * powers[i - i // 2])
    factors = [float(np.exp(middle**2 - (i - middle) ** 2)) for i in range(cells)]
    bells = [None] + [powers[i] * factors[i] for i in range(1, cells)]
    scale = 1.0 / (add_all(bells[1:]) + factors[0])
    weights = [scale * factors[0]] + [bell * scale for bell in bells[1:]]
    mean = add_all(
        [
            (weights[cells - 1 - i] - weights[i]) * (2.0 * (middle - i))
            for i in range(cells // 2)
        ]
    )
    slopes = [w * (2.0 * (i - middle) - mean) for i, w in enumerate(weights)]
    return weights, slopes


def dot(a, b):
    return jnp.dot(a, b, preferred_element_type=f32)


def gradients(products, weights, markers):
    weight_x, slope_x, weight_y, slope_y = ([weights[4 * n + i] for i in range(4)] for n in range(4))
    grads = []
    for c in range(3):
        lines = [[], [], []]
        for i in range(BX):
            rows = [((c * BX + i) * BY + j) * HALF for j in range(BY)]
            still = [products[row : row + HALF, :markers] for row in rows]
            rising = [products[row : row + HALF, markers:] for row in rows]
            lines[0].append(slope_x[i] * add_all([w * t for w, t in zip(weight_y, still)]))
            lines[1].append(weight_x[i] * add_all([w * t for w, t in zip(slope_y, still)]))
            lines[2].append(weight_x[i] * add_all([w * t for w, t in zip(weight_y, rising)]))
        grads.append([add_all(line) for line in lines])
    return grads


def own_lanes():
    shape = (HALF, 4 * BZ * HALF)
    lane = lax.broadcasted_iota(jnp.int32, shape, 1)
    return (lane % HALF == lax.broadcasted_iota(jnp.int32, shape, 0)).astype(f32)


def marker_groups(groups, counts, ins, outs, buffers, sums):
    spread, gather, places, start, dens, brick = ins
    visc_out, moments_out = outs
    permuted, left, right, products, weights, factors, planes_high, planes_low = buffers
    markers = places.shape[-1]
    inside = BZ * HALF
    own = own_lanes()
    halves = [
        (owner, 2 * group + half, half, 2 * n + half)
        for n, (owner, group) in enumerate(groups)
        for half in range(2)
    ]
    parts = [split(brick[owner, group]) for owner, group in groups]
    for _, _, half, n in halves:
        high, low = parts[n // 2]
        permuted[n][...] = dot(high, spread[half, 0]) + dot(low, spread[half, 1])
    heights = []
    for owner, part, _, n in halves:
        weight_z, slope_z = axis_weights(places[owner, 2, part], BZ)
        heights.append(weight_z)
        for z in range(0, BZ, 2):
            for column, values in ((0, weight_z), (1, slope_z)):
                high, low = split(jnp.concatenate(values[z : z + 2], axis=0))
                columns = slice(column * markers, (column + 1) * markers)
                for k in range(4):
                    begin = k * inside + z * HALF
                    right[n][begin : begin + 2 * HALF, columns] = low if k % 2 else high
    for _, _, _, n in halves:
        for row in range(0, ROWS, 2):
            pair = [
                jnp.broadcast_to(permuted[n][r : r + 1, :], own.shape) * own for r in (row, row + 1)
            ]
            left[n][row * HALF : (row + 2) * HALF, :] = jnp.concatenate(pair, axis=0).astype(bf16)
    for _, _, _, n in halves:
        products[n][...] = dot(left[n][...], right[n][...])
    for owner, part, _, n in halves:
        weights_x = axis_weights(places[owner, 0, part], BX)
        weights_y = axis_weights(places[owner, 1, part], BY)
        for k, values in enumerate((*weights_x, *weights_y)):
            for i, value in enumerate(values):
                weights[n][4 * k + i] = value
        for j in range(BY):
            for z in range(0, BZ, 2):
                pair = [weights_y[0][j] * heights[n][z + k] for k in range(2)]
                rows = slice((j * BZ + z) * HALF, (j * BZ + z + 2) * HALF)
                high, low = split(jnp.concatenate(pair, axis=0))
                planes_high[n][rows, :] = high
                planes_low[n][rows, :] = low

    count = 3 * BX * HALF
    for owner, part, _, n in halves:
        grads = gradients(products[n], weights[n], markers)
        normal = grads[0][0] ** 2 + grads[1][1] ** 2 + grads[2][2] ** 2
        shear_xy = 0.5 * (grads[0][1] + grads[1][0])
        shear_xz = 0.5 * (grads[0][2] + grads[2][0])
        shear_yz = 0.5 * (grads[1][2] + grads[2][1])
        invariant = 0.5 * normal + shear_xy**2 + shear_xz**2 + shear_yz**2
        scaled = invariant * (1.0 / (STRAIN_SCALE * STRAIN_SCALE))
        third = jnp.log(1.0 + scaled) * (1.0 / 3.0)
        first = start[owner, part]
        slot = lax.broadcasted_iota(jnp.int32, first.shape, 0) + part * HALF
        live = slot < counts[0, owner]
        visc_out[owner, part] = jnp.where(live, first * jnp.exp(-third), 0.0)
        carried = (
            live.astype(f32),
            jnp.where(live, jnp.log(first) - third, 0.0),
            jnp.where(live, dens[owner, part], 0.0),
        )
        for c in range(3):
            for i in range(0, BX, 2):
                pair = [carried[c] * weights[n][i + k] for k in range(2)]
                row = (c * BX + i) * HALF
                high, low = split(jnp.concatenate(pair, axis=0))
                factors[n][row : row + 2 * HALF, :] = high
                factors[n][count + row : count + row + 2 * HALF, :] = low

    contract = (((1,), (1,)), ((), ()))
    found = []
    for _, _, _, n in halves:
        both = lax.dot_general(
            factors[n][...], planes_high[n][...], contract, preferred_element_type=f32
        )
        rest = lax.dot_general(
            factors[n][:count], planes_low[n][...], contract, preferred_element_type=f32
        )
        found.append((both, rest))
    for _, _, half, n in halves:
        both, rest = found[n]
        total = both[:count] + both[count:] + rest
        chosen = total.reshape(3 * BX, HALF, BY * inside) * own[None]
        high, low = split(jnp.sum(chosen, axis=1))
        columns = slice(half * BY * inside, (half + 1) * BY * inside)
        row = (n // 2) * 32
        sums[row : row + 3 * BX, columns] = high.astype(f32)
        sums[row + 16 : row + 16 + 3 * BX, columns] = low.astype(f32)
    moved = dot(sums[...].astype(bf16), gather[...])
    for n, (owner, group) in enumerate(groups):
        mine = moved[32 * n : 32 * n + 3 * BX] + moved[32 * n + 16 : 32 * n + 16 + 3 * BX]
        for j in range(BY):
            rows = pl.ds(j, 3 * BX, stride=BY)
            moments_out[owner, group, rows, :] = mine[:, j * LANES : (j + 1) * LANES]


TOGETHER = 3


def marker_body(counts, *refs):
    sources, targets, scratch = refs[:6], refs[7:9], refs[9:]
    ins, outs, (got, sent, listed, sums, *flat) = scratch[:6], scratch[6:8], scratch[8:]
    fetches = [
        pltpu.make_async_copy(there, here, got.at[n])
        for n, (there, here) in enumerate(zip(sources, ins))
    ]
    for fetch in fetches:
        fetch.start()
    held = 2 * TOGETHER
    buffers = [flat[n * held : (n + 1) * held] for n in range(len(flat) // held)]
    visc_out, moments_out = outs
    owners, groups = moments_out.shape[:2]
    visc_out[...] = jnp.zeros_like(visc_out)
    moments_out[...] = jnp.zeros_like(moments_out)
    sums[...] = jnp.zeros_like(sums)

    def list_groups(index, number):
        owner, group = index // groups, index % groups
        live = group * GROUP < counts[0, owner]

        @pl.when(live)
        def _():
            for n in range(TOGETHER):
                listed[2 * (number + n)] = owner
                listed[2 * (number + n) + 1] = group

        return jnp.where(live, number + 1, number)

    number = lax.fori_loop(0, owners * groups, list_groups, 0)

    def step(index, carry):
        first = TOGETHER * index
        taken = [
            (listed[2 * (first + n)], listed[2 * (first + n) + 1]) for n in range(TOGETHER)
        ]
        marker_groups(taken, counts, ins, outs, buffers, sums)
        return carry

    for fetch in fetches:
        fetch.wait()
    lax.fori_loop(0, (number + TOGETHER - 1) // TOGETHER, step, 0)
    sends = [
        pltpu.make_async_copy(here, there, sent.at[n])
        for n, (here, there) in enumerate(zip(outs, targets))
    ]
    for send in sends:
        send.start()
    for send in sends:
        send.wait()


def marker_work(counts, positions, start_visc, marker_dens, bricks, after):
    owners, _, slots, markers = positions.shape
    groups, parts = slots // GROUP, slots // HALF
    spread, gather = permutations()
    width = 4 * BZ * HALF
    anywhere = pl.BlockSpec(memory_space=pl.ANY)
    fetched = (
        spread,
        gather,
        positions.reshape(owners, 3, parts, HALF, markers),
        start_visc.reshape(owners, parts, HALF, markers),
        marker_dens.reshape(owners, parts, HALF, markers),
        bricks,
    )
    shapes = ((owners, parts, HALF, markers), (owners, groups, ROWS, LANES))
    buffers = (
        pltpu.VMEM((ROWS, width), f32),
        pltpu.VMEM((ROWS * HALF, width), bf16),
        pltpu.VMEM((width, 2 * markers), bf16),
        pltpu.VMEM((ROWS * HALF, 2 * markers), f32),
        pltpu.VMEM((4 * 4, HALF, markers), f32),
        pltpu.VMEM((2 * 3 * BX * HALF, markers), bf16),
        pltpu.VMEM((BY * BZ * HALF, markers), bf16),
        pltpu.VMEM((BY * BZ * HALF, markers), bf16),
    )
    visc, moments = pl.pallas_call(
        marker_body,
        out_shape=tuple(jax.ShapeDtypeStruct(shape, f32) for shape in shapes),
        in_specs=[pl.BlockSpec(memory_space=pltpu.SMEM)] + [anywhere] * 7,
        out_specs=(anywhere, anywhere),
        scratch_shapes=[pltpu.VMEM(array.shape, array.dtype) for array in fetched]
        + [pltpu.VMEM(shape, f32) for shape in shapes]
        + [
            pltpu.SemaphoreType.DMA((len(fetched),)),
            pltpu.SemaphoreType.DMA((len(shapes),)),
            pltpu.SMEM((2 * (owners * groups + TOGETHER),), jnp.int32),
            pltpu.VMEM((32 * TOGETHER, 2 * BY * BZ * HALF), f32),
        ]
        + [buffer for buffer in buffers for _ in range(2 * TOGETHER)],
        compiler_params=vmem_limit(40),
        cost_estimate=cost(25),
        name="marker_work",
    )(counts, *in_hbm(*fetched), after)
    return visc.reshape(owners, slots, markers), moments


def settle_body(asked, moments_in, visc_in, dens_in, visc_far, dens_far, *scratch):
    moments, visc, dens, visc_out, dens_out, done, sent, *tables = scratch
    size_x, size_y, size_z = visc.shape
    copies = [
        pltpu.make_async_copy(there, here, done.at[n])
        for n, (there, here) in enumerate(
            ((moments_in, moments), (visc_in, visc), (dens_in, dens))
        )
    ]
    for copy in copies:
        copy.start()
    bricks_y, halves = size_y // BY, size_z // LANES
    for table in tables:
        table[...] = jnp.zeros_like(table)
    copies[0].wait()
    groups = moments.shape[1]
    lane_slot = lax.broadcasted_iota(jnp.int32, (ROWS, LANES), 1) // BZ

    def one_group(step, carry):
        device, group = step // groups, step % groups
        packed = moments[device, group]
        for slot in range(GROUP):
            table = tables[slot % len(tables)]
            place, lane = place_of(asked[device, group * GROUP + slot])
            piece = jnp.where(lane_slot == slot, packed, 0.0)
            piece = pltpu.roll(piece, (lane - BZ * slot) & (LANES - 1), 1)
            table[place] = table[place] + piece
        return carry

    lax.fori_loop(0, moments.shape[0] * groups, one_group, 0)
    copies[1].wait()
    copies[2].wait()

    def sends(block_x):
        planes = pl.ds(block_x * BX, BX)
        return [
            pltpu.make_async_copy(here.at[planes], there.at[planes], sent.at[n, block_x])
            for n, (here, there) in enumerate(((visc_out, visc_far), (dens_out, dens_far)))
        ]

    def finish(block_x, carry):
        for block_y in range(0, bricks_y, 2):
            for half in range(halves):
                for i in range(BX):
                    here = (
                        block_x * BX + i,
                        slice(block_y * BY, (block_y + 2) * BY),
                        slice(half * LANES, (half + 1) * LANES),
                    )
                    sums = []
                    for c in range(3):
                        rows = slice((c * BX + i) * BY, (c * BX + i + 1) * BY)
                        places = [
                            (block_x * bricks_y + block_y + k) * halves + half for k in range(2)
                        ]
                        sums.append(
                            jnp.concatenate(
                                [add_all([t[place, rows, :] for t in tables]) for place in places]
                            )
                        )
                    scale = 1.0 / (sums[0] + 1.0)
                    visc_out[here] = jnp.exp((sums[1] + jnp.log(visc[here])) * scale)
                    dens_out[here] = (sums[2] + dens[here]) * scale
        for send in sends(block_x):
            send.start()
        return carry

    def drain(block_x, carry):
        for send in sends(block_x):
            send.wait()
        return carry

    lax.fori_loop(0, size_x // BX, finish, 0)
    lax.fori_loop(0, size_x // BX, drain, 0)


def settle(asked, moments, cell_visc, cell_dens):
    size_x, size_y, size_z = cell_visc.shape
    places = (size_x // BX) * (size_y // BY) * (size_z // LANES)
    shape = jax.ShapeDtypeStruct(cell_visc.shape, f32)
    return pl.pallas_call(
        settle_body,
        out_shape=(shape, shape),
        in_specs=[pl.BlockSpec(memory_space=pltpu.SMEM)]
        + [pl.BlockSpec(memory_space=pl.ANY)] * 3,
        out_specs=(pl.BlockSpec(memory_space=pl.ANY),) * 2,
        scratch_shapes=[
            pltpu.VMEM(moments.shape, f32),
            pltpu.VMEM(cell_visc.shape, f32),
            pltpu.VMEM(cell_visc.shape, f32),
            pltpu.VMEM(cell_visc.shape, f32),
            pltpu.VMEM(cell_visc.shape, f32),
            pltpu.SemaphoreType.DMA((3,)),
            pltpu.SemaphoreType.DMA((2, size_x // BX)),
        ]
        + [pltpu.VMEM((places, ROWS, LANES), f32)],
        compiler_params=vmem_limit(24),
        cost_estimate=cost(7),
        name="settle",
    )(asked, *in_hbm(moments, cell_visc, cell_dens))


def field_of(fields, index):
    return fields[0].at[index] if index < 3 else fields[index - 2]


def pack_x_body(*refs):
    ends, outs = refs[:8], refs[8:]
    for side in range(2):
        for f in range(6):
            outs[side][f] = field_of(ends[side::2], f)[...]


def pack_x(velocity, pressure, cell_visc, cell_dens):
    size_x, size_y, size_z = cell_visc.shape
    width = SWEEPS
    ends = (0, size_x // width - 1)
    vel = [
        pl.BlockSpec((3, width, size_y, size_z), lambda i, e=e: (0, e, 0, 0)) for e in ends
    ]
    block = [pl.BlockSpec((width, size_y, size_z), lambda i, e=e: (e, 0, 0)) for e in ends]
    whole = pl.BlockSpec((6, width, size_y, size_z), lambda i: (0, 0, 0, 0))
    shape = jax.ShapeDtypeStruct((6, width, size_y, size_z), f32)
    return pl.pallas_call(
        pack_x_body,
        grid=(1,),
        out_shape=(shape, shape),
        in_specs=vel + block * 3,
        out_specs=(whole, whole),
        compiler_params=vmem_limit(60),
        cost_estimate=cost(2),
        name="pack_x",
    )(velocity, velocity, pressure, pressure, cell_visc, cell_visc, cell_dens, cell_dens)


def corner_rows(upward, size_x):
    width = SWEEPS
    spare = (5 * width,) if upward else (4 * width - 1, 6 * width - 1)
    places = [(plane, row) for plane in range(size_x) for row in spare]
    found = []
    for field in range(6):
        for side in range(2):
            near = field == 5 or (field == 3 and side == 1 and not upward)
            reach = width - 1 if near else width
            for far_x in range(1, width):
                for far_y in range(1, reach - far_x + 1):
                    found.append((field, side, far_x, far_y))
    more = max(0, len(found) - len(places))
    places += [(size_x + n // (6 * width), n % (6 * width)) for n in range(more)]
    return [cell + at for cell, at in zip(found, places)], size_x + -(-more // (6 * width))


def pack_y_body(size_x, vel, pres, visc, dens, low_x, high_x, upward, downward):
    step_x, size_y, _ = pres.shape
    width = SWEEPS
    step = pl.program_id(0)
    planes = pl.ds(pl.multiple_of(step * step_x, step_x), step_x)
    for f in range(6):
        field = field_of((vel, pres, visc, dens), f)
        rows = slice(f * width, (f + 1) * width)
        upward[planes, rows, :] = field[:, size_y - width :, :]
        downward[planes, rows, :] = field[:, :width, :]

    @pl.when(step == pl.num_programs(0) - 1)
    def _():
        for up, face in ((True, upward), (False, downward)):
            for f, side, far_x, far_y, plane, row in corner_rows(up, size_x)[0]:
                halo, at = (high_x, far_x - 1) if side else (low_x, width - far_x)
                face[plane, row] = halo[f, at, size_y - far_y if up else far_y - 1]


def pack_y(velocity, pressure, cell_visc, cell_dens, low_x, high_x):
    size_x, size_y, size_z = cell_visc.shape
    step = 8
    block = pl.BlockSpec((step, size_y, size_z), lambda i: (i, 0, 0))
    halo = pl.BlockSpec(low_x.shape, lambda i: (0, 0, 0, 0))
    shapes = [(corner_rows(up, size_x)[1], 6 * SWEEPS, size_z) for up in (True, False)]
    return pl.pallas_call(
        functools.partial(pack_y_body, size_x),
        grid=(size_x // step,),
        out_shape=tuple(jax.ShapeDtypeStruct(shape, f32) for shape in shapes),
        in_specs=[
            pl.BlockSpec((3, step, size_y, size_z), lambda i: (0, i, 0, 0)),
            block,
            block,
            block,
            halo,
            halo,
        ],
        out_specs=tuple(pl.BlockSpec(shape, lambda i: (0, 0, 0)) for shape in shapes),
        compiler_params=vmem_limit(24),
        cost_estimate=cost(15),
        name="pack_y",
    )(*in_hbm(velocity, pressure, cell_visc, cell_dens), low_x, high_x)


def place(per, x, y, rows):
    return x % per, pl.ds(y * SUBLANES + x // per, rows, stride=SUBLANES)


def put(target, x, y, rows, value):
    per, halves = target.shape[:2]
    plane, lines = place(per, x, y, rows)
    for half in range(halves):
        target[plane, half, lines, :] = value[:, half * LANES : (half + 1) * LANES]


def tile(y):
    if isinstance(y, int):
        return pl.ds(y * SUBLANES, SUBLANES)
    return pl.ds(pl.multiple_of(y * SUBLANES, SUBLANES), SUBLANES)


def row_work(cells, coefs, relax, forcing, rate):
    per, halves = cells.shape[1:3]
    lane = lax.broadcasted_iota(jnp.int32, (SUBLANES, LANES), 1)
    at_first, at_last = lane == 0, lane == LANES - 1

    def take(field, plane, y):
        return jnp.concatenate([field[plane, half, tile(y), :] for half in range(halves)], axis=1)

    def store(field, plane, y, value):
        for half in range(halves):
            field[plane, half, tile(y), :] = value[:, half * LANES : (half + 1) * LANES]

    def up_x(field, plane, y):
        if plane < per - 1:
            return take(field, plane + 1, y)
        return pltpu.roll(take(field, 0, y), SUBLANES - 1, 0)

    def down_x(field, plane, y):
        if plane > 0:
            return take(field, plane - 1, y)
        return pltpu.roll(take(field, per - 1, y), 1, 0)

    def rolled(a, shift):
        return [
            pltpu.roll(a[:, half * LANES : (half + 1) * LANES], shift, 1) for half in range(halves)
        ]

    def up_z(a):
        parts = rolled(a, LANES - 1)
        after = parts[1:] + [jnp.zeros_like(parts[0])]
        return jnp.concatenate([jnp.where(at_last, n, p) for p, n in zip(parts, after)], axis=1)

    def down_z(a):
        parts = rolled(a, 1)
        before = [jnp.zeros_like(parts[0])] + parts[:-1]
        return jnp.concatenate([jnp.where(at_first, b, p) for p, b in zip(parts, before)], axis=1)

    def prepare(y):
        visc, dens = cells.at[0], cells.at[1]
        for plane in range(per):
            here = take(visc, plane, y)
            near = [
                up_x(visc, plane, y),
                down_x(visc, plane, y),
                take(visc, plane, y + 1),
                take(visc, plane, y - 1),
                up_z(here),
                down_z(here),
            ]
            links = [0.5 * (here + other) for other in near]
            scale = jnp.where(here > 0.0, RELAX / add_all(links), 0.0)
            for n in range(6):
                coefs[n, plane, tile(y), :] = links[n] * scale
            relax[plane, tile(y), :] = scale
            forcing[plane, tile(y), :] = take(dens, plane, y) * (-GRAVITY * scale)
            rate[plane, tile(y), :] = PRESSURE_RATE * here

    def sweep(y, old, new):
        for plane in range(per):
            links = [coefs[n, plane, tile(y), :] for n in range(6)]
            scale = relax[plane, tile(y), :]
            pressure = take(old.at[3], plane, y)
            before = (
                down_x(old.at[3], plane, y),
                take(old.at[3], plane, y - 1),
                down_z(pressure),
            )
            changes = []
            for c in range(3):
                field = old.at[c]
                here = take(field, plane, y)
                near = [
                    up_x(field, plane, y),
                    down_x(field, plane, y),
                    take(field, plane, y + 1),
                    take(field, plane, y - 1),
                    up_z(here),
                    down_z(here),
                ]
                terms = [link * other for link, other in zip(links, near)]
                total = (terms[0] + terms[1]) + (terms[2] + terms[3])
                total = total + (terms[4] + terms[5])
                rest = (1.0 - RELAX) * here - scale * (pressure - before[c])
                if c == 2:
                    rest = rest + forcing[plane, tile(y), :]
                changes.append(near[2 * c] - here)
                store(new.at[c], plane, y, total + rest)
            pressed = pressure - rate[plane, tile(y), :] * add_all(changes)
            store(new.at[3], plane, y, pressed)

    return prepare, sweep


def kept_rows(size_y):
    width = SWEEPS
    return (
        ((width, size_y),),
        ((width + 1, width), (size_y - 1, width)),
        ((width, width + 1), (size_y - 1, width + 1)),
    )


def kept_copies(pairs, size_y, done):
    copies = []
    for (source, target), strips in zip(pairs, kept_rows(size_y)):
        for begin, rows in strips:
            span = (slice(None),) * 3 + (pl.ds(begin * SUBLANES, rows * SUBLANES),)
            copies.append(
                pltpu.make_async_copy(source.at[span], target.at[span], done.at[len(copies)])
            )
    return copies


def inner_body(vel, pres, visc, dens, low_x, high_x, _, even_out, odd_out, cells_out, *work):
    blocks, sides_x, even, odd, cells, coefs, relax, forcing, rate, done, more = work
    size_x, size_y, size_z = blocks.shape[1:]
    width = SWEEPS
    inputs = (
        (visc, blocks.at[4]),
        (dens, blocks.at[5]),
        (low_x, sides_x.at[0]),
        (high_x, sides_x.at[1]),
        (vel, blocks.at[0:3]),
        (pres, blocks.at[3]),
    )
    copies = [
        pltpu.make_async_copy(there, here, done.at[n]) for n, (there, here) in enumerate(inputs)
    ]
    for copy in copies:
        copy.start()
    targets = [even.at[n] for n in range(4)] + [cells.at[n] for n in range(2)]

    def lay_out(f):
        for i in range(size_x):
            for y in range(0, size_y, SUBLANES):
                value = blocks[f, i, y : y + SUBLANES, :]
                put(targets[f], i + width, y + width, SUBLANES, value)
        for side, begin in enumerate((0, width + size_x)):
            for i in range(width):
                for y in range(0, size_y, SUBLANES):
                    value = sides_x[side, f, i, y : y + SUBLANES, :]
                    put(targets[f], begin + i, y + width, SUBLANES, value)

    for copy in copies[:4]:
        copy.wait()
    lay_out(4)
    lay_out(5)
    sends = kept_copies(((even, even_out), (odd, odd_out), (cells, cells_out)), size_y, more)
    for send in sends[3:]:
        send.start()

    prepare, sweep = row_work(cells, coefs, relax, forcing, rate)

    def prepare_row(y, carry):
        prepare(y)
        return carry

    first, last = width + 1, width + size_y - 1
    lax.fori_loop(first, last, prepare_row, 0, unroll=2)
    for copy in copies[4:]:
        copy.wait()
    for f in range(4):
        lay_out(f)
    early, late = (sends[1:3], sends[:1]) if SWEEPS % 2 == 0 else (sends[:1], sends[1:3])
    for step in range(SWEEPS):
        old, new = (odd, even) if step % 2 else (even, odd)
        if step == SWEEPS - 1:
            for send in early:
                send.start()

        def sweep_row(y, carry, old=old, new=new):
            sweep(y, old, new)
            return carry

        lax.fori_loop(first + step, last - step, sweep_row, 0, unroll=2)
    for send in late:
        send.start()
    for send in sends:
        send.wait()


def inner_sweeps(velocity, pressure, cell_visc, cell_dens, low_x, high_x, after):
    size_x, size_y, size_z = cell_visc.shape
    width = low_x.shape[1]
    per, rows = (size_x + 2 * width) // SUBLANES, (size_y + 2 * width) * SUBLANES
    block, cut = (per, rows, size_z), (per, size_z // LANES, rows, LANES)
    shapes = [(4,) + cut, (4,) + cut, (2,) + cut]
    anywhere = pl.BlockSpec(memory_space=pl.ANY)
    return pl.pallas_call(
        inner_body,
        out_shape=tuple(jax.ShapeDtypeStruct(shape, f32) for shape in shapes),
        in_specs=[anywhere] * 7,
        out_specs=(anywhere,) * 3,
        scratch_shapes=[
            pltpu.VMEM((6,) + cell_visc.shape, f32),
            pltpu.VMEM((2,) + low_x.shape, f32),
        ]
        + [pltpu.VMEM(shape, f32) for shape in shapes]
        + [
            pltpu.VMEM((6,) + block, f32),
            pltpu.VMEM(block, f32),
            pltpu.VMEM(block, f32),
            pltpu.VMEM(block, f32),
            pltpu.SemaphoreType.DMA((6,)),
            pltpu.SemaphoreType.DMA((5,)),
        ],
        compiler_params=vmem_limit(40),
        cost_estimate=cost(25),
        name="inner_sweeps",
    )(*in_hbm(velocity, pressure, cell_visc, cell_dens, low_x, high_x), after)


def edge_body(even_in, odd_in, cells_in, low_y, high_y, vel_out, pres_out, *work):
    from_low, from_high, results, even, odd, cells, coefs, relax, forcing, rate, done, more = work
    size_x, size_y, size_z = results.shape[1:]
    width = SWEEPS
    long_y = size_y + 2 * width
    halos = [
        pltpu.make_async_copy(low_y, from_low, more.at[0]),
        pltpu.make_async_copy(high_y, from_high, more.at[1]),
    ]
    kept = kept_copies(((even_in, even), (odd_in, odd), (cells_in, cells)), size_y, done)
    for copy in (*halos, *kept[3:], *kept[:3]):
        copy.start()
    targets = [even.at[n] for n in range(4)] + [cells.at[n] for n in range(2)]

    def lay_out(chosen):
        for f in chosen:
            for x in (*range(width), *range(width + size_x, size_x + 2 * width)):
                for y in (0, width + size_y):
                    put(targets[f], x, y, width, jnp.zeros((width, size_z), f32))
            rows = slice(f * width, (f + 1) * width)
            for halo, begin in ((from_low, 0), (from_high, width + size_y)):
                for i in range(size_x):
                    put(targets[f], i + width, begin, width, halo[i, rows, :])
        for up, halo in ((True, from_low), (False, from_high)):
            for f, side, far_x, far_y, plane, row in corner_rows(up, size_x)[0]:
                if f in chosen:
                    x = width + size_x - 1 + far_x if side else width - far_x
                    y = width - far_y if up else width + size_y - 1 + far_y
                    put(targets[f], x, y, 1, halo[plane, row : row + 1, :])

    for copy in halos:
        copy.wait()
    lay_out((4, 5))
    for copy in kept[3:]:
        copy.wait()

    prepare, sweep = row_work(cells, coefs, relax, forcing, rate)

    def prepare_rows(n, carry):
        prepare(1 + n)
        prepare(long_y - 2 * width + n)
        return carry

    lax.fori_loop(0, 2 * width - 1, prepare_rows, 0)
    lay_out((0, 1, 2, 3))
    for copy in kept[:3]:
        copy.wait()
    for step in range(SWEEPS):
        old, new = (odd, even) if step % 2 else (even, odd)

        def sweep_rows(n, carry, old=old, new=new, step=step):
            sweep(1 + step + n, old, new)
            sweep(width + size_y - 1 - step + n, old, new)
            return carry

        lax.fori_loop(0, width, sweep_rows, 0)

    final = odd if SWEEPS % 2 else even
    outs = [vel_out.at[0], vel_out.at[1], vel_out.at[2], pres_out]
    sends = [pltpu.make_async_copy(results.at[n], out, done.at[n]) for n, out in enumerate(outs)]
    per, halves = even.shape[1:3]
    for field, send in enumerate(sends):
        for i in range(size_x):
            for y in range(0, size_y, SUBLANES):
                plane, lines = place(per, i + width, y + width, SUBLANES)
                for half in range(halves):
                    columns = slice(half * LANES, (half + 1) * LANES)
                    results[field, i, y : y + SUBLANES, columns] = final[
                        field, plane, half, lines, :
                    ]
        send.start()
    for send in sends:
        send.wait()


def edge_sweeps(even, odd, cells, low_y, high_y, size_x, size_y):
    per, halves, rows = even.shape[1:4]
    size_z = halves * LANES
    block = (per, rows, size_z)
    anywhere = pl.BlockSpec(memory_space=pl.ANY)
    return pl.pallas_call(
        edge_body,
        out_shape=(
            jax.ShapeDtypeStruct((3, size_x, size_y, size_z), f32),
            jax.ShapeDtypeStruct((size_x, size_y, size_z), f32),
        ),
        in_specs=[anywhere] * 5,
        out_specs=(anywhere,) * 2,
        scratch_shapes=[
            pltpu.VMEM(low_y.shape, f32),
            pltpu.VMEM(high_y.shape, f32),
            pltpu.VMEM((4, size_x, size_y, size_z), f32),
            pltpu.VMEM(even.shape, f32),
            pltpu.VMEM(odd.shape, f32),
            pltpu.VMEM(cells.shape, f32),
            pltpu.VMEM((6,) + block, f32),
            pltpu.VMEM(block, f32),
            pltpu.VMEM(block, f32),
            pltpu.VMEM(block, f32),
            pltpu.SemaphoreType.DMA((5,)),
            pltpu.SemaphoreType.DMA((2,)),
        ],
        compiler_params=vmem_limit(40),
        cost_estimate=cost(1),
        name="edge_sweeps",
    )(even, odd, cells, low_y, high_y)


def shift(value, axis, step):
    size = lax.axis_size(axis)
    pairs = [(i, i + step) for i in range(size) if 0 <= i + step < size]
    return lax.ppermute(value, axis, pairs)


def per_device(
    velocity,
    pressure,
    cell_visc,
    cell_dens,
    block_brick,
    block_counts,
    positions,
    start_visc,
    marker_dens,
):
    asked = lax.all_to_all(block_brick, "mark", 0, 0, tiled=True)
    fields = (velocity, pressure, cell_visc, cell_dens)
    to_low, to_high = pack_x(*fields)
    low_x, high_x = shift(to_high, "grid", 1), shift(to_low, "grid", -1)
    upward, downward = pack_y(*fields, low_x, high_x)
    low_y, high_y = shift(upward, "mark", 1), shift(downward, "mark", -1)

    picked = pick_bricks(asked, velocity)
    bricks = lax.all_to_all(picked, "mark", 0, 0, tiled=True)
    marker_visc, moments = marker_work(
        block_counts, positions, start_visc, marker_dens, bricks, upward
    )
    gathered = lax.all_to_all(moments, "mark", 0, 0, tiled=True)
    state = inner_sweeps(*fields, low_x, high_x, moments)
    velocity_next, pressure_next = edge_sweeps(*state, low_y, high_y, *pressure.shape[:2])
    visc_next, dens_next = settle(asked, gathered, cell_visc, cell_dens)
    return velocity_next, pressure_next, visc_next, dens_next, marker_visc


def solution(mesh):
    in_specs = (
        P(None, "grid", "mark", None),
        P("grid", "mark", None),
        P("grid", "mark", None),
        P("grid", "mark", None),
        P(("grid", "mark"), None),
        P(("grid", "mark"), None),
        P(("grid", "mark"), None, None, None),
        P(("grid", "mark"), None, None),
        P(("grid", "mark"), None, None),
    )
    out_specs = (
        P(None, "grid", "mark", None),
        P("grid", "mark", None),
        P("grid", "mark", None),
        P("grid", "mark", None),
        P(("grid", "mark"), None, None),
    )
    return jax.shard_map(
        per_device, mesh=mesh, in_specs=in_specs, out_specs=out_specs, check_vma=False
    )
```

```python
import functools

import jax
import jax.numpy as jnp
import numpy as np
from jax import lax
from jax.experimental import pallas as pl
from jax.experimental.pallas import tpu as pltpu
from jax.sharding import PartitionSpec as P

SWEEPS = 4
RELAX = 0.6
PRESSURE_RATE = 0.25
GRAVITY = 1.0
STRAIN_SCALE = 0.5

BX, BY, BZ = 4, 4, 8
PLANE = BX * BY
ROWS = 3 * PLANE
LANES = 128
GROUP = LANES // BZ
HALF = 8
SUBLANES = 8

f32, bf16 = jnp.float32, jnp.bfloat16


def vmem_limit(mib):
    return pltpu.CompilerParams(vmem_limit_bytes=mib * 1024 * 1024)


def in_hbm(*arrays):
    return [pltpu.with_memory_space_constraint(array, pltpu.HBM) for array in arrays]


def cost(microseconds):
    return pl.CostEstimate(
        flops=int(microseconds * 1.15e9), bytes_accessed=0, transcendentals=0
    )


def place_of(brick):
    return lax.shift_right_logical(brick, GROUP.bit_length() - 1), (brick & (GROUP - 1)) * BZ


def pick_body(asked, vel, far, out, table, sent):
    size_x, size_y, size_z = vel.shape[1:]
    bricks_y, halves = size_y // BY, size_z // LANES

    def repack(block_x, carry):
        for block_y in range(bricks_y):
            for half in range(halves):
                place = (block_x * bricks_y + block_y) * halves + half
                for c in range(3):
                    for i in range(BX):
                        row = (c * BX + i) * BY
                        table[place, row : row + BY, :] = vel[
                            c,
                            block_x * BX + i,
                            block_y * BY : (block_y + 1) * BY,
                            half * LANES : (half + 1) * LANES,
                        ]
        return carry

    lax.fori_loop(0, size_x // BX, repack, 0)
    groups = out.shape[1]
    lane_slot = lax.broadcasted_iota(jnp.int32, (ROWS, LANES), 1) // BZ

    def one_group(device, group):
        packed = jnp.zeros((ROWS, LANES), f32)
        for slot in range(GROUP):
            place, lane = place_of(asked[device, group * GROUP + slot])
            rolled = pltpu.roll(table[place], (BZ * slot - lane) & (LANES - 1), 1)
            packed = jnp.where(lane_slot == slot, rolled, packed)
        out[device, group] = packed

    def send(device):
        return pltpu.make_async_copy(out.at[device], far.at[device], sent.at[device])

    def one_device(device, carry):
        def each(group, inner):
            one_group(device, group)
            return inner

        lax.fori_loop(0, groups, each, 0)
        send(device).start()
        return carry

    def drain(device, carry):
        send(device).wait()
        return carry

    lax.fori_loop(0, out.shape[0], one_device, 0)
    lax.fori_loop(0, out.shape[0], drain, 0)


def pick_bricks(asked, velocity):
    devices, slots = asked.shape
    size_x, size_y, size_z = velocity.shape[1:]
    places = (size_x // BX) * (size_y // BY) * (size_z // LANES)
    return pl.pallas_call(
        pick_body,
        out_shape=jax.ShapeDtypeStruct((devices, slots // GROUP, ROWS, LANES), f32),
        in_specs=[
            pl.BlockSpec(memory_space=pltpu.SMEM),
            pl.BlockSpec(memory_space=pltpu.VMEM),
        ],
        out_specs=pl.BlockSpec(memory_space=pl.ANY),
        scratch_shapes=[
            pltpu.VMEM((devices, slots // GROUP, ROWS, LANES), f32),
            pltpu.VMEM((places, ROWS, LANES), f32),
            pltpu.SemaphoreType.DMA((devices,)),
        ],
        compiler_params=vmem_limit(24),
        cost_estimate=cost(25),
        name="pick_bricks",
    )(asked, velocity)


def permutations():
    inside = BZ * HALF
    spread = np.zeros((2, 2, LANES, 4 * inside), np.float32)
    gather = np.zeros((2 * BY * inside, BY * LANES), np.float32)
    for half in range(2):
        for slot in range(HALF):
            for z in range(BZ):
                outer, inner = (half * HALF + slot) * BZ + z, z * HALF + slot
                for part in range(4):
                    spread[half, part // 2, outer, part * inside + inner] = 1
                for j in range(BY):
                    gather[(half * BY + j) * inside + inner, j * LANES + outer] = 1
    return jnp.asarray(spread, bf16), jnp.asarray(gather, bf16)


def split(value):
    high = value.astype(bf16)
    return high, (value - high.astype(f32)).astype(bf16)


def add_all(values):
    return functools.reduce(jnp.add, values)


def axis_weights(fraction, cells):
    middle = (cells - 1) / 2
    base = jnp.exp(fraction * (2.0 * cells) - float(cells))
    powers = [None, base]
    for i in range(2, cells):
        powers.append(powers[i // 2] * powers[i - i // 2])
    factors = [float(np.exp(middle**2 - (i - middle) ** 2)) for i in range(cells)]
    bells = [None] + [powers[i] * factors[i] for i in range(1, cells)]
    scale = 1.0 / (add_all(bells[1:]) + factors[0])
    weights = [scale * factors[0]] + [bell * scale for bell in bells[1:]]
    mean = add_all(
        [
            (weights[cells - 1 - i] - weights[i]) * (2.0 * (middle - i))
            for i in range(cells // 2)
        ]
    )
    slopes = [w * (2.0 * (i - middle) - mean) for i, w in enumerate(weights)]
    return weights, slopes


def dot(a, b):
    return jnp.dot(a, b, preferred_element_type=f32)


def gradients(products, weights, markers):
    weight_x, slope_x, weight_y, slope_y = ([weights[4 * n + i] for i in range(4)] for n in range(4))
    grads = []
    for c in range(3):
        lines = [[], [], []]
        for i in range(BX):
            rows = [((c * BX + i) * BY + j) * HALF for j in range(BY)]
            still = [products[row : row + HALF, :markers] for row in rows]
            rising = [products[row : row + HALF, markers:] for row in rows]
            lines[0].append(slope_x[i] * add_all([w * t for w, t in zip(weight_y, still)]))
            lines[1].append(weight_x[i] * add_all([w * t for w, t in zip(slope_y, still)]))
            lines[2].append(weight_x[i] * add_all([w * t for w, t in zip(weight_y, rising)]))
        grads.append([add_all(line) for line in lines])
    return grads


def own_lanes():
    shape = (HALF, 4 * BZ * HALF)
    lane = lax.broadcasted_iota(jnp.int32, shape, 1)
    return (lane % HALF == lax.broadcasted_iota(jnp.int32, shape, 0)).astype(f32)


def marker_groups(groups, counts, ins, outs, buffers, sums):
    spread, gather, places, start, dens, brick = ins
    visc_out, moments_out = outs
    permuted, left, right, products, weights, factors, planes_high, planes_low = buffers
    markers = places.shape[-1]
    inside = BZ * HALF
    own = own_lanes()
    halves = [
        (owner, 2 * group + half, half, 2 * n + half)
        for n, (owner, group) in enumerate(groups)
        for half in range(2)
    ]
    parts = [split(brick[owner, group]) for owner, group in groups]
    for _, _, half, n in halves:
        high, low = parts[n // 2]
        permuted[n][...] = dot(high, spread[half, 0]) + dot(low, spread[half, 1])
    heights = []
    for owner, part, _, n in halves:
        weight_z, slope_z = axis_weights(places[owner, 2, part], BZ)
        heights.append(weight_z)
        for z in range(0, BZ, 2):
            for column, values in ((0, weight_z), (1, slope_z)):
                high, low = split(jnp.concatenate(values[z : z + 2], axis=0))
                columns = slice(column * markers, (column + 1) * markers)
                for k in range(4):
                    begin = k * inside + z * HALF
                    right[n][begin : begin + 2 * HALF, columns] = low if k % 2 else high
    for _, _, _, n in halves:
        for row in range(0, ROWS, 2):
            pair = [
                jnp.broadcast_to(permuted[n][r : r + 1, :], own.shape) * own for r in (row, row + 1)
            ]
            left[n][row * HALF : (row + 2) * HALF, :] = jnp.concatenate(pair, axis=0).astype(bf16)
    for _, _, _, n in halves:
        products[n][...] = dot(left[n][...], right[n][...])
    for owner, part, _, n in halves:
        weights_x = axis_weights(places[owner, 0, part], BX)
        weights_y = axis_weights(places[owner, 1, part], BY)
        for k, values in enumerate((*weights_x, *weights_y)):
            for i, value in enumerate(values):
                weights[n][4 * k + i] = value
        for j in range(BY):
            for z in range(0, BZ, 2):
                pair = [weights_y[0][j] * heights[n][z + k] for k in range(2)]
                rows = slice((j * BZ + z) * HALF, (j * BZ + z + 2) * HALF)
                high, low = split(jnp.concatenate(pair, axis=0))
                planes_high[n][rows, :] = high
                planes_low[n][rows, :] = low

    count = 3 * BX * HALF
    for owner, part, _, n in halves:
        grads = gradients(products[n], weights[n], markers)
        normal = grads[0][0] ** 2 + grads[1][1] ** 2 + grads[2][2] ** 2
        shear_xy = 0.5 * (grads[0][1] + grads[1][0])
        shear_xz = 0.5 * (grads[0][2] + grads[2][0])
        shear_yz = 0.5 * (grads[1][2] + grads[2][1])
        invariant = 0.5 * normal + shear_xy**2 + shear_xz**2 + shear_yz**2
        scaled = invariant * (1.0 / (STRAIN_SCALE * STRAIN_SCALE))
        third = jnp.log(1.0 + scaled) * (1.0 / 3.0)
        first = start[owner, part]
        slot = lax.broadcasted_iota(jnp.int32, first.shape, 0) + part * HALF
        live = slot < counts[0, owner]
        visc_out[owner, part] = jnp.where(live, first * jnp.exp(-third), 0.0)
        carried = (
            live.astype(f32),
            jnp.where(live, jnp.log(first) - third, 0.0),
            jnp.where(live, dens[owner, part], 0.0),
        )
        for c in range(3):
            for i in range(0, BX, 2):
                pair = [carried[c] * weights[n][i + k] for k in range(2)]
                row = (c * BX + i) * HALF
                high, low = split(jnp.concatenate(pair, axis=0))
                factors[n][row : row + 2 * HALF, :] = high
                factors[n][count + row : count + row + 2 * HALF, :] = low

    contract = (((1,), (1,)), ((), ()))
    found = []
    for _, _, _, n in halves:
        both = lax.dot_general(
            factors[n][...], planes_high[n][...], contract, preferred_element_type=f32
        )
        rest = lax.dot_general(
            factors[n][:count], planes_low[n][...], contract, preferred_element_type=f32
        )
        found.append((both, rest))
    for _, _, half, n in halves:
        both, rest = found[n]
        total = both[:count] + both[count:] + rest
        chosen = total.reshape(3 * BX, HALF, BY * inside) * own[None]
        high, low = split(jnp.sum(chosen, axis=1))
        columns = slice(half * BY * inside, (half + 1) * BY * inside)
        row = (n // 2) * 32
        sums[row : row + 3 * BX, columns] = high.astype(f32)
        sums[row + 16 : row + 16 + 3 * BX, columns] = low.astype(f32)
    moved = dot(sums[...].astype(bf16), gather[...])
    for n, (owner, group) in enumerate(groups):
        mine = moved[32 * n : 32 * n + 3 * BX] + moved[32 * n + 16 : 32 * n + 16 + 3 * BX]
        for j in range(BY):
            rows = pl.ds(j, 3 * BX, stride=BY)
            moments_out[owner, group, rows, :] = mine[:, j * LANES : (j + 1) * LANES]


TOGETHER = 3


def marker_body(counts, *refs):
    sources, targets, scratch = refs[:6], refs[7:9], refs[9:]
    ins, outs, (got, sent, listed, sums, *flat) = scratch[:6], scratch[6:8], scratch[8:]
    fetches = [
        pltpu.make_async_copy(there, here, got.at[n])
        for n, (there, here) in enumerate(zip(sources, ins))
    ]
    for fetch in fetches:
        fetch.start()
    held = 2 * TOGETHER
    buffers = [flat[n * held : (n + 1) * held] for n in range(len(flat) // held)]
    visc_out, moments_out = outs
    owners, groups = moments_out.shape[:2]
    visc_out[...] = jnp.zeros_like(visc_out)
    moments_out[...] = jnp.zeros_like(moments_out)
    sums[...] = jnp.zeros_like(sums)

    def list_groups(index, number):
        owner, group = index // groups, index % groups
        live = group * GROUP < counts[0, owner]

        @pl.when(live)
        def _():
            for n in range(TOGETHER):
                listed[2 * (number + n)] = owner
                listed[2 * (number + n) + 1] = group

        return jnp.where(live, number + 1, number)

    number = lax.fori_loop(0, owners * groups, list_groups, 0)

    def step(index, carry):
        first = TOGETHER * index
        taken = [
            (listed[2 * (first + n)], listed[2 * (first + n) + 1]) for n in range(TOGETHER)
        ]
        marker_groups(taken, counts, ins, outs, buffers, sums)
        return carry

    for fetch in fetches:
        fetch.wait()
    lax.fori_loop(0, (number + TOGETHER - 1) // TOGETHER, step, 0)
    sends = [
        pltpu.make_async_copy(here, there, sent.at[n])
        for n, (here, there) in enumerate(zip(outs, targets))
    ]
    for send in sends:
        send.start()
    for send in sends:
        send.wait()


def marker_work(counts, positions, start_visc, marker_dens, bricks, after):
    owners, _, slots, markers = positions.shape
    groups, parts = slots // GROUP, slots // HALF
    spread, gather = permutations()
    width = 4 * BZ * HALF
    anywhere = pl.BlockSpec(memory_space=pl.ANY)
    fetched = (
        spread,
        gather,
        positions.reshape(owners, 3, parts, HALF, markers),
        start_visc.reshape(owners, parts, HALF, markers),
        marker_dens.reshape(owners, parts, HALF, markers),
        bricks,
    )
    shapes = ((owners, parts, HALF, markers), (owners, groups, ROWS, LANES))
    buffers = (
        pltpu.VMEM((ROWS, width), f32),
        pltpu.VMEM((ROWS * HALF, width), bf16),
        pltpu.VMEM((width, 2 * markers), bf16),
        pltpu.VMEM((ROWS * HALF, 2 * markers), f32),
        pltpu.VMEM((4 * 4, HALF, markers), f32),
        pltpu.VMEM((2 * 3 * BX * HALF, markers), bf16),
        pltpu.VMEM((BY * BZ * HALF, markers), bf16),
        pltpu.VMEM((BY * BZ * HALF, markers), bf16),
    )
    visc, moments = pl.pallas_call(
        marker_body,
        out_shape=tuple(jax.ShapeDtypeStruct(shape, f32) for shape in shapes),
        in_specs=[pl.BlockSpec(memory_space=pltpu.SMEM)] + [anywhere] * 7,
        out_specs=(anywhere, anywhere),
        scratch_shapes=[pltpu.VMEM(array.shape, array.dtype) for array in fetched]
        + [pltpu.VMEM(shape, f32) for shape in shapes]
        + [
            pltpu.SemaphoreType.DMA((len(fetched),)),
            pltpu.SemaphoreType.DMA((len(shapes),)),
            pltpu.SMEM((2 * (owners * groups + TOGETHER),), jnp.int32),
            pltpu.VMEM((32 * TOGETHER, 2 * BY * BZ * HALF), f32),
        ]
        + [buffer for buffer in buffers for _ in range(2 * TOGETHER)],
        compiler_params=vmem_limit(40),
        cost_estimate=cost(25),
        name="marker_work",
    )(counts, *in_hbm(*fetched), after)
    return visc.reshape(owners, slots, markers), moments


def settle_body(asked, moments_in, visc_in, dens_in, visc_far, dens_far, *scratch):
    moments, visc, dens, visc_out, dens_out, done, sent, *tables = scratch
    size_x, size_y, size_z = visc.shape
    copies = [
        pltpu.make_async_copy(there, here, done.at[n])
        for n, (there, here) in enumerate(
            ((moments_in, moments), (visc_in, visc), (dens_in, dens))
        )
    ]
    for copy in copies:
        copy.start()
    bricks_y, halves = size_y // BY, size_z // LANES
    for table in tables:
        table[...] = jnp.zeros_like(table)
    copies[0].wait()
    groups = moments.shape[1]
    lane_slot = lax.broadcasted_iota(jnp.int32, (ROWS, LANES), 1) // BZ

    def one_group(step, carry):
        device, group = step // groups, step % groups
        packed = moments[device, group]
        for slot in range(GROUP):
            table = tables[slot % len(tables)]
            place, lane = place_of(asked[device, group * GROUP + slot])
            piece = jnp.where(lane_slot == slot, packed, 0.0)
            piece = pltpu.roll(piece, (lane - BZ * slot) & (LANES - 1), 1)
            table[place] = table[place] + piece
        return carry

    lax.fori_loop(0, moments.shape[0] * groups, one_group, 0)
    copies[1].wait()
    copies[2].wait()

    def sends(block_x):
        planes = pl.ds(block_x * BX, BX)
        return [
            pltpu.make_async_copy(here.at[planes], there.at[planes], sent.at[n, block_x])
            for n, (here, there) in enumerate(((visc_out, visc_far), (dens_out, dens_far)))
        ]

    def finish(block_x, carry):
        for block_y in range(0, bricks_y, 2):
            for half in range(halves):
                for i in range(BX):
                    here = (
                        block_x * BX + i,
                        slice(block_y * BY, (block_y + 2) * BY),
                        slice(half * LANES, (half + 1) * LANES),
                    )
                    sums = []
                    for c in range(3):
                        rows = slice((c * BX + i) * BY, (c * BX + i + 1) * BY)
                        places = [
                            (block_x * bricks_y + block_y + k) * halves + half for k in range(2)
                        ]
                        sums.append(
                            jnp.concatenate(
                                [add_all([t[place, rows, :] for t in tables]) for place in places]
                            )
                        )
                    scale = 1.0 / (sums[0] + 1.0)
                    visc_out[here] = jnp.exp((sums[1] + jnp.log(visc[here])) * scale)
                    dens_out[here] = (sums[2] + dens[here]) * scale
        for send in sends(block_x):
            send.start()
        return carry

    def drain(block_x, carry):
        for send in sends(block_x):
            send.wait()
        return carry

    lax.fori_loop(0, size_x // BX, finish, 0)
    lax.fori_loop(0, size_x // BX, drain, 0)


def settle(asked, moments, cell_visc, cell_dens):
    size_x, size_y, size_z = cell_visc.shape
    places = (size_x // BX) * (size_y // BY) * (size_z // LANES)
    shape = jax.ShapeDtypeStruct(cell_visc.shape, f32)
    return pl.pallas_call(
        settle_body,
        out_shape=(shape, shape),
        in_specs=[pl.BlockSpec(memory_space=pltpu.SMEM)]
        + [pl.BlockSpec(memory_space=pl.ANY)] * 3,
        out_specs=(pl.BlockSpec(memory_space=pl.ANY),) * 2,
        scratch_shapes=[
            pltpu.VMEM(moments.shape, f32),
            pltpu.VMEM(cell_visc.shape, f32),
            pltpu.VMEM(cell_visc.shape, f32),
            pltpu.VMEM(cell_visc.shape, f32),
            pltpu.VMEM(cell_visc.shape, f32),
            pltpu.SemaphoreType.DMA((3,)),
            pltpu.SemaphoreType.DMA((2, size_x // BX)),
        ]
        + [pltpu.VMEM((places, ROWS, LANES), f32)],
        compiler_params=vmem_limit(24),
        cost_estimate=cost(7),
        name="settle",
    )(asked, *in_hbm(moments, cell_visc, cell_dens))


def field_of(fields, index):
    return fields[0].at[index] if index < 3 else fields[index - 2]


def pack_x_body(*refs):
    ends, outs = refs[:8], refs[8:]
    for side in range(2):
        for f in range(6):
            outs[side][f] = field_of(ends[side::2], f)[...]


def pack_x(velocity, pressure, cell_visc, cell_dens):
    size_x, size_y, size_z = cell_visc.shape
    width = SWEEPS
    ends = (0, size_x // width - 1)
    vel = [
        pl.BlockSpec((3, width, size_y, size_z), lambda i, e=e: (0, e, 0, 0)) for e in ends
    ]
    block = [pl.BlockSpec((width, size_y, size_z), lambda i, e=e: (e, 0, 0)) for e in ends]
    whole = pl.BlockSpec((6, width, size_y, size_z), lambda i: (0, 0, 0, 0))
    shape = jax.ShapeDtypeStruct((6, width, size_y, size_z), f32)
    return pl.pallas_call(
        pack_x_body,
        grid=(1,),
        out_shape=(shape, shape),
        in_specs=vel + block * 3,
        out_specs=(whole, whole),
        compiler_params=vmem_limit(60),
        cost_estimate=cost(2),
        name="pack_x",
    )(velocity, velocity, pressure, pressure, cell_visc, cell_visc, cell_dens, cell_dens)


def corner_rows(upward, size_x):
    width = SWEEPS
    spare = (5 * width,) if upward else (4 * width - 1, 6 * width - 1)
    places = [(plane, row) for plane in range(size_x) for row in spare]
    found = []
    for field in range(6):
        for side in range(2):
            near = field == 5 or (field == 3 and side == 1 and not upward)
            reach = width - 1 if near else width
            for far_x in range(1, width):
                for far_y in range(1, reach - far_x + 1):
                    found.append((field, side, far_x, far_y))
    more = max(0, len(found) - len(places))
    places += [(size_x + n // (6 * width), n % (6 * width)) for n in range(more)]
    return [cell + at for cell, at in zip(found, places)], size_x + -(-more // (6 * width))


def pack_y_body(size_x, vel, pres, visc, dens, low_x, high_x, upward, downward):
    step_x, size_y, _ = pres.shape
    width = SWEEPS
    step = pl.program_id(0)
    planes = pl.ds(pl.multiple_of(step * step_x, step_x), step_x)
    for f in range(6):
        field = field_of((vel, pres, visc, dens), f)
        rows = slice(f * width, (f + 1) * width)
        upward[planes, rows, :] = field[:, size_y - width :, :]
        downward[planes, rows, :] = field[:, :width, :]

    @pl.when(step == pl.num_programs(0) - 1)
    def _():
        for up, face in ((True, upward), (False, downward)):
            for f, side, far_x, far_y, plane, row in corner_rows(up, size_x)[0]:
                halo, at = (high_x, far_x - 1) if side else (low_x, width - far_x)
                face[plane, row] = halo[f, at, size_y - far_y if up else far_y - 1]


def pack_y(velocity, pressure, cell_visc, cell_dens, low_x, high_x):
    size_x, size_y, size_z = cell_visc.shape
    step = 8
    block = pl.BlockSpec((step, size_y, size_z), lambda i: (i, 0, 0))
    halo = pl.BlockSpec(low_x.shape, lambda i: (0, 0, 0, 0))
    shapes = [(corner_rows(up, size_x)[1], 6 * SWEEPS, size_z) for up in (True, False)]
    return pl.pallas_call(
        functools.partial(pack_y_body, size_x),
        grid=(size_x // step,),
        out_shape=tuple(jax.ShapeDtypeStruct(shape, f32) for shape in shapes),
        in_specs=[
            pl.BlockSpec((3, step, size_y, size_z), lambda i: (0, i, 0, 0)),
            block,
            block,
            block,
            halo,
            halo,
        ],
        out_specs=tuple(pl.BlockSpec(shape, lambda i: (0, 0, 0)) for shape in shapes),
        compiler_params=vmem_limit(24),
        cost_estimate=cost(15),
        name="pack_y",
    )(*in_hbm(velocity, pressure, cell_visc, cell_dens), low_x, high_x)


def place(per, x, y, rows):
    return x % per, pl.ds(y * SUBLANES + x // per, rows, stride=SUBLANES)


def put(target, x, y, rows, value):
    per, halves = target.shape[:2]
    plane, lines = place(per, x, y, rows)
    for half in range(halves):
        target[plane, half, lines, :] = value[:, half * LANES : (half + 1) * LANES]


def tile(y):
    if isinstance(y, int):
        return pl.ds(y * SUBLANES, SUBLANES)
    return pl.ds(pl.multiple_of(y * SUBLANES, SUBLANES), SUBLANES)


def row_work(cells, coefs, relax, forcing, rate):
    per, halves = cells.shape[1:3]
    lane = lax.broadcasted_iota(jnp.int32, (SUBLANES, LANES), 1)
    at_first, at_last = lane == 0, lane == LANES - 1

    def take(field, plane, y):
        return jnp.concatenate([field[plane, half, tile(y), :] for half in range(halves)], axis=1)

    def store(field, plane, y, value):
        for half in range(halves):
            field[plane, half, tile(y), :] = value[:, half * LANES : (half + 1) * LANES]

    def up_x(field, plane, y):
        if plane < per - 1:
            return take(field, plane + 1, y)
        return pltpu.roll(take(field, 0, y), SUBLANES - 1, 0)

    def down_x(field, plane, y):
        if plane > 0:
            return take(field, plane - 1, y)
        return pltpu.roll(take(field, per - 1, y), 1, 0)

    def rolled(a, shift):
        return [
            pltpu.roll(a[:, half * LANES : (half + 1) * LANES], shift, 1) for half in range(halves)
        ]

    def up_z(a):
        parts = rolled(a, LANES - 1)
        after = parts[1:] + [jnp.zeros_like(parts[0])]
        return jnp.concatenate([jnp.where(at_last, n, p) for p, n in zip(parts, after)], axis=1)

    def down_z(a):
        parts = rolled(a, 1)
        before = [jnp.zeros_like(parts[0])] + parts[:-1]
        return jnp.concatenate([jnp.where(at_first, b, p) for p, b in zip(parts, before)], axis=1)

    def prepare(y):
        visc, dens = cells.at[0], cells.at[1]
        for plane in range(per):
            here = take(visc, plane, y)
            near = [
                up_x(visc, plane, y),
                down_x(visc, plane, y),
                take(visc, plane, y + 1),
                take(visc, plane, y - 1),
                up_z(here),
                down_z(here),
            ]
            links = [here + other for other in near]
            scale = jnp.where(here > 0.0, RELAX / add_all(links), 0.0)
            for n in range(6):
                coefs[n, plane, tile(y), :] = links[n] * scale
            relax[plane, tile(y), :] = 2.0 * scale
            forcing[plane, tile(y), :] = take(dens, plane, y) * (-2.0 * GRAVITY * scale)
            rate[plane, tile(y), :] = PRESSURE_RATE * here

    def sweep(y, old, new):
        for plane in range(per):
            links = [coefs[n, plane, tile(y), :] for n in range(6)]
            scale = relax[plane, tile(y), :]
            pressure = take(old.at[3], plane, y)
            before = (
                down_x(old.at[3], plane, y),
                take(old.at[3], plane, y - 1),
                down_z(pressure),
            )
            changes = []
            for c in range(3):
                field = old.at[c]
                here = take(field, plane, y)
                near = [
                    up_x(field, plane, y),
                    down_x(field, plane, y),
                    take(field, plane, y + 1),
                    take(field, plane, y - 1),
                    up_z(here),
                    down_z(here),
                ]
                terms = [link * other for link, other in zip(links, near)]
                total = (terms[0] + terms[1]) + (terms[2] + terms[3])
                total = total + (terms[4] + terms[5])
                rest = (1.0 - RELAX) * here - scale * (pressure - before[c])
                if c == 2:
                    rest = rest + forcing[plane, tile(y), :]
                changes.append(near[2 * c] - here)
                store(new.at[c], plane, y, total + rest)
            pressed = pressure - rate[plane, tile(y), :] * add_all(changes)
            store(new.at[3], plane, y, pressed)

    return prepare, sweep


def kept_rows(size_y):
    width = SWEEPS
    return (
        ((width, size_y),),
        ((width + 1, width), (size_y - 1, width)),
        ((width, width + 1), (size_y - 1, width + 1)),
    )


def kept_copies(pairs, size_y, done):
    copies = []
    for (source, target), strips in zip(pairs, kept_rows(size_y)):
        for begin, rows in strips:
            span = (slice(None),) * 3 + (pl.ds(begin * SUBLANES, rows * SUBLANES),)
            copies.append(
                pltpu.make_async_copy(source.at[span], target.at[span], done.at[len(copies)])
            )
    return copies


def inner_body(vel, pres, visc, dens, low_x, high_x, _, even_out, odd_out, cells_out, *work):
    blocks, sides_x, even, odd, cells, coefs, relax, forcing, rate, done, more = work
    size_x, size_y, size_z = blocks.shape[1:]
    width = SWEEPS
    inputs = (
        (visc, blocks.at[4]),
        (dens, blocks.at[5]),
        (low_x, sides_x.at[0]),
        (high_x, sides_x.at[1]),
        (vel, blocks.at[0:3]),
        (pres, blocks.at[3]),
    )
    copies = [
        pltpu.make_async_copy(there, here, done.at[n]) for n, (there, here) in enumerate(inputs)
    ]
    for copy in copies:
        copy.start()
    targets = [even.at[n] for n in range(4)] + [cells.at[n] for n in range(2)]

    def lay_out(f):
        for i in range(size_x):
            for y in range(0, size_y, SUBLANES):
                value = blocks[f, i, y : y + SUBLANES, :]
                put(targets[f], i + width, y + width, SUBLANES, value)
        for side, begin in enumerate((0, width + size_x)):
            for i in range(width):
                for y in range(0, size_y, SUBLANES):
                    value = sides_x[side, f, i, y : y + SUBLANES, :]
                    put(targets[f], begin + i, y + width, SUBLANES, value)

    for copy in copies[:4]:
        copy.wait()
    lay_out(4)
    lay_out(5)
    sends = kept_copies(((even, even_out), (odd, odd_out), (cells, cells_out)), size_y, more)
    for send in sends[3:]:
        send.start()

    prepare, sweep = row_work(cells, coefs, relax, forcing, rate)

    def prepare_row(y, carry):
        prepare(y)
        return carry

    first, last = width + 1, width + size_y - 1
    lax.fori_loop(first, last, prepare_row, 0, unroll=2)
    for copy in copies[4:]:
        copy.wait()
    for f in range(4):
        lay_out(f)
    early, late = (sends[1:3], sends[:1]) if SWEEPS % 2 == 0 else (sends[:1], sends[1:3])
    for step in range(SWEEPS):
        old, new = (odd, even) if step % 2 else (even, odd)
        if step == SWEEPS - 1:
            for send in early:
                send.start()

        def sweep_row(y, carry, old=old, new=new):
            sweep(y, old, new)
            return carry

        lax.fori_loop(first + step, last - step, sweep_row, 0, unroll=2)
    for send in late:
        send.start()
    for send in sends:
        send.wait()


def inner_sweeps(velocity, pressure, cell_visc, cell_dens, low_x, high_x, after):
    size_x, size_y, size_z = cell_visc.shape
    width = low_x.shape[1]
    per, rows = (size_x + 2 * width) // SUBLANES, (size_y + 2 * width) * SUBLANES
    block, cut = (per, rows, size_z), (per, size_z // LANES, rows, LANES)
    shapes = [(4,) + cut, (4,) + cut, (2,) + cut]
    anywhere = pl.BlockSpec(memory_space=pl.ANY)
    return pl.pallas_call(
        inner_body,
        out_shape=tuple(jax.ShapeDtypeStruct(shape, f32) for shape in shapes),
        in_specs=[anywhere] * 7,
        out_specs=(anywhere,) * 3,
        scratch_shapes=[
            pltpu.VMEM((6,) + cell_visc.shape, f32),
            pltpu.VMEM((2,) + low_x.shape, f32),
        ]
        + [pltpu.VMEM(shape, f32) for shape in shapes]
        + [
            pltpu.VMEM((6,) + block, f32),
            pltpu.VMEM(block, f32),
            pltpu.VMEM(block, f32),
            pltpu.VMEM(block, f32),
            pltpu.SemaphoreType.DMA((6,)),
            pltpu.SemaphoreType.DMA((5,)),
        ],
        compiler_params=vmem_limit(40),
        cost_estimate=cost(25),
        name="inner_sweeps",
    )(*in_hbm(velocity, pressure, cell_visc, cell_dens, low_x, high_x), after)


def edge_body(even_in, odd_in, cells_in, low_y, high_y, vel_out, pres_out, *work):
    from_low, from_high, results, even, odd, cells, coefs, relax, forcing, rate, done, more = work
    size_x, size_y, size_z = results.shape[1:]
    width = SWEEPS
    long_y = size_y + 2 * width
    halos = [
        pltpu.make_async_copy(low_y, from_low, more.at[0]),
        pltpu.make_async_copy(high_y, from_high, more.at[1]),
    ]
    kept = kept_copies(((even_in, even), (odd_in, odd), (cells_in, cells)), size_y, done)
    for copy in (*halos, *kept[3:], *kept[:3]):
        copy.start()
    targets = [even.at[n] for n in range(4)] + [cells.at[n] for n in range(2)]

    def lay_out(chosen):
        for f in chosen:
            for x in (*range(width), *range(width + size_x, size_x + 2 * width)):
                for y in (0, width + size_y):
                    put(targets[f], x, y, width, jnp.zeros((width, size_z), f32))
            rows = slice(f * width, (f + 1) * width)
            for halo, begin in ((from_low, 0), (from_high, width + size_y)):
                for i in range(size_x):
                    put(targets[f], i + width, begin, width, halo[i, rows, :])
        for up, halo in ((True, from_low), (False, from_high)):
            for f, side, far_x, far_y, plane, row in corner_rows(up, size_x)[0]:
                if f in chosen:
                    x = width + size_x - 1 + far_x if side else width - far_x
                    y = width - far_y if up else width + size_y - 1 + far_y
                    put(targets[f], x, y, 1, halo[plane, row : row + 1, :])

    for copy in halos:
        copy.wait()
    lay_out((4, 5))
    for copy in kept[3:]:
        copy.wait()

    prepare, sweep = row_work(cells, coefs, relax, forcing, rate)

    def prepare_rows(n, carry):
        prepare(1 + n)
        prepare(long_y - 2 * width + n)
        return carry

    lax.fori_loop(0, 2 * width - 1, prepare_rows, 0)
    lay_out((0, 1, 2, 3))
    for copy in kept[:3]:
        copy.wait()
    for step in range(SWEEPS):
        old, new = (odd, even) if step % 2 else (even, odd)

        def sweep_rows(n, carry, old=old, new=new, step=step):
            sweep(1 + step + n, old, new)
            sweep(width + size_y - 1 - step + n, old, new)
            return carry

        lax.fori_loop(0, width, sweep_rows, 0, unroll=2)

    final = odd if SWEEPS % 2 else even
    outs = [vel_out.at[0], vel_out.at[1], vel_out.at[2], pres_out]
    sends = [pltpu.make_async_copy(results.at[n], out, done.at[n]) for n, out in enumerate(outs)]
    per, halves = even.shape[1:3]
    for field, send in enumerate(sends):
        for i in range(size_x):
            for y in range(0, size_y, SUBLANES):
                plane, lines = place(per, i + width, y + width, SUBLANES)
                for half in range(halves):
                    columns = slice(half * LANES, (half + 1) * LANES)
                    results[field, i, y : y + SUBLANES, columns] = final[
                        field, plane, half, lines, :
                    ]
        send.start()
    for send in sends:
        send.wait()


def edge_sweeps(even, odd, cells, low_y, high_y, size_x, size_y):
    per, halves, rows = even.shape[1:4]
    size_z = halves * LANES
    block = (per, rows, size_z)
    anywhere = pl.BlockSpec(memory_space=pl.ANY)
    return pl.pallas_call(
        edge_body,
        out_shape=(
            jax.ShapeDtypeStruct((3, size_x, size_y, size_z), f32),
            jax.ShapeDtypeStruct((size_x, size_y, size_z), f32),
        ),
        in_specs=[anywhere] * 5,
        out_specs=(anywhere,) * 2,
        scratch_shapes=[
            pltpu.VMEM(low_y.shape, f32),
            pltpu.VMEM(high_y.shape, f32),
            pltpu.VMEM((4, size_x, size_y, size_z), f32),
            pltpu.VMEM(even.shape, f32),
            pltpu.VMEM(odd.shape, f32),
            pltpu.VMEM(cells.shape, f32),
            pltpu.VMEM((6,) + block, f32),
            pltpu.VMEM(block, f32),
            pltpu.VMEM(block, f32),
            pltpu.VMEM(block, f32),
            pltpu.SemaphoreType.DMA((5,)),
            pltpu.SemaphoreType.DMA((2,)),
        ],
        compiler_params=vmem_limit(40),
        cost_estimate=cost(1),
        name="edge_sweeps",
    )(even, odd, cells, low_y, high_y)


def shift(value, axis, step):
    size = lax.axis_size(axis)
    pairs = [(i, i + step) for i in range(size) if 0 <= i + step < size]
    return lax.ppermute(value, axis, pairs)


def per_device(
    velocity,
    pressure,
    cell_visc,
    cell_dens,
    block_brick,
    block_counts,
    positions,
    start_visc,
    marker_dens,
):
    asked = lax.all_to_all(block_brick, "mark", 0, 0, tiled=True)
    fields = (velocity, pressure, cell_visc, cell_dens)
    to_low, to_high = pack_x(*fields)
    low_x, high_x = shift(to_high, "grid", 1), shift(to_low, "grid", -1)
    upward, downward = pack_y(*fields, low_x, high_x)
    low_y, high_y = shift(upward, "mark", 1), shift(downward, "mark", -1)

    picked = pick_bricks(asked, velocity)
    bricks = lax.all_to_all(picked, "mark", 0, 0, tiled=True)
    marker_visc, moments = marker_work(
        block_counts, positions, start_visc, marker_dens, bricks, upward
    )
    gathered = lax.all_to_all(moments, "mark", 0, 0, tiled=True)
    state = inner_sweeps(*fields, low_x, high_x, moments)
    velocity_next, pressure_next = edge_sweeps(*state, low_y, high_y, *pressure.shape[:2])
    visc_next, dens_next = settle(asked, gathered, cell_visc, cell_dens)
    return velocity_next, pressure_next, visc_next, dens_next, marker_visc


def solution(mesh):
    in_specs = (
        P(None, "grid", "mark", None),
        P("grid", "mark", None),
        P("grid", "mark", None),
        P("grid", "mark", None),
        P(("grid", "mark"), None),
        P(("grid", "mark"), None),
        P(("grid", "mark"), None, None, None),
        P(("grid", "mark"), None, None),
        P(("grid", "mark"), None, None),
    )
    out_specs = (
        P(None, "grid", "mark", None),
        P("grid", "mark", None),
        P("grid", "mark", None),
        P("grid", "mark", None),
        P(("grid", "mark"), None, None),
    )
    return jax.shard_map(
        per_device, mesh=mesh, in_specs=in_specs, out_specs=out_specs, check_vma=False
    )
```

```python
import functools

import jax
import jax.numpy as jnp
import numpy as np
from jax import lax
from jax.experimental import pallas as pl
from jax.experimental.pallas import tpu as pltpu
from jax.sharding import PartitionSpec as P

SWEEPS = 4
RELAX = 0.6
PRESSURE_RATE = 0.25
GRAVITY = 1.0
STRAIN_SCALE = 0.5

BX, BY, BZ = 4, 4, 8
PLANE = BX * BY
ROWS = 3 * PLANE
LANES = 128
GROUP = LANES // BZ
HALF = 8
SUBLANES = 8

f32, bf16 = jnp.float32, jnp.bfloat16


def vmem_limit(mib):
    return pltpu.CompilerParams(vmem_limit_bytes=mib * 1024 * 1024)


def in_hbm(*arrays):
    return [pltpu.with_memory_space_constraint(array, pltpu.HBM) for array in arrays]


def cost(microseconds):
    return pl.CostEstimate(
        flops=int(microseconds * 1.15e9), bytes_accessed=0, transcendentals=0
    )


def place_of(brick):
    return lax.shift_right_logical(brick, GROUP.bit_length() - 1), (brick & (GROUP - 1)) * BZ


def pick_body(asked, vel, far, out, table, sent):
    size_x, size_y, size_z = vel.shape[1:]
    bricks_y, halves = size_y // BY, size_z // LANES

    def repack(block_x, carry):
        for block_y in range(bricks_y):
            for half in range(halves):
                place = (block_x * bricks_y + block_y) * halves + half
                for c in range(3):
                    for i in range(BX):
                        row = (c * BX + i) * BY
                        table[place, row : row + BY, :] = vel[
                            c,
                            block_x * BX + i,
                            block_y * BY : (block_y + 1) * BY,
                            half * LANES : (half + 1) * LANES,
                        ]
        return carry

    lax.fori_loop(0, size_x // BX, repack, 0)
    groups = out.shape[1]
    lane_slot = lax.broadcasted_iota(jnp.int32, (ROWS, LANES), 1) // BZ

    def one_group(device, group):
        packed = jnp.zeros((ROWS, LANES), f32)
        for slot in range(GROUP):
            place, lane = place_of(asked[device, group * GROUP + slot])
            rolled = pltpu.roll(table[place], (BZ * slot - lane) & (LANES - 1), 1)
            packed = jnp.where(lane_slot == slot, rolled, packed)
        out[device, group] = packed

    def send(device):
        return pltpu.make_async_copy(out.at[device], far.at[device], sent.at[device])

    def one_device(device, carry):
        def each(group, inner):
            one_group(device, group)
            return inner

        lax.fori_loop(0, groups, each, 0)
        send(device).start()
        return carry

    def drain(device, carry):
        send(device).wait()
        return carry

    lax.fori_loop(0, out.shape[0], one_device, 0)
    lax.fori_loop(0, out.shape[0], drain, 0)


def pick_bricks(asked, velocity):
    devices, slots = asked.shape
    size_x, size_y, size_z = velocity.shape[1:]
    places = (size_x // BX) * (size_y // BY) * (size_z // LANES)
    return pl.pallas_call(
        pick_body,
        out_shape=jax.ShapeDtypeStruct((devices, slots // GROUP, ROWS, LANES), f32),
        in_specs=[
            pl.BlockSpec(memory_space=pltpu.SMEM),
            pl.BlockSpec(memory_space=pltpu.VMEM),
        ],
        out_specs=pl.BlockSpec(memory_space=pl.ANY),
        scratch_shapes=[
            pltpu.VMEM((devices, slots // GROUP, ROWS, LANES), f32),
            pltpu.VMEM((places, ROWS, LANES), f32),
            pltpu.SemaphoreType.DMA((devices,)),
        ],
        compiler_params=vmem_limit(24),
        cost_estimate=cost(25),
        name="pick_bricks",
    )(asked, velocity)


def permutations():
    inside = BZ * HALF
    spread = np.zeros((2, 2, LANES, 4 * inside), np.float32)
    gather = np.zeros((2 * BY * inside, BY * LANES), np.float32)
    for half in range(2):
        for slot in range(HALF):
            for z in range(BZ):
                outer, inner = (half * HALF + slot) * BZ + z, z * HALF + slot
                for part in range(4):
                    spread[half, part // 2, outer, part * inside + inner] = 1
                for j in range(BY):
                    gather[(half * BY + j) * inside + inner, j * LANES + outer] = 1
    return jnp.asarray(spread, bf16), jnp.asarray(gather, bf16)


def split(value):
    high = value.astype(bf16)
    return high, (value - high.astype(f32)).astype(bf16)


def add_all(values):
    return functools.reduce(jnp.add, values)


def axis_weights(fraction, cells):
    middle = (cells - 1) / 2
    base = jnp.exp(fraction * (2.0 * cells) - float(cells))
    powers = [None, base]
    for i in range(2, cells):
        powers.append(powers[i // 2] * powers[i - i // 2])
    factors = [float(np.exp(middle**2 - (i - middle) ** 2)) for i in range(cells)]
    bells = [None] + [powers[i] * factors[i] for i in range(1, cells)]
    scale = 1.0 / (add_all(bells[1:]) + factors[0])
    weights = [scale * factors[0]] + [bell * scale for bell in bells[1:]]
    mean = add_all(
        [
            (weights[cells - 1 - i] - weights[i]) * (2.0 * (middle - i))
            for i in range(cells // 2)
        ]
    )
    slopes = [w * (2.0 * (i - middle) - mean) for i, w in enumerate(weights)]
    return weights, slopes


def dot(a, b):
    return jnp.dot(a, b, preferred_element_type=f32)


def gradients(products, weights, markers):
    weight_x, slope_x, weight_y, slope_y = ([weights[4 * n + i] for i in range(4)] for n in range(4))
    grads = []
    for c in range(3):
        lines = [[], [], []]
        for i in range(BX):
            rows = [((c * BX + i) * BY + j) * HALF for j in range(BY)]
            still = [products[row : row + HALF, :markers] for row in rows]
            rising = [products[row : row + HALF, markers:] for row in rows]
            lines[0].append(slope_x[i] * add_all([w * t for w, t in zip(weight_y, still)]))
            lines[1].append(weight_x[i] * add_all([w * t for w, t in zip(slope_y, still)]))
            lines[2].append(weight_x[i] * add_all([w * t for w, t in zip(weight_y, rising)]))
        grads.append([add_all(line) for line in lines])
    return grads


def own_lanes():
    shape = (HALF, 4 * BZ * HALF)
    lane = lax.broadcasted_iota(jnp.int32, shape, 1)
    return (lane % HALF == lax.broadcasted_iota(jnp.int32, shape, 0)).astype(f32)


def marker_groups(groups, counts, ins, outs, buffers, sums):
    spread, gather, places, start, dens, brick = ins
    visc_out, moments_out = outs
    permuted, left, right, products, weights, factors, planes_high, planes_low = buffers
    markers = places.shape[-1]
    inside = BZ * HALF
    own = own_lanes()
    halves = [
        (owner, 2 * group + half, half, 2 * n + half)
        for n, (owner, group) in enumerate(groups)
        for half in range(2)
    ]
    parts = [split(brick[owner, group]) for owner, group in groups]
    for _, _, half, n in halves:
        high, low = parts[n // 2]
        permuted[n][...] = dot(high, spread[half, 0]) + dot(low, spread[half, 1])
    heights = []
    for owner, part, _, n in halves:
        weight_z, slope_z = axis_weights(places[owner, 2, part], BZ)
        heights.append(weight_z)
        for z in range(0, BZ, 2):
            for column, values in ((0, weight_z), (1, slope_z)):
                high, low = split(jnp.concatenate(values[z : z + 2], axis=0))
                columns = slice(column * markers, (column + 1) * markers)
                for k in range(4):
                    begin = k * inside + z * HALF
                    right[n][begin : begin + 2 * HALF, columns] = low if k % 2 else high
    for _, _, _, n in halves:
        for row in range(0, ROWS, 2):
            pair = [
                jnp.broadcast_to(permuted[n][r : r + 1, :], own.shape) * own for r in (row, row + 1)
            ]
            left[n][row * HALF : (row + 2) * HALF, :] = jnp.concatenate(pair, axis=0).astype(bf16)
    for _, _, _, n in halves:
        products[n][...] = dot(left[n][...], right[n][...])
    for owner, part, _, n in halves:
        weights_x = axis_weights(places[owner, 0, part], BX)
        weights_y = axis_weights(places[owner, 1, part], BY)
        for k, values in enumerate((*weights_x, *weights_y)):
            for i, value in enumerate(values):
                weights[n][4 * k + i] = value
        for j in range(BY):
            for z in range(0, BZ, 2):
                pair = [weights_y[0][j] * heights[n][z + k] for k in range(2)]
                rows = slice((j * BZ + z) * HALF, (j * BZ + z + 2) * HALF)
                high, low = split(jnp.concatenate(pair, axis=0))
                planes_high[n][rows, :] = high
                planes_low[n][rows, :] = low

    count = 3 * BX * HALF
    for owner, part, _, n in halves:
        grads = gradients(products[n], weights[n], markers)
        normal = grads[0][0] ** 2 + grads[1][1] ** 2 + grads[2][2] ** 2
        shear_xy = 0.5 * (grads[0][1] + grads[1][0])
        shear_xz = 0.5 * (grads[0][2] + grads[2][0])
        shear_yz = 0.5 * (grads[1][2] + grads[2][1])
        invariant = 0.5 * normal + shear_xy**2 + shear_xz**2 + shear_yz**2
        scaled = invariant * (1.0 / (STRAIN_SCALE * STRAIN_SCALE))
        third = jnp.log(1.0 + scaled) * (1.0 / 3.0)
        first = start[owner, part]
        slot = lax.broadcasted_iota(jnp.int32, first.shape, 0) + part * HALF
        live = slot < counts[0, owner]
        visc_out[owner, part] = jnp.where(live, first * jnp.exp(-third), 0.0)
        carried = (
            live.astype(f32),
            jnp.where(live, jnp.log(first) - third, 0.0),
            jnp.where(live, dens[owner, part], 0.0),
        )
        for c in range(3):
            for i in range(0, BX, 2):
                pair = [carried[c] * weights[n][i + k] for k in range(2)]
                row = (c * BX + i) * HALF
                high, low = split(jnp.concatenate(pair, axis=0))
                factors[n][row : row + 2 * HALF, :] = high
                factors[n][count + row : count + row + 2 * HALF, :] = low

    contract = (((1,), (1,)), ((), ()))
    found = []
    for _, _, _, n in halves:
        both = lax.dot_general(
            factors[n][...], planes_high[n][...], contract, preferred_element_type=f32
        )
        rest = lax.dot_general(
            factors[n][:count], planes_low[n][...], contract, preferred_element_type=f32
        )
        found.append((both, rest))
    for _, _, half, n in halves:
        both, rest = found[n]
        total = both[:count] + both[count:] + rest
        chosen = total.reshape(3 * BX, HALF, BY * inside) * own[None]
        high, low = split(jnp.sum(chosen, axis=1))
        columns = slice(half * BY * inside, (half + 1) * BY * inside)
        row = (n // 2) * 32
        sums[row : row + 3 * BX, columns] = high.astype(f32)
        sums[row + 16 : row + 16 + 3 * BX, columns] = low.astype(f32)
    moved = dot(sums[...].astype(bf16), gather[...])
    for n, (owner, group) in enumerate(groups):
        mine = moved[32 * n : 32 * n + 3 * BX] + moved[32 * n + 16 : 32 * n + 16 + 3 * BX]
        for j in range(BY):
            rows = pl.ds(j, 3 * BX, stride=BY)
            moments_out[owner, group, rows, :] = mine[:, j * LANES : (j + 1) * LANES]


TOGETHER = 3


def marker_body(counts, *refs):
    sources, targets, scratch = refs[:6], refs[7:9], refs[9:]
    ins, outs, (got, sent, listed, sums, *flat) = scratch[:6], scratch[6:8], scratch[8:]
    fetches = [
        pltpu.make_async_copy(there, here, got.at[n])
        for n, (there, here) in enumerate(zip(sources, ins))
    ]
    for fetch in fetches:
        fetch.start()
    held = 2 * TOGETHER
    buffers = [flat[n * held : (n + 1) * held] for n in range(len(flat) // held)]
    visc_out, moments_out = outs
    owners, groups = moments_out.shape[:2]
    visc_out[...] = jnp.zeros_like(visc_out)
    moments_out[...] = jnp.zeros_like(moments_out)
    sums[...] = jnp.zeros_like(sums)

    def list_groups(index, number):
        owner, group = index // groups, index % groups
        live = group * GROUP < counts[0, owner]

        @pl.when(live)
        def _():
            for n in range(TOGETHER):
                listed[2 * (number + n)] = owner
                listed[2 * (number + n) + 1] = group

        return jnp.where(live, number + 1, number)

    number = lax.fori_loop(0, owners * groups, list_groups, 0)

    def step(index, carry):
        first = TOGETHER * index
        taken = [
            (listed[2 * (first + n)], listed[2 * (first + n) + 1]) for n in range(TOGETHER)
        ]
        marker_groups(taken, counts, ins, outs, buffers, sums)
        return carry

    for fetch in fetches:
        fetch.wait()
    lax.fori_loop(0, (number + TOGETHER - 1) // TOGETHER, step, 0)
    sends = [
        pltpu.make_async_copy(here, there, sent.at[n])
        for n, (here, there) in enumerate(zip(outs, targets))
    ]
    for send in sends:
        send.start()
    for send in sends:
        send.wait()


def marker_work(counts, positions, start_visc, marker_dens, bricks, after):
    owners, _, slots, markers = positions.shape
    groups, parts = slots // GROUP, slots // HALF
    spread, gather = permutations()
    width = 4 * BZ * HALF
    anywhere = pl.BlockSpec(memory_space=pl.ANY)
    fetched = (
        spread,
        gather,
        positions.reshape(owners, 3, parts, HALF, markers),
        start_visc.reshape(owners, parts, HALF, markers),
        marker_dens.reshape(owners, parts, HALF, markers),
        bricks,
    )
    shapes = ((owners, parts, HALF, markers), (owners, groups, ROWS, LANES))
    buffers = (
        pltpu.VMEM((ROWS, width), f32),
        pltpu.VMEM((ROWS * HALF, width), bf16),
        pltpu.VMEM((width, 2 * markers), bf16),
        pltpu.VMEM((ROWS * HALF, 2 * markers), f32),
        pltpu.VMEM((4 * 4, HALF, markers), f32),
        pltpu.VMEM((2 * 3 * BX * HALF, markers), bf16),
        pltpu.VMEM((BY * BZ * HALF, markers), bf16),
        pltpu.VMEM((BY * BZ * HALF, markers), bf16),
    )
    visc, moments = pl.pallas_call(
        marker_body,
        out_shape=tuple(jax.ShapeDtypeStruct(shape, f32) for shape in shapes),
        in_specs=[pl.BlockSpec(memory_space=pltpu.SMEM)] + [anywhere] * 7,
        out_specs=(anywhere, anywhere),
        scratch_shapes=[pltpu.VMEM(array.shape, array.dtype) for array in fetched]
        + [pltpu.VMEM(shape, f32) for shape in shapes]
        + [
            pltpu.SemaphoreType.DMA((len(fetched),)),
            pltpu.SemaphoreType.DMA((len(shapes),)),
            pltpu.SMEM((2 * (owners * groups + TOGETHER),), jnp.int32),
            pltpu.VMEM((32 * TOGETHER, 2 * BY * BZ * HALF), f32),
        ]
        + [buffer for buffer in buffers for _ in range(2 * TOGETHER)],
        compiler_params=vmem_limit(40),
        cost_estimate=cost(25),
        name="marker_work",
    )(counts, *in_hbm(*fetched), after)
    return visc.reshape(owners, slots, markers), moments


def settle_body(asked, moments_in, visc_in, dens_in, visc_far, dens_far, *scratch):
    moments, visc, dens, visc_out, dens_out, done, sent, *tables = scratch
    size_x, size_y, size_z = visc.shape
    copies = [
        pltpu.make_async_copy(there, here, done.at[n])
        for n, (there, here) in enumerate(
            ((moments_in, moments), (visc_in, visc), (dens_in, dens))
        )
    ]
    for copy in copies:
        copy.start()
    bricks_y, halves = size_y // BY, size_z // LANES
    for table in tables:
        table[...] = jnp.zeros_like(table)
    copies[0].wait()
    groups = moments.shape[1]
    lane_slot = lax.broadcasted_iota(jnp.int32, (ROWS, LANES), 1) // BZ

    def one_group(step, carry):
        device, group = step // groups, step % groups
        packed = moments[device, group]
        for slot in range(GROUP):
            table = tables[slot % len(tables)]
            place, lane = place_of(asked[device, group * GROUP + slot])
            piece = jnp.where(lane_slot == slot, packed, 0.0)
            piece = pltpu.roll(piece, (lane - BZ * slot) & (LANES - 1), 1)
            table[place] = table[place] + piece
        return carry

    lax.fori_loop(0, moments.shape[0] * groups, one_group, 0)
    copies[1].wait()
    copies[2].wait()

    def sends(block_x):
        planes = pl.ds(block_x * BX, BX)
        return [
            pltpu.make_async_copy(here.at[planes], there.at[planes], sent.at[n, block_x])
            for n, (here, there) in enumerate(((visc_out, visc_far), (dens_out, dens_far)))
        ]

    def finish(block_x, carry):
        for block_y in range(0, bricks_y, 2):
            for half in range(halves):
                for i in range(BX):
                    here = (
                        block_x * BX + i,
                        slice(block_y * BY, (block_y + 2) * BY),
                        slice(half * LANES, (half + 1) * LANES),
                    )
                    sums = []
                    for c in range(3):
                        rows = slice((c * BX + i) * BY, (c * BX + i + 1) * BY)
                        places = [
                            (block_x * bricks_y + block_y + k) * halves + half for k in range(2)
                        ]
                        sums.append(
                            jnp.concatenate(
                                [add_all([t[place, rows, :] for t in tables]) for place in places]
                            )
                        )
                    scale = 1.0 / (sums[0] + 1.0)
                    visc_out[here] = jnp.exp((sums[1] + jnp.log(visc[here])) * scale)
                    dens_out[here] = (sums[2] + dens[here]) * scale
        for send in sends(block_x):
            send.start()
        return carry

    def drain(block_x, carry):
        for send in sends(block_x):
            send.wait()
        return carry

    lax.fori_loop(0, size_x // BX, finish, 0)
    lax.fori_loop(0, size_x // BX, drain, 0)


def settle(asked, moments, cell_visc, cell_dens):
    size_x, size_y, size_z = cell_visc.shape
    places = (size_x // BX) * (size_y // BY) * (size_z // LANES)
    shape = jax.ShapeDtypeStruct(cell_visc.shape, f32)
    return pl.pallas_call(
        settle_body,
        out_shape=(shape, shape),
        in_specs=[pl.BlockSpec(memory_space=pltpu.SMEM)]
        + [pl.BlockSpec(memory_space=pl.ANY)] * 3,
        out_specs=(pl.BlockSpec(memory_space=pl.ANY),) * 2,
        scratch_shapes=[
            pltpu.VMEM(moments.shape, f32),
            pltpu.VMEM(cell_visc.shape, f32),
            pltpu.VMEM(cell_visc.shape, f32),
            pltpu.VMEM(cell_visc.shape, f32),
            pltpu.VMEM(cell_visc.shape, f32),
            pltpu.SemaphoreType.DMA((3,)),
            pltpu.SemaphoreType.DMA((2, size_x // BX)),
        ]
        + [pltpu.VMEM((places, ROWS, LANES), f32)],
        compiler_params=vmem_limit(24),
        cost_estimate=cost(7),
        name="settle",
    )(asked, *in_hbm(moments, cell_visc, cell_dens))


def field_of(fields, index):
    return fields[0].at[index] if index < 3 else fields[index - 2]


def pack_x_body(*refs):
    ends, outs = refs[:8], refs[8:]
    for side in range(2):
        for f in range(6):
            outs[side][f] = field_of(ends[side::2], f)[...]


def pack_x(velocity, pressure, cell_visc, cell_dens):
    size_x, size_y, size_z = cell_visc.shape
    width = SWEEPS
    ends = (0, size_x // width - 1)
    vel = [
        pl.BlockSpec((3, width, size_y, size_z), lambda i, e=e: (0, e, 0, 0)) for e in ends
    ]
    block = [pl.BlockSpec((width, size_y, size_z), lambda i, e=e: (e, 0, 0)) for e in ends]
    whole = pl.BlockSpec((6, width, size_y, size_z), lambda i: (0, 0, 0, 0))
    shape = jax.ShapeDtypeStruct((6, width, size_y, size_z), f32)
    return pl.pallas_call(
        pack_x_body,
        grid=(1,),
        out_shape=(shape, shape),
        in_specs=vel + block * 3,
        out_specs=(whole, whole),
        compiler_params=vmem_limit(60),
        cost_estimate=cost(2),
        name="pack_x",
    )(velocity, velocity, pressure, pressure, cell_visc, cell_visc, cell_dens, cell_dens)


def corner_rows(upward, size_x):
    width = SWEEPS
    spare = (5 * width,) if upward else (4 * width - 1, 6 * width - 1)
    places = [(plane, row) for plane in range(size_x) for row in spare]
    found = []
    for field in range(6):
        for side in range(2):
            near = field == 5 or (field == 3 and side == 1 and not upward)
            reach = width - 1 if near else width
            for far_x in range(1, width):
                for far_y in range(1, reach - far_x + 1):
                    found.append((field, side, far_x, far_y))
    more = max(0, len(found) - len(places))
    places += [(size_x + n // (6 * width), n % (6 * width)) for n in range(more)]
    return [cell + at for cell, at in zip(found, places)], size_x + -(-more // (6 * width))


def pack_y_body(size_x, vel, pres, visc, dens, low_x, high_x, upward, downward):
    step_x, size_y, _ = pres.shape
    width = SWEEPS
    step = pl.program_id(0)
    planes = pl.ds(pl.multiple_of(step * step_x, step_x), step_x)
    for f in range(6):
        field = field_of((vel, pres, visc, dens), f)
        rows = slice(f * width, (f + 1) * width)
        upward[planes, rows, :] = field[:, size_y - width :, :]
        downward[planes, rows, :] = field[:, :width, :]

    @pl.when(step == pl.num_programs(0) - 1)
    def _():
        for up, face in ((True, upward), (False, downward)):
            for f, side, far_x, far_y, plane, row in corner_rows(up, size_x)[0]:
                halo, at = (high_x, far_x - 1) if side else (low_x, width - far_x)
                face[plane, row] = halo[f, at, size_y - far_y if up else far_y - 1]


def pack_y(velocity, pressure, cell_visc, cell_dens, low_x, high_x):
    size_x, size_y, size_z = cell_visc.shape
    step = 16
    block = pl.BlockSpec((step, size_y, size_z), lambda i: (i, 0, 0))
    halo = pl.BlockSpec(low_x.shape, lambda i: (0, 0, 0, 0))
    shapes = [(corner_rows(up, size_x)[1], 6 * SWEEPS, size_z) for up in (True, False)]
    return pl.pallas_call(
        functools.partial(pack_y_body, size_x),
        grid=(size_x // step,),
        out_shape=tuple(jax.ShapeDtypeStruct(shape, f32) for shape in shapes),
        in_specs=[
            pl.BlockSpec((3, step, size_y, size_z), lambda i: (0, i, 0, 0)),
            block,
            block,
            block,
            halo,
            halo,
        ],
        out_specs=tuple(pl.BlockSpec(shape, lambda i: (0, 0, 0)) for shape in shapes),
        compiler_params=vmem_limit(24),
        cost_estimate=cost(15),
        name="pack_y",
    )(*in_hbm(velocity, pressure, cell_visc, cell_dens), low_x, high_x)


def place(per, x, y, rows):
    return x % per, pl.ds(y * SUBLANES + x // per, rows, stride=SUBLANES)


def put(target, x, y, rows, value):
    per, halves = target.shape[:2]
    plane, lines = place(per, x, y, rows)
    for half in range(halves):
        target[plane, half, lines, :] = value[:, half * LANES : (half + 1) * LANES]


def tile(y):
    if isinstance(y, int):
        return pl.ds(y * SUBLANES, SUBLANES)
    return pl.ds(pl.multiple_of(y * SUBLANES, SUBLANES), SUBLANES)


def row_work(cells, coefs, relax, forcing, rate):
    per, halves = cells.shape[1:3]
    lane = lax.broadcasted_iota(jnp.int32, (SUBLANES, LANES), 1)
    at_first, at_last = lane == 0, lane == LANES - 1

    def take(field, plane, y):
        return jnp.concatenate([field[plane, half, tile(y), :] for half in range(halves)], axis=1)

    def store(field, plane, y, value):
        for half in range(halves):
            field[plane, half, tile(y), :] = value[:, half * LANES : (half + 1) * LANES]

    def up_x(field, plane, y):
        if plane < per - 1:
            return take(field, plane + 1, y)
        return pltpu.roll(take(field, 0, y), SUBLANES - 1, 0)

    def down_x(field, plane, y):
        if plane > 0:
            return take(field, plane - 1, y)
        return pltpu.roll(take(field, per - 1, y), 1, 0)

    def rolled(a, shift):
        return [
            pltpu.roll(a[:, half * LANES : (half + 1) * LANES], shift, 1) for half in range(halves)
        ]

    def up_z(a):
        parts = rolled(a, LANES - 1)
        after = parts[1:] + [jnp.zeros_like(parts[0])]
        return jnp.concatenate([jnp.where(at_last, n, p) for p, n in zip(parts, after)], axis=1)

    def down_z(a):
        parts = rolled(a, 1)
        before = [jnp.zeros_like(parts[0])] + parts[:-1]
        return jnp.concatenate([jnp.where(at_first, b, p) for p, b in zip(parts, before)], axis=1)

    def prepare(y):
        visc, dens = cells.at[0], cells.at[1]
        for plane in range(per):
            here = take(visc, plane, y)
            near = [
                up_x(visc, plane, y),
                down_x(visc, plane, y),
                take(visc, plane, y + 1),
                take(visc, plane, y - 1),
                up_z(here),
                down_z(here),
            ]
            links = [here + other for other in near]
            scale = jnp.where(here > 0.0, RELAX / add_all(links), 0.0)
            for n in range(6):
                coefs[n, plane, tile(y), :] = links[n] * scale
            relax[plane, tile(y), :] = 2.0 * scale
            forcing[plane, tile(y), :] = take(dens, plane, y) * (-2.0 * GRAVITY * scale)
            rate[plane, tile(y), :] = PRESSURE_RATE * here

    def sweep(y, old, new):
        for plane in range(per):
            links = [coefs[n, plane, tile(y), :] for n in range(6)]
            scale = relax[plane, tile(y), :]
            pressure = take(old.at[3], plane, y)
            before = (
                down_x(old.at[3], plane, y),
                take(old.at[3], plane, y - 1),
                down_z(pressure),
            )
            changes = []
            for c in range(3):
                field = old.at[c]
                here = take(field, plane, y)
                near = [
                    up_x(field, plane, y),
                    down_x(field, plane, y),
                    take(field, plane, y + 1),
                    take(field, plane, y - 1),
                    up_z(here),
                    down_z(here),
                ]
                terms = [link * other for link, other in zip(links, near)]
                total = (terms[0] + terms[1]) + (terms[2] + terms[3])
                total = total + (terms[4] + terms[5])
                rest = (1.0 - RELAX) * here - scale * (pressure - before[c])
                if c == 2:
                    rest = rest + forcing[plane, tile(y), :]
                changes.append(near[2 * c] - here)
                store(new.at[c], plane, y, total + rest)
            pressed = pressure - rate[plane, tile(y), :] * add_all(changes)
            store(new.at[3], plane, y, pressed)

    return prepare, sweep


def kept_rows(size_y):
    width = SWEEPS
    return (
        ((width, size_y),),
        ((width + 1, width), (size_y - 1, width)),
        ((width, width + 1), (size_y - 1, width + 1)),
    )


def kept_copies(pairs, size_y, done):
    copies = []
    for (source, target), strips in zip(pairs, kept_rows(size_y)):
        for begin, rows in strips:
            span = (slice(None),) * 3 + (pl.ds(begin * SUBLANES, rows * SUBLANES),)
            copies.append(
                pltpu.make_async_copy(source.at[span], target.at[span], done.at[len(copies)])
            )
    return copies


def inner_body(vel, pres, visc, dens, low_x, high_x, _, even_out, odd_out, cells_out, *work):
    blocks, sides_x, even, odd, cells, coefs, relax, forcing, rate, done, more = work
    size_x, size_y, size_z = blocks.shape[1:]
    width = SWEEPS
    inputs = (
        (visc, blocks.at[4]),
        (dens, blocks.at[5]),
        (low_x, sides_x.at[0]),
        (high_x, sides_x.at[1]),
        (vel, blocks.at[0:3]),
        (pres, blocks.at[3]),
    )
    copies = [
        pltpu.make_async_copy(there, here, done.at[n]) for n, (there, here) in enumerate(inputs)
    ]
    for copy in copies:
        copy.start()
    targets = [even.at[n] for n in range(4)] + [cells.at[n] for n in range(2)]

    def lay_out(f):
        for i in range(size_x):
            for y in range(0, size_y, SUBLANES):
                value = blocks[f, i, y : y + SUBLANES, :]
                put(targets[f], i + width, y + width, SUBLANES, value)
        for side, begin in enumerate((0, width + size_x)):
            for i in range(width):
                for y in range(0, size_y, SUBLANES):
                    value = sides_x[side, f, i, y : y + SUBLANES, :]
                    put(targets[f], begin + i, y + width, SUBLANES, value)

    for copy in copies[:4]:
        copy.wait()
    lay_out(4)
    lay_out(5)
    sends = kept_copies(((even, even_out), (odd, odd_out), (cells, cells_out)), size_y, more)
    for send in sends[3:]:
        send.start()

    prepare, sweep = row_work(cells, coefs, relax, forcing, rate)

    def prepare_row(y, carry):
        prepare(y)
        return carry

    first, last = width + 1, width + size_y - 1
    lax.fori_loop(first, last, prepare_row, 0, unroll=2)
    for copy in copies[4:]:
        copy.wait()
    for f in range(4):
        lay_out(f)
    early, late = (sends[1:3], sends[:1]) if SWEEPS % 2 == 0 else (sends[:1], sends[1:3])
    for step in range(SWEEPS):
        old, new = (odd, even) if step % 2 else (even, odd)
        if step == SWEEPS - 1:
            for send in early:
                send.start()

        def sweep_row(y, carry, old=old, new=new):
            sweep(y, old, new)
            return carry

        lax.fori_loop(first + step, last - step, sweep_row, 0, unroll=2)
    for send in late:
        send.start()
    for send in sends:
        send.wait()


def inner_sweeps(velocity, pressure, cell_visc, cell_dens, low_x, high_x, after):
    size_x, size_y, size_z = cell_visc.shape
    width = low_x.shape[1]
    per, rows = (size_x + 2 * width) // SUBLANES, (size_y + 2 * width) * SUBLANES
    block, cut = (per, rows, size_z), (per, size_z // LANES, rows, LANES)
    shapes = [(4,) + cut, (4,) + cut, (2,) + cut]
    anywhere = pl.BlockSpec(memory_space=pl.ANY)
    return pl.pallas_call(
        inner_body,
        out_shape=tuple(jax.ShapeDtypeStruct(shape, f32) for shape in shapes),
        in_specs=[anywhere] * 7,
        out_specs=(anywhere,) * 3,
        scratch_shapes=[
            pltpu.VMEM((6,) + cell_visc.shape, f32),
            pltpu.VMEM((2,) + low_x.shape, f32),
        ]
        + [pltpu.VMEM(shape, f32) for shape in shapes]
        + [
            pltpu.VMEM((6,) + block, f32),
            pltpu.VMEM(block, f32),
            pltpu.VMEM(block, f32),
            pltpu.VMEM(block, f32),
            pltpu.SemaphoreType.DMA((6,)),
            pltpu.SemaphoreType.DMA((5,)),
        ],
        compiler_params=vmem_limit(40),
        cost_estimate=cost(25),
        name="inner_sweeps",
    )(*in_hbm(velocity, pressure, cell_visc, cell_dens, low_x, high_x), after)


def edge_body(even_in, odd_in, cells_in, low_y, high_y, vel_out, pres_out, *work):
    from_low, from_high, results, even, odd, cells, coefs, relax, forcing, rate, done, more = work
    size_x, size_y, size_z = results.shape[1:]
    width = SWEEPS
    long_y = size_y + 2 * width
    halos = [
        pltpu.make_async_copy(low_y, from_low, more.at[0]),
        pltpu.make_async_copy(high_y, from_high, more.at[1]),
    ]
    kept = kept_copies(((even_in, even), (odd_in, odd), (cells_in, cells)), size_y, done)
    for copy in (*halos, *kept[3:], *kept[:3]):
        copy.start()
    targets = [even.at[n] for n in range(4)] + [cells.at[n] for n in range(2)]

    def lay_out(chosen):
        for f in chosen:
            for x in (*range(width), *range(width + size_x, size_x + 2 * width)):
                for y in (0, width + size_y):
                    put(targets[f], x, y, width, jnp.zeros((width, size_z), f32))
            rows = slice(f * width, (f + 1) * width)
            for halo, begin in ((from_low, 0), (from_high, width + size_y)):
                for i in range(size_x):
                    put(targets[f], i + width, begin, width, halo[i, rows, :])
        for up, halo in ((True, from_low), (False, from_high)):
            for f, side, far_x, far_y, plane, row in corner_rows(up, size_x)[0]:
                if f in chosen:
                    x = width + size_x - 1 + far_x if side else width - far_x
                    y = width - far_y if up else width + size_y - 1 + far_y
                    put(targets[f], x, y, 1, halo[plane, row : row + 1, :])

    for copy in halos:
        copy.wait()
    lay_out((4, 5))
    for copy in kept[3:]:
        copy.wait()

    prepare, sweep = row_work(cells, coefs, relax, forcing, rate)

    def prepare_rows(n, carry):
        prepare(1 + n)
        prepare(long_y - 2 * width + n)
        return carry

    lax.fori_loop(0, 2 * width - 1, prepare_rows, 0)
    lay_out((0, 1, 2, 3))
    for copy in kept[:3]:
        copy.wait()
    for step in range(SWEEPS):
        old, new = (odd, even) if step % 2 else (even, odd)

        def sweep_rows(n, carry, old=old, new=new, step=step):
            sweep(1 + step + n, old, new)
            sweep(width + size_y - 1 - step + n, old, new)
            return carry

        lax.fori_loop(0, width, sweep_rows, 0, unroll=2)

    final = odd if SWEEPS % 2 else even
    outs = [vel_out.at[0], vel_out.at[1], vel_out.at[2], pres_out]
    sends = [pltpu.make_async_copy(results.at[n], out, done.at[n]) for n, out in enumerate(outs)]
    per, halves = even.shape[1:3]
    for field, send in enumerate(sends):
        for i in range(size_x):
            for y in range(0, size_y, SUBLANES):
                plane, lines = place(per, i + width, y + width, SUBLANES)
                for half in range(halves):
                    columns = slice(half * LANES, (half + 1) * LANES)
                    results[field, i, y : y + SUBLANES, columns] = final[
                        field, plane, half, lines, :
                    ]
        send.start()
    for send in sends:
        send.wait()


def edge_sweeps(even, odd, cells, low_y, high_y, size_x, size_y):
    per, halves, rows = even.shape[1:4]
    size_z = halves * LANES
    block = (per, rows, size_z)
    anywhere = pl.BlockSpec(memory_space=pl.ANY)
    return pl.pallas_call(
        edge_body,
        out_shape=(
            jax.ShapeDtypeStruct((3, size_x, size_y, size_z), f32),
            jax.ShapeDtypeStruct((size_x, size_y, size_z), f32),
        ),
        in_specs=[anywhere] * 5,
        out_specs=(anywhere,) * 2,
        scratch_shapes=[
            pltpu.VMEM(low_y.shape, f32),
            pltpu.VMEM(high_y.shape, f32),
            pltpu.VMEM((4, size_x, size_y, size_z), f32),
            pltpu.VMEM(even.shape, f32),
            pltpu.VMEM(odd.shape, f32),
            pltpu.VMEM(cells.shape, f32),
            pltpu.VMEM((6,) + block, f32),
            pltpu.VMEM(block, f32),
            pltpu.VMEM(block, f32),
            pltpu.VMEM(block, f32),
            pltpu.SemaphoreType.DMA((5,)),
            pltpu.SemaphoreType.DMA((2,)),
        ],
        compiler_params=vmem_limit(40),
        cost_estimate=cost(1),
        name="edge_sweeps",
    )(even, odd, cells, low_y, high_y)


def shift(value, axis, step):
    size = lax.axis_size(axis)
    pairs = [(i, i + step) for i in range(size) if 0 <= i + step < size]
    return lax.ppermute(value, axis, pairs)


def per_device(
    velocity,
    pressure,
    cell_visc,
    cell_dens,
    block_brick,
    block_counts,
    positions,
    start_visc,
    marker_dens,
):
    asked = lax.all_to_all(block_brick, "mark", 0, 0, tiled=True)
    fields = (velocity, pressure, cell_visc, cell_dens)
    to_low, to_high = pack_x(*fields)
    low_x, high_x = shift(to_high, "grid", 1), shift(to_low, "grid", -1)
    upward, downward = pack_y(*fields, low_x, high_x)
    low_y, high_y = shift(upward, "mark", 1), shift(downward, "mark", -1)

    picked = pick_bricks(asked, velocity)
    bricks = lax.all_to_all(picked, "mark", 0, 0, tiled=True)
    marker_visc, moments = marker_work(
        block_counts, positions, start_visc, marker_dens, bricks, upward
    )
    gathered = lax.all_to_all(moments, "mark", 0, 0, tiled=True)
    state = inner_sweeps(*fields, low_x, high_x, moments)
    velocity_next, pressure_next = edge_sweeps(*state, low_y, high_y, *pressure.shape[:2])
    visc_next, dens_next = settle(asked, gathered, cell_visc, cell_dens)
    return velocity_next, pressure_next, visc_next, dens_next, marker_visc


def solution(mesh):
    in_specs = (
        P(None, "grid", "mark", None),
        P("grid", "mark", None),
        P("grid", "mark", None),
        P("grid", "mark", None),
        P(("grid", "mark"), None),
        P(("grid", "mark"), None),
        P(("grid", "mark"), None, None, None),
        P(("grid", "mark"), None, None),
        P(("grid", "mark"), None, None),
    )
    out_specs = (
        P(None, "grid", "mark", None),
        P("grid", "mark", None),
        P("grid", "mark", None),
        P("grid", "mark", None),
        P(("grid", "mark"), None, None),
    )
    return jax.shard_map(
        per_device, mesh=mesh, in_specs=in_specs, out_specs=out_specs, check_vma=False
    )
```
